32 devices in a mesh: ch: 4 (over x, core), rows: 8 (over z, y).
Axes of the slice: x: 2, y: 2, z: 4, core: 2. Of those that a mesh axis runs over, the one named last changes fastest.
Arguments:
- fields: float32 [32, 3, 32, 128], P(None, None, 'rows'), may hold values from -6 to 6
- targets: float32 [3, 32, 32, 128], P(None, None, 'rows'), may hold values from -6 to 6
- fluid: int32 [32, 128], P('rows'), may hold values 0 or 1
- keyframes: int32 [32, 3], replicated, may hold values from 0 to 1, as said below
- w_in: float32 [3, 3, 4, 64], P(None, None, None, 'ch'), may hold values from -1 to 1
- w_mid: float32 [3, 3, 64, 64], P(None, None, None, 'ch'), may hold values from -0.25 to 0.25
- w_head: float32 [64, 2], P('ch'), may hold values from -0.75 to 0.75
- norm_params: float32 [4, 64], P(None, 'ch'), may hold values from 0.25 to 1.75
- first_in: float32 [3, 3, 4, 64], P(None, None, None, 'ch'), may hold values from -8.34465e-07 to 8.34465e-07
- first_mid: float32 [3, 3, 64, 64], P(None, None, None, 'ch'), may hold values from -8.34465e-07 to 8.34465e-07
- first_head: float32 [64, 2], P('ch'), may hold values from -8.34465e-07 to 8.34465e-07
- first_norm: float32 [4, 64], P(None, 'ch'), may hold values from -8.34465e-07 to 8.34465e-07
- second_in: float32 [3, 3, 4, 64], P(None, None, None, 'ch'), may hold values from 2.528317e-16 to 1.0113268e-15
- second_mid: float32 [3, 3, 64, 64], P(None, None, None, 'ch'), may hold values from 2.528317e-16 to 1.0113268e-15
- second_head: float32 [64, 2], P('ch'), may hold values from 2.528317e-16 to 1.0113268e-15
- second_norm: float32 [4, 64], P(None, 'ch'), may hold values from 2.528317e-16 to 1.0113268e-15
Outputs:
- new_in: float32 [3, 3, 4, 64], P(None, None, None, 'ch')
- new_mid: float32 [3, 3, 64, 64], P(None, None, None, 'ch')
- new_head: float32 [64, 2], P('ch')
- new_norm: float32 [4, 64], P(None, 'ch')
- moment_in: float32 [3, 3, 4, 64], P(None, None, None, 'ch')
- moment_mid: float32 [3, 3, 64, 64], P(None, None, None, 'ch')
- moment_head: float32 [64, 2], P('ch')
- moment_norm: float32 [4, 64], P(None, 'ch')
- square_in: float32 [3, 3, 4, 64], P(None, None, None, 'ch')
- square_mid: float32 [3, 3, 64, 64], P(None, None, None, 'ch')
- square_head: float32 [64, 2], P('ch')
- square_norm: float32 [4, 64], P(None, 'ch')
- grad_norm: float32 [], replicated
- loss_sum: float32 [], replicated
- valid_count: float32 [], replicated
The draws below stay inside these ranges and needn't reach their ends.
Inputs may be any that keep to these rules, and one draw needn't show every extreme that they name: `keyframes`: every sample is supervised at the last step.
All inputs are finite; a program needn't handle non-finite values. No bound on the sum of `fluid` on one device may be relied on, other than what follows from the above.
Results may differ from the reference program's by a relative error of at most 0.0003.
The reference program's roundings to bfloat16 on the way (of `features`) count: a program that leaves them out, or rounds other values in their place, can miss the bound.
Values may be sent and summed in bfloat16 or wider, within the bound.
A program may use at most 192 MiB of HBM per device.

```python
import math
import jax
import jax.numpy as jnp
from jax import lax

WIDTH = 64
GROUPS = 8
CIN = 4
COLS = 128
BATCH = 32
STEPS = 3
JACOBI = 3
STEP_NUM = 10
GRID_ROWS = 32
NPARAMS = 39552


def draw_keyframes(key, part):
    key = jax.random.fold_in(key, 11)
    marks = jax.random.randint(key, (BATCH, STEPS), 0, 2).astype(jnp.int32)
    return marks.at[:, STEPS - 1].set(1)


def place_ends(values, own_key, smallest, largest):
    extent = values.shape
    spot = [jax.random.randint(jax.random.fold_in(own_key, axis), (), 0, extent[axis]) for axis in range(len(extent))]
    values = values.at[tuple(spot)].set(smallest)
    longest = extent.index(max(extent))
    spot[longest] = (spot[longest] + 1) % extent[longest]
    return values.at[tuple(spot)].set(largest)


def steps_of(stream_key, extent, shards, low, largest):
    loudness, own = 1.0, jax.random.fold_in(stream_key, 6)
    for position, parts in shards:
        heights = jnp.exp(jax.random.uniform(jax.random.fold_in(own, position), (parts,), jnp.float32, low / len(shards), largest / len(shards)))
        loudness = loudness * jnp.repeat(heights, extent[position] // parts).reshape([-1 if axis == position else 1 for axis in range(len(extent))])
    return loudness


def bell_draw(rng, dims, scale, reach, pieces=(), kind=jnp.bfloat16):
    array = jax.random.normal(rng, dims, jnp.float32) * scale
    if len(pieces) > 0:
        array = steps_of(rng, dims, pieces, -0.22, 0.18) * array
    return jnp.clip(array, min=-reach, max=reach).astype(kind)


def setup_inputs(seed: int = 0) -> dict:
    seeds = jax.random.split(jax.random.key(seed), 17)
    return {
        "fields": bell_draw(seeds[0], (BATCH, 3, GRID_ROWS, COLS), 1.0, 6.0, ((2, 8),), jnp.float32),
        "targets": bell_draw(seeds[1], (STEPS, BATCH, GRID_ROWS, COLS), 1.0, 6.0, ((2, 8),), jnp.float32),
        "fluid": place_ends((jax.random.randint(seeds[2], (GRID_ROWS, COLS), 0, 8) < 7).astype(jnp.int32), jax.random.fold_in(seeds[2], 1), 0, 1),
        "keyframes": draw_keyframes(jax.random.fold_in(seeds[16], 71), 0),
        "w_in": bell_draw(seeds[4], (3, 3, CIN, WIDTH), (9 * CIN) ** -0.5, 1.0, ((3, 4),), jnp.float32),
        "w_mid": bell_draw(seeds[5], (3, 3, WIDTH, WIDTH), (9 * WIDTH) ** -0.5, 0.25, ((3, 4),), jnp.float32),
        "w_head": bell_draw(seeds[6], (WIDTH, 2), WIDTH ** -0.5, 0.75, ((0, 4),), jnp.float32),
        "norm_params": jnp.clip(1.0 + 0.15 * jax.random.normal(seeds[7], (4, WIDTH), jnp.float32), 0.25, 1.75),
        "first_in": bell_draw(seeds[8], (3, 3, CIN, WIDTH), (0.0001 * NPARAMS ** -0.5 * 0.11), 8.344650268554688e-07, ((3, 4),), jnp.float32),
        "first_mid": bell_draw(seeds[9], (3, 3, WIDTH, WIDTH), (0.0001 * NPARAMS ** -0.5 * 0.11), 8.344650268554688e-07, ((3, 4),), jnp.float32),
        "first_head": bell_draw(seeds[10], (WIDTH, 2), (0.0001 * NPARAMS ** -0.5 * 0.11), 8.344650268554688e-07, ((0, 4),), jnp.float32),
        "first_norm": bell_draw(seeds[11], (4, WIDTH), (0.0001 * NPARAMS ** -0.5 * 0.11), 8.344650268554688e-07, ((1, 4),), jnp.float32),
        "second_in": jnp.clip(jnp.exp(math.log(1.0113268458355335e-15) - 1.3862944 * jax.random.uniform(seeds[12], (3, 3, CIN, WIDTH), jnp.float32) ** steps_of(seeds[12], (3, 3, CIN, WIDTH), ((3, 4),), -0.2, 0.2)), 2.5283171145888336e-16, 1.0113268458355335e-15),
        "second_mid": jnp.clip(jnp.exp(math.log(1.0113268458355335e-15) - 1.3862944 * jax.random.uniform(seeds[13], (3, 3, WIDTH, WIDTH), jnp.float32) ** steps_of(seeds[13], (3, 3, WIDTH, WIDTH), ((3, 4),), -0.2, 0.2)), 2.5283171145888336e-16, 1.0113268458355335e-15),
        "second_head": jnp.clip(jnp.exp(math.log(1.0113268458355335e-15) - 1.3862944 * jax.random.uniform(seeds[14], (WIDTH, 2), jnp.float32) ** steps_of(seeds[14], (WIDTH, 2), ((0, 4),), -0.2, 0.2)), 2.5283171145888336e-16, 1.0113268458355335e-15),
        "second_norm": jnp.clip(jnp.exp(math.log(1.0113268458355335e-15) - 1.3862944 * jax.random.uniform(seeds[15], (4, WIDTH), jnp.float32) ** steps_of(seeds[15], (4, WIDTH), ((1, 4),), -0.2, 0.2)), 2.5283171145888336e-16, 1.0113268458355335e-15),
    }


TIME_STEP = 0.5
COURANT = 0.8
FORCE_WEIGHT = 0.5
NORM_EPS = 1e-05
CLIP = 0.0001
BETA_ONE = 0.9
BETA_TWO = 0.999
ADAM_EPS = 1e-10
RATE = 0.1
GAIN_RATE = 0.6
DECAY = 0.01
HIGHEST = lax.Precision.HIGHEST

@jax.custom_vjp
def low(v):
    return lax.optimization_barrier(v.astype(jnp.bfloat16)).astype(jnp.float32)

@jax.custom_vjp
def low_back(v):
    return v

def low_keep(v):
    return (low(v), None)

def low_pass(kept, grad):
    return (grad,)

def back_keep(v):
    return (v, None)

def back_low(kept, grad):
    return (low(grad),)
low.defvjp(low_keep, low_pass)
low_back.defvjp(back_keep, back_low)

def col_pad(field):
    return jnp.pad(field, ((0, 0), (0, 0), (0, 0), (1, 1)))

def row_pad(field):
    return jnp.pad(field, ((0, 0), (0, 0), (1, 1), (0, 0)))

def quadratic(shift):
    return (0.5 * shift * (shift + 1.0), 1.0 - shift * shift, 0.5 * shift * (shift - 1.0))

def advect_local(padded, u_forced, v_forced):
    row_count = u_forced.shape[2]
    col_count = u_forced.shape[3]
    weight_rows = quadratic(COURANT * jnp.tanh(u_forced))
    weight_cols = quadratic(COURANT * jnp.tanh(v_forced))
    wide = col_pad(padded)
    output = jnp.zeros(padded.shape[:2] + (row_count, col_count), jnp.float32)
    for row_off in range(3):
        for col_off in range(3):
            window = wide[:, :, row_off:row_off + row_count, col_off:col_off + col_count]
            output = output + weight_rows[row_off] * weight_cols[col_off] * window
    return output

def diverge_local(u_padded, v_field):
    wide = col_pad(v_field)
    return 0.5 * (u_padded[:, :, 2:] - u_padded[:, :, :-2] + wide[:, :, :, 2:] - wide[:, :, :, :-2])

def neighbours(padded):
    wide = col_pad(padded[:, :, 1:-1])
    return padded[:, :, 2:] + padded[:, :, :-2] + wide[:, :, :, 2:] + wide[:, :, :, :-2]

def jacobi_local(fluid_field, padded, divergence):
    return 0.25 * fluid_field * (neighbours(padded) - divergence)

def project_local(fluid_field, padded, u_field, v_field):
    wide = col_pad(padded[:, :, 1:-1])
    u_new = fluid_field * (u_field - 0.5 * (padded[:, :, 2:] - padded[:, :, :-2]))
    v_new = fluid_field * (v_field - 0.5 * (wide[:, :, :, 2:] - wide[:, :, :, :-2]))
    return (u_new, v_new)

def conv_layer(padded_in, weight):
    row_count = padded_in.shape[2] - 2
    col_count = padded_in.shape[3]
    wide = col_pad(padded_in)
    output = jnp.zeros((padded_in.shape[0], weight.shape[3], row_count, col_count), jnp.float32)
    for row_off in range(3):
        for col_off in range(3):
            window = wide[:, :, row_off:row_off + row_count, col_off:col_off + col_count]
            output = output + jnp.einsum('bcrw,cd->bdrw', window, weight[row_off, col_off], precision=HIGHEST)
    return output

def group_norm(conv_out, gain, bias):
    batch_size, chans, row_count, col_count = conv_out.shape
    grouped = conv_out.reshape(batch_size, GROUPS, chans // GROUPS, row_count, col_count)
    average = lax.optimization_barrier(jnp.mean(grouped, axis=(2, 3, 4), keepdims=True))
    variance = lax.optimization_barrier(jnp.mean((grouped - average) ** 2, axis=(2, 3, 4), keepdims=True))
    normed = ((grouped - average) * lax.rsqrt(variance + NORM_EPS)).reshape(conv_out.shape)
    return normed * gain[None, :, None, None] + bias[None, :, None, None]

def physics_step(params, current, fluid_field, target, key_weights):
    w_in, w_mid, w_head, gains = params
    features = low(jnp.concatenate([current, fluid_field], axis=1))
    conv_one = low_back(conv_layer(row_pad(features), low(w_in)))
    hidden = jax.nn.silu(group_norm(conv_one, gains[0], gains[1]))
    conv_two = low_back(conv_layer(row_pad(low(hidden)), low(w_mid)))
    mixed_out = hidden + jax.nn.silu(group_norm(conv_two, gains[2], gains[3]))
    logits = low_back(jnp.einsum('bcrw,ck->bkrw', low(mixed_out), low(w_head), precision=HIGHEST))
    forcing = jnp.tanh(logits)
    u_forced = current[:, 1:2] + TIME_STEP * forcing[:, 0:1]
    v_forced = current[:, 2:3] + TIME_STEP * forcing[:, 1:2]
    advected = advect_local(row_pad(jnp.concatenate([current[:, 0:1], u_forced, v_forced], axis=1)), u_forced, v_forced)
    divergence = diverge_local(row_pad(advected[:, 1:2]), advected[:, 2:3])
    pressure = -0.25 * fluid_field * divergence
    for sweep in range(JACOBI - 1):
        pressure = jacobi_local(fluid_field, row_pad(pressure), divergence)
    u_new, v_new = project_local(fluid_field, row_pad(pressure), advected[:, 1:2], advected[:, 2:3])
    next_state = jnp.concatenate([advected[:, 0:1], u_new, v_new], axis=1)
    misfit = advected[:, 0:1] - target[:, None]
    step_loss = FORCE_WEIGHT * jnp.sum(forcing * forcing) + jnp.sum(key_weights[:, None, None, None] * misfit * misfit)
    return (next_state, step_loss)

def adam_update(weight, grad, moment, square, rate, decay):
    moment = BETA_ONE * moment + (1.0 - BETA_ONE) * grad
    square = BETA_TWO * square + (1.0 - BETA_TWO) * grad * grad
    fix_one = 1.0 - BETA_ONE ** STEP_NUM
    fix_two = 1.0 - BETA_TWO ** STEP_NUM
    updated = weight - rate * (moment / fix_one / (jnp.sqrt(square / fix_two) + ADAM_EPS) + decay * weight)
    return (updated, moment, square)

def reference(fields, targets, fluid, keyframes, w_in, w_mid, w_head, norm_params, first_in, first_mid, first_head, first_norm, second_in, second_mid, second_head, second_norm):
    batch_size = fields.shape[0]
    fluid_map = fluid.astype(jnp.float32)
    fluid_field = jnp.broadcast_to(fluid_map[None, None], (batch_size, 1) + fluid_map.shape)
    key_weights = keyframes.astype(jnp.float32)
    valid_count = jnp.sum(key_weights) * (GRID_ROWS * COLS)

    def rollout(params):
        current = fields
        accumulated = jnp.zeros((), jnp.float32)
        for step_index in range(STEPS):
            current, step_loss = jax.checkpoint(physics_step)(params, current, fluid_field, targets[step_index], key_weights[:, step_index])
            accumulated = accumulated + step_loss
        return accumulated
    params = (w_in, w_mid, w_head, norm_params)
    loss_sum, pullback = jax.vjp(rollout, params)
    grads = pullback(jnp.ones((), jnp.float32) / valid_count)[0]
    squares = jnp.zeros((), jnp.float32)
    for grad in grads:
        squares = squares + jnp.sum(grad * grad)
    grad_norm = jnp.sqrt(squares)
    factor = CLIP / jnp.maximum(grad_norm, CLIP)
    firsts = (first_in, first_mid, first_head, first_norm)
    seconds = (second_in, second_mid, second_head, second_norm)
    rates = (RATE, RATE, RATE, GAIN_RATE)
    decays = (DECAY, DECAY, DECAY, 0.0)
    results = [adam_update(params[index], grads[index] * factor, firsts[index], seconds[index], rates[index], decays[index]) for index in range(4)]
    return (results[0][0], results[1][0], results[2][0], results[3][0], results[0][1], results[1][1], results[2][1], results[3][1], results[0][2], results[1][2], results[2][2], results[3][2], grad_norm, loss_sum, valid_count)
```

```python
import functools

import jax
import jax.numpy as jnp
from jax import lax
from jax.experimental import pallas as pl
from jax.experimental.pallas import tpu as pltpu
from jax.sharding import PartitionSpec as P

GROUPS = 8
JACOBI = 3
STEP_NUM = 10
TIME_STEP = 0.5
COURANT = 0.8
FORCE_WEIGHT = 0.5
NORM_EPS = 1e-05
CLIP = 0.0001
BETA_ONE = 0.9
BETA_TWO = 0.999
ADAM_EPS = 1e-10
RATE = 0.1
GAIN_RATE = 0.6
DECAY = 0.01

MESH = pl.DeviceIdType.MESH
F32 = jnp.float32
BF16 = jnp.bfloat16
LANES = 128
GSIZE = 8
TAPS = 3
SAVED = 11
NT = (((1,), (1,)), ((), ()))


def lane_ids(shape):
    return lax.broadcasted_iota(jnp.int32, shape, len(shape) - 1)


def row_ids(shape):
    return lax.broadcasted_iota(jnp.int32, shape, 0)


def from_left(x):
    return jnp.where(lane_ids(x.shape) == 0, 0.0, pltpu.roll(x, 1, 1))


def from_right(x):
    size = x.shape[1]
    return jnp.where(lane_ids(x.shape) == size - 1, 0.0, pltpu.roll(x, size - 1, 1))


def from_above(x):
    return jnp.where(row_ids(x.shape) == 0, 0.0, pltpu.roll(x, 1, 0))


def from_below(x):
    size = x.shape[0]
    return jnp.where(row_ids(x.shape) == size - 1, 0.0, pltpu.roll(x, size - 1, 0))


def diff_rows(x):
    return from_below(x) - from_above(x)


def diff_cols(x):
    return from_right(x) - from_left(x)


def around(x):
    return from_below(x) + from_above(x) + from_right(x) + from_left(x)


def quadratic(s):
    return (0.5 * s * (s + 1.0), 1.0 - s * s, 0.5 * s * (s - 1.0))


def quadratic_slope(s):
    return (s + 0.5, -2.0 * s, s - 0.5)


def dot(a, b):
    return jnp.dot(a, b, preferred_element_type=F32)


def dot_nt(a, b):
    return lax.dot_general(a, b, NT, preferred_element_type=F32)


def row_pair(ref, i, extra=None):
    depth = ref.shape[1] * TAPS
    sides = []
    for k in range(2):
        side = ref[pl.ds(i + k, TAPS)].reshape(depth, LANES)
        if extra is not None:
            side = jnp.concatenate([side, extra[i + k]], axis=0)
        sides.append(side)
    return jnp.concatenate(sides, axis=1)


def combine(p, height):
    out = []
    for k in range(2):
        part = p[:, k * LANES : (k + 1) * LANES]
        out.append(
            part[height : 2 * height]
            + from_left(part[:height])
            + from_right(part[2 * height : 3 * height])
        )
    return out


def group_sum(x):
    return jnp.sum(jnp.sum(x.reshape(-1, GSIZE, LANES), axis=1, keepdims=True), axis=2, keepdims=True)


def spread(x, width):
    return jnp.broadcast_to(x, (x.shape[0], GSIZE, LANES)).reshape(width, LANES)


class Sizes:
    def __init__(self, mesh, fields_shape, targets_shape, co):
        self.ch = mesh.shape["ch"]
        self.rows = mesh.shape["rows"]
        self.batch = fields_shape[0]
        self.local = fields_shape[2]
        self.grid = self.local * self.rows
        self.cols = fields_shape[3]
        self.steps = targets_shape[0]
        self.co = co
        self.width = co * self.ch
        self.per_rows = self.batch // self.rows
        self.ways = self.ch if self.per_rows == self.ch else 1
        assert self.per_rows == self.ways and self.batch % self.rows == 0
        assert self.cols == LANES
        slot = self.grid * self.width * LANES * 20
        self.slots = self.steps if slot * self.steps < (24 << 20) else 1
        self.mid_lanes = TAPS * TAPS * self.width
        self.lanes = -(-(self.mid_lanes + 64) // LANES) * LANES
        self.tiles = self.lanes // LANES
        assert self.width == 64


IN_AT = 64
HEAD_AT = IN_AT + 36
NORM_AT = HEAD_AT + 2
LOSS_AT = NORM_AT + 4


def train_kernel(sz, fields, targets, fluid, keyframes, w_in, w_mid, w_head, norms, out, out_total, *scratch):
    z = dict(zip(scratch_of(sz), scratch))
    f_stage = z["f_stage"]
    t_stage = z["t_stage"]
    m_stage = z["m_stage"]
    w_all = z["w_all"]
    small = z["small"]
    w_fwd = z["w_fwd"]
    w_bwd = z["w_bwd"]
    v_fwd = z["v_fwd"]
    v_bwd = z["v_bwd"]
    head = z["head"]
    gains = z["gains"]
    current = z["current"]
    states = z["states"]
    mask = z["mask"]
    target = z["target"]
    feat32 = z["feat32"]
    feat = z["feat"]
    conv = z["conv"]
    slope = z["slope"]
    hidden = z["hidden"]
    hidden_low = z["hidden_low"]
    mixed_low = z["mixed_low"]
    logits = z["logits"]
    saved = z["saved"]
    dy = z["dy"]
    glog32 = z["glog32"]
    glog = z["glog"]
    g_pad = z["g_pad"]
    g_taps = z["g_taps"]
    gs_rows = z["gs_rows"]
    grad_state = z["grad_state"]
    d_mid = z["d_mid"]
    d_in = z["d_in"]
    d_head = z["d_head"]
    d_norm = z["d_norm"]
    loss = z["loss"]
    packed = z["packed"]
    part = z["part"]
    rs_one = z["rs_one"]
    rs_two = z["rs_two"]
    fin = z["fin"]
    ssq = z["ssq"]
    local_sem = z["local_sem"]
    f_send = z["f_send"]
    f_recv = z["f_recv"]
    t_send = z["t_send"]
    t_recv = z["t_recv"]
    m_send = z["m_send"]
    m_recv = z["m_recv"]
    w_send = z["w_send"]
    w_recv = z["w_recv"]
    a_send = z["a_send"]
    a_recv = z["a_recv"]
    b_send = z["b_send"]
    b_recv = z["b_recv"]
    c_send = z["c_send"]
    c_recv = z["c_recv"]
    n_send = z["n_send"]
    n_recv = z["n_recv"]
    inv_std = z["inv_std"]
    c = lax.axis_index("ch")
    r = lax.axis_index("rows")
    width, grid, steps = sz.width, sz.grid, sz.steps
    co = sz.co

    def row_peer(k):
        return lax.rem(r + k, sz.rows)

    def ch_peer(k):
        return lax.rem(c + k, sz.ch)

    def sample_of(row):
        return row * sz.per_rows + (c if sz.ways > 1 else 0)

    def to(ch, row):
        return (ch, row)

    peers = sz.rows - 1 + sz.ch - 1
    if peers:
        barrier = pltpu.get_barrier_semaphore()
        for k in range(1, sz.rows):
            pl.semaphore_signal(barrier, inc=1, device_id=to(c, row_peer(k)), device_id_type=MESH)
        for k in range(1, sz.ch):
            pl.semaphore_signal(barrier, inc=1, device_id=to(ch_peer(k), r), device_id_type=MESH)

    small[...] = jnp.zeros_like(small)
    for ky in range(TAPS):
        for kx in range(TAPS):
            at = IN_AT + (ky * TAPS + kx) * 4
            small[at : at + 4, 0:co] = w_in[ky, kx]
    small[HEAD_AT : HEAD_AT + 2, 0:co] = w_head[...]
    small[NORM_AT : NORM_AT + 4, 0:co] = norms[...]
    blocks = [
        w_mid[ky, kx] for kx in range(TAPS) for ky in range(TAPS)
    ]
    blocks.append(jnp.transpose(small[...])[0:co, IN_AT : IN_AT + 64])
    mine = jnp.concatenate(blocks, axis=1)
    w_all[pl.ds(pl.multiple_of(c * co, 8), co), :] = mine

    if peers:
        pl.semaphore_wait(barrier, peers)

    copies = []

    def remote(src, dst, send, recv, where):
        return pltpu.make_async_remote_copy(
            src_ref=src, dst_ref=dst, send_sem=send, recv_sem=recv, device_id=where, device_id_type=MESH
        )

    def weights_copy(k, shard):
        rows = pl.ds(pl.multiple_of(shard * co, 8), co)
        return remote(w_all.at[rows], w_all.at[rows], w_send.at[k], w_recv.at[shard], to(ch_peer(k), r))

    def field_copy(k, row, src):
        return remote(fields.at[src], f_stage.at[row], f_send.at[k], f_recv.at[row], to(c, row_peer(k)))

    def mask_copy(k, row):
        return remote(fluid, m_stage.at[row], m_send.at[k], m_recv.at[row], to(c, row_peer(k)))

    def target_copy(k, row, src):
        return remote(targets.at[:, src], t_stage.at[row], t_send.at[k], t_recv.at[row], to(c, row_peer(k)))

    own = [
        pltpu.make_async_copy(fields.at[sample_of(r)], f_stage.at[r], local_sem.at[0]),
        pltpu.make_async_copy(targets.at[:, sample_of(r)], t_stage.at[r], local_sem.at[1]),
        pltpu.make_async_copy(fluid, m_stage.at[r], local_sem.at[2]),
    ]
    for copy in own:
        copy.start()
    for k in range(1, sz.ch):
        copy = weights_copy(k, c)
        copy.start()
        copies.append(copy)
    for k in range(1, sz.rows):
        copy = field_copy(k, r, sample_of(row_peer(k)))
        copy.start()
        copies.append(copy)
    for k in range(1, sz.rows):
        copy = mask_copy(k, r)
        copy.start()
        copies.append(copy)
    for k in range(1, sz.rows):
        copy = target_copy(k, r, sample_of(row_peer(k)))
        copy.start()
        copies.append(copy)

    for ref in (feat, hidden_low):
        for slot in range(sz.slots):
            ref[slot, 0] = jnp.zeros_like(ref[slot, 0])
            ref[slot, grid + 1] = jnp.zeros_like(ref[slot, 0])
    g_pad[0] = jnp.zeros_like(g_pad[0])
    g_pad[grid + 1] = jnp.zeros_like(g_pad[0])
    feat32[...] = jnp.zeros_like(feat32)
    glog32[...] = jnp.zeros_like(glog32)
    for ref in (d_mid, d_in, d_head, d_norm, loss):
        ref[...] = jnp.zeros_like(ref)

    for k in range(1, sz.ch):
        weights_copy(k, ch_peer(k)).wait_recv()
    for kx in range(TAPS):
        w_fwd[kx * width : (kx + 1) * width, :] = w_all[:, kx * TAPS * width : (kx + 1) * TAPS * width].astype(BF16)
    tail = w_all[:, sz.lanes - LANES : sz.lanes]
    tail_t = jnp.transpose(tail)
    for kx in range(TAPS):
        parts = []
        for ky in range(TAPS):
            at = ((2 - kx) * TAPS + 2 - ky) * width
            parts.append(jnp.transpose(w_all[:, at : at + width]))
        if kx == 1:
            pad = jnp.zeros((width, 14), F32)
            parts.append(jnp.concatenate([tail[:, HEAD_AT : HEAD_AT + 2], pad], axis=1))
        else:
            parts.append(jnp.zeros((width, 16), F32))
        w_bwd[kx * width : (kx + 1) * width, :] = jnp.concatenate(parts, axis=1).astype(BF16)
    parts = []
    for ky in range(TAPS):
        at = IN_AT + ky * 12
        parts.append(jnp.concatenate([tail[:, at : at + 12], jnp.zeros((width, 4), F32)], axis=1))
    v_fwd[...] = jnp.concatenate(parts, axis=1).astype(BF16)
    parts = []
    for kx in range(TAPS):
        line = []
        for ky in range(TAPS):
            at = IN_AT + ((2 - ky) * TAPS + 2 - kx) * 4
            line.append(tail_t[at : at + 4])
        parts.append(jnp.concatenate(line, axis=1))
        parts.append(jnp.zeros((4, TAPS * width), F32))
    v_bwd[...] = jnp.concatenate(parts, axis=0).astype(BF16)
    head[...] = jnp.concatenate([tail_t[HEAD_AT : HEAD_AT + 2], jnp.zeros((14, width), F32)], axis=0).astype(BF16)
    for k in range(4):
        gains[k] = jnp.broadcast_to(tail[:, NORM_AT + k : NORM_AT + k + 1], (width, LANES))

    for k in range(1, sz.rows):
        field_copy(k, row_peer(k), 0).wait_recv()
        mask_copy(k, row_peer(k)).wait_recv()
    own[0].wait()
    own[2].wait()
    for row in range(sz.rows):
        at = pl.ds(row * sz.local, sz.local)
        for q in range(3):
            current[q, at, :] = f_stage[row, q]
        mask[at, :] = m_stage[row].astype(F32)
    for k in range(1, sz.rows):
        target_copy(k, row_peer(k), 0).wait_recv()
    own[1].wait()
    for row in range(sz.rows):
        at = pl.ds(row * sz.local, sz.local)
        for t in range(steps):
            target[t, at, :] = t_stage[row, t]

    marks = keyframes[...].astype(F32)
    valid = jnp.sum(jnp.sum(marks, axis=1, keepdims=True), axis=0, keepdims=True) * float(grid * sz.cols)
    inv_count = 1.0 / valid
    picked = jnp.where(lane_ids(marks.shape) == sample_of(r), marks, 0.0)
    marked = jnp.sum(picked, axis=1, keepdims=True)

    def key_of(t):
        return jnp.sum(jnp.where(row_ids(marked.shape) == t, marked, 0.0), axis=0, keepdims=True)

    def conv_and_stats(x_ref, w, height, store):
        zero = jnp.zeros((width, LANES), F32)

        def body(it, carry):
            base, total, squares = carry
            for k in range(2):
                i = it * 4 + k * 2
                p = dot(w[...], row_pair(x_ref, i))
                rows = combine(p, width) if height else [p[:, :LANES], p[:, LANES:]]
                if k == 0:
                    base = jnp.where(it == 0, rows[0], base)
                for j in range(2):
                    store[i + j] = rows[j]
                    d = rows[j] - base
                    total = total + d
                    squares = squares + d * d
            return base, total, squares

        base, total, squares = lax.fori_loop(0, grid // 4, body, (zero, zero, zero))
        lane_mean = base + total * (1.0 / grid)
        lane_dev = squares - total * total * (1.0 / grid)
        count = float(GSIZE * LANES)
        mean = spread(group_sum(lane_mean) * (1.0 / count), width)
        d = lane_mean - mean
        var = spread(group_sum(lane_dev + grid * d * d) * (1.0 / (count * grid)), width)
        inv = lax.rsqrt(var + NORM_EPS)
        return mean, inv

    def silu_parts(y):
        s = 0.5 * jnp.tanh(0.5 * y) + 0.5
        h = y * s
        return h, s + h - h * s

    def step_forward(t, slot, first):
        if sz.slots == 1:
            for q in range(3):
                if first:
                    states[t, q] = current[q]
                else:
                    current[q] = states[t, q]
        x = [current[q] for q in range(3)]
        planes = [x[0], x[1], x[2], mask[...]]
        for q in range(4):
            for kx, plane in enumerate((from_left(planes[q]), planes[q], from_right(planes[q]))):
                feat32[pl.ds(kx * 4 + q, grid, stride=16), :] = plane

        def pack(it, carry):
            for k in range(4):
                i = it * 4 + k
                feat[slot, i + 1] = feat32[pl.ds(pl.multiple_of(i * 16, 16), 16), :].astype(BF16)
            return carry

        lax.fori_loop(0, grid // 4, pack, 0)

        mean, inv = conv_and_stats(feat.at[slot], v_fwd, 0, conv.at[slot, 0])
        off = mean * inv
        gain, bias = gains[0], gains[1]
        inv_std[0, slot] = inv

        def norm_one(it, carry):
            for k in range(2):
                i = it * 2 + k
                n = conv[slot, 0, i] * inv - off
                h, sl = silu_parts(n * gain + bias)
                conv[slot, 0, i] = n
                slope[slot, 0, i] = sl
                hidden[i] = h
                hidden_low[slot, i + 1] = h.astype(BF16)
            return carry

        lax.fori_loop(0, grid // 2, norm_one, 0)

        mean, inv = conv_and_stats(hidden_low.at[slot], w_fwd, 1, conv.at[slot, 1])
        off = mean * inv
        gain, bias = gains[2], gains[3]
        inv_std[1, slot] = inv

        def norm_two(it, carry):
            i = it * 2
            lows = []
            for k in range(2):
                n = conv[slot, 1, i + k] * inv - off
                h, sl = silu_parts(n * gain + bias)
                conv[slot, 1, i + k] = n
                slope[slot, 1, i + k] = sl
                low = (hidden[i + k] + h).astype(BF16)
                mixed_low[slot, i + k] = low
                lows.append(low)
            p = dot(head[...], jnp.concatenate(lows, axis=1))
            for k in range(2):
                logits[0, pl.ds(i + k, 1), :] = p[0:1, k * LANES : (k + 1) * LANES]
                logits[1, pl.ds(i + k, 1), :] = p[1:2, k * LANES : (k + 1) * LANES]
            return carry

        lax.fori_loop(0, grid // 2, norm_two, 0)

        f0, f1 = jnp.tanh(logits[0]), jnp.tanh(logits[1])
        u1 = x[1] + TIME_STEP * f0
        v1 = x[2] + TIME_STEP * f1
        sy = COURANT * jnp.tanh(u1)
        sx = COURANT * jnp.tanh(v1)
        wy, wx = quadratic(sy), quadratic(sx)
        dwy, dwx = quadratic_slope(sy), quadratic_slope(sx)
        moved = []
        for n, q in enumerate((x[0], u1, v1)):
            val = jnp.zeros_like(q)
            by_y = jnp.zeros_like(q)
            by_x = jnp.zeros_like(q)
            for a, line in enumerate((from_above(q), q, from_below(q))):
                windows = (from_left(line), line, from_right(line))
                along = wx[0] * windows[0] + wx[1] * windows[1] + wx[2] * windows[2]
                slant = dwx[0] * windows[0] + dwx[1] * windows[1] + dwx[2] * windows[2]
                val = val + wy[a] * along
                by_y = by_y + dwy[a] * along
                by_x = by_x + wy[a] * slant
            moved.append(val)
            saved[slot, 4 + n] = by_y
            saved[slot, 7 + n] = by_x
        solid = mask[...]
        rho2, u2, v2 = moved
        div = 0.5 * (diff_rows(u2) + diff_cols(v2))
        press = -0.25 * solid * div
        for _ in range(JACOBI - 1):
            press = 0.25 * solid * (around(press) - div)
        if first:
            current[0] = rho2
            current[1] = solid * (u2 - 0.5 * diff_rows(press))
            current[2] = solid * (v2 - 0.5 * diff_cols(press))
        pull = key_of(t) * (rho2 - target[t])
        if first:
            loss[...] += FORCE_WEIGHT * (f0 * f0 + f1 * f1) + pull * (rho2 - target[t])
        saved[slot, 0] = f0
        saved[slot, 1] = f1
        saved[slot, 2] = sy
        saved[slot, 3] = sx
        saved[slot, 10] = pull

    def forward_body(t, carry):
        step_forward(t, t if sz.slots > 1 else 0, True)
        return carry

    lax.fori_loop(0, steps, forward_body, 0)

    def norm_back(k, inv, sums_d, sums_n):
        gain = gains[k]
        scale = 1.0 / float(GSIZE * LANES * grid)
        m1 = spread(group_sum(sums_d * gain) * scale, width)
        m2 = spread(group_sum(sums_n * gain) * scale, width)
        d_norm[k] += sums_n
        d_norm[k + 1] += sums_d
        return inv * gain, inv * m1, inv * m2

    def step_backward(t, slot, last):
        zero = jnp.zeros((width, LANES), F32)
        solid = mask[...]
        sy, sx = saved[slot, 2], saved[slot, 3]
        f0, f1 = saved[slot, 0], saved[slot, 1]
        grad_rho = grad_state[0] + 2.0 * inv_count * saved[slot, 10]
        gu = solid * grad_state[1]
        gv = solid * grad_state[2]
        g_press = 0.5 * (diff_rows(gu) + diff_cols(gv))
        g_div = jnp.zeros_like(g_press)
        for _ in range(JACOBI - 1):
            term = 0.25 * solid * g_press
            g_div = g_div - term
            g_press = around(term)
        g_div = g_div - 0.25 * solid * g_press
        gu = gu - 0.5 * diff_rows(g_div)
        gv = gv - 0.5 * diff_cols(g_div)
        wy, wx = quadratic(sy), quadratic(sx)
        spots = []
        g_sy = jnp.zeros_like(gu)
        g_sx = jnp.zeros_like(gu)
        for n, g in enumerate((grad_rho, gu, gv)):
            g_sy = g_sy + g * saved[slot, 4 + n]
            g_sx = g_sx + g * saved[slot, 7 + n]
            acc = None
            for a, shift in enumerate((from_below, lambda v: v, from_above)):
                ga = wy[a] * g
                line = from_right(wx[0] * ga) + wx[1] * ga + from_left(wx[2] * ga)
                line = shift(line)
                acc = line if acc is None else acc + line
            spots.append(acc)
        ty, tx = sy * (1.0 / COURANT), sx * (1.0 / COURANT)
        g_u1 = spots[1] + g_sy * (COURANT * (1.0 - ty * ty))
        g_v1 = spots[2] + g_sx * (COURANT * (1.0 - tx * tx))
        l0 = (TIME_STEP * g_u1 + 2.0 * FORCE_WEIGHT * inv_count * f0) * (1.0 - f0 * f0)
        l1 = (TIME_STEP * g_v1 + 2.0 * FORCE_WEIGHT * inv_count * f1) * (1.0 - f1 * f1)
        grad_state[0] = spots[0]
        grad_state[1] = g_u1
        grad_state[2] = g_v1
        glog32[pl.ds(0, grid, stride=16), :] = l0
        glog32[pl.ds(1, grid, stride=16), :] = l1

        def pack(it, carry):
            for k in range(4):
                i = it * 4 + k
                glog[i] = glog32[pl.ds(pl.multiple_of(i * 16, 16), 16), :].astype(BF16)
            return carry

        lax.fori_loop(0, grid // 4, pack, 0)

        def back_a(it, carry):
            sums_d, sums_n = carry
            i = it * 2
            gl = jnp.concatenate([glog[i], glog[i + 1]], axis=1)
            p = dot(w_bwd[width : 2 * width, TAPS * width :], gl)
            for k in range(2):
                d = p[:, k * LANES : (k + 1) * LANES] * slope[slot, 1, i + k]
                dy[i + k] = d
                sums_d = sums_d + d
                sums_n = sums_n + d * conv[slot, 1, i + k]
            ml = jnp.concatenate([mixed_low[slot, i], mixed_low[slot, i + 1]], axis=1)
            d_head[...] += dot_nt(gl, ml)
            return sums_d, sums_n

        sums = lax.fori_loop(0, grid // 2, back_a, (zero, zero))
        fd, f1_, fn = norm_back(2, inv_std[1, slot], *sums)

        def back_b(it, carry):
            for k in range(2):
                i = it * 2 + k
                g = fd * dy[i] - f1_ - fn * conv[slot, 1, i]
                low = g.astype(BF16)
                g_pad[i + 1] = low
                g = low.astype(F32)
                g_taps[i, 0:width] = from_right(g).astype(BF16)
                g_taps[i, width : 2 * width] = low
                g_taps[i, 2 * width : 3 * width] = from_left(g).astype(BF16)
            return carry

        lax.fori_loop(0, grid // 2, back_b, 0)

        def wgrad(it, carry):
            acc = None
            for k in range(2):
                i = it * 4 + k * 2
                gt = jnp.concatenate([g_taps[i], g_taps[i + 1]], axis=1)
                term = dot_nt(gt, row_pair(hidden_low.at[slot], i))
                acc = term if acc is None else acc + term
            d_mid[...] += acc
            return carry

        lax.fori_loop(0, grid // 4, wgrad, 0)

        def back_c(it, carry):
            sums_d, sums_n = carry
            i = it * 2
            rows = combine(dot(w_bwd[...], row_pair(g_pad, i, glog)), width)
            for k in range(2):
                d = rows[k] * slope[slot, 0, i + k]
                dy[i + k] = d
                sums_d = sums_d + d
                sums_n = sums_n + d * conv[slot, 0, i + k]
            return sums_d, sums_n

        sums = lax.fori_loop(0, grid // 2, back_c, (zero, zero))
        fd, f1_, fn = norm_back(0, inv_std[0, slot], *sums)

        def back_d(it, carry):
            i = it * 2
            lows = []
            for k in range(2):
                low = (fd * dy[i + k] - f1_ - fn * conv[slot, 0, i + k]).astype(BF16)
                g_pad[i + k + 1] = low
                lows.append(low)
            d_in[...] += dot_nt(jnp.concatenate(lows, axis=1), row_pair(feat.at[slot], i))
            return carry

        lax.fori_loop(0, grid // 2, back_d, 0)

        @pl.when(t > 0)
        def _():
            def back_e(it, carry):
                i = it * 2
                rows = combine(dot(v_bwd[...], row_pair(g_pad, i)), 8)
                for k in range(2):
                    gs_rows[pl.ds(pl.multiple_of((i + k) * 8, 8), 8), :] = rows[k]
                return carry

            lax.fori_loop(0, grid // 2, back_e, 0)
            for q in range(3):
                grad_state[q] += gs_rows[pl.ds(q, grid, stride=8), :]

    grad_state[...] = jnp.zeros_like(grad_state)

    def backward_body(it, carry):
        t = steps - 1 - it
        if sz.slots == 1:
            step_forward(t, 0, False)
        step_backward(t, t if sz.slots > 1 else 0, False)
        return carry

    lax.fori_loop(0, steps, backward_body, 0)

    lane = lane_ids((width, LANES))
    low_half = lane < 64

    def half_turn(x):
        return pltpu.roll(x, 64, 1)

    ab = []
    for kx in range(TAPS):
        full = d_mid[kx * width : (kx + 1) * width, :]
        first = full[:, :LANES]
        second = jnp.concatenate([full[:, LANES:], jnp.zeros((width, 64), F32)], axis=1)
        ab.append((first, second))
    packed[:, 0:128] = ab[0][0]
    packed[:, 128:256] = jnp.where(low_half, ab[0][1], half_turn(ab[1][0]))
    packed[:, 256:384] = jnp.where(low_half, half_turn(ab[1][0]), half_turn(ab[1][1]))
    packed[:, 384:512] = ab[2][0]
    pieces = [d_in[:, ky * 16 : ky * 16 + 12] for ky in range(TAPS)]
    pieces.append(jnp.transpose(d_head[...])[:, 0:2])
    for k in range(4):
        pieces.append(jnp.sum(d_norm[k], axis=1, keepdims=True))
    total = jnp.sum(jnp.sum(loss[...], axis=1, keepdims=True), axis=0, keepdims=True)
    pieces.append(jnp.broadcast_to(total, (width, 1)))
    pieces.append(jnp.zeros((width, 64 - 43), F32))
    packed[:, 512:640] = jnp.concatenate([ab[2][1][:, 0:64]] + pieces, axis=1)

    my_rows = pl.ds(pl.multiple_of(c * co, 8), co)
    if sz.ways > 1:

        def one_copy(k, src_shard, dst_slot):
            return remote(
                packed.at[pl.ds(pl.multiple_of(src_shard * co, 8), co)],
                rs_one.at[dst_slot],
                a_send.at[k],
                a_recv.at[dst_slot],
                to(ch_peer(k), r),
            )

        for k in range(1, sz.ch):
            copy = one_copy(k, ch_peer(k), c)
            copy.start()
            copies.append(copy)
        rs_one[c] = packed[my_rows, :]
        for k in range(1, sz.ch):
            one_copy(k, c, ch_peer(k)).wait_recv()
        acc = rs_one[0]
        for k in range(1, sz.ch):
            acc = acc + rs_one[k]
        part[...] = acc
    else:
        part[...] = packed[my_rows, :]

    def tile_of(j):
        return pl.ds(j * LANES, LANES)

    def two_copy(j, slot):
        return remote(part.at[:, tile_of(j)], rs_two.at[j, slot], b_send.at[j], b_recv.at[j, slot], to(c, j % sz.rows))

    for j in range(sz.tiles):
        if sz.rows > 1:

            @pl.when(r != j % sz.rows)
            def _():
                two_copy(j, r).start()

    for j in range(sz.tiles):
        owner = j % sz.rows

        @pl.when(r == owner)
        def _():
            for k in range(1, sz.rows):
                two_copy(j, row_peer(k)).wait_recv()
            rs_two[j, owner] = part[:, tile_of(j)]
            acc = rs_two[j, 0]
            for k in range(1, sz.rows):
                acc = acc + rs_two[j, k]
            fin[j] = acc
            for k in range(1, sz.rows):
                remote(fin.at[j], fin.at[j], c_send.at[j, k], c_recv.at[j], to(c, row_peer(k))).start()

    for j in range(sz.tiles):
        owner = j % sz.rows
        if sz.rows > 1:

            @pl.when(r != owner)
            def _():
                remote(fin.at[j], fin.at[j], c_send.at[j, 0], c_recv.at[j], to(c, owner)).wait_recv()
                two_copy(j, r).wait_send()

            @pl.when(r == owner)
            def _():
                for k in range(1, sz.rows):
                    remote(fin.at[j], fin.at[j], c_send.at[j, k], c_recv.at[j], to(c, row_peer(k))).wait_send()

    acc = jnp.zeros((co, LANES), F32)
    for j in range(sz.tiles):
        g = fin[j]
        if j == sz.tiles - 1:
            g = jnp.where(lane_ids(g.shape) < LOSS_AT, g, 0.0)
        acc = acc + g * g
    ones = jnp.sum(jnp.sum(acc, axis=1, keepdims=True), axis=0, keepdims=True)
    ssq[c] = jnp.broadcast_to(ones, (8, LANES))

    def norm_copy(k, slot):
        return remote(ssq.at[slot], ssq.at[slot], n_send.at[k], n_recv.at[slot], to(ch_peer(k), r))

    for k in range(1, sz.ch):
        copy = norm_copy(k, c)
        copy.start()
        copies.append(copy)
    for k in range(1, sz.ch):
        norm_copy(k, ch_peer(k)).wait_recv()
    acc = ssq[0]
    for k in range(1, sz.ch):
        acc = acc + ssq[k]
    out_total[...] = acc
    for j in range(sz.tiles):
        out[:, tile_of(j)] = fin[j]
    for copy in copies:
        copy.wait_send()


def adam(weight, grad, moment, square, rate, decay):
    moment = BETA_ONE * moment + (1.0 - BETA_ONE) * grad
    square = BETA_TWO * square + (1.0 - BETA_TWO) * grad * grad
    fix_one = 1.0 - BETA_ONE**STEP_NUM
    fix_two = 1.0 - BETA_TWO**STEP_NUM
    updated = weight - rate * (moment / fix_one / (jnp.sqrt(square / fix_two) + ADAM_EPS) + decay * weight)
    return updated, moment, square


def adam_kernel(sz, grads, total, keyframes, *refs):
    params, firsts, seconds = refs[0:4], refs[4:8], refs[8:12]
    news, moments, squares = refs[12:16], refs[16:20], refs[20:24]
    scalars = refs[24]
    co, width = sz.co, sz.width
    norm = jnp.sqrt(total[0:1, 0:1])
    factor = CLIP / jnp.maximum(norm, CLIP)
    g = grads[...] * factor

    def put(n, at, grad):
        rate, decay = (RATE, DECAY) if n < 3 else (GAIN_RATE, 0.0)
        new, moment, square = adam(params[n][at], grad, firsts[n][at], seconds[n][at], rate, decay)
        news[n][at] = new
        moments[n][at] = moment
        squares[n][at] = square

    for kx in range(TAPS):
        for ky in range(TAPS):
            at = (kx * TAPS + ky) * width
            put(1, (ky, kx), g[:, at : at + width])
    tail = g[:, sz.lanes - LANES : sz.lanes]
    tail = jnp.concatenate([tail, jnp.zeros((LANES - co, LANES), F32)], axis=0)
    tail = jnp.transpose(tail)
    for ky in range(TAPS):
        for kx in range(TAPS):
            at = IN_AT + (ky * TAPS + kx) * 4
            put(0, (ky, kx), tail[at : at + 4, 0:co])
    put(2, Ellipsis, tail[HEAD_AT : HEAD_AT + 2, 0:co])
    put(3, Ellipsis, tail[NORM_AT : NORM_AT + 4, 0:co])
    marks = keyframes[...].astype(F32)
    valid = jnp.sum(jnp.sum(marks, axis=1, keepdims=True), axis=0, keepdims=True) * float(sz.grid * sz.cols)
    loss = grads[0:1, sz.lanes - LANES + LOSS_AT : sz.lanes - LANES + LOSS_AT + 1]
    scalars[0:1, :] = jnp.broadcast_to(norm, (1, LANES))
    scalars[1:2, :] = jnp.broadcast_to(loss, (1, LANES))
    scalars[2:3, :] = jnp.broadcast_to(valid, (1, LANES))


def scratch_of(sz):
    grid, width, rows, ch, slots, steps = sz.grid, sz.width, sz.rows, sz.ch, sz.slots, sz.steps
    wide = TAPS * width

    def f32(*shape):
        return pltpu.VMEM(shape, F32)

    def bf16(*shape):
        return pltpu.VMEM(shape, BF16)

    dma = lambda *shape: pltpu.SemaphoreType.DMA(shape)
    return {
        "f_stage": f32(rows, 3, sz.local, LANES),
        "t_stage": f32(rows, steps, sz.local, LANES),
        "m_stage": pltpu.VMEM((rows, sz.local, LANES), jnp.int32),
        "w_all": f32(width, sz.lanes),
        "small": f32(LANES, LANES),
        "w_fwd": bf16(wide, wide),
        "w_bwd": bf16(wide, wide + 16),
        "v_fwd": bf16(width, TAPS * 16),
        "v_bwd": bf16(TAPS * 8, wide),
        "head": bf16(16, width),
        "gains": f32(4, width, LANES),
        "current": f32(3, grid, LANES),
        "states": f32(1 if slots > 1 else steps, 3, grid, LANES),
        "mask": f32(grid, LANES),
        "target": f32(steps, grid, LANES),
        "feat32": f32(grid * 16, LANES),
        "feat": bf16(slots, grid + 2, 16, LANES),
        "conv": f32(slots, 2, grid, width, LANES),
        "slope": f32(slots, 2, grid, width, LANES),
        "inv_std": f32(2, slots, width, LANES),
        "hidden": f32(grid, width, LANES),
        "hidden_low": bf16(slots, grid + 2, width, LANES),
        "mixed_low": bf16(slots, grid, width, LANES),
        "logits": f32(2, grid, LANES),
        "saved": f32(slots, SAVED, grid, LANES),
        "dy": f32(grid, width, LANES),
        "glog32": f32(grid * 16, LANES),
        "glog": bf16(grid, 16, LANES),
        "g_pad": bf16(grid + 2, width, LANES),
        "g_taps": bf16(grid, wide, LANES),
        "gs_rows": f32(grid * 8, LANES),
        "grad_state": f32(3, grid, LANES),
        "d_mid": f32(wide, wide),
        "d_in": f32(width, TAPS * 16),
        "d_head": f32(16, width),
        "d_norm": f32(4, width, LANES),
        "loss": f32(grid, LANES),
        "packed": f32(width, sz.lanes),
        "part": f32(sz.co, sz.lanes),
        "rs_one": f32(ch, sz.co, sz.lanes),
        "rs_two": f32(sz.tiles, rows, sz.co, LANES),
        "fin": f32(sz.tiles, sz.co, LANES),
        "ssq": f32(ch, 8, LANES),
        "local_sem": dma(3),
        "f_send": dma(rows),
        "f_recv": dma(rows),
        "t_send": dma(rows),
        "t_recv": dma(rows),
        "m_send": dma(rows),
        "m_recv": dma(rows),
        "w_send": dma(ch),
        "w_recv": dma(ch),
        "a_send": dma(ch),
        "a_recv": dma(ch),
        "b_send": dma(sz.tiles),
        "b_recv": dma(sz.tiles, rows),
        "c_send": dma(sz.tiles, rows),
        "c_recv": dma(sz.tiles),
        "n_send": dma(ch),
        "n_recv": dma(ch),
    }


def shards(mesh, fields, targets, fluid, keyframes, *rest):
    params, firsts, seconds = rest[0:4], rest[4:8], rest[8:12]

    def native(leaves):
        return (leaves[0], jnp.swapaxes(leaves[1], 2, 3), leaves[2].T, leaves[3])

    params, firsts, seconds = native(params), native(firsts), native(seconds)
    sz = Sizes(mesh, fields.shape, targets.shape, params[0].shape[3])
    marks = keyframes.T
    vmem = pl.BlockSpec(memory_space=pltpu.VMEM)
    hbm = pl.BlockSpec(memory_space=pl.ANY)
    alone = sz.rows == 1 and sz.ch == 1
    grads, total = pl.pallas_call(
        functools.partial(train_kernel, sz),
        out_shape=(
            jax.ShapeDtypeStruct((sz.co, sz.lanes), F32),
            jax.ShapeDtypeStruct((8, LANES), F32),
        ),
        in_specs=[hbm, hbm, hbm] + [vmem] * 5,
        out_specs=(vmem, vmem),
        scratch_shapes=list(scratch_of(sz).values()),
        compiler_params=pltpu.CompilerParams(
            collective_id=None if alone else 0, has_side_effects=True, vmem_limit_bytes=60 << 20
        ),
        name="train",
    )(fields, targets, fluid, marks, *params)
    shapes = [jax.ShapeDtypeStruct(leaf.shape, F32) for leaf in params] * 3
    shapes.append(jax.ShapeDtypeStruct((3, LANES), F32))
    results = pl.pallas_call(
        functools.partial(adam_kernel, sz),
        out_shape=tuple(shapes),
        in_specs=[vmem] * 15,
        out_specs=tuple([vmem] * 13),
        name="adamw",
    )(grads, total, marks, *params, *firsts, *seconds)
    outs = []
    for n in range(3):
        outs.extend(native(results[4 * n : 4 * n + 4]))
    scalars = results[12]
    return (*outs, scalars[0, 0], scalars[1, 0], scalars[2, 0])


def solution(mesh):
    split = (P(None, None, None, "ch"), P(None, None, None, "ch"), P("ch", None), P(None, "ch"))
    return jax.shard_map(
        functools.partial(shards, mesh),
        mesh=mesh,
        in_specs=(
            P(None, None, "rows", None),
            P(None, None, "rows", None),
            P("rows", None),
            P(),
            *split,
            *split,
            *split,
        ),
        out_specs=(*split, *split, *split, P(), P(), P()),
        check_vma=False,
    )
```

```python
import functools

import jax
import jax.numpy as jnp
from jax import lax
from jax.experimental import pallas as pl
from jax.experimental.pallas import tpu as pltpu
from jax.sharding import PartitionSpec as P

GROUPS = 8
JACOBI = 3
STEP_NUM = 10
TIME_STEP = 0.5
COURANT = 0.8
FORCE_WEIGHT = 0.5
NORM_EPS = 1e-05
CLIP = 0.0001
BETA_ONE = 0.9
BETA_TWO = 0.999
ADAM_EPS = 1e-10
RATE = 0.1
GAIN_RATE = 0.6
DECAY = 0.01

MESH = pl.DeviceIdType.MESH
F32 = jnp.float32
BF16 = jnp.bfloat16
LANES = 128
GSIZE = 8
TAPS = 3
SAVED = 11
NT = (((1,), (1,)), ((), ()))


def lane_ids(shape):
    return lax.broadcasted_iota(jnp.int32, shape, len(shape) - 1)


def row_ids(shape):
    return lax.broadcasted_iota(jnp.int32, shape, 0)


def from_left(x):
    return jnp.where(lane_ids(x.shape) == 0, 0.0, pltpu.roll(x, 1, 1))


def from_right(x):
    size = x.shape[1]
    return jnp.where(lane_ids(x.shape) == size - 1, 0.0, pltpu.roll(x, size - 1, 1))


def from_above(x):
    return jnp.where(row_ids(x.shape) == 0, 0.0, pltpu.roll(x, 1, 0))


def from_below(x):
    size = x.shape[0]
    return jnp.where(row_ids(x.shape) == size - 1, 0.0, pltpu.roll(x, size - 1, 0))


def diff_rows(x):
    return from_below(x) - from_above(x)


def diff_cols(x):
    return from_right(x) - from_left(x)


def around(x):
    return from_below(x) + from_above(x) + from_right(x) + from_left(x)


def quadratic(s):
    return (0.5 * s * (s + 1.0), 1.0 - s * s, 0.5 * s * (s - 1.0))


def quadratic_slope(s):
    return (s + 0.5, -2.0 * s, s - 0.5)


def dot(a, b):
    return jnp.dot(a, b, preferred_element_type=F32)


def dot_nt(a, b):
    return lax.dot_general(a, b, NT, preferred_element_type=F32)


def row_pair(ref, i, extra=None):
    depth = ref.shape[1] * TAPS
    sides = []
    for k in range(2):
        side = ref[pl.ds(i + k, TAPS)].reshape(depth, LANES)
        if extra is not None:
            side = jnp.concatenate([side, extra[i + k]], axis=0)
        sides.append(side)
    return jnp.concatenate(sides, axis=1)


def combine(p, height):
    out = []
    for k in range(2):
        part = p[:, k * LANES : (k + 1) * LANES]
        out.append(
            part[height : 2 * height]
            + from_left(part[:height])
            + from_right(part[2 * height : 3 * height])
        )
    return out


def group_sum(x):
    return jnp.sum(jnp.sum(x.reshape(-1, GSIZE, LANES), axis=1, keepdims=True), axis=2, keepdims=True)


def spread(x, width):
    return jnp.broadcast_to(x, (x.shape[0], GSIZE, LANES)).reshape(width, LANES)


def loop(count, per, body, carry):
    per = min(per, count)

    def several(it, carry):
        for k in range(per):
            carry = body(it * per + k, carry)
        return carry

    if count == per:
        return several(0, carry)
    return lax.fori_loop(0, count // per, several, carry)


class Sizes:
    def __init__(self, mesh, fields_shape, targets_shape, co):
        self.ch = mesh.shape["ch"]
        self.rows = mesh.shape["rows"]
        self.batch = fields_shape[0]
        self.local = fields_shape[2]
        self.grid = self.local * self.rows
        self.cols = fields_shape[3]
        self.steps = targets_shape[0]
        self.co = co
        self.width = co * self.ch
        self.per_rows = self.batch // self.rows
        self.ways = self.ch if self.per_rows == self.ch else 1
        assert self.per_rows == self.ways and self.batch % self.rows == 0
        assert self.cols == LANES
        slot = self.grid * self.width * LANES * 20
        self.slots = self.steps if slot * self.steps < (24 << 20) else 1
        self.mid_lanes = TAPS * TAPS * self.width
        self.lanes = -(-(self.mid_lanes + 64) // LANES) * LANES
        self.tiles = self.lanes // LANES
        assert self.width == 64


IN_AT = 64
HEAD_AT = IN_AT + 36
NORM_AT = HEAD_AT + 2
LOSS_AT = NORM_AT + 4


def train_kernel(sz, fields, targets, fluid, keyframes, w_in, w_mid, w_head, norms, out, out_total, *scratch):
    z = dict(zip(scratch_of(sz), scratch))
    f_stage = z["f_stage"]
    t_stage = z["t_stage"]
    m_stage = z["m_stage"]
    w_all = z["w_all"]
    small = z["small"]
    w_fwd = z["w_fwd"]
    w_bwd = z["w_bwd"]
    v_fwd = z["v_fwd"]
    v_bwd = z["v_bwd"]
    head = z["head"]
    gains = z["gains"]
    current = z["current"]
    states = z["states"]
    mask = z["mask"]
    target = z["target"]
    feat32 = z["feat32"]
    feat = z["feat"]
    conv = z["conv"]
    slope = z["slope"]
    hidden = z["hidden"]
    hidden_low = z["hidden_low"]
    mixed_low = z["mixed_low"]
    logits = z["logits"]
    saved = z["saved"]
    dy = z["dy"]
    glog32 = z["glog32"]
    glog = z["glog"]
    g_pad = z["g_pad"]
    g_taps = z["g_taps"]
    gs_rows = z["gs_rows"]
    grad_state = z["grad_state"]
    d_mid = z["d_mid"]
    d_in = z["d_in"]
    d_head = z["d_head"]
    d_norm = z["d_norm"]
    loss = z["loss"]
    packed = z["packed"]
    part = z["part"]
    rs_one = z["rs_one"]
    rs_two = z["rs_two"]
    fin = z["fin"]
    ssq = z["ssq"]
    local_sem = z["local_sem"]
    f_send = z["f_send"]
    f_recv = z["f_recv"]
    t_send = z["t_send"]
    t_recv = z["t_recv"]
    m_send = z["m_send"]
    m_recv = z["m_recv"]
    w_send = z["w_send"]
    w_recv = z["w_recv"]
    a_send = z["a_send"]
    a_recv = z["a_recv"]
    b_send = z["b_send"]
    b_recv = z["b_recv"]
    c_send = z["c_send"]
    c_recv = z["c_recv"]
    n_send = z["n_send"]
    n_recv = z["n_recv"]
    inv_std = z["inv_std"]
    c = lax.axis_index("ch")
    r = lax.axis_index("rows")
    width, grid, steps = sz.width, sz.grid, sz.steps
    co = sz.co

    def row_peer(k):
        return lax.rem(r + k, sz.rows)

    def ch_peer(k):
        return lax.rem(c + k, sz.ch)

    def sample_of(row):
        return row * sz.per_rows + (c if sz.ways > 1 else 0)

    def to(ch, row):
        return (ch, row)

    peers = sz.rows - 1 + sz.ch - 1
    if peers:
        barrier = pltpu.get_barrier_semaphore()
        for k in range(1, sz.rows):
            pl.semaphore_signal(barrier, inc=1, device_id=to(c, row_peer(k)), device_id_type=MESH)
        for k in range(1, sz.ch):
            pl.semaphore_signal(barrier, inc=1, device_id=to(ch_peer(k), r), device_id_type=MESH)

    small[...] = jnp.zeros_like(small)
    for ky in range(TAPS):
        for kx in range(TAPS):
            at = IN_AT + (ky * TAPS + kx) * 4
            small[at : at + 4, 0:co] = w_in[ky, kx]
    small[HEAD_AT : HEAD_AT + 2, 0:co] = w_head[...]
    small[NORM_AT : NORM_AT + 4, 0:co] = norms[...]
    blocks = [
        w_mid[ky, kx] for kx in range(TAPS) for ky in range(TAPS)
    ]
    blocks.append(jnp.transpose(small[...])[0:co, IN_AT : IN_AT + 64])
    mine = jnp.concatenate(blocks, axis=1)
    w_all[pl.ds(pl.multiple_of(c * co, 8), co), :] = mine

    if peers:
        pl.semaphore_wait(barrier, peers)

    copies = []

    def remote(src, dst, send, recv, where):
        return pltpu.make_async_remote_copy(
            src_ref=src, dst_ref=dst, send_sem=send, recv_sem=recv, device_id=where, device_id_type=MESH
        )

    def weights_copy(k, shard):
        rows = pl.ds(pl.multiple_of(shard * co, 8), co)
        return remote(w_all.at[rows], w_all.at[rows], w_send.at[k], w_recv.at[shard], to(ch_peer(k), r))

    def field_copy(k, row, src):
        return remote(fields.at[src], f_stage.at[row], f_send.at[k], f_recv.at[row], to(c, row_peer(k)))

    def mask_copy(k, row):
        return remote(fluid, m_stage.at[row], m_send.at[k], m_recv.at[row], to(c, row_peer(k)))

    def target_copy(k, row, src):
        return remote(targets.at[:, src], t_stage.at[row], t_send.at[k], t_recv.at[row], to(c, row_peer(k)))

    own = [
        pltpu.make_async_copy(fields.at[sample_of(r)], f_stage.at[r], local_sem.at[0]),
        pltpu.make_async_copy(targets.at[:, sample_of(r)], t_stage.at[r], local_sem.at[1]),
        pltpu.make_async_copy(fluid, m_stage.at[r], local_sem.at[2]),
    ]
    for copy in own:
        copy.start()
    for k in range(1, sz.ch):
        copy = weights_copy(k, c)
        copy.start()
        copies.append(copy)
    for k in range(1, sz.rows):
        copy = field_copy(k, r, sample_of(row_peer(k)))
        copy.start()
        copies.append(copy)
    for k in range(1, sz.rows):
        copy = mask_copy(k, r)
        copy.start()
        copies.append(copy)
    for k in range(1, sz.rows):
        copy = target_copy(k, r, sample_of(row_peer(k)))
        copy.start()
        copies.append(copy)

    for ref in (feat, hidden_low):
        for slot in range(sz.slots):
            ref[slot, 0] = jnp.zeros_like(ref[slot, 0])
            ref[slot, grid + 1] = jnp.zeros_like(ref[slot, 0])
    g_pad[0] = jnp.zeros_like(g_pad[0])
    g_pad[grid + 1] = jnp.zeros_like(g_pad[0])
    feat32[...] = jnp.zeros_like(feat32)
    glog32[...] = jnp.zeros_like(glog32)
    for ref in (d_mid, d_in, d_head, d_norm, loss):
        ref[...] = jnp.zeros_like(ref)

    for k in range(1, sz.ch):
        weights_copy(k, ch_peer(k)).wait_recv()
    for kx in range(TAPS):
        w_fwd[kx * width : (kx + 1) * width, :] = w_all[:, kx * TAPS * width : (kx + 1) * TAPS * width].astype(BF16)
    tail = w_all[:, sz.lanes - LANES : sz.lanes]
    tail_t = jnp.transpose(tail)
    for kx in range(TAPS):
        parts = []
        for ky in range(TAPS):
            at = ((2 - kx) * TAPS + 2 - ky) * width
            parts.append(jnp.transpose(w_all[:, at : at + width]))
        if kx == 1:
            pad = jnp.zeros((width, 14), F32)
            parts.append(jnp.concatenate([tail[:, HEAD_AT : HEAD_AT + 2], pad], axis=1))
        else:
            parts.append(jnp.zeros((width, 16), F32))
        w_bwd[kx * width : (kx + 1) * width, :] = jnp.concatenate(parts, axis=1).astype(BF16)
    parts = []
    for ky in range(TAPS):
        at = IN_AT + ky * 12
        parts.append(jnp.concatenate([tail[:, at : at + 12], jnp.zeros((width, 4), F32)], axis=1))
    v_fwd[...] = jnp.concatenate(parts, axis=1).astype(BF16)
    parts = []
    for kx in range(TAPS):
        line = []
        for ky in range(TAPS):
            at = IN_AT + ((2 - ky) * TAPS + 2 - kx) * 4
            line.append(tail_t[at : at + 4])
        parts.append(jnp.concatenate(line, axis=1))
        parts.append(jnp.zeros((4, TAPS * width), F32))
    v_bwd[...] = jnp.concatenate(parts, axis=0).astype(BF16)
    head[...] = jnp.concatenate([tail_t[HEAD_AT : HEAD_AT + 2], jnp.zeros((14, width), F32)], axis=0).astype(BF16)
    for k in range(4):
        gains[k] = jnp.broadcast_to(tail[:, NORM_AT + k : NORM_AT + k + 1], (width, LANES))

    for k in range(1, sz.rows):
        field_copy(k, row_peer(k), 0).wait_recv()
        mask_copy(k, row_peer(k)).wait_recv()
    own[0].wait()
    own[2].wait()
    for row in range(sz.rows):
        at = pl.ds(row * sz.local, sz.local)
        for q in range(3):
            current[q, at, :] = f_stage[row, q]
        mask[at, :] = m_stage[row].astype(F32)
    for k in range(1, sz.rows):
        target_copy(k, row_peer(k), 0).wait_recv()
    own[1].wait()
    for row in range(sz.rows):
        at = pl.ds(row * sz.local, sz.local)
        for t in range(steps):
            target[t, at, :] = t_stage[row, t]

    marks = keyframes[...].astype(F32)
    valid = jnp.sum(jnp.sum(marks, axis=1, keepdims=True), axis=0, keepdims=True) * float(grid * sz.cols)
    inv_count = 1.0 / valid
    picked = jnp.where(lane_ids(marks.shape) == sample_of(r), marks, 0.0)
    marked = jnp.sum(picked, axis=1, keepdims=True)

    def key_of(t):
        return jnp.sum(jnp.where(row_ids(marked.shape) == t, marked, 0.0), axis=0, keepdims=True)

    def conv_and_stats(x_ref, w, height, store):
        zero = jnp.zeros((width, LANES), F32)

        def body(it, carry):
            base, total, squares = carry
            for k in range(2):
                i = it * 4 + k * 2
                p = dot(w[...], row_pair(x_ref, i))
                rows = combine(p, width) if height else [p[:, :LANES], p[:, LANES:]]
                if k == 0:
                    base = jnp.where(it == 0, rows[0], base)
                for j in range(2):
                    store[i + j] = rows[j]
                    d = rows[j] - base
                    total = total + d
                    squares = squares + d * d
            return base, total, squares

        base, total, squares = loop(grid // 4, 8, body, (zero, zero, zero))
        lane_mean = base + total * (1.0 / grid)
        lane_dev = squares - total * total * (1.0 / grid)
        count = float(GSIZE * LANES)
        mean = spread(group_sum(lane_mean) * (1.0 / count), width)
        d = lane_mean - mean
        var = spread(group_sum(lane_dev + grid * d * d) * (1.0 / (count * grid)), width)
        inv = lax.rsqrt(var + NORM_EPS)
        return mean, inv

    def silu_parts(y):
        s = 0.5 * jnp.tanh(0.5 * y) + 0.5
        h = y * s
        return h, s + h - h * s

    def step_forward(t, slot, first):
        if sz.slots == 1:
            for q in range(3):
                if first:
                    states[t, q] = current[q]
                else:
                    current[q] = states[t, q]
        x = [current[q] for q in range(3)]
        planes = [x[0], x[1], x[2], mask[...]]
        for q in range(4):
            for kx, plane in enumerate((from_left(planes[q]), planes[q], from_right(planes[q]))):
                feat32[pl.ds(kx * 4 + q, grid, stride=16), :] = plane

        def pack(it, carry):
            for k in range(4):
                i = it * 4 + k
                feat[slot, i + 1] = feat32[pl.ds(pl.multiple_of(i * 16, 16), 16), :].astype(BF16)
            return carry

        loop(grid // 4, 8, pack, 0)

        mean, inv = conv_and_stats(feat.at[slot], v_fwd, 0, conv.at[slot, 0])
        off = mean * inv
        gain, bias = gains[0], gains[1]
        inv_std[0, slot] = inv

        def norm_one(it, carry):
            for k in range(2):
                i = it * 2 + k
                n = conv[slot, 0, i] * inv - off
                h, sl = silu_parts(n * gain + bias)
                conv[slot, 0, i] = n
                slope[slot, 0, i] = sl
                hidden[i] = h
                hidden_low[slot, i + 1] = h.astype(BF16)
            return carry

        loop(grid // 2, 16, norm_one, 0)

        mean, inv = conv_and_stats(hidden_low.at[slot], w_fwd, 1, conv.at[slot, 1])
        off = mean * inv
        gain, bias = gains[2], gains[3]
        inv_std[1, slot] = inv

        def norm_two(it, carry):
            i = it * 2
            lows = []
            for k in range(2):
                n = conv[slot, 1, i + k] * inv - off
                h, sl = silu_parts(n * gain + bias)
                conv[slot, 1, i + k] = n
                slope[slot, 1, i + k] = sl
                low = (hidden[i + k] + h).astype(BF16)
                mixed_low[slot, i + k] = low
                lows.append(low)
            p = dot(head[...], jnp.concatenate(lows, axis=1))
            for k in range(2):
                logits[0, pl.ds(i + k, 1), :] = p[0:1, k * LANES : (k + 1) * LANES]
                logits[1, pl.ds(i + k, 1), :] = p[1:2, k * LANES : (k + 1) * LANES]
            return carry

        loop(grid // 2, 16, norm_two, 0)

        f0, f1 = jnp.tanh(logits[0]), jnp.tanh(logits[1])
        u1 = x[1] + TIME_STEP * f0
        v1 = x[2] + TIME_STEP * f1
        sy = COURANT * jnp.tanh(u1)
        sx = COURANT * jnp.tanh(v1)
        wy, wx = quadratic(sy), quadratic(sx)
        dwy, dwx = quadratic_slope(sy), quadratic_slope(sx)
        moved = []
        for n, q in enumerate((x[0], u1, v1)):
            val = jnp.zeros_like(q)
            by_y = jnp.zeros_like(q)
            by_x = jnp.zeros_like(q)
            for a, line in enumerate((from_above(q), q, from_below(q))):
                windows = (from_left(line), line, from_right(line))
                along = wx[0] * windows[0] + wx[1] * windows[1] + wx[2] * windows[2]
                slant = dwx[0] * windows[0] + dwx[1] * windows[1] + dwx[2] * windows[2]
                val = val + wy[a] * along
                by_y = by_y + dwy[a] * along
                by_x = by_x + wy[a] * slant
            moved.append(val)
            saved[slot, 4 + n] = by_y
            saved[slot, 7 + n] = by_x
        solid = mask[...]
        rho2, u2, v2 = moved
        div = 0.5 * (diff_rows(u2) + diff_cols(v2))
        press = -0.25 * solid * div
        for _ in range(JACOBI - 1):
            press = 0.25 * solid * (around(press) - div)
        if first:
            current[0] = rho2
            current[1] = solid * (u2 - 0.5 * diff_rows(press))
            current[2] = solid * (v2 - 0.5 * diff_cols(press))
        pull = key_of(t) * (rho2 - target[t])
        if first:
            loss[...] += FORCE_WEIGHT * (f0 * f0 + f1 * f1) + pull * (rho2 - target[t])
        saved[slot, 0] = f0
        saved[slot, 1] = f1
        saved[slot, 2] = sy
        saved[slot, 3] = sx
        saved[slot, 10] = pull

    def forward_body(t, carry):
        step_forward(t, t if sz.slots > 1 else 0, True)
        return carry

    lax.fori_loop(0, steps, forward_body, 0)

    def norm_back(k, inv, sums_d, sums_n):
        gain = gains[k]
        scale = 1.0 / float(GSIZE * LANES * grid)
        m1 = spread(group_sum(sums_d * gain) * scale, width)
        m2 = spread(group_sum(sums_n * gain) * scale, width)
        d_norm[k] += sums_n
        d_norm[k + 1] += sums_d
        return inv * gain, inv * m1, inv * m2

    def step_backward(t, slot, last):
        zero = jnp.zeros((width, LANES), F32)
        solid = mask[...]
        sy, sx = saved[slot, 2], saved[slot, 3]
        f0, f1 = saved[slot, 0], saved[slot, 1]
        grad_rho = grad_state[0] + 2.0 * inv_count * saved[slot, 10]
        gu = solid * grad_state[1]
        gv = solid * grad_state[2]
        g_press = 0.5 * (diff_rows(gu) + diff_cols(gv))
        g_div = jnp.zeros_like(g_press)
        for _ in range(JACOBI - 1):
            term = 0.25 * solid * g_press
            g_div = g_div - term
            g_press = around(term)
        g_div = g_div - 0.25 * solid * g_press
        gu = gu - 0.5 * diff_rows(g_div)
        gv = gv - 0.5 * diff_cols(g_div)
        wy, wx = quadratic(sy), quadratic(sx)
        spots = []
        g_sy = jnp.zeros_like(gu)
        g_sx = jnp.zeros_like(gu)
        for n, g in enumerate((grad_rho, gu, gv)):
            g_sy = g_sy + g * saved[slot, 4 + n]
            g_sx = g_sx + g * saved[slot, 7 + n]
            acc = None
            for a, shift in enumerate((from_below, lambda v: v, from_above)):
                ga = wy[a] * g
                line = from_right(wx[0] * ga) + wx[1] * ga + from_left(wx[2] * ga)
                line = shift(line)
                acc = line if acc is None else acc + line
            spots.append(acc)
        ty, tx = sy * (1.0 / COURANT), sx * (1.0 / COURANT)
        g_u1 = spots[1] + g_sy * (COURANT * (1.0 - ty * ty))
        g_v1 = spots[2] + g_sx * (COURANT * (1.0 - tx * tx))
        l0 = (TIME_STEP * g_u1 + 2.0 * FORCE_WEIGHT * inv_count * f0) * (1.0 - f0 * f0)
        l1 = (TIME_STEP * g_v1 + 2.0 * FORCE_WEIGHT * inv_count * f1) * (1.0 - f1 * f1)
        grad_state[0] = spots[0]
        grad_state[1] = g_u1
        grad_state[2] = g_v1
        glog32[pl.ds(0, grid, stride=16), :] = l0
        glog32[pl.ds(1, grid, stride=16), :] = l1

        def pack(it, carry):
            for k in range(4):
                i = it * 4 + k
                glog[i] = glog32[pl.ds(pl.multiple_of(i * 16, 16), 16), :].astype(BF16)
            return carry

        loop(grid // 4, 8, pack, 0)

        def back_a(it, carry):
            sums_d, sums_n = carry
            i = it * 2
            gl = jnp.concatenate([glog[i], glog[i + 1]], axis=1)
            p = dot(w_bwd[width : 2 * width, TAPS * width :], gl)
            for k in range(2):
                d = p[:, k * LANES : (k + 1) * LANES] * slope[slot, 1, i + k]
                dy[i + k] = d
                sums_d = sums_d + d
                sums_n = sums_n + d * conv[slot, 1, i + k]
            ml = jnp.concatenate([mixed_low[slot, i], mixed_low[slot, i + 1]], axis=1)
            d_head[...] += dot_nt(gl, ml)
            return sums_d, sums_n

        sums = loop(grid // 2, 16, back_a, (zero, zero))
        fd, f1_, fn = norm_back(2, inv_std[1, slot], *sums)

        def back_b(it, carry):
            for k in range(2):
                i = it * 2 + k
                g = fd * dy[i] - f1_ - fn * conv[slot, 1, i]
                low = g.astype(BF16)
                g_pad[i + 1] = low
                g = low.astype(F32)
                g_taps[i, 0:width] = from_right(g).astype(BF16)
                g_taps[i, width : 2 * width] = low
                g_taps[i, 2 * width : 3 * width] = from_left(g).astype(BF16)
            return carry

        loop(grid // 2, 16, back_b, 0)

        def wgrad(it, carry):
            acc = None
            for k in range(2):
                i = it * 4 + k * 2
                gt = jnp.concatenate([g_taps[i], g_taps[i + 1]], axis=1)
                term = dot_nt(gt, row_pair(hidden_low.at[slot], i))
                acc = term if acc is None else acc + term
            d_mid[...] += acc
            return carry

        loop(grid // 4, 8, wgrad, 0)

        def back_c(it, carry):
            sums_d, sums_n = carry
            i = it * 2
            rows = combine(dot(w_bwd[...], row_pair(g_pad, i, glog)), width)
            for k in range(2):
                d = rows[k] * slope[slot, 0, i + k]
                dy[i + k] = d
                sums_d = sums_d + d
                sums_n = sums_n + d * conv[slot, 0, i + k]
            return sums_d, sums_n

        sums = loop(grid // 2, 16, back_c, (zero, zero))
        fd, f1_, fn = norm_back(0, inv_std[0, slot], *sums)

        def back_d(it, carry):
            i = it * 2
            lows = []
            for k in range(2):
                low = (fd * dy[i + k] - f1_ - fn * conv[slot, 0, i + k]).astype(BF16)
                g_pad[i + k + 1] = low
                lows.append(low)
            d_in[...] += dot_nt(jnp.concatenate(lows, axis=1), row_pair(feat.at[slot], i))
            return carry

        loop(grid // 2, 16, back_d, 0)

        @pl.when(t > 0)
        def _():
            def back_e(it, carry):
                i = it * 2
                rows = combine(dot(v_bwd[...], row_pair(g_pad, i)), 8)
                for k in range(2):
                    gs_rows[pl.ds(pl.multiple_of((i + k) * 8, 8), 8), :] = rows[k]
                return carry

            loop(grid // 2, 16, back_e, 0)
            for q in range(3):
                grad_state[q] += gs_rows[pl.ds(q, grid, stride=8), :]

    grad_state[...] = jnp.zeros_like(grad_state)

    def backward_body(it, carry):
        t = steps - 1 - it
        if sz.slots == 1:
            step_forward(t, 0, False)
        step_backward(t, t if sz.slots > 1 else 0, False)
        return carry

    lax.fori_loop(0, steps, backward_body, 0)

    lane = lane_ids((width, LANES))
    low_half = lane < 64

    def half_turn(x):
        return pltpu.roll(x, 64, 1)

    ab = []
    for kx in range(TAPS):
        full = d_mid[kx * width : (kx + 1) * width, :]
        first = full[:, :LANES]
        second = jnp.concatenate([full[:, LANES:], jnp.zeros((width, 64), F32)], axis=1)
        ab.append((first, second))
    packed[:, 0:128] = ab[0][0]
    packed[:, 128:256] = jnp.where(low_half, ab[0][1], half_turn(ab[1][0]))
    packed[:, 256:384] = jnp.where(low_half, half_turn(ab[1][0]), half_turn(ab[1][1]))
    packed[:, 384:512] = ab[2][0]
    pieces = [d_in[:, ky * 16 : ky * 16 + 12] for ky in range(TAPS)]
    pieces.append(jnp.transpose(d_head[...])[:, 0:2])
    for k in range(4):
        pieces.append(jnp.sum(d_norm[k], axis=1, keepdims=True))
    total = jnp.sum(jnp.sum(loss[...], axis=1, keepdims=True), axis=0, keepdims=True)
    pieces.append(jnp.broadcast_to(total, (width, 1)))
    pieces.append(jnp.zeros((width, 64 - 43), F32))
    packed[:, 512:640] = jnp.concatenate([ab[2][1][:, 0:64]] + pieces, axis=1)

    my_rows = pl.ds(pl.multiple_of(c * co, 8), co)
    if sz.ways > 1:

        def one_copy(k, src_shard, dst_slot):
            return remote(
                packed.at[pl.ds(pl.multiple_of(src_shard * co, 8), co)],
                rs_one.at[dst_slot],
                a_send.at[k],
                a_recv.at[dst_slot],
                to(ch_peer(k), r),
            )

        for k in range(1, sz.ch):
            copy = one_copy(k, ch_peer(k), c)
            copy.start()
            copies.append(copy)
        rs_one[c] = packed[my_rows, :]
        for k in range(1, sz.ch):
            one_copy(k, c, ch_peer(k)).wait_recv()
        acc = rs_one[0]
        for k in range(1, sz.ch):
            acc = acc + rs_one[k]
        part[...] = acc
    else:
        part[...] = packed[my_rows, :]

    def tile_of(j):
        return pl.ds(j * LANES, LANES)

    def two_copy(j, slot):
        return remote(part.at[:, tile_of(j)], rs_two.at[j, slot], b_send.at[j], b_recv.at[j, slot], to(c, j % sz.rows))

    for j in range(sz.tiles):
        if sz.rows > 1:

            @pl.when(r != j % sz.rows)
            def _():
                two_copy(j, r).start()

    for j in range(sz.tiles):
        owner = j % sz.rows

        @pl.when(r == owner)
        def _():
            for k in range(1, sz.rows):
                two_copy(j, row_peer(k)).wait_recv()
            rs_two[j, owner] = part[:, tile_of(j)]
            acc = rs_two[j, 0]
            for k in range(1, sz.rows):
                acc = acc + rs_two[j, k]
            fin[j] = acc
            for k in range(1, sz.rows):
                remote(fin.at[j], fin.at[j], c_send.at[j, k], c_recv.at[j], to(c, row_peer(k))).start()

    for j in range(sz.tiles):
        owner = j % sz.rows
        if sz.rows > 1:

            @pl.when(r != owner)
            def _():
                remote(fin.at[j], fin.at[j], c_send.at[j, 0], c_recv.at[j], to(c, owner)).wait_recv()
                two_copy(j, r).wait_send()

            @pl.when(r == owner)
            def _():
                for k in range(1, sz.rows):
                    remote(fin.at[j], fin.at[j], c_send.at[j, k], c_recv.at[j], to(c, row_peer(k))).wait_send()

    acc = jnp.zeros((co, LANES), F32)
    for j in range(sz.tiles):
        g = fin[j]
        if j == sz.tiles - 1:
            g = jnp.where(lane_ids(g.shape) < LOSS_AT, g, 0.0)
        acc = acc + g * g
    ones = jnp.sum(jnp.sum(acc, axis=1, keepdims=True), axis=0, keepdims=True)
    ssq[c] = jnp.broadcast_to(ones, (8, LANES))

    def norm_copy(k, slot):
        return remote(ssq.at[slot], ssq.at[slot], n_send.at[k], n_recv.at[slot], to(ch_peer(k), r))

    for k in range(1, sz.ch):
        copy = norm_copy(k, c)
        copy.start()
        copies.append(copy)
    for k in range(1, sz.ch):
        norm_copy(k, ch_peer(k)).wait_recv()
    acc = ssq[0]
    for k in range(1, sz.ch):
        acc = acc + ssq[k]
    out_total[...] = acc
    for j in range(sz.tiles):
        out[:, tile_of(j)] = fin[j]
    for copy in copies:
        copy.wait_send()


def adam(weight, grad, moment, square, rate, decay):
    moment = BETA_ONE * moment + (1.0 - BETA_ONE) * grad
    square = BETA_TWO * square + (1.0 - BETA_TWO) * grad * grad
    fix_one = 1.0 - BETA_ONE**STEP_NUM
    fix_two = 1.0 - BETA_TWO**STEP_NUM
    updated = weight - rate * (moment / fix_one / (jnp.sqrt(square / fix_two) + ADAM_EPS) + decay * weight)
    return updated, moment, square


def adam_kernel(sz, grads, total, keyframes, *refs):
    params, firsts, seconds = refs[0:4], refs[4:8], refs[8:12]
    news, moments, squares = refs[12:16], refs[16:20], refs[20:24]
    scalars = refs[24]
    co, width = sz.co, sz.width
    norm = jnp.sqrt(total[0:1, 0:1])
    factor = CLIP / jnp.maximum(norm, CLIP)
    g = grads[...] * factor

    def put(n, at, grad):
        rate, decay = (RATE, DECAY) if n < 3 else (GAIN_RATE, 0.0)
        new, moment, square = adam(params[n][at], grad, firsts[n][at], seconds[n][at], rate, decay)
        news[n][at] = new
        moments[n][at] = moment
        squares[n][at] = square

    for kx in range(TAPS):
        for ky in range(TAPS):
            at = (kx * TAPS + ky) * width
            put(1, (ky, kx), g[:, at : at + width])
    tail = g[:, sz.lanes - LANES : sz.lanes]
    tail = jnp.concatenate([tail, jnp.zeros((LANES - co, LANES), F32)], axis=0)
    tail = jnp.transpose(tail)
    for ky in range(TAPS):
        for kx in range(TAPS):
            at = IN_AT + (ky * TAPS + kx) * 4
            put(0, (ky, kx), tail[at : at + 4, 0:co])
    put(2, Ellipsis, tail[HEAD_AT : HEAD_AT + 2, 0:co])
    put(3, Ellipsis, tail[NORM_AT : NORM_AT + 4, 0:co])
    marks = keyframes[...].astype(F32)
    valid = jnp.sum(jnp.sum(marks, axis=1, keepdims=True), axis=0, keepdims=True) * float(sz.grid * sz.cols)
    loss = grads[0:1, sz.lanes - LANES + LOSS_AT : sz.lanes - LANES + LOSS_AT + 1]
    scalars[0:1, :] = jnp.broadcast_to(norm, (1, LANES))
    scalars[1:2, :] = jnp.broadcast_to(loss, (1, LANES))
    scalars[2:3, :] = jnp.broadcast_to(valid, (1, LANES))


def scratch_of(sz):
    grid, width, rows, ch, slots, steps = sz.grid, sz.width, sz.rows, sz.ch, sz.slots, sz.steps
    wide = TAPS * width

    def f32(*shape):
        return pltpu.VMEM(shape, F32)

    def bf16(*shape):
        return pltpu.VMEM(shape, BF16)

    dma = lambda *shape: pltpu.SemaphoreType.DMA(shape)
    return {
        "f_stage": f32(rows, 3, sz.local, LANES),
        "t_stage": f32(rows, steps, sz.local, LANES),
        "m_stage": pltpu.VMEM((rows, sz.local, LANES), jnp.int32),
        "w_all": f32(width, sz.lanes),
        "small": f32(LANES, LANES),
        "w_fwd": bf16(wide, wide),
        "w_bwd": bf16(wide, wide + 16),
        "v_fwd": bf16(width, TAPS * 16),
        "v_bwd": bf16(TAPS * 8, wide),
        "head": bf16(16, width),
        "gains": f32(4, width, LANES),
        "current": f32(3, grid, LANES),
        "states": f32(1 if slots > 1 else steps, 3, grid, LANES),
        "mask": f32(grid, LANES),
        "target": f32(steps, grid, LANES),
        "feat32": f32(grid * 16, LANES),
        "feat": bf16(slots, grid + 2, 16, LANES),
        "conv": f32(slots, 2, grid, width, LANES),
        "slope": f32(slots, 2, grid, width, LANES),
        "inv_std": f32(2, slots, width, LANES),
        "hidden": f32(grid, width, LANES),
        "hidden_low": bf16(slots, grid + 2, width, LANES),
        "mixed_low": bf16(slots, grid, width, LANES),
        "logits": f32(2, grid, LANES),
        "saved": f32(slots, SAVED, grid, LANES),
        "dy": f32(grid, width, LANES),
        "glog32": f32(grid * 16, LANES),
        "glog": bf16(grid, 16, LANES),
        "g_pad": bf16(grid + 2, width, LANES),
        "g_taps": bf16(grid, wide, LANES),
        "gs_rows": f32(grid * 8, LANES),
        "grad_state": f32(3, grid, LANES),
        "d_mid": f32(wide, wide),
        "d_in": f32(width, TAPS * 16),
        "d_head": f32(16, width),
        "d_norm": f32(4, width, LANES),
        "loss": f32(grid, LANES),
        "packed": f32(width, sz.lanes),
        "part": f32(sz.co, sz.lanes),
        "rs_one": f32(ch, sz.co, sz.lanes),
        "rs_two": f32(sz.tiles, rows, sz.co, LANES),
        "fin": f32(sz.tiles, sz.co, LANES),
        "ssq": f32(ch, 8, LANES),
        "local_sem": dma(3),
        "f_send": dma(rows),
        "f_recv": dma(rows),
        "t_send": dma(rows),
        "t_recv": dma(rows),
        "m_send": dma(rows),
        "m_recv": dma(rows),
        "w_send": dma(ch),
        "w_recv": dma(ch),
        "a_send": dma(ch),
        "a_recv": dma(ch),
        "b_send": dma(sz.tiles),
        "b_recv": dma(sz.tiles, rows),
        "c_send": dma(sz.tiles, rows),
        "c_recv": dma(sz.tiles),
        "n_send": dma(ch),
        "n_recv": dma(ch),
    }


def shards(mesh, fields, targets, fluid, keyframes, *rest):
    params, firsts, seconds = rest[0:4], rest[4:8], rest[8:12]

    def native(leaves):
        return (leaves[0], jnp.swapaxes(leaves[1], 2, 3), leaves[2].T, leaves[3])

    params, firsts, seconds = native(params), native(firsts), native(seconds)
    sz = Sizes(mesh, fields.shape, targets.shape, params[0].shape[3])
    marks = keyframes.T
    vmem = pl.BlockSpec(memory_space=pltpu.VMEM)
    hbm = pl.BlockSpec(memory_space=pl.ANY)
    alone = sz.rows == 1 and sz.ch == 1
    grads, total = pl.pallas_call(
        functools.partial(train_kernel, sz),
        out_shape=(
            jax.ShapeDtypeStruct((sz.co, sz.lanes), F32),
            jax.ShapeDtypeStruct((8, LANES), F32),
        ),
        in_specs=[hbm, hbm, hbm] + [vmem] * 5,
        out_specs=(vmem, vmem),
        scratch_shapes=list(scratch_of(sz).values()),
        compiler_params=pltpu.CompilerParams(
            collective_id=None if alone else 0, has_side_effects=True, vmem_limit_bytes=60 << 20
        ),
        name="train",
    )(fields, targets, fluid, marks, *params)
    shapes = [jax.ShapeDtypeStruct(leaf.shape, F32) for leaf in params] * 3
    shapes.append(jax.ShapeDtypeStruct((3, LANES), F32))
    results = pl.pallas_call(
        functools.partial(adam_kernel, sz),
        out_shape=tuple(shapes),
        in_specs=[vmem] * 15,
        out_specs=tuple([vmem] * 13),
        name="adamw",
    )(grads, total, marks, *params, *firsts, *seconds)
    outs = []
    for n in range(3):
        outs.extend(native(results[4 * n : 4 * n + 4]))
    scalars = results[12]
    return (*outs, scalars[0, 0], scalars[1, 0], scalars[2, 0])


def solution(mesh):
    split = (P(None, None, None, "ch"), P(None, None, None, "ch"), P("ch", None), P(None, "ch"))
    return jax.shard_map(
        functools.partial(shards, mesh),
        mesh=mesh,
        in_specs=(
            P(None, None, "rows", None),
            P(None, None, "rows", None),
            P("rows", None),
            P(),
            *split,
            *split,
            *split,
        ),
        out_specs=(*split, *split, *split, P(), P(), P()),
        check_vma=False,
    )
```

```python
import functools

import jax
import jax.numpy as jnp
from jax import lax
from jax.experimental import pallas as pl
from jax.experimental.pallas import tpu as pltpu
from jax.sharding import PartitionSpec as P

GROUPS = 8
JACOBI = 3
STEP_NUM = 10
TIME_STEP = 0.5
COURANT = 0.8
FORCE_WEIGHT = 0.5
NORM_EPS = 1e-05
CLIP = 0.0001
BETA_ONE = 0.9
BETA_TWO = 0.999
ADAM_EPS = 1e-10
RATE = 0.1
GAIN_RATE = 0.6
DECAY = 0.01

MESH = pl.DeviceIdType.MESH
F32 = jnp.float32
BF16 = jnp.bfloat16
LANES = 128
GSIZE = 8
TAPS = 3
SAVED = 11
NT = (((1,), (1,)), ((), ()))


def lane_ids(shape):
    return lax.broadcasted_iota(jnp.int32, shape, len(shape) - 1)


def row_ids(shape):
    return lax.broadcasted_iota(jnp.int32, shape, 0)


def from_left(x):
    return jnp.where(lane_ids(x.shape) == 0, 0.0, pltpu.roll(x, 1, 1))


def from_right(x):
    size = x.shape[1]
    return jnp.where(lane_ids(x.shape) == size - 1, 0.0, pltpu.roll(x, size - 1, 1))


def from_above(x):
    return jnp.where(row_ids(x.shape) == 0, 0.0, pltpu.roll(x, 1, 0))


def from_below(x):
    size = x.shape[0]
    return jnp.where(row_ids(x.shape) == size - 1, 0.0, pltpu.roll(x, size - 1, 0))


def diff_rows(x):
    return from_below(x) - from_above(x)


def diff_cols(x):
    return from_right(x) - from_left(x)


def around(x):
    return from_below(x) + from_above(x) + from_right(x) + from_left(x)


def quadratic(s):
    return (0.5 * s * (s + 1.0), 1.0 - s * s, 0.5 * s * (s - 1.0))


def quadratic_slope(s):
    return (s + 0.5, -2.0 * s, s - 0.5)


def dot(a, b):
    return jnp.dot(a, b, preferred_element_type=F32)


def dot_nt(a, b):
    return lax.dot_general(a, b, NT, preferred_element_type=F32)


def row_pair(ref, i, extra=None):
    depth = ref.shape[1] * TAPS
    sides = []
    for k in range(2):
        side = ref[pl.ds(i + k, TAPS)].reshape(depth, LANES)
        if extra is not None:
            side = jnp.concatenate([side, extra[i + k]], axis=0)
        sides.append(side)
    return jnp.concatenate(sides, axis=1)


def combine(p, height):
    out = []
    for k in range(2):
        part = p[:, k * LANES : (k + 1) * LANES]
        out.append(
            part[height : 2 * height]
            + from_left(part[:height])
            + from_right(part[2 * height : 3 * height])
        )
    return out


def group_sum(x):
    return jnp.sum(jnp.sum(x.reshape(-1, GSIZE, LANES), axis=1, keepdims=True), axis=2, keepdims=True)


def spread(x, width):
    return jnp.broadcast_to(x, (x.shape[0], GSIZE, LANES)).reshape(width, LANES)


def loop(count, per, body, carry):
    per = min(per, count)

    def several(it, carry):
        for k in range(per):
            carry = body(it * per + k, carry)
        return carry

    if count == per:
        return several(0, carry)
    return lax.fori_loop(0, count // per, several, carry)


class Sizes:
    def __init__(self, mesh, fields_shape, targets_shape, co):
        self.ch = mesh.shape["ch"]
        self.rows = mesh.shape["rows"]
        self.batch = fields_shape[0]
        self.local = fields_shape[2]
        self.grid = self.local * self.rows
        self.cols = fields_shape[3]
        self.steps = targets_shape[0]
        self.co = co
        self.width = co * self.ch
        self.per_rows = self.batch // self.rows
        self.ways = self.ch if self.per_rows == self.ch else 1
        assert self.per_rows == self.ways and self.batch % self.rows == 0
        assert self.cols == LANES
        slot = self.grid * self.width * LANES * 20
        self.slots = self.steps if slot * self.steps < (24 << 20) else 1
        self.halves = co // 8
        self.early = 4 * self.halves
        self.owned = -(-self.early // self.rows)
        self.sources = self.ways * self.rows
        self.mid_lanes = TAPS * TAPS * self.width
        assert self.width == 64 and co % 8 == 0


IN_AT = 64
HEAD_AT = IN_AT + 36
NORM_AT = HEAD_AT + 2
LOSS_AT = NORM_AT + 4


def train_kernel(sz, fields, targets, fluid, keyframes, w_in, w_mid, w_head, norms, out, out_total, *scratch):
    z = dict(zip(scratch_of(sz), scratch))
    f_stage = z["f_stage"]
    t_stage = z["t_stage"]
    m_stage = z["m_stage"]
    w_in_own = z["w_in_own"]
    w_mid_own = z["w_mid_own"]
    w_head_own = z["w_head_own"]
    norms_own = z["norms_own"]
    small = z["small"]
    ws_all = z["ws_all"]
    wm_all = z["wm_all"]
    w_fwd = z["w_fwd"]
    w_bwd = z["w_bwd"]
    v_fwd = z["v_fwd"]
    v_bwd = z["v_bwd"]
    head = z["head"]
    gains = z["gains"]
    current = z["current"]
    states = z["states"]
    mask = z["mask"]
    target = z["target"]
    feat32 = z["feat32"]
    feat = z["feat"]
    conv = z["conv"]
    slope = z["slope"]
    inv_std = z["inv_std"]
    hidden = z["hidden"]
    hidden_low = z["hidden_low"]
    mixed_low = z["mixed_low"]
    logits = z["logits"]
    saved = z["saved"]
    dy = z["dy"]
    glog32 = z["glog32"]
    glog = z["glog"]
    g_pad = z["g_pad"]
    g_taps = z["g_taps"]
    gs_rows = z["gs_rows"]
    grad_state = z["grad_state"]
    d_mid = z["d_mid"]
    d_in = z["d_in"]
    d_head = z["d_head"]
    d_norm = z["d_norm"]
    loss = z["loss"]
    early = z["early"]
    early_in = z["early_in"]
    early_fin = z["early_fin"]
    ssq_early = z["ssq_early"]
    late = z["late"]
    late_ch = z["late_ch"]
    late_part = z["late_part"]
    late_rows = z["late_rows"]
    ssq_late = z["ssq_late"]
    ready = z["ready"]
    local_sem = z["local_sem"]
    f_send = z["f_send"]
    f_recv = z["f_recv"]
    t_send = z["t_send"]
    t_recv = z["t_recv"]
    m_send = z["m_send"]
    m_recv = z["m_recv"]
    v_send = z["v_send"]
    v_recv = z["v_recv"]
    w_send = z["w_send"]
    w_recv = z["w_recv"]
    e_send = z["e_send"]
    e_recv = z["e_recv"]
    g_send = z["g_send"]
    g_recv = z["g_recv"]
    s_send = z["s_send"]
    s_recv = z["s_recv"]
    a_send = z["a_send"]
    a_recv = z["a_recv"]
    b_send = z["b_send"]
    b_recv = z["b_recv"]
    n_send = z["n_send"]
    n_recv = z["n_recv"]
    c = lax.axis_index("ch")
    r = lax.axis_index("rows")
    width, grid, steps = sz.width, sz.grid, sz.steps
    co = sz.co

    def row_peer(k):
        return lax.rem(r + k, sz.rows)

    def ch_peer(k):
        return lax.rem(c + k, sz.ch)

    def sample_of(row):
        return row * sz.per_rows + (c if sz.ways > 1 else 0)

    peers = sz.rows - 1 + sz.ch - 1
    if peers:
        barrier = pltpu.get_barrier_semaphore()
        for k in range(1, sz.rows):
            pl.semaphore_signal(barrier, inc=1, device_id=(c, row_peer(k)), device_id_type=MESH)
        for k in range(1, sz.ch):
            pl.semaphore_signal(barrier, inc=1, device_id=(ch_peer(k), r), device_id_type=MESH)

    copies = []

    def remote(src, dst, send, recv, where):
        return pltpu.make_async_remote_copy(
            src_ref=src, dst_ref=dst, send_sem=send, recv_sem=recv, device_id=where, device_id_type=MESH
        )

    def send(copy):
        copy.start()
        copies.append(copy)

    own = [
        pltpu.make_async_copy(src, dst, local_sem.at[n])
        for n, (src, dst) in enumerate(
            (
                (w_in, w_in_own),
                (w_head, w_head_own),
                (norms, norms_own),
                (w_mid, w_mid_own),
                (fields.at[sample_of(r)], f_stage.at[r]),
                (fluid, m_stage.at[r]),
                (targets.at[:, sample_of(r)], t_stage.at[r]),
            )
        )
    ]
    for copy in own:
        copy.start()

    small[...] = jnp.zeros_like(small)
    for n in range(4):
        own[n].wait()
    for ky in range(TAPS):
        for kx in range(TAPS):
            at = IN_AT + (ky * TAPS + kx) * 4
            small[at : at + 4, 0:co] = w_in_own[ky, kx]
    small[HEAD_AT : HEAD_AT + 2, 0:co] = w_head_own[...]
    small[NORM_AT : NORM_AT + 4, 0:co] = norms_own[...]
    ws_all[c] = jnp.transpose(small[...])[0:co]
    mine = jnp.concatenate([w_mid_own[ky, kx] for kx in range(TAPS) for ky in range(TAPS)], axis=1)
    wm_all[c, 0:co, :] = mine.astype(BF16)

    if peers:
        pl.semaphore_wait(barrier, peers)

    def small_copy(k, shard):
        return remote(ws_all.at[shard], ws_all.at[shard], v_send.at[k], v_recv.at[shard], (ch_peer(k), r))

    def mid_copy(k, shard):
        return remote(wm_all.at[shard], wm_all.at[shard], w_send.at[k], w_recv.at[shard], (ch_peer(k), r))

    def field_copy(k, row, src):
        return remote(fields.at[src], f_stage.at[row], f_send.at[k], f_recv.at[row], (c, row_peer(k)))

    def mask_copy(k, row):
        return remote(fluid, m_stage.at[row], m_send.at[k], m_recv.at[row], (c, row_peer(k)))

    def target_copy(k, row, src):
        return remote(targets.at[:, src], t_stage.at[row], t_send.at[k], t_recv.at[row], (c, row_peer(k)))

    for k in range(1, sz.rows):
        send(field_copy(k, r, sample_of(row_peer(k))))
    for k in range(1, sz.ch):
        send(small_copy(k, c))
    for k in range(1, sz.rows):
        send(mask_copy(k, r))
    for k in range(1, sz.ch):
        send(mid_copy(k, c))
    for k in range(1, sz.rows):
        send(target_copy(k, r, sample_of(row_peer(k))))
    if peers:
        for k in range(1, sz.ch):
            pl.semaphore_signal(ready, inc=1, device_id=(ch_peer(k), r), device_id_type=MESH)

    for ref in (feat, hidden_low):
        for slot in range(sz.slots):
            ref[slot, 0] = jnp.zeros_like(ref[slot, 0])
            ref[slot, grid + 1] = jnp.zeros_like(ref[slot, 0])
    g_pad[0] = jnp.zeros_like(g_pad[0])
    g_pad[grid + 1] = jnp.zeros_like(g_pad[0])
    feat32[...] = jnp.zeros_like(feat32)
    glog32[...] = jnp.zeros_like(glog32)
    for ref in (d_mid, d_in, d_head, d_norm, loss):
        ref[...] = jnp.zeros_like(ref)

    for k in range(1, sz.ch):
        small_copy(k, ch_peer(k)).wait_recv()
    tail = ws_all[...].reshape(width, LANES)
    tail_t = jnp.transpose(tail)
    parts = []
    for ky in range(TAPS):
        at = IN_AT + ky * 12
        parts.append(jnp.concatenate([tail[:, at : at + 12], jnp.zeros((width, 4), F32)], axis=1))
    v_fwd[...] = jnp.concatenate(parts, axis=1).astype(BF16)
    parts = []
    for kx in range(TAPS):
        line = []
        for ky in range(TAPS):
            at = IN_AT + ((2 - ky) * TAPS + 2 - kx) * 4
            line.append(tail_t[at : at + 4])
        parts.append(jnp.concatenate(line, axis=1))
        parts.append(jnp.zeros((4, TAPS * width), F32))
    v_bwd[...] = jnp.concatenate(parts, axis=0).astype(BF16)
    head[...] = jnp.concatenate([tail_t[HEAD_AT : HEAD_AT + 2], jnp.zeros((14, width), F32)], axis=0).astype(BF16)
    for k in range(4):
        gains[k] = jnp.broadcast_to(tail[:, NORM_AT + k : NORM_AT + k + 1], (width, LANES))

    for k in range(1, sz.rows):
        field_copy(k, row_peer(k), 0).wait_recv()
        mask_copy(k, row_peer(k)).wait_recv()
    own[4].wait()
    own[5].wait()
    for row in range(sz.rows):
        at = pl.ds(row * sz.local, sz.local)
        for q in range(3):
            current[q, at, :] = f_stage[row, q]
        mask[at, :] = m_stage[row].astype(F32)

    def second_layer():
        for k in range(1, sz.ch):
            mid_copy(k, ch_peer(k)).wait_recv()
        mid = jnp.concatenate([wm_all[k, 0:co, :].astype(F32) for k in range(sz.ch)], axis=0)
        for kx in range(TAPS):
            w_fwd[kx * width : (kx + 1) * width, :] = mid[:, kx * TAPS * width : (kx + 1) * TAPS * width].astype(BF16)
        for kx in range(TAPS):
            parts = []
            for ky in range(TAPS):
                at = ((2 - kx) * TAPS + 2 - ky) * width
                parts.append(jnp.transpose(mid[:, at : at + width]))
            if kx == 1:
                pad = jnp.zeros((width, 14), F32)
                parts.append(jnp.concatenate([tail[:, HEAD_AT : HEAD_AT + 2], pad], axis=1))
            else:
                parts.append(jnp.zeros((width, 16), F32))
            w_bwd[kx * width : (kx + 1) * width, :] = jnp.concatenate(parts, axis=1).astype(BF16)

    def all_targets():
        for k in range(1, sz.rows):
            target_copy(k, row_peer(k), 0).wait_recv()
        own[6].wait()
        for row in range(sz.rows):
            at = pl.ds(row * sz.local, sz.local)
            for t in range(steps):
                target[t, at, :] = t_stage[row, t]

    marks = keyframes[...].astype(F32)
    valid = jnp.sum(jnp.sum(marks, axis=1, keepdims=True), axis=0, keepdims=True) * float(grid * sz.cols)
    inv_count = 1.0 / valid
    picked = jnp.where(lane_ids(marks.shape) == sample_of(r), marks, 0.0)
    marked = jnp.sum(picked, axis=1, keepdims=True)

    def key_of(t):
        return jnp.sum(jnp.where(row_ids(marked.shape) == t, marked, 0.0), axis=0, keepdims=True)

    def conv_and_stats(x_ref, w, height, store):
        zero = jnp.zeros((width, LANES), F32)

        def body(it, carry):
            base, total, squares = carry
            for k in range(2):
                i = it * 4 + k * 2
                p = dot(w[...], row_pair(x_ref, i))
                rows = combine(p, width) if height else [p[:, :LANES], p[:, LANES:]]
                if k == 0:
                    base = jnp.where(it == 0, rows[0], base)
                for j in range(2):
                    store[i + j] = rows[j]
                    d = rows[j] - base
                    total = total + d
                    squares = squares + d * d
            return base, total, squares

        base, total, squares = loop(grid // 4, 8, body, (zero, zero, zero))
        lane_mean = base + total * (1.0 / grid)
        lane_dev = squares - total * total * (1.0 / grid)
        count = float(GSIZE * LANES)
        mean = spread(group_sum(lane_mean) * (1.0 / count), width)
        d = lane_mean - mean
        var = spread(group_sum(lane_dev + grid * d * d) * (1.0 / (count * grid)), width)
        inv = lax.rsqrt(var + NORM_EPS)
        return mean, inv

    def silu_parts(y):
        s = 0.5 * jnp.tanh(0.5 * y) + 0.5
        h = y * s
        return h, s + h - h * s

    def step_forward(t, slot, first):
        if sz.slots == 1:
            for q in range(3):
                if first:
                    states[t, q] = current[q]
                else:
                    current[q] = states[t, q]
        x = [current[q] for q in range(3)]
        planes = [x[0], x[1], x[2], mask[...]]
        for q in range(4):
            for kx, plane in enumerate((from_left(planes[q]), planes[q], from_right(planes[q]))):
                feat32[pl.ds(kx * 4 + q, grid, stride=16), :] = plane

        def pack(it, carry):
            for k in range(4):
                i = it * 4 + k
                feat[slot, i + 1] = feat32[pl.ds(pl.multiple_of(i * 16, 16), 16), :].astype(BF16)
            return carry

        loop(grid // 4, 8, pack, 0)

        mean, inv = conv_and_stats(feat.at[slot], v_fwd, 0, conv.at[slot, 0])
        off = mean * inv
        gain, bias = gains[0], gains[1]
        inv_std[0, slot] = inv

        def norm_one(it, carry):
            for k in range(2):
                i = it * 2 + k
                n = conv[slot, 0, i] * inv - off
                h, sl = silu_parts(n * gain + bias)
                conv[slot, 0, i] = n
                slope[slot, 0, i] = sl
                hidden[i] = h
                hidden_low[slot, i + 1] = h.astype(BF16)
            return carry

        loop(grid // 2, 16, norm_one, 0)
        if first and t == 0:
            second_layer()

        mean, inv = conv_and_stats(hidden_low.at[slot], w_fwd, 1, conv.at[slot, 1])
        off = mean * inv
        gain, bias = gains[2], gains[3]
        inv_std[1, slot] = inv

        def norm_two(it, carry):
            i = it * 2
            lows = []
            for k in range(2):
                n = conv[slot, 1, i + k] * inv - off
                h, sl = silu_parts(n * gain + bias)
                conv[slot, 1, i + k] = n
                slope[slot, 1, i + k] = sl
                low = (hidden[i + k] + h).astype(BF16)
                mixed_low[slot, i + k] = low
                lows.append(low)
            p = dot(head[...], jnp.concatenate(lows, axis=1))
            for k in range(2):
                logits[0, pl.ds(i + k, 1), :] = p[0:1, k * LANES : (k + 1) * LANES]
                logits[1, pl.ds(i + k, 1), :] = p[1:2, k * LANES : (k + 1) * LANES]
            return carry

        loop(grid // 2, 16, norm_two, 0)

        if first and t == 0:
            all_targets()
        f0, f1 = jnp.tanh(logits[0]), jnp.tanh(logits[1])
        u1 = x[1] + TIME_STEP * f0
        v1 = x[2] + TIME_STEP * f1
        sy = COURANT * jnp.tanh(u1)
        sx = COURANT * jnp.tanh(v1)
        wy, wx = quadratic(sy), quadratic(sx)
        dwy, dwx = quadratic_slope(sy), quadratic_slope(sx)
        moved = []
        for n, q in enumerate((x[0], u1, v1)):
            val = jnp.zeros_like(q)
            by_y = jnp.zeros_like(q)
            by_x = jnp.zeros_like(q)
            for a, line in enumerate((from_above(q), q, from_below(q))):
                windows = (from_left(line), line, from_right(line))
                along = wx[0] * windows[0] + wx[1] * windows[1] + wx[2] * windows[2]
                slant = dwx[0] * windows[0] + dwx[1] * windows[1] + dwx[2] * windows[2]
                val = val + wy[a] * along
                by_y = by_y + dwy[a] * along
                by_x = by_x + wy[a] * slant
            moved.append(val)
            saved[slot, 4 + n] = by_y
            saved[slot, 7 + n] = by_x
        solid = mask[...]
        rho2, u2, v2 = moved
        div = 0.5 * (diff_rows(u2) + diff_cols(v2))
        press = -0.25 * solid * div
        for _ in range(JACOBI - 1):
            press = 0.25 * solid * (around(press) - div)
        if first:
            current[0] = rho2
            current[1] = solid * (u2 - 0.5 * diff_rows(press))
            current[2] = solid * (v2 - 0.5 * diff_cols(press))
        pull = key_of(t) * (rho2 - target[t])
        if first:
            loss[...] += FORCE_WEIGHT * (f0 * f0 + f1 * f1) + pull * (rho2 - target[t])
        saved[slot, 0] = f0
        saved[slot, 1] = f1
        saved[slot, 2] = sy
        saved[slot, 3] = sx
        saved[slot, 10] = pull

    for t in range(steps):
        step_forward(t, t if sz.slots > 1 else 0, True)

    def owner_of(j):
        return lax.rem(j, sz.rows)

    me = c * sz.rows + r if sz.ways > 1 else r

    def early_copy(k, j, shard, where, slot):
        tile = early.at[shard * sz.early + j]
        return remote(tile, early_in.at[j // sz.rows, slot], e_send.at[k], e_recv.at[j // sz.rows, slot], where)

    def gather_copy(k, j):
        return remote(early_fin.at[j], early_fin.at[j], g_send.at[j // sz.rows, k], g_recv.at[j], (c, row_peer(k)))

    def norm_copy(k, shard, j, where):
        line = ssq_early.at[shard, j]
        return remote(line, line, s_send.at[j // sz.rows, k], s_recv.at[shard, j], where)

    def for_owned(action):
        for m in range(sz.owned):
            j = r + m * sz.rows
            if (m + 1) * sz.rows <= sz.early:
                action(m, j)
            else:
                pl.when(j < sz.early)(functools.partial(action, m, j))

    def early_start():
        low_half = lane_ids((width, LANES)) < 64
        tiles = [d_mid[kx * width : (kx + 1) * width, 0:LANES] for kx in range(TAPS)]
        rest = [d_mid[kx * width : (kx + 1) * width, LANES:] for kx in range(2)]
        tiles.append(jnp.concatenate(rest, axis=1))
        for n, tile in enumerate(tiles):
            for h in range(width // 8):
                early[h * 4 + n] = tile[h * 8 : (h + 1) * 8]
        if sz.ch > 1:
            pl.semaphore_wait(ready, sz.ch - 1)
        for dc in range(sz.ways):
            shard = ch_peer(dc)
            for k in range(sz.early):
                j = lax.rem(r + k, sz.early)
                copy = early_copy(dc * sz.early + k, j, shard, (shard, owner_of(j)), me)
                if dc:
                    copy.start()
                else:
                    pl.when(owner_of(j) != r)(copy.start)

    def early_sum():
        def total(m, j):
            early_in[m, me] = early[c * sz.early + j]
            for k in range(1, sz.sources):
                slot = lax.rem(me + k, sz.sources)
                early_copy(0, j, c, (c, r), slot).wait_recv()
            acc = early_in[m, 0]
            for k in range(1, sz.sources):
                acc = acc + early_in[m, k]
            early_fin[j] = acc
            for k in range(1, sz.rows):
                gather_copy(k, j).start()
            ssq_early[c, j] = jnp.sum(acc * acc, axis=0, keepdims=True)
            for dc in range(1, sz.ch):
                for k in range(sz.rows):
                    norm_copy((dc - 1) * sz.rows + k, c, j, (ch_peer(dc), row_peer(k))).start()

        for_owned(total)

    def early_end():
        for j in range(sz.early):
            owner = j % sz.rows

            def arrived(j=j):
                gather_copy(0, j).wait_recv()
                acc = early_fin[j]
                ssq_early[c, j] = jnp.sum(acc * acc, axis=0, keepdims=True)

            if sz.rows > 1:
                pl.when(r != owner)(arrived)
            out[j] = early_fin[j]
        for dc in range(1, sz.ch):
            for j in range(sz.early):
                norm_copy(0, ch_peer(dc), j, (c, r)).wait_recv()
        for dc in range(sz.ways):
            for k in range(sz.early):
                j = lax.rem(r + k, sz.early)
                copy = early_copy(dc * sz.early + k, j, ch_peer(dc), (ch_peer(dc), owner_of(j)), me)
                if dc:
                    copy.wait_send()
                else:
                    pl.when(owner_of(j) != r)(copy.wait_send)

        def sent(m, j):
            for k in range(1, sz.rows):
                gather_copy(k, j).wait_send()
            for dc in range(1, sz.ch):
                for k in range(sz.rows):
                    norm_copy((dc - 1) * sz.rows + k, c, j, (ch_peer(dc), row_peer(k))).wait_send()

        for_owned(sent)

    def norm_back(k, inv, sums_d, sums_n):
        gain = gains[k]
        scale = 1.0 / float(GSIZE * LANES * grid)
        m1 = spread(group_sum(sums_d * gain) * scale, width)
        m2 = spread(group_sum(sums_n * gain) * scale, width)
        d_norm[k] += sums_n
        d_norm[k + 1] += sums_d
        return inv * gain, inv * m1, inv * m2

    def step_backward(t, slot):
        zero = jnp.zeros((width, LANES), F32)
        solid = mask[...]
        sy, sx = saved[slot, 2], saved[slot, 3]
        f0, f1 = saved[slot, 0], saved[slot, 1]
        grad_rho = grad_state[0] + 2.0 * inv_count * saved[slot, 10]
        gu = solid * grad_state[1]
        gv = solid * grad_state[2]
        g_press = 0.5 * (diff_rows(gu) + diff_cols(gv))
        g_div = jnp.zeros_like(g_press)
        for _ in range(JACOBI - 1):
            term = 0.25 * solid * g_press
            g_div = g_div - term
            g_press = around(term)
        g_div = g_div - 0.25 * solid * g_press
        gu = gu - 0.5 * diff_rows(g_div)
        gv = gv - 0.5 * diff_cols(g_div)
        wy, wx = quadratic(sy), quadratic(sx)
        spots = []
        g_sy = jnp.zeros_like(gu)
        g_sx = jnp.zeros_like(gu)
        for n, g in enumerate((grad_rho, gu, gv)):
            g_sy = g_sy + g * saved[slot, 4 + n]
            g_sx = g_sx + g * saved[slot, 7 + n]
            acc = None
            for a, shift in enumerate((from_below, lambda v: v, from_above)):
                ga = wy[a] * g
                line = from_right(wx[0] * ga) + wx[1] * ga + from_left(wx[2] * ga)
                line = shift(line)
                acc = line if acc is None else acc + line
            spots.append(acc)
        ty, tx = sy * (1.0 / COURANT), sx * (1.0 / COURANT)
        g_u1 = spots[1] + g_sy * (COURANT * (1.0 - ty * ty))
        g_v1 = spots[2] + g_sx * (COURANT * (1.0 - tx * tx))
        l0 = (TIME_STEP * g_u1 + 2.0 * FORCE_WEIGHT * inv_count * f0) * (1.0 - f0 * f0)
        l1 = (TIME_STEP * g_v1 + 2.0 * FORCE_WEIGHT * inv_count * f1) * (1.0 - f1 * f1)
        grad_state[0] = spots[0]
        grad_state[1] = g_u1
        grad_state[2] = g_v1
        glog32[pl.ds(0, grid, stride=16), :] = l0
        glog32[pl.ds(1, grid, stride=16), :] = l1

        def pack(it, carry):
            for k in range(4):
                i = it * 4 + k
                glog[i] = glog32[pl.ds(pl.multiple_of(i * 16, 16), 16), :].astype(BF16)
            return carry

        loop(grid // 4, 8, pack, 0)

        def back_a(it, carry):
            sums_d, sums_n = carry
            i = it * 2
            gl = jnp.concatenate([glog[i], glog[i + 1]], axis=1)
            p = dot(w_bwd[width : 2 * width, TAPS * width :], gl)
            for k in range(2):
                d = p[:, k * LANES : (k + 1) * LANES] * slope[slot, 1, i + k]
                dy[i + k] = d
                sums_d = sums_d + d
                sums_n = sums_n + d * conv[slot, 1, i + k]
            ml = jnp.concatenate([mixed_low[slot, i], mixed_low[slot, i + 1]], axis=1)
            d_head[...] += dot_nt(gl, ml)
            return sums_d, sums_n

        sums = loop(grid // 2, 16, back_a, (zero, zero))
        fd, f1_, fn = norm_back(2, inv_std[1, slot], *sums)

        def back_b(it, carry):
            for k in range(2):
                i = it * 2 + k
                g = fd * dy[i] - f1_ - fn * conv[slot, 1, i]
                low = g.astype(BF16)
                g_pad[i + 1] = low
                g = low.astype(F32)
                g_taps[i, 0:width] = from_right(g).astype(BF16)
                g_taps[i, width : 2 * width] = low
                g_taps[i, 2 * width : 3 * width] = from_left(g).astype(BF16)
            return carry

        loop(grid // 2, 16, back_b, 0)

        def wgrad(it, carry):
            acc = None
            for k in range(2):
                i = it * 4 + k * 2
                gt = jnp.concatenate([g_taps[i], g_taps[i + 1]], axis=1)
                term = dot_nt(gt, row_pair(hidden_low.at[slot], i))
                acc = term if acc is None else acc + term
            d_mid[...] += acc
            return carry

        loop(grid // 4, 8, wgrad, 0)
        if t == 0:
            early_start()

        def back_c(it, carry):
            sums_d, sums_n = carry
            i = it * 2
            rows = combine(dot(w_bwd[...], row_pair(g_pad, i, glog)), width)
            for k in range(2):
                d = rows[k] * slope[slot, 0, i + k]
                dy[i + k] = d
                sums_d = sums_d + d
                sums_n = sums_n + d * conv[slot, 0, i + k]
            return sums_d, sums_n

        sums = loop(grid // 2, 16, back_c, (zero, zero))
        fd, f1_, fn = norm_back(0, inv_std[0, slot], *sums)

        def back_d(it, carry):
            i = it * 2
            lows = []
            for k in range(2):
                low = (fd * dy[i + k] - f1_ - fn * conv[slot, 0, i + k]).astype(BF16)
                g_pad[i + k + 1] = low
                lows.append(low)
            d_in[...] += dot_nt(jnp.concatenate(lows, axis=1), row_pair(feat.at[slot], i))
            return carry

        loop(grid // 2, 16, back_d, 0)

        if t > 0:

            def back_e(it, carry):
                i = it * 2
                rows = combine(dot(v_bwd[...], row_pair(g_pad, i)), 8)
                for k in range(2):
                    gs_rows[pl.ds(pl.multiple_of((i + k) * 8, 8), 8), :] = rows[k]
                return carry

            loop(grid // 2, 16, back_e, 0)
            for q in range(3):
                grad_state[q] += gs_rows[pl.ds(q, grid, stride=8), :]

    grad_state[...] = jnp.zeros_like(grad_state)

    for t in reversed(range(steps)):
        if sz.slots == 1:
            step_forward(t, 0, False)
        step_backward(t, t if sz.slots > 1 else 0)

    pieces = [d_mid[2 * width : 3 * width, LANES:]]
    pieces += [d_in[:, ky * 16 : ky * 16 + 12] for ky in range(TAPS)]
    pieces.append(jnp.transpose(d_head[...])[:, 0:2])
    for k in range(4):
        pieces.append(jnp.sum(d_norm[k], axis=1, keepdims=True))
    total = jnp.sum(jnp.sum(loss[...], axis=1, keepdims=True), axis=0, keepdims=True)
    pieces.append(jnp.broadcast_to(total, (width, 1)))
    pieces.append(jnp.zeros((width, 64 - 43), F32))
    late[...] = jnp.concatenate(pieces, axis=1)

    def shard_rows(shard):
        return pl.ds(pl.multiple_of(shard * co, 8), co)

    def late_one(k, src_shard, dst_slot):
        return remote(late.at[shard_rows(src_shard)], late_ch.at[dst_slot], a_send.at[k], a_recv.at[dst_slot], (ch_peer(k), r))

    def late_two(k, slot):
        return remote(late_part, late_rows.at[slot], b_send.at[k], b_recv.at[slot], (c, row_peer(k)))

    def late_norm(k, slot):
        return remote(ssq_late.at[slot], ssq_late.at[slot], n_send.at[k], n_recv.at[slot], (ch_peer(k), r))

    if sz.ways > 1:
        for k in range(1, sz.ch):
            send(late_one(k, ch_peer(k), c))

    early_sum()

    if sz.ways > 1:
        late_ch[c] = late[shard_rows(c), :]
        for k in range(1, sz.ch):
            late_one(k, c, ch_peer(k)).wait_recv()
        acc = late_ch[0]
        for k in range(1, sz.ch):
            acc = acc + late_ch[k]
    else:
        acc = late[shard_rows(c), :]
    late_part[...] = acc
    late_rows[r] = acc
    for k in range(1, sz.rows):
        send(late_two(k, r))
    for k in range(1, sz.rows):
        late_two(k, row_peer(k)).wait_recv()
    acc = late_rows[0]
    for k in range(1, sz.rows):
        acc = acc + late_rows[k]
    for h in range(sz.halves):
        out[sz.early + h] = acc[h * 8 : (h + 1) * 8]
    acc = jnp.where(lane_ids(acc.shape) < LOSS_AT, acc, 0.0)
    ssq_late[c] = jnp.sum(acc * acc, axis=0, keepdims=True)
    for k in range(1, sz.ch):
        send(late_norm(k, c))

    early_end()
    for k in range(1, sz.ch):
        late_norm(k, ch_peer(k)).wait_recv()
    acc = ssq_late[0]
    for k in range(1, sz.ch):
        acc = acc + ssq_late[k]
    for k in range(sz.ch):
        for j in range(sz.early):
            acc = acc + ssq_early[k, j]
    out_total[...] = jnp.broadcast_to(jnp.sum(acc, axis=1, keepdims=True), (8, LANES))
    for copy in copies:
        copy.wait_send()


def adam(weight, grad, moment, square, rate, decay):
    moment = BETA_ONE * moment + (1.0 - BETA_ONE) * grad
    square = BETA_TWO * square + (1.0 - BETA_TWO) * grad * grad
    fix_one = 1.0 - BETA_ONE**STEP_NUM
    fix_two = 1.0 - BETA_TWO**STEP_NUM
    updated = weight - rate * (moment / fix_one / (jnp.sqrt(square / fix_two) + ADAM_EPS) + decay * weight)
    return updated, moment, square


def adam_kernel(sz, grads, total, keyframes, *refs):
    params, firsts, seconds = refs[0:4], refs[4:8], refs[8:12]
    news, moments, squares = refs[12:16], refs[16:20], refs[20:24]
    co, width = sz.co, sz.width
    norm = jnp.sqrt(total[0:1, 0:1])
    factor = CLIP / jnp.maximum(norm, CLIP)

    def put(n, at, grad):
        rate, decay = (RATE, DECAY) if n < 3 else (GAIN_RATE, 0.0)
        new, moment, square = adam(params[n][at], grad, firsts[n][at], seconds[n][at], rate, decay)
        news[n][at] = new
        moments[n][at] = moment
        squares[n][at] = square

    tiles = []
    for n in range(4):
        tiles.append(jnp.concatenate([grads[h * 4 + n] for h in range(sz.halves)], axis=0) * factor)
    tail = jnp.concatenate([grads[sz.early + h] for h in range(sz.halves)], axis=0)
    loss = tail[0:1, LOSS_AT : LOSS_AT + 1]
    tail = tail * factor
    thirds = [tiles[3][:, :width], tiles[3][:, width:], tail[:, :width]]
    for kx in range(TAPS):
        put(1, (0, kx), tiles[kx][:, :width])
        put(1, (1, kx), tiles[kx][:, width:])
        put(1, (2, kx), thirds[kx])
    tail = jnp.concatenate([tail, jnp.zeros((LANES - co, LANES), F32)], axis=0)
    tail = jnp.transpose(tail)
    for ky in range(TAPS):
        for kx in range(TAPS):
            at = IN_AT + (ky * TAPS + kx) * 4
            put(0, (ky, kx), tail[at : at + 4, 0:co])
    put(2, Ellipsis, tail[HEAD_AT : HEAD_AT + 2, 0:co])
    put(3, Ellipsis, tail[NORM_AT : NORM_AT + 4, 0:co])
    marks = keyframes[...].astype(F32)
    valid = jnp.sum(jnp.sum(marks, axis=1, keepdims=True), axis=0, keepdims=True) * float(sz.grid * sz.cols)
    refs[24][...] = norm
    refs[25][...] = loss
    refs[26][...] = valid


def scratch_of(sz):
    grid, width, rows, ch, slots, steps = sz.grid, sz.width, sz.rows, sz.ch, sz.slots, sz.steps
    wide = TAPS * width

    def f32(*shape):
        return pltpu.VMEM(shape, F32)

    def bf16(*shape):
        return pltpu.VMEM(shape, BF16)

    dma = lambda *shape: pltpu.SemaphoreType.DMA(shape)
    return {
        "f_stage": f32(rows, 3, sz.local, LANES),
        "t_stage": f32(rows, steps, sz.local, LANES),
        "m_stage": pltpu.VMEM((rows, sz.local, LANES), jnp.int32),
        "w_in_own": f32(TAPS, TAPS, 4, sz.co),
        "w_mid_own": f32(TAPS, TAPS, sz.co, width),
        "w_head_own": f32(2, sz.co),
        "norms_own": f32(4, sz.co),
        "small": f32(LANES, LANES),
        "ws_all": f32(ch, sz.co, LANES),
        "wm_all": bf16(ch, -(-sz.co // 16) * 16, sz.mid_lanes),
        "w_fwd": bf16(wide, wide),
        "w_bwd": bf16(wide, wide + 16),
        "v_fwd": bf16(width, TAPS * 16),
        "v_bwd": bf16(TAPS * 8, wide),
        "head": bf16(16, width),
        "gains": f32(4, width, LANES),
        "current": f32(3, grid, LANES),
        "states": f32(1 if slots > 1 else steps, 3, grid, LANES),
        "mask": f32(grid, LANES),
        "target": f32(steps, grid, LANES),
        "feat32": f32(grid * 16, LANES),
        "feat": bf16(slots, grid + 2, 16, LANES),
        "conv": f32(slots, 2, grid, width, LANES),
        "slope": f32(slots, 2, grid, width, LANES),
        "inv_std": f32(2, slots, width, LANES),
        "hidden": f32(grid, width, LANES),
        "hidden_low": bf16(slots, grid + 2, width, LANES),
        "mixed_low": bf16(slots, grid, width, LANES),
        "logits": f32(2, grid, LANES),
        "saved": f32(slots, SAVED, grid, LANES),
        "dy": f32(grid, width, LANES),
        "glog32": f32(grid * 16, LANES),
        "glog": bf16(grid, 16, LANES),
        "g_pad": bf16(grid + 2, width, LANES),
        "g_taps": bf16(grid, wide, LANES),
        "gs_rows": f32(grid * 8, LANES),
        "grad_state": f32(3, grid, LANES),
        "d_mid": f32(wide, wide),
        "d_in": f32(width, TAPS * 16),
        "d_head": f32(16, width),
        "d_norm": f32(4, width, LANES),
        "loss": f32(grid, LANES),
        "early": f32(width // 8 * 4, 8, LANES),
        "early_in": f32(sz.owned, sz.sources, 8, LANES),
        "early_fin": f32(sz.early, 8, LANES),
        "ssq_early": f32(ch, sz.early, 1, LANES),
        "late": f32(width, LANES),
        "late_ch": f32(ch, sz.co, LANES),
        "late_part": f32(sz.co, LANES),
        "late_rows": f32(rows, sz.co, LANES),
        "ssq_late": f32(ch, 1, LANES),
        "ready": pltpu.SemaphoreType.REGULAR,
        "local_sem": dma(7),
        "f_send": dma(rows),
        "f_recv": dma(rows),
        "t_send": dma(rows),
        "t_recv": dma(rows),
        "m_send": dma(rows),
        "m_recv": dma(rows),
        "v_send": dma(ch),
        "v_recv": dma(ch),
        "w_send": dma(ch),
        "w_recv": dma(ch),
        "e_send": dma(sz.ways * sz.early),
        "e_recv": dma(sz.owned, sz.sources),
        "g_send": dma(sz.owned, rows),
        "g_recv": dma(sz.early),
        "s_send": dma(sz.owned, ch * rows),
        "s_recv": dma(ch, sz.early),
        "a_send": dma(ch),
        "a_recv": dma(ch),
        "b_send": dma(rows),
        "b_recv": dma(rows),
        "n_send": dma(ch),
        "n_recv": dma(ch),
    }


def shards(mesh, fields, targets, fluid, keyframes, *rest):
    params, firsts, seconds = rest[0:4], rest[4:8], rest[8:12]

    def native(leaves):
        return (leaves[0], jnp.swapaxes(leaves[1], 2, 3), leaves[2].T, leaves[3])

    params, firsts, seconds = native(params), native(firsts), native(seconds)
    sz = Sizes(mesh, fields.shape, targets.shape, params[0].shape[3])
    marks = keyframes.T
    vmem = pl.BlockSpec(memory_space=pltpu.VMEM)
    hbm = pl.BlockSpec(memory_space=pl.ANY)
    alone = sz.rows == 1 and sz.ch == 1
    grads, total = pl.pallas_call(
        functools.partial(train_kernel, sz),
        out_shape=(
            jax.ShapeDtypeStruct((sz.early + sz.halves, 8, LANES), F32),
            jax.ShapeDtypeStruct((8, LANES), F32),
        ),
        in_specs=[hbm, hbm, hbm, vmem] + [hbm] * 4,
        out_specs=(vmem, vmem),
        scratch_shapes=list(scratch_of(sz).values()),
        compiler_params=pltpu.CompilerParams(
            collective_id=None if alone else 0, has_side_effects=True, vmem_limit_bytes=60 << 20
        ),
        name="train",
    )(fields, targets, fluid, marks, *params)
    shapes = [jax.ShapeDtypeStruct(leaf.shape, F32) for leaf in params] * 3
    shapes += [jax.ShapeDtypeStruct((1, 1), F32)] * 3
    results = pl.pallas_call(
        functools.partial(adam_kernel, sz),
        out_shape=tuple(shapes),
        in_specs=[vmem] * 15,
        out_specs=tuple([vmem] * 15),
        name="adamw",
    )(grads, total, marks, *params, *firsts, *seconds)
    outs = []
    for n in range(3):
        outs.extend(native(results[4 * n : 4 * n + 4]))
    return (*outs, *[leaf.reshape(()) for leaf in results[12:]])


def solution(mesh):
    split = (P(None, None, None, "ch"), P(None, None, None, "ch"), P("ch", None), P(None, "ch"))
    return jax.shard_map(
        functools.partial(shards, mesh),
        mesh=mesh,
        in_specs=(
            P(None, None, "rows", None),
            P(None, None, "rows", None),
            P("rows", None),
            P(),
            *split,
            *split,
            *split,
        ),
        out_specs=(*split, *split, *split, P(), P(), P()),
        check_vma=False,
    )
```

```python
import functools

import jax
import jax.numpy as jnp
from jax import lax
from jax.experimental import pallas as pl
from jax.experimental.pallas import tpu as pltpu
from jax.sharding import PartitionSpec as P

GROUPS = 8
JACOBI = 3
STEP_NUM = 10
TIME_STEP = 0.5
COURANT = 0.8
FORCE_WEIGHT = 0.5
NORM_EPS = 1e-05
CLIP = 0.0001
BETA_ONE = 0.9
BETA_TWO = 0.999
ADAM_EPS = 1e-10
RATE = 0.1
GAIN_RATE = 0.6
DECAY = 0.01

MESH = pl.DeviceIdType.MESH
F32 = jnp.float32
BF16 = jnp.bfloat16
LANES = 128
GSIZE = 8
TAPS = 3
SAVED = 11
NT = (((1,), (1,)), ((), ()))


def lane_ids(shape):
    return lax.broadcasted_iota(jnp.int32, shape, len(shape) - 1)


def row_ids(shape):
    return lax.broadcasted_iota(jnp.int32, shape, 0)


def from_left(x):
    return jnp.where(lane_ids(x.shape) == 0, jnp.zeros_like(x), pltpu.roll(x, 1, 1))


def from_right(x):
    size = x.shape[1]
    return jnp.where(lane_ids(x.shape) == size - 1, jnp.zeros_like(x), pltpu.roll(x, size - 1, 1))


def from_above(x):
    return jnp.where(row_ids(x.shape) == 0, 0.0, pltpu.roll(x, 1, 0))


def from_below(x):
    size = x.shape[0]
    return jnp.where(row_ids(x.shape) == size - 1, 0.0, pltpu.roll(x, size - 1, 0))


def diff_rows(x):
    return from_below(x) - from_above(x)


def diff_cols(x):
    return from_right(x) - from_left(x)


def around(x):
    return from_below(x) + from_above(x) + from_right(x) + from_left(x)


def quadratic(s):
    return (0.5 * s * (s + 1.0), 1.0 - s * s, 0.5 * s * (s - 1.0))


def quadratic_slope(s):
    return (s + 0.5, -2.0 * s, s - 0.5)


def dot(a, b):
    return jnp.dot(a, b, preferred_element_type=F32)


def dot_nt(a, b):
    return lax.dot_general(a, b, NT, preferred_element_type=F32)


def row_pair(ref, i, extra=None):
    depth = ref.shape[1] * TAPS
    sides = []
    for k in range(2):
        side = ref[pl.ds(i + k, TAPS)].reshape(depth, LANES)
        if extra is not None:
            side = jnp.concatenate([side, extra[i + k]], axis=0)
        sides.append(side)
    return jnp.concatenate(sides, axis=1)


PACKED = True


def side_by_side(ref, first):
    return jnp.concatenate([ref[i] for i in range(first, ref.shape[0])], axis=1)


def combine(p, height):
    out = []
    for k in range(2):
        part = p[:, k * LANES : (k + 1) * LANES]
        out.append(
            part[height : 2 * height]
            + from_left(part[:height])
            + from_right(part[2 * height : 3 * height])
        )
    return out


def group_sum(x):
    return jnp.sum(jnp.sum(x.reshape(-1, GSIZE, LANES), axis=1), axis=1, keepdims=True)


def spread(x, width):
    return jnp.broadcast_to(x[:, :, None], (x.shape[0], GSIZE, LANES)).reshape(width, LANES)


def loop(count, per, body, carry):
    per = min(per, count)

    def several(it, carry):
        for k in range(per):
            carry = body(it * per + k, carry)
        return carry

    if count == per:
        return several(0, carry)
    return lax.fori_loop(0, count // per, several, carry)


class Sizes:
    def __init__(self, mesh, fields_shape, targets_shape, co):
        self.ch = mesh.shape["ch"]
        self.rows = mesh.shape["rows"]
        self.batch = fields_shape[0]
        self.local = fields_shape[2]
        self.grid = self.local * self.rows
        self.cols = fields_shape[3]
        self.steps = targets_shape[0]
        self.co = co
        self.width = co * self.ch
        self.per_rows = self.batch // self.rows
        self.ways = self.ch if self.per_rows == self.ch else 1
        assert self.per_rows == self.ways and self.batch % self.rows == 0
        assert self.cols == LANES
        slot = self.grid * self.width * LANES * 20
        self.slots = self.steps if slot * self.steps < (24 << 20) else 1
        self.halves = co // 8
        self.early = 4 * self.halves + 1
        self.owned = -(-self.early // self.rows)
        self.sources = self.ways * self.rows
        self.cores = 2 if self.ways > 1 else 1
        self.chips = self.sources // self.cores
        self.late = 4 // self.cores
        assert self.ways % self.cores == 0
        self.mid_lanes = TAPS * TAPS * self.width
        assert self.width == 64 and co % 8 == 0


IN_AT = 64
HEAD_AT = IN_AT + 36
NORM_AT = HEAD_AT + 2
LOSS_AT = NORM_AT + 4


def train_kernel(sz, fields, targets, fluid, keyframes, w_in, w_mid, w_head, norms, out, out_total, *scratch):
    z = dict(zip(scratch_of(sz), scratch))
    f_stage = z["f_stage"]
    t_stage = z["t_stage"]
    m_stage = z["m_stage"]
    w_in_own = z["w_in_own"]
    w_mid_own = z["w_mid_own"]
    w_head_own = z["w_head_own"]
    norms_own = z["norms_own"]
    small = z["small"]
    ws_all = z["ws_all"]
    wm_all = z["wm_all"]
    w_fwd = z["w_fwd"]
    w_bwd = z["w_bwd"]
    v_fwd = z["v_fwd"]
    v_bwd = z["v_bwd"]
    head = z["head"]
    gains = z["gains"]
    current = z["current"]
    states = z["states"]
    mask = z["mask"]
    target = z["target"]
    feat32 = z["feat32"]
    feat = z["feat"]
    conv = z["conv"]
    slope = z["slope"]
    norm_stats = z["norm_stats"]
    hidden = z["hidden"]
    hidden_low = z["hidden_low"]
    mixed_low = z["mixed_low"]
    logits = z["logits"]
    saved = z["saved"]
    dy = z["dy"]
    glog32 = z["glog32"]
    glog = z["glog"]
    g_pad = z["g_pad"]
    g_taps = z["g_taps"]
    gs_rows = z["gs_rows"]
    grad_state = z["grad_state"]
    d_mid = z["d_mid"]
    d_in = z["d_in"]
    d_head = z["d_head"]
    d_norm = z["d_norm"]
    loss = z["loss"]
    early = z["early"]
    early_in = z["early_in"]
    early_fin = z["early_fin"]
    blank = z["blank"]
    ssq_early = z["ssq_early"]
    late_pair = z["late_pair"]
    late_sum = z["late_sum"]
    late_in = z["late_in"]
    late_fin = z["late_fin"]
    ready = z["ready"]
    local_sem = z["local_sem"]
    f_sem = z["f_sem"]
    t_sem = z["t_sem"]
    m_sem = z["m_sem"]
    v_sem = z["v_sem"]
    w_sem = z["w_sem"]
    e_send = z["e_send"]
    e_recv = z["e_recv"]
    g_send = z["g_send"]
    g_recv = z["g_recv"]
    s_send = z["s_send"]
    s_recv = z["s_recv"]
    b_send = z["b_send"]
    b_recv = z["b_recv"]
    p_send = z["p_send"]
    p_recv = z["p_recv"]
    c = lax.axis_index("ch")
    r = lax.axis_index("rows")
    width, grid, steps = sz.width, sz.grid, sz.steps
    co = sz.co

    def row_peer(k):
        return lax.rem(r + k, sz.rows)

    def ch_peer(k):
        return lax.rem(c + k, sz.ch)

    def sample_of(row):
        return row * sz.per_rows + (c if sz.ways > 1 else 0)

    peers = sz.rows - 1 + sz.ch - 1
    if peers:
        barrier = pltpu.get_barrier_semaphore()
        for k in range(1, sz.rows):
            pl.semaphore_signal(barrier, inc=1, device_id=(c, row_peer(k)), device_id_type=MESH)
        for k in range(1, sz.ch):
            pl.semaphore_signal(barrier, inc=1, device_id=(ch_peer(k), r), device_id_type=MESH)

    def remote(src, dst, send, recv, where):
        return pltpu.make_async_remote_copy(
            src_ref=src, dst_ref=dst, send_sem=send, recv_sem=recv, device_id=where, device_id_type=MESH
        )

    def arrived(ref, sem):
        remote(ref, ref, sem, sem, (c, r)).wait_recv()

    def sent(ref, sem):
        remote(ref, ref, sem, sem, (c, r)).wait_send()

    def but_one(ref):
        return ref.at[pl.ds(0, ref.shape[0] - 1)]

    own = [
        pltpu.make_async_copy(src, dst, local_sem.at[n])
        for n, (src, dst) in enumerate(
            (
                (w_in, w_in_own),
                (w_head, w_head_own),
                (norms, norms_own),
                (w_mid, w_mid_own),
                (fields.at[sample_of(r)], f_stage.at[r]),
                (fluid, m_stage.at[r]),
                (targets.at[:, sample_of(r)], t_stage.at[r]),
            )
        )
    ]
    for copy in own:
        copy.start()

    small[...] = jnp.zeros_like(small)
    for n in range(4):
        own[n].wait()
    for ky in range(TAPS):
        for kx in range(TAPS):
            at = IN_AT + (ky * TAPS + kx) * 4
            small[at : at + 4, 0:co] = w_in_own[ky, kx]
    small[HEAD_AT : HEAD_AT + 2, 0:co] = w_head_own[...]
    small[NORM_AT : NORM_AT + 4, 0:co] = norms_own[...]
    ws_all[c] = jnp.transpose(small[...])[0:co]
    mine = jnp.concatenate([w_mid_own[ky, kx] for kx in range(TAPS) for ky in range(TAPS)], axis=1)
    wm_all[c, 0:co, :] = mine.astype(BF16)

    if peers:
        pl.semaphore_wait(barrier, peers)

    for k in range(1, sz.rows):
        src = fields.at[sample_of(row_peer(k))]
        remote(src, f_stage.at[r], f_sem.at[0], f_sem.at[1], (c, row_peer(k))).start()
    for k in range(1, sz.ch):
        remote(ws_all.at[c], ws_all.at[c], v_sem.at[0], v_sem.at[1], (ch_peer(k), r)).start()
    for k in range(1, sz.rows):
        remote(fluid, m_stage.at[r], m_sem.at[0], m_sem.at[1], (c, row_peer(k))).start()
    for k in range(1, sz.ch):
        remote(wm_all.at[c], wm_all.at[c], w_sem.at[0], w_sem.at[1], (ch_peer(k), r)).start()
    for k in range(1, sz.rows):
        src = targets.at[:, sample_of(row_peer(k))]
        remote(src, t_stage.at[r], t_sem.at[0], t_sem.at[1], (c, row_peer(k))).start()
    row_groups = ((f_stage, f_sem), (m_stage, m_sem), (t_stage, t_sem)) if sz.rows > 1 else ()
    ch_groups = ((ws_all, v_sem), (wm_all, w_sem)) if sz.ch > 1 else ()
    if peers:
        for k in range(1, sz.ch):
            pl.semaphore_signal(ready, inc=1, device_id=(ch_peer(k), r), device_id_type=MESH)

    for ref in (feat, hidden_low, g_pad):
        for slot in range(sz.slots):
            ref[slot, 0] = jnp.zeros_like(ref[slot, 0])
            ref[slot, grid + 1] = jnp.zeros_like(ref[slot, 0])
    feat32[...] = jnp.zeros_like(feat32)
    glog32[...] = jnp.zeros_like(glog32)
    for ref in (d_mid, d_in, d_head, d_norm, loss):
        ref[...] = jnp.zeros_like(ref)

    if ch_groups:
        arrived(but_one(ws_all), v_sem.at[1])
    tail = ws_all[...].reshape(width, LANES)
    tail_t = jnp.transpose(tail)
    parts = []
    for ky in range(TAPS):
        at = IN_AT + ky * 12
        parts.append(jnp.concatenate([tail[:, at : at + 12], jnp.zeros((width, 4), F32)], axis=1))
    v_fwd[...] = jnp.concatenate(parts, axis=1).astype(BF16)
    parts = []
    for kx in range(TAPS):
        line = []
        for ky in range(TAPS):
            at = IN_AT + ((2 - ky) * TAPS + 2 - kx) * 4
            line.append(tail_t[at : at + 4])
        parts.append(jnp.concatenate(line, axis=1))
        parts.append(jnp.zeros((4, TAPS * width), F32))
    v_bwd[...] = jnp.concatenate(parts, axis=0).astype(BF16)
    head[...] = jnp.concatenate([tail_t[HEAD_AT : HEAD_AT + 2], jnp.zeros((14, width), F32)], axis=0).astype(BF16)
    for k in range(4):
        gains[k] = jnp.broadcast_to(tail[:, NORM_AT + k : NORM_AT + k + 1], (width, LANES))

    for ref, sem in row_groups[:2]:
        arrived(but_one(ref), sem.at[1])
    own[4].wait()
    own[5].wait()
    for row in range(sz.rows):
        at = pl.ds(row * sz.local, sz.local)
        for q in range(3):
            current[q, at, :] = f_stage[row, q]
        mask[at, :] = m_stage[row].astype(F32)

    def second_layer():
        if ch_groups:
            arrived(but_one(wm_all), w_sem.at[1])
        mid = jnp.concatenate([wm_all[k, 0:co, :].astype(F32) for k in range(sz.ch)], axis=0)
        for kx in range(TAPS):
            w_fwd[kx * width : (kx + 1) * width, :] = mid[:, kx * TAPS * width : (kx + 1) * TAPS * width].astype(BF16)
        for kx in range(TAPS):
            parts = []
            for ky in range(TAPS):
                at = ((2 - kx) * TAPS + 2 - ky) * width
                parts.append(jnp.transpose(mid[:, at : at + width]))
            if kx == 1:
                pad = jnp.zeros((width, 14), F32)
                parts.append(jnp.concatenate([tail[:, HEAD_AT : HEAD_AT + 2], pad], axis=1))
            else:
                parts.append(jnp.zeros((width, 16), F32))
            w_bwd[kx * width : (kx + 1) * width, :] = jnp.concatenate(parts, axis=1).astype(BF16)

    def all_targets():
        if row_groups:
            arrived(but_one(t_stage), t_sem.at[1])
        own[6].wait()
        for row in range(sz.rows):
            at = pl.ds(row * sz.local, sz.local)
            for t in range(steps):
                target[t, at, :] = t_stage[row, t]

    marks = keyframes[...].astype(F32)
    valid = jnp.sum(jnp.sum(marks, axis=1, keepdims=True), axis=0, keepdims=True) * float(grid * sz.cols)
    inv_count = 1.0 / valid
    picked = jnp.where(lane_ids(marks.shape) == sample_of(r), marks, 0.0)
    marked = jnp.sum(picked, axis=1, keepdims=True)

    def key_of(t):
        return jnp.sum(jnp.where(row_ids(marked.shape) == t, marked, 0.0), axis=0, keepdims=True)

    def conv_and_stats(x_ref, w, height, store):
        zero = jnp.zeros((width, LANES), F32)

        def body(it, carry):
            base, total, squares = carry
            for k in range(2):
                i = it * 4 + k * 2
                p = dot(w[...], row_pair(x_ref, i))
                rows = combine(p, width) if height else [p[:, :LANES], p[:, LANES:]]
                if k == 0:
                    base = jnp.where(it == 0, rows[0], base)
                for j in range(2):
                    store[i + j] = rows[j]
                    d = rows[j] - base
                    total = total + d
                    squares = squares + d * d
            return base, total, squares

        base, total, squares = loop(grid // 4, 8, body, (zero, zero, zero))
        lane_mean = base + total * (1.0 / grid)
        lane_dev = squares - total * total * (1.0 / grid)
        count = float(GSIZE * LANES)
        middle = spread(group_sum(base) * (1.0 / count), width)
        d = lane_mean - middle
        first = spread(group_sum(d) * (1.0 / count), width)
        second = spread(group_sum(lane_dev + grid * d * d) * (1.0 / (count * grid)), width)
        return middle + first, lax.rsqrt(second - first * first + NORM_EPS)

    def silu_parts(half):
        t = jnp.tanh(half)
        a = 1.0 + t
        h = half * a
        return h, a + h * (1.0 - t)

    def half_affine(mean, inv, k):
        scale = 0.5 * inv * gains[k]
        return scale, 0.5 * gains[k + 1] - mean * scale

    def step_forward(t, slot, first):
        if sz.slots == 1:
            for q in range(3):
                if first:
                    states[t, q] = current[q]
                else:
                    current[q] = states[t, q]
        x = [current[q] for q in range(3)]
        planes = [x[0], x[1], x[2], mask[...]]
        for q in range(4):
            for kx, plane in enumerate((from_left(planes[q]), planes[q], from_right(planes[q]))):
                feat32[pl.ds(kx * 4 + q, grid, stride=16), :] = plane

        def pack(it, carry):
            for k in range(4):
                i = it * 4 + k
                feat[slot, i + 1] = feat32[pl.ds(pl.multiple_of(i * 16, 16), 16), :].astype(BF16)
            return carry

        loop(grid // 4, 8, pack, 0)

        mean, inv = conv_and_stats(feat.at[slot], v_fwd, 0, conv.at[slot, 0])
        if first and t == 0:
            second_layer()
        mul, add = half_affine(mean, inv, 0)
        norm_stats[0, slot] = mean
        norm_stats[1, slot] = inv

        def norm_one(it, carry):
            for k in range(2):
                i = it * 2 + k
                h, slope[slot, 0, i] = silu_parts(conv[slot, 0, i] * mul + add)
                hidden[i] = h
                hidden_low[slot, i + 1] = h.astype(BF16)
            return carry

        loop(grid // 2, 16, norm_one, 0)

        mean, inv = conv_and_stats(hidden_low.at[slot], w_fwd, 1, conv.at[slot, 1])
        mul, add = half_affine(mean, inv, 2)
        norm_stats[2, slot] = mean
        norm_stats[3, slot] = inv

        def norm_two(it, carry):
            i = it * 2
            lows = []
            for k in range(2):
                h, slope[slot, 1, i + k] = silu_parts(conv[slot, 1, i + k] * mul + add)
                low = (hidden[i + k] + h).astype(BF16)
                mixed_low[slot, i + k] = low
                lows.append(low)
            p = dot(head[...], jnp.concatenate(lows, axis=1))
            for k in range(2):
                logits[0, pl.ds(i + k, 1), :] = p[0:1, k * LANES : (k + 1) * LANES]
                logits[1, pl.ds(i + k, 1), :] = p[1:2, k * LANES : (k + 1) * LANES]
            return carry

        loop(grid // 2, 16, norm_two, 0)

        if first and t == 0:
            all_targets()
        f0, f1 = jnp.tanh(logits[0]), jnp.tanh(logits[1])
        u1 = x[1] + TIME_STEP * f0
        v1 = x[2] + TIME_STEP * f1
        sy = COURANT * jnp.tanh(u1)
        sx = COURANT * jnp.tanh(v1)
        wy, wx = quadratic(sy), quadratic(sx)
        dwy, dwx = quadratic_slope(sy), quadratic_slope(sx)
        moved = []
        for n, q in enumerate((x[0], u1, v1)):
            val = jnp.zeros_like(q)
            by_y = jnp.zeros_like(q)
            by_x = jnp.zeros_like(q)
            for a, line in enumerate((from_above(q), q, from_below(q))):
                windows = (from_left(line), line, from_right(line))
                along = wx[0] * windows[0] + wx[1] * windows[1] + wx[2] * windows[2]
                slant = dwx[0] * windows[0] + dwx[1] * windows[1] + dwx[2] * windows[2]
                val = val + wy[a] * along
                by_y = by_y + dwy[a] * along
                by_x = by_x + wy[a] * slant
            moved.append(val)
            saved[slot, 4 + n] = by_y
            saved[slot, 7 + n] = by_x
        solid = mask[...]
        rho2, u2, v2 = moved
        div = 0.5 * (diff_rows(u2) + diff_cols(v2))
        press = -0.25 * solid * div
        for _ in range(JACOBI - 1):
            press = 0.25 * solid * (around(press) - div)
        if first:
            current[0] = rho2
            current[1] = solid * (u2 - 0.5 * diff_rows(press))
            current[2] = solid * (v2 - 0.5 * diff_cols(press))
        pull = key_of(t) * (rho2 - target[t])
        if first:
            loss[...] += FORCE_WEIGHT * (f0 * f0 + f1 * f1) + pull * (rho2 - target[t])
        saved[slot, 0] = f0
        saved[slot, 1] = f1
        saved[slot, 2] = sy
        saved[slot, 3] = sx
        saved[slot, 10] = pull

    for t in range(steps):
        step_forward(t, t if sz.slots > 1 else 0, True)
    for ref, sem in row_groups + ch_groups:
        sent(but_one(ref), sem.at[0])

    def owner_of(j):
        return lax.rem(j, sz.rows)

    me = c * sz.rows + r if sz.ways > 1 else r
    chip_slot = (c // 2) * sz.rows + r if sz.ways > 1 else r

    def by_owned(action):
        least, more = sz.early // sz.rows, sz.early % sz.rows
        if more:
            pl.when(r < more)(functools.partial(action, least + 1))
            pl.when(r >= more)(functools.partial(action, least))
        else:
            action(least)

    def for_owned(action):
        for m in range(sz.owned):
            j = r + m * sz.rows
            if (m + 1) * sz.rows <= sz.early:
                action(m, j)
            else:
                pl.when(j < sz.early)(functools.partial(action, m, j))

    def early_start():
        low_half = lane_ids((width, LANES)) < 64
        tiles = [d_mid[kx * width : (kx + 1) * width, 0:LANES] for kx in range(TAPS)]
        rest = [d_mid[kx * width : (kx + 1) * width, LANES:] for kx in range(2)]
        tiles.append(jnp.concatenate(rest, axis=1))
        last = d_mid[2 * width : 3 * width, LANES:]
        for shard in range(sz.ch):
            for h in range(sz.halves):
                at = shard * co + h * 8
                for n, tile in enumerate(tiles):
                    early[shard * sz.early + h * 4 + n] = tile[at : at + 8]
            ends = [last[shard * co + h * 8 : shard * co + h * 8 + 8] for h in range(sz.halves)]
            if sz.halves == 1:
                ends.append(jnp.zeros_like(ends[0]))
            early[shard * sz.early + 4 * sz.halves] = jnp.concatenate(ends, axis=1)
        if sz.ch > 1:
            pl.semaphore_wait(ready, sz.ch - 1)
        for dc in range(sz.ways):
            shard = ch_peer(dc)
            for k in range(sz.early):
                j = lax.rem(r + k, sz.early)
                slot = j // sz.rows
                copy = remote(
                    early.at[shard * sz.early + j],
                    early_in.at[slot, me],
                    e_send.at[0],
                    e_recv.at[slot],
                    (shard, owner_of(j)),
                )
                if dc:
                    copy.start()
                else:
                    pl.when(owner_of(j) != r)(copy.start)

    def early_sum():
        def total(m, j):
            early_in[m, me] = early[c * sz.early + j]
            if sz.sources > 1:
                arrived(but_one(early_in.at[m]), e_recv.at[m])
            acc = early_in[m, 0]
            for k in range(1, sz.sources):
                acc = acc + early_in[m, k]
            early_fin[j] = acc
            line = ssq_early.at[c, j]
            line[...] = jnp.sum(acc * acc, axis=0, keepdims=True)
            for dc in range(1, sz.ch):
                for k in range(sz.rows):
                    remote(line, line, s_send.at[m], s_recv.at[0], (ch_peer(dc), row_peer(k))).start()
            for k in range(1, sz.rows):
                remote(early_fin.at[j], early_fin.at[j], g_send.at[m], g_recv.at[0], (c, row_peer(k))).start()

        for_owned(total)

    def early_left():
        if sz.sources > 1:
            by_owned(lambda n: sent(early.at[pl.ds(0, sz.ways * sz.early - n)], e_send.at[0]))

    def put_line(j, acc):
        ssq_early[c, j] = jnp.sum(acc * acc, axis=0, keepdims=True)

    def early_end():
        if sz.rows > 1:
            by_owned(lambda n: arrived(early_fin.at[pl.ds(0, sz.early - n)], g_recv.at[0]))
        for j in range(sz.early):
            acc = early_fin[j]
            out[j] = acc
            if sz.rows > 1:
                pl.when(r != j % sz.rows)(functools.partial(put_line, j, acc))
        if sz.ch > 1:
            arrived(but_one(ssq_early), s_recv.at[0])

    def early_shared():
        def last(m, j):
            if sz.ch > 1:
                sent(but_one(blank), s_send.at[m])
            if sz.rows > 1:
                sent(but_one(early_in.at[m, pl.ds(0, sz.rows)]), g_send.at[m])

        for_owned(last)

    def norm_back(k, slot, sums_d, sums_c):
        gain, mean, inv = gains[k], norm_stats[k, slot], norm_stats[k + 1, slot]
        sums_d = 0.5 * sums_d
        sums_n = inv * (0.5 * sums_c - mean * sums_d)
        scale = 1.0 / float(GSIZE * LANES * grid)
        m1 = spread(group_sum(sums_d * gain) * scale, width)
        m2 = spread(group_sum(sums_n * gain) * scale, width)
        d_norm[k] += sums_n
        d_norm[k + 1] += sums_d
        fc = inv * inv * m2
        return 0.5 * inv * gain, inv * m1 - fc * mean, fc

    def step_backward(t, slot):
        zero = jnp.zeros((width, LANES), F32)
        solid = mask[...]
        sy, sx = saved[slot, 2], saved[slot, 3]
        f0, f1 = saved[slot, 0], saved[slot, 1]
        grad_rho = grad_state[0] + 2.0 * inv_count * saved[slot, 10]
        gu = solid * grad_state[1]
        gv = solid * grad_state[2]
        g_press = 0.5 * (diff_rows(gu) + diff_cols(gv))
        g_div = jnp.zeros_like(g_press)
        for _ in range(JACOBI - 1):
            term = 0.25 * solid * g_press
            g_div = g_div - term
            g_press = around(term)
        g_div = g_div - 0.25 * solid * g_press
        gu = gu - 0.5 * diff_rows(g_div)
        gv = gv - 0.5 * diff_cols(g_div)
        wy, wx = quadratic(sy), quadratic(sx)
        spots = []
        g_sy = jnp.zeros_like(gu)
        g_sx = jnp.zeros_like(gu)
        for n, g in enumerate((grad_rho, gu, gv)):
            g_sy = g_sy + g * saved[slot, 4 + n]
            g_sx = g_sx + g * saved[slot, 7 + n]
            acc = None
            for a, shift in enumerate((from_below, lambda v: v, from_above)):
                ga = wy[a] * g
                line = from_right(wx[0] * ga) + wx[1] * ga + from_left(wx[2] * ga)
                line = shift(line)
                acc = line if acc is None else acc + line
            spots.append(acc)
        ty, tx = sy * (1.0 / COURANT), sx * (1.0 / COURANT)
        g_u1 = spots[1] + g_sy * (COURANT * (1.0 - ty * ty))
        g_v1 = spots[2] + g_sx * (COURANT * (1.0 - tx * tx))
        l0 = (TIME_STEP * g_u1 + 2.0 * FORCE_WEIGHT * inv_count * f0) * (1.0 - f0 * f0)
        l1 = (TIME_STEP * g_v1 + 2.0 * FORCE_WEIGHT * inv_count * f1) * (1.0 - f1 * f1)
        grad_state[0] = spots[0]
        grad_state[1] = g_u1
        grad_state[2] = g_v1
        glog32[pl.ds(0, grid, stride=16), :] = l0
        glog32[pl.ds(1, grid, stride=16), :] = l1

        def pack(it, carry):
            for k in range(4):
                i = it * 4 + k
                glog[slot, i] = glog32[pl.ds(pl.multiple_of(i * 16, 16), 16), :].astype(BF16)
            return carry

        loop(grid // 4, 8, pack, 0)

        def back_a(it, carry):
            sums_d, sums_n = carry
            i = it * 2
            gl = jnp.concatenate([glog[slot, i], glog[slot, i + 1]], axis=1)
            p = dot(w_bwd[width : 2 * width, TAPS * width :], gl)
            for k in range(2):
                d = p[:, k * LANES : (k + 1) * LANES] * slope[slot, 1, i + k]
                dy[i + k] = d
                sums_d = sums_d + d
                sums_n = sums_n + d * conv[slot, 1, i + k]
            ml = jnp.concatenate([mixed_low[slot, i], mixed_low[slot, i + 1]], axis=1)
            d_head[...] += dot_nt(gl, ml)
            return sums_d, sums_n

        sums = loop(grid // 2, 16, back_a, (zero, zero))
        fd, f1_, fn = norm_back(2, slot, *sums)

        def back_b(it, carry):
            for k in range(2):
                i = it * 2 + k
                g = fd * dy[i] - f1_ - fn * conv[slot, 1, i]
                low = g.astype(BF16)
                g_pad[slot, i + 1] = low
                if PACKED:
                    g_taps[i, 0:width] = from_right(low)
                    g_taps[i, 2 * width : 3 * width] = from_left(low)
                else:
                    g = low.astype(F32)
                    g_taps[i, 0:width] = from_right(g).astype(BF16)
                    g_taps[i, 2 * width : 3 * width] = from_left(g).astype(BF16)
                g_taps[i, width : 2 * width] = low
            return carry

        loop(grid // 2, 16, back_b, 0)

        def wgrad(it, carry):
            i = it * long
            left = jnp.concatenate([g_taps[i + k] for k in range(long)], axis=1)
            right = jnp.concatenate([hidden_low[slot, pl.ds(i + k, TAPS)].reshape(TAPS * width, LANES) for k in range(long)], axis=1)
            d_mid[...] += dot_nt(left, right)
            return carry

        long = 16 if t == 0 or grid > 32 else 32
        loop(grid // long, 2, wgrad, 0)
        if t == 0:
            early_start()

        def back_c(it, carry):
            sums_d, sums_n = carry
            i = it * 2
            rows = combine(dot(w_bwd[...], row_pair(g_pad.at[slot], i, glog.at[slot])), width)
            for k in range(2):
                d = rows[k] * slope[slot, 0, i + k]
                dy[i + k] = d
                sums_d = sums_d + d
                sums_n = sums_n + d * conv[slot, 0, i + k]
            return sums_d, sums_n

        sums = loop(grid // 2, 16, back_c, (zero, zero))
        fd, f1_, fn = norm_back(0, slot, *sums)

        def back_d(it, carry):
            i = it * 2
            lows = []
            for k in range(2):
                low = (fd * dy[i + k] - f1_ - fn * conv[slot, 0, i + k]).astype(BF16)
                g_pad[slot, i + k + 1] = low
                lows.append(low)
            d_in[...] += dot_nt(row_pair(feat.at[slot], i), jnp.concatenate(lows, axis=1))
            return carry

        loop(grid // 2, 16, back_d, 0)
        if t > 0:

            def back_e(it, carry):
                i = it * 2
                rows = combine(dot(v_bwd[...], row_pair(g_pad.at[slot], i)), 8)
                for k in range(2):
                    gs_rows[pl.ds(pl.multiple_of((i + k) * 8, 8), 8), :] = rows[k]
                return carry

            loop(grid // 2, 16, back_e, 0)
            for q in range(3):
                grad_state[q] += gs_rows[pl.ds(q, grid, stride=8), :]

    grad_state[...] = jnp.zeros_like(grad_state)

    for t in reversed(range(steps)):
        if sz.slots == 1:
            step_forward(t, 0, False)
        step_backward(t, t if sz.slots > 1 else 0)

    core = lax.rem(c, sz.cores)
    mate = (c + 1 - 2 * core, r)
    mine = pl.ds(core * sz.late, sz.late)

    def chip_peer(k):
        if sz.ways == 1:
            return (c, row_peer(k))
        return (lax.rem(c + 2 * (k // sz.rows), sz.ch), row_peer(k))

    columns = [jnp.sum(d_norm[k], axis=1, keepdims=True) for k in range(4)]
    columns.append(jnp.zeros((width, LANES - 4), F32))
    lines = jnp.transpose(jnp.concatenate(columns, axis=1))
    total = jnp.sum(jnp.sum(loss[...], axis=1, keepdims=True), axis=0, keepdims=True)
    pack = late_pair.at[core] if sz.cores > 1 else late_sum
    inputs = jnp.concatenate([d_in[0:24], d_in[24:48]], axis=1)
    for n in range(3):
        pack[n] = inputs[n * 8 : (n + 1) * 8]
    pack[3] = jnp.zeros((8, LANES), F32)
    pack[3, 0:4, 0:width] = lines[0:4, :]
    pack[3, 4:6, 0:width] = d_head[0:2]
    pack[3, 6:7, 0:width] = jnp.broadcast_to(total, (1, width))
    if sz.cores > 1:
        remote(pack, pack, p_send.at[0], p_recv.at[0], mate).start()
        arrived(pack, p_recv.at[0])
        late_sum[...] = late_pair[0] + late_pair[1]
    for k in range(1, sz.chips):
        remote(late_sum.at[mine], late_in.at[chip_slot], b_send.at[0], b_recv.at[0], chip_peer(k)).start()

    early_sum()

    late_in[chip_slot] = late_sum[mine]
    if sz.chips > 1:
        arrived(but_one(late_in), b_recv.at[0])
    acc = late_in[0]
    for k in range(1, sz.chips):
        acc = acc + late_in[k]
    late_fin[mine] = acc
    if sz.cores > 1:
        remote(late_fin.at[mine], late_fin.at[mine], p_send.at[1], p_recv.at[1], mate).start()
        sent(pack, p_send.at[0])
    early_left()
    if sz.chips > 1:
        sent(but_one(late_in), b_send.at[0])
    if sz.cores > 1:
        arrived(late_fin.at[mine], p_recv.at[1])
    acc = late_fin[...].reshape(32, LANES)
    turned = pltpu.roll(acc, lax.rem(LANES - c * co, LANES), 1)
    for n in range(4):
        out[sz.early + n] = turned[n * 8 : (n + 1) * 8]
    acc = jnp.where(row_ids(acc.shape) < 30, acc, 0.0)
    late_norm = jnp.sum(acc * acc, axis=0, keepdims=True)

    early_end()
    acc = late_norm
    for k in range(sz.ch):
        for j in range(sz.early):
            acc = acc + ssq_early[k, j]
    out_total[...] = jnp.broadcast_to(jnp.sum(acc, axis=1, keepdims=True), (8, LANES))
    early_shared()
    if sz.cores > 1:
        sent(late_fin.at[mine], p_send.at[1])


def adam(weight, grad, moment, square, rate, decay):
    moment = BETA_ONE * moment + (1.0 - BETA_ONE) * grad
    square = BETA_TWO * square + (1.0 - BETA_TWO) * grad * grad
    fix_one = 1.0 - BETA_ONE**STEP_NUM
    fix_two = 1.0 - BETA_TWO**STEP_NUM
    updated = weight - rate * (moment / fix_one / (jnp.sqrt(square / fix_two) + ADAM_EPS) + decay * weight)
    return updated, moment, square


def adam_kernel(sz, grads, total, keyframes, *refs):
    params, firsts, seconds = refs[0:4], refs[4:8], refs[8:12]
    news, moments, squares = refs[12:16], refs[16:20], refs[20:24]
    co, width = sz.co, sz.width
    norm = jnp.sqrt(total[0:1, 0:1])
    factor = CLIP / jnp.maximum(norm, CLIP)

    def put(n, at, grad):
        rate, decay = (RATE, DECAY) if n < 3 else (GAIN_RATE, 0.0)
        new, moment, square = adam(params[n][at], grad, firsts[n][at], seconds[n][at], rate, decay)
        news[n][at] = new
        moments[n][at] = moment
        squares[n][at] = square

    tiles = []
    for n in range(4):
        tiles.append(jnp.concatenate([grads[h * 4 + n] for h in range(sz.halves)], axis=0) * factor)
    last = grads[4 * sz.halves] * factor
    last = jnp.concatenate([last[:, h * width : (h + 1) * width] for h in range(sz.halves)], axis=0)
    thirds = [tiles[3][:, :width], tiles[3][:, width:], last]
    for kx in range(TAPS):
        put(1, (0, kx), tiles[kx][:, :width])
        put(1, (1, kx), tiles[kx][:, width:])
        put(1, (2, kx), thirds[kx])
    tail = jnp.concatenate([grads[sz.early + n] for n in range(3)], axis=0) * factor
    for ky in range(TAPS):
        for kx in range(TAPS):
            at = ky * 16 + kx * 4
            side = width if at >= 24 else 0
            at = at - 24 if at >= 24 else at
            put(0, (ky, kx), tail[at : at + 4, side : side + co])
    tail = grads[sz.early + 3]
    loss = tail[6:7, 0:1]
    tail = tail * factor
    put(2, Ellipsis, tail[4:6, 0:co])
    put(3, Ellipsis, tail[0:4, 0:co])
    marks = keyframes[...].astype(F32)
    valid = jnp.sum(jnp.sum(marks, axis=1, keepdims=True), axis=0, keepdims=True) * float(sz.grid * sz.cols)
    refs[24][...] = norm
    refs[25][...] = loss
    refs[26][...] = valid


def scratch_of(sz):
    grid, width, rows, ch, slots, steps = sz.grid, sz.width, sz.rows, sz.ch, sz.slots, sz.steps
    wide = TAPS * width

    def f32(*shape):
        return pltpu.VMEM(shape, F32)

    def bf16(*shape):
        return pltpu.VMEM(shape, BF16)

    dma = lambda *shape: pltpu.SemaphoreType.DMA(shape)
    return {
        "f_stage": f32(rows, 3, sz.local, LANES),
        "t_stage": f32(rows, steps, sz.local, LANES),
        "m_stage": pltpu.VMEM((rows, sz.local, LANES), jnp.int32),
        "w_in_own": f32(TAPS, TAPS, 4, sz.co),
        "w_mid_own": f32(TAPS, TAPS, sz.co, width),
        "w_head_own": f32(2, sz.co),
        "norms_own": f32(4, sz.co),
        "small": f32(LANES, LANES),
        "ws_all": f32(ch, sz.co, LANES),
        "wm_all": bf16(ch, -(-sz.co // 16) * 16, sz.mid_lanes),
        "w_fwd": bf16(wide, wide),
        "w_bwd": bf16(wide, wide + 16),
        "v_fwd": bf16(width, TAPS * 16),
        "v_bwd": bf16(TAPS * 8, wide),
        "head": bf16(16, width),
        "gains": f32(4, width, LANES),
        "current": f32(3, grid, LANES),
        "states": f32(1 if slots > 1 else steps, 3, grid, LANES),
        "mask": f32(grid, LANES),
        "target": f32(steps, grid, LANES),
        "feat32": f32(grid * 16, LANES),
        "feat": bf16(slots, grid + 2, 16, LANES),
        "conv": f32(slots, 2, grid, width, LANES),
        "slope": f32(slots, 2, grid, width, LANES),
        "norm_stats": f32(4, slots, width, LANES),
        "hidden": f32(grid, width, LANES),
        "hidden_low": bf16(slots, grid + 2, width, LANES),
        "mixed_low": bf16(slots, grid, width, LANES),
        "logits": f32(2, grid, LANES),
        "saved": f32(slots, SAVED, grid, LANES),
        "dy": f32(grid, width, LANES),
        "glog32": f32(grid * 16, LANES),
        "glog": bf16(slots, grid, 16, LANES),
        "g_pad": bf16(slots, grid + 2, width, LANES),
        "g_taps": bf16(grid, wide, LANES),
        "gs_rows": f32(grid * 8, LANES),
        "grad_state": f32(3, grid, LANES),
        "d_mid": f32(wide, wide),
        "d_in": f32(TAPS * 16, width),
        "d_head": f32(16, width),
        "d_norm": f32(4, width, LANES),
        "loss": f32(grid, LANES),
        "early": f32(ch * sz.early, 8, LANES),
        "early_in": f32(sz.owned, sz.sources, 8, LANES),
        "early_fin": f32(sz.early, 8, LANES),
        "blank": f32(ch, rows, 1, LANES),
        "ssq_early": f32(ch, sz.early, 1, LANES),
        "late_pair": f32(2, 4, 8, LANES),
        "late_sum": f32(4, 8, LANES),
        "late_in": f32(sz.chips, sz.late, 8, LANES),
        "late_fin": f32(4, 8, LANES),
        "ready": pltpu.SemaphoreType.REGULAR,
        "local_sem": dma(7),
        "f_sem": dma(2),
        "t_sem": dma(2),
        "m_sem": dma(2),
        "v_sem": dma(2),
        "w_sem": dma(2),
        "e_send": dma(1),
        "e_recv": dma(sz.owned),
        "g_send": dma(sz.owned),
        "g_recv": dma(1),
        "s_send": dma(sz.owned),
        "s_recv": dma(1),
        "b_send": dma(1),
        "b_recv": dma(1),
        "p_send": dma(2),
        "p_recv": dma(2),
    }


def shards(mesh, fields, targets, fluid, keyframes, *rest):
    params, firsts, seconds = rest[0:4], rest[4:8], rest[8:12]

    def native(leaves):
        return (leaves[0], jnp.swapaxes(leaves[1], 2, 3), leaves[2].T, leaves[3])

    params, firsts, seconds = native(params), native(firsts), native(seconds)
    sz = Sizes(mesh, fields.shape, targets.shape, params[0].shape[3])
    marks = keyframes.T
    vmem = pl.BlockSpec(memory_space=pltpu.VMEM)
    hbm = pl.BlockSpec(memory_space=pl.ANY)
    alone = sz.rows == 1 and sz.ch == 1
    grads, total = pl.pallas_call(
        functools.partial(train_kernel, sz),
        out_shape=(
            jax.ShapeDtypeStruct((sz.early + 4, 8, LANES), F32),
            jax.ShapeDtypeStruct((8, LANES), F32),
        ),
        in_specs=[hbm, hbm, hbm, vmem] + [hbm] * 4,
        out_specs=(vmem, vmem),
        scratch_shapes=list(scratch_of(sz).values()),
        compiler_params=pltpu.CompilerParams(
            collective_id=None if alone else 0, has_side_effects=True, vmem_limit_bytes=60 << 20
        ),
        name="train",
    )(fields, targets, fluid, marks, *params)
    shapes = [jax.ShapeDtypeStruct(leaf.shape, F32) for leaf in params] * 3
    shapes += [jax.ShapeDtypeStruct((1, 1), F32)] * 3
    results = pl.pallas_call(
        functools.partial(adam_kernel, sz),
        out_shape=tuple(shapes),
        in_specs=[vmem] * 15,
        out_specs=tuple([vmem] * 15),
        name="adamw",
    )(grads, total, marks, *params, *firsts, *seconds)
    outs = []
    for n in range(3):
        outs.extend(native(results[4 * n : 4 * n + 4]))
    return (*outs, *[leaf.reshape(()) for leaf in results[12:]])


def solution(mesh):
    split = (P(None, None, None, "ch"), P(None, None, None, "ch"), P("ch", None), P(None, "ch"))
    return jax.shard_map(
        functools.partial(shards, mesh),
        mesh=mesh,
        in_specs=(
            P(None, None, "rows", None),
            P(None, None, "rows", None),
            P("rows", None),
            P(),
            *split,
            *split,
            *split,
        ),
        out_specs=(*split, *split, *split, P(), P(), P()),
        check_vma=False,
    )
```

```python
import functools

import jax
import jax.numpy as jnp
from jax import lax
from jax.experimental import pallas as pl
from jax.experimental.pallas import tpu as pltpu
from jax.sharding import PartitionSpec as P

GROUPS = 8
NEAR = (-1, 0, 1)
STEP_NUM = 10
TIME_STEP = 0.5
COURANT = 0.8
FORCE_WEIGHT = 0.5
NORM_EPS = 1e-05
CLIP = 0.0001
BETA_ONE = 0.9
BETA_TWO = 0.999
ADAM_EPS = 1e-10
RATE = 0.1
GAIN_RATE = 0.6
DECAY = 0.01

MESH = pl.DeviceIdType.MESH
F32 = jnp.float32
BF16 = jnp.bfloat16
LANES = 128
GSIZE = 8
TAPS = 3
SAVED = 11
NT = (((1,), (1,)), ((), ()))


def lane_ids(shape):
    return lax.broadcasted_iota(jnp.int32, shape, len(shape) - 1)


def row_ids(shape):
    return lax.broadcasted_iota(jnp.int32, shape, 0)


def from_left(x):
    return jnp.where(lane_ids(x.shape) == 0, jnp.zeros_like(x), pltpu.roll(x, 1, 1))


def from_right(x):
    size = x.shape[1]
    return jnp.where(lane_ids(x.shape) == size - 1, jnp.zeros_like(x), pltpu.roll(x, size - 1, 1))


def from_above(x):
    return jnp.where(row_ids(x.shape) == 0, 0.0, pltpu.roll(x, 1, 0))


def from_below(x):
    size = x.shape[0]
    return jnp.where(row_ids(x.shape) == size - 1, 0.0, pltpu.roll(x, size - 1, 0))


def diff_rows(x):
    return from_below(x) - from_above(x)


def column(x, d):
    if d == 0:
        return x
    size = x.shape[1]
    lane = lane_ids(x.shape)
    inside = lane < size - d if d > 0 else lane >= -d
    return jnp.where(inside, pltpu.roll(x, -d % size, 1), jnp.zeros_like(x))


def columns_of(x, reach):
    return {d: column(x, d) for d in range(-reach, reach + 1)}


def rows_around(x):
    return from_below(x) + from_above(x)


def quadratic(s):
    return (0.5 * s * (s + 1.0), 1.0 - s * s, 0.5 * s * (s - 1.0))


def quadratic_slope(s):
    return (s + 0.5, -2.0 * s, s - 0.5)


def wrap(x, n):
    return x & (n - 1) if n & (n - 1) == 0 else lax.rem(x, n)


def dot(a, b):
    return jnp.dot(a, b, preferred_element_type=F32)


def dot_nt(a, b):
    return lax.dot_general(a, b, NT, preferred_element_type=F32)


def row_pair(ref, i, extra=None):
    depth = ref.shape[1] * TAPS
    sides = []
    for k in range(2):
        side = ref[pl.ds(i + k, TAPS)].reshape(depth, LANES)
        if extra is not None:
            side = jnp.concatenate([side, extra[i + k]], axis=0)
        sides.append(side)
    return jnp.concatenate(sides, axis=1)


def side_by_side(ref, first):
    return jnp.concatenate([ref[i] for i in range(first, ref.shape[0])], axis=1)


def four_rows(ref, i):
    taps = ref.shape[1] // 64
    parts = []
    for n in range(taps):
        sides = [ref[pl.ds(i + 2 * k, 4), n * 64 : (n + 1) * 64].reshape(4 * 64, LANES) for k in range(2)]
        parts.append(jnp.concatenate(sides, axis=1))
    return jnp.concatenate(parts, axis=0) if taps > 1 else parts[0]


def rows_of(p):
    half = p.shape[0] // 2
    return [p[o * half : (o + 1) * half, k * LANES : (k + 1) * LANES] for k in range(2) for o in range(2)]


def two_rows(blocks):
    zero = jnp.zeros_like(blocks[0])
    first = jnp.concatenate(list(blocks) + [zero], axis=1)
    second = jnp.concatenate([zero] + list(blocks), axis=1)
    return jnp.concatenate([first, second], axis=0)


def combine(part, height):
    return (
        part[height : 2 * height] + from_left(part[:height]) + from_right(part[2 * height : 3 * height])
    )


def group_sum(x):
    return jnp.sum(jnp.sum(x.reshape(-1, GSIZE, LANES), axis=1), axis=1, keepdims=True)


def spread(x, width):
    return jnp.broadcast_to(x[:, :, None], (x.shape[0], GSIZE, LANES)).reshape(width, LANES)


def loop(count, per, body, carry):
    per = min(per, count)

    def several(it, carry):
        for k in range(per):
            carry = body(it * per + k, carry)
        return carry

    if count == per:
        return several(0, carry)
    return lax.fori_loop(0, count // per, several, carry)


class Sizes:
    def __init__(self, mesh, fields_shape, targets_shape, co):
        self.ch = mesh.shape["ch"]
        self.rows = mesh.shape["rows"]
        self.batch = fields_shape[0]
        self.local = fields_shape[2]
        self.grid = self.local * self.rows
        self.cols = fields_shape[3]
        self.steps = targets_shape[0]
        self.co = co
        self.width = co * self.ch
        self.per_rows = self.batch // self.rows
        self.ways = self.ch if self.per_rows == self.ch else 1
        assert self.per_rows == self.ways and self.batch % self.rows == 0
        assert self.cols == LANES
        slot = self.grid * self.width * LANES * 20
        self.slots = self.steps if slot * self.steps < (24 << 20) else 1
        self.halves = co // 8
        self.early = 4 * self.halves
        self.owned = -(-self.early // self.rows)
        self.sources = self.ways * self.rows
        self.cores = 2 if self.ways > 1 else 1
        self.chips = self.sources // self.cores
        self.late = 4 // self.cores
        assert self.ways % self.cores == 0
        self.mid_lanes = TAPS * TAPS * self.width
        assert self.width == 64 and co % 8 == 0


IN_AT = 64
HEAD_AT = IN_AT + 36
NORM_AT = HEAD_AT + 2
LOSS_AT = NORM_AT + 4


def train_kernel(sz, fields, targets, fluid, keyframes, w_in, w_mid, w_head, norms, out, out_total, *scratch):
    z = dict(zip(scratch_of(sz), scratch))
    f_stage = z["f_stage"]
    t_stage = z["t_stage"]
    m_stage = z["m_stage"]
    w_in_own = z["w_in_own"]
    w_mid_own = z["w_mid_own"]
    w_head_own = z["w_head_own"]
    norms_own = z["norms_own"]
    small = z["small"]
    ws_all = z["ws_all"]
    wm_all = z["wm_all"]
    w_fwd = z["w_fwd"]
    w_bwd = z["w_bwd"]
    v_fwd = z["v_fwd"]
    v_bwd = z["v_bwd"]
    head_back = z["head_back"]
    head = z["head"]
    gains = z["gains"]
    current = z["current"]
    states = z["states"]
    mask = z["mask"]
    target = z["target"]
    feat32 = z["feat32"]
    feat = z["feat"]
    conv = z["conv"]
    slope = z["slope"]
    norm_stats = z["norm_stats"]
    back_factors = z["back_factors"]
    hidden = z["hidden"]
    hidden_low = z["hidden_low"]
    mixed_low = z["mixed_low"]
    logits = z["logits"]
    saved = z["saved"]
    dy = z["dy"]
    mixed_grad = z["mixed_grad"]
    glog32 = z["glog32"]
    glog = z["glog"]
    g_pad = z["g_pad"]
    g_taps = z["g_taps"]
    gs_rows = z["gs_rows"]
    grad_state = z["grad_state"]
    d_mid = z["d_mid"]
    d_in = z["d_in"]
    d_head = z["d_head"]
    d_norm = z["d_norm"]
    loss = z["loss"]
    early = z["early"]
    early_in = z["early_in"]
    early_fin = z["early_fin"]
    blank = z["blank"]
    ssq_early = z["ssq_early"]
    late_pair = z["late_pair"]
    late_sum = z["late_sum"]
    late_in = z["late_in"]
    late_fin = z["late_fin"]
    ready = z["ready"]
    local_sem = z["local_sem"]
    f_sem = z["f_sem"]
    t_sem = z["t_sem"]
    m_sem = z["m_sem"]
    v_sem = z["v_sem"]
    w_sem = z["w_sem"]
    e_send = z["e_send"]
    e_recv = z["e_recv"]
    g_send = z["g_send"]
    g_recv = z["g_recv"]
    s_send = z["s_send"]
    s_recv = z["s_recv"]
    b_send = z["b_send"]
    b_recv = z["b_recv"]
    p_send = z["p_send"]
    p_recv = z["p_recv"]
    c = lax.axis_index("ch")
    r = lax.axis_index("rows")
    width, grid, steps = sz.width, sz.grid, sz.steps
    co = sz.co

    def row_peer(k):
        return wrap(r + k, sz.rows)

    def ch_peer(k):
        return wrap(c + k, sz.ch)

    def sample_of(row):
        return row * sz.per_rows + (c if sz.ways > 1 else 0)

    def block(work):
        pl.when(r >= 0)(work)

    peers = sz.rows - 1 + sz.ch - 1
    if peers:
        barrier = pltpu.get_barrier_semaphore()
        for k in range(1, sz.rows):
            pl.semaphore_signal(barrier, inc=1, device_id=(c, row_peer(k)), device_id_type=MESH)
        for k in range(1, sz.ch):
            pl.semaphore_signal(barrier, inc=1, device_id=(ch_peer(k), r), device_id_type=MESH)

    def remote(src, dst, send, recv, where):
        return pltpu.make_async_remote_copy(
            src_ref=src, dst_ref=dst, send_sem=send, recv_sem=recv, device_id=where, device_id_type=MESH
        )

    def arrived(ref, sem):
        remote(ref, ref, sem, sem, (c, r)).wait_recv()

    def sent(ref, sem):
        remote(ref, ref, sem, sem, (c, r)).wait_send()

    def but_one(ref):
        return ref.at[pl.ds(0, ref.shape[0] - 1)]

    own = [
        pltpu.make_async_copy(src, dst, local_sem.at[n])
        for n, (src, dst) in enumerate(
            (
                (w_in, w_in_own),
                (w_head, w_head_own),
                (norms, norms_own),
                (w_mid, w_mid_own),
                (fields.at[sample_of(r)], f_stage.at[r]),
                (fluid, m_stage.at[r]),
                (targets.at[:, sample_of(r)], t_stage.at[r]),
            )
        )
    ]
    for copy in own:
        copy.start()

    small[...] = jnp.zeros_like(small)
    for n in range(4):
        own[n].wait()
    for ky in range(TAPS):
        for kx in range(TAPS):
            at = IN_AT + (ky * TAPS + kx) * 4
            small[at : at + 4, 0:co] = w_in_own[ky, kx]
    small[HEAD_AT : HEAD_AT + 2, 0:co] = w_head_own[...]
    small[NORM_AT : NORM_AT + 4, 0:co] = norms_own[...]
    ws_all[c] = jnp.transpose(small[...])[0:co]
    mine = jnp.concatenate([w_mid_own[ky, kx] for kx in range(TAPS) for ky in range(TAPS)], axis=1)
    wm_all[c, 0:co, :] = mine.astype(BF16)

    if peers:
        pl.semaphore_wait(barrier, peers)

    for k in range(1, sz.rows):
        src = fields.at[sample_of(row_peer(k))]
        remote(src, f_stage.at[r], f_sem.at[0], f_sem.at[1], (c, row_peer(k))).start()
    for k in range(1, sz.ch):
        remote(ws_all.at[c], ws_all.at[c], v_sem.at[0], v_sem.at[1], (ch_peer(k), r)).start()
    for k in range(1, sz.rows):
        remote(fluid, m_stage.at[r], m_sem.at[0], m_sem.at[1], (c, row_peer(k))).start()
    for k in range(1, sz.ch):
        remote(wm_all.at[c], wm_all.at[c], w_sem.at[0], w_sem.at[1], (ch_peer(k), r)).start()
    for k in range(1, sz.rows):
        src = targets.at[:, sample_of(row_peer(k))]
        remote(src, t_stage.at[r], t_sem.at[0], t_sem.at[1], (c, row_peer(k))).start()
    row_groups = ((f_stage, f_sem), (m_stage, m_sem), (t_stage, t_sem)) if sz.rows > 1 else ()
    ch_groups = ((ws_all, v_sem), (wm_all, w_sem)) if sz.ch > 1 else ()
    if peers:
        for k in range(1, sz.ch):
            pl.semaphore_signal(ready, inc=1, device_id=(ch_peer(k), r), device_id_type=MESH)

    for i in (0, grid + 1):
        g_taps[i] = jnp.zeros_like(g_taps[i])
    for ref in (feat, hidden_low, g_pad):
        for slot in range(sz.slots):
            ref[slot, 0] = jnp.zeros_like(ref[slot, 0])
            ref[slot, grid + 1] = jnp.zeros_like(ref[slot, 0])
    feat32[...] = jnp.zeros_like(feat32)
    glog32[...] = jnp.zeros_like(glog32)
    for ref in (d_mid, d_in, d_head, d_norm, loss):
        ref[...] = jnp.zeros_like(ref)

    if ch_groups:
        arrived(but_one(ws_all), v_sem.at[1])
    tail = ws_all[...].reshape(width, LANES)
    tail_t = jnp.transpose(tail)
    parts = []
    for ky in range(TAPS):
        at = IN_AT + ky * 12
        parts.append(jnp.concatenate([tail[:, at : at + 12], jnp.zeros((width, 4), F32)], axis=1))
    v_fwd[...] = jnp.concatenate(parts, axis=1).astype(BF16)
    pieces = []
    for ky in range(TAPS):
        column_taps = []
        for kx in range(TAPS):
            at = IN_AT + ((2 - ky) * TAPS + 2 - kx) * 4
            column_taps += [tail_t[at : at + 4], jnp.zeros((4, width), F32)]
        pieces.append(jnp.concatenate(column_taps, axis=0))
    v_bwd[...] = two_rows(pieces).astype(BF16)
    head_back[...] = jnp.concatenate([tail[:, HEAD_AT : HEAD_AT + 2], jnp.zeros((width, 14), F32)], axis=1).astype(BF16)
    head[...] = jnp.concatenate([tail_t[HEAD_AT : HEAD_AT + 2], jnp.zeros((14, width), F32)], axis=0).astype(BF16)
    for k in range(4):
        gains[k] = jnp.broadcast_to(tail[:, NORM_AT + k : NORM_AT + k + 1], (width, LANES))

    for ref, sem in row_groups[:2]:
        arrived(but_one(ref), sem.at[1])
    own[4].wait()
    own[5].wait()
    for row in range(sz.rows):
        at = pl.ds(row * sz.local, sz.local)
        for q in range(3):
            current[q, 1, at, :] = f_stage[row, q]
        mask[2, at, :] = m_stage[row].astype(F32)
    for q in range(3):
        for d in (-1, 1):
            current[q, d + 1] = column(current[q, 1], d)
    for d in (-2, -1, 1, 2):
        mask[d + 2] = column(mask[2], d)
    for d in NEAR:
        feat32[pl.ds((d + 1) * 4 + 3, grid, stride=16), :] = mask[d + 2]

    def second_layer():
        if ch_groups:
            arrived(but_one(wm_all), w_sem.at[1])
        kind = BF16 if co % 16 == 0 else F32
        mid = jnp.concatenate([wm_all[k, 0:co, :].astype(kind) for k in range(sz.ch)], axis=0)
        for kx in range(TAPS):
            at = [(kx * TAPS + ky) * width for ky in range(TAPS)]
            w_fwd[:, kx * 4 * width : (kx + 1) * 4 * width] = two_rows([mid[:, a : a + width] for a in at]).astype(BF16)

    def second_layer_back():
        for kx in range(TAPS):
            at = kx * 4 * width
            blocks = [w_fwd[0:width, at + ky * width : at + (ky + 1) * width].astype(F32) for ky in range(TAPS)]
            w_bwd[:, at : at + 4 * width] = two_rows([jnp.transpose(b) for b in reversed(blocks)]).astype(BF16)

    def all_targets():
        if row_groups:
            arrived(but_one(t_stage), t_sem.at[1])
        own[6].wait()
        for row in range(sz.rows):
            at = pl.ds(row * sz.local, sz.local)
            for t in range(steps):
                target[t, at, :] = t_stage[row, t]

    second_layer()

    marks = keyframes[...].astype(F32)
    valid = jnp.sum(jnp.sum(marks, axis=1, keepdims=True), axis=0, keepdims=True) * float(grid * sz.cols)
    inv_count = 1.0 / valid
    picked = jnp.where(lane_ids(marks.shape) == sample_of(r), marks, 0.0)
    marked = jnp.sum(picked, axis=1, keepdims=True)

    def key_of(t):
        return jnp.sum(jnp.where(row_ids(marked.shape) == t, marked, 0.0), axis=0, keepdims=True)

    def conv_and_stats(x_ref, w, store, layer, slot):
        zero = jnp.zeros((width, LANES), F32)

        def body(it, carry):
            base, total, squares = carry
            i = it * 4
            if layer:
                rows = rows_of(dot(w[...], four_rows(x_ref, i)))
            else:
                rows = []
                for k in range(2):
                    p = dot(w[...], row_pair(x_ref, i + 2 * k))
                    rows += [p[:, :LANES], p[:, LANES:]]
            base = jnp.where(it == 0, rows[0], base)
            for j in range(4):
                store[i + j] = rows[j]
                d = rows[j] - base
                total = total + d
                squares = squares + d * d
            return base, total, squares

        base, total, squares = loop(grid // 4, 8, body, (zero, zero, zero))
        lane_mean = base + total * (1.0 / grid)
        lane_dev = squares - total * total * (1.0 / grid)
        count = float(GSIZE * LANES)
        middle = spread(group_sum(base) * (1.0 / count), width)
        d = lane_mean - middle
        first = spread(group_sum(d) * (1.0 / count), width)
        second = spread(group_sum(lane_dev + grid * d * d) * (1.0 / (count * grid)), width)
        norm_stats[2 * layer, slot] = middle + first
        norm_stats[2 * layer + 1, slot] = lax.rsqrt(second - first * first + NORM_EPS)

    def silu_parts(half):
        t = jnp.tanh(half)
        a = 1.0 + t
        h = half * a
        return h, a + h * (1.0 - t)

    def half_affine(layer, slot):
        k = 2 * layer
        mean, inv = norm_stats[k, slot], norm_stats[k + 1, slot]
        scale = 0.5 * inv * gains[k]
        return scale, 0.5 * gains[k + 1] - mean * scale

    def step_forward(t, slot, first):
        last = t == steps - 1
        if sz.slots == 1:
            for q in range(3):
                for d in NEAR:
                    if first:
                        states[t, q, d + 1] = current[q, d + 1]
                    else:
                        current[q, d + 1] = states[t, q, d + 1]
        @block
        def _():
            x = [{d: current[q, d + 1] for d in NEAR} for q in range(3)]
            for q in range(3):
                for d in NEAR:
                    feat32[pl.ds((d + 1) * 4 + q, grid, stride=16), :] = x[q][d]

            def pack(it, carry):
                for k in range(4):
                    i = it * 4 + k
                    feat[slot, i + 1] = feat32[pl.ds(pl.multiple_of(i * 16, 16), 16), :].astype(BF16)
                return carry

            loop(grid // 4, 8, pack, 0)

            conv_and_stats(feat.at[slot], v_fwd, conv.at[slot, 0], 0, slot)
        @block
        def _():
            mul, add = half_affine(0, slot)

            def norm_one(it, carry):
                for k in range(2):
                    i = it * 2 + k
                    h, slope[slot, 0, i] = silu_parts(conv[slot, 0, i] * mul + add)
                    hidden[i] = h
                    low = h.astype(BF16)
                    for kx, tap in enumerate((from_left(low), low, from_right(low))):
                        hidden_low[slot, i + 1, kx * width : (kx + 1) * width] = tap
                return carry

            loop(grid // 2, 16, norm_one, 0)

            conv_and_stats(hidden_low.at[slot], w_fwd, conv.at[slot, 1], 1, slot)
        @block
        def _():
            mul, add = half_affine(1, slot)

            def norm_two(it, carry):
                i = it * 2
                lows = []
                for k in range(2):
                    h, slope[slot, 1, i + k] = silu_parts(conv[slot, 1, i + k] * mul + add)
                    low = (hidden[i + k] + h).astype(BF16)
                    mixed_low[slot, i + k] = low
                    lows.append(low)
                p = dot(head[...], jnp.concatenate(lows, axis=1))
                for k in range(2):
                    logits[0, pl.ds(i + k, 1), :] = p[0:1, k * LANES : (k + 1) * LANES]
                    logits[1, pl.ds(i + k, 1), :] = p[1:2, k * LANES : (k + 1) * LANES]
                return carry

            loop(grid // 2, 16, norm_two, 0)

        if first and t == 0:
            all_targets()
            second_layer_back()
        @block
        def _():
            x = [{d: current[q, d + 1] for d in NEAR} for q in range(3)]
            f0, f1 = jnp.tanh(logits[0]), jnp.tanh(logits[1])
            force0, force1 = columns_of(f0, 1), columns_of(f1, 1)
            u1 = {d: x[1][d] + TIME_STEP * force0[d] for d in NEAR}
            v1 = {d: x[2][d] + TIME_STEP * force1[d] for d in NEAR}
            sy = COURANT * jnp.tanh(u1[0])
            sx = COURANT * jnp.tanh(v1[0])
            wy, wx = quadratic(sy), quadratic(sx)
            dwy, dwx = quadratic_slope(sy), quadratic_slope(sx)
            moved = []
            for n, q in enumerate((x[0], u1, v1)):
                lines = [(from_above(q[d]), q[d], from_below(q[d])) for d in NEAR]
                along = [wx[0] * lines[0][a] + wx[1] * lines[1][a] + wx[2] * lines[2][a] for a in range(3)]
                moved.append(wy[0] * along[0] + wy[1] * along[1] + wy[2] * along[2])
                if last and n:
                    continue
                slant = [dwx[0] * lines[0][a] + dwx[1] * lines[1][a] + dwx[2] * lines[2][a] for a in range(3)]
                saved[slot, 4 + n] = dwy[0] * along[0] + dwy[1] * along[1] + dwy[2] * along[2]
                saved[slot, 7 + n] = wy[0] * slant[0] + wy[1] * slant[1] + wy[2] * slant[2]
            rho2 = moved[0]
            if first and not last:
                solid = {d: mask[d + 2] for d in range(-2, 3)}
                rho2s, u2, v2 = columns_of(rho2, 1), columns_of(moved[1], 1), columns_of(moved[2], 2)
                div = {d: 0.5 * (diff_rows(u2[d]) + (v2[d + 1] - v2[d - 1])) for d in NEAR}
                press = {d: -0.25 * solid[d] * div[d] for d in NEAR}
                press = 0.25 * solid[0] * (rows_around(press[0]) + press[1] + press[-1] - div[0])
                press = columns_of(press, 3)
                div[2], div[-2] = column(div[0], 2), column(div[0], -2)
                press = {
                    d: 0.25 * solid[d] * (rows_around(press[d]) + press[d + 1] + press[d - 1] - div[d])
                    for d in range(-2, 3)
                }
                for d in NEAR:
                    current[0, d + 1] = rho2s[d]
                    current[1, d + 1] = solid[d] * (u2[d] - 0.5 * diff_rows(press[d]))
                    current[2, d + 1] = solid[d] * (v2[d] - 0.5 * (press[d + 1] - press[d - 1]))
            pull = key_of(t) * (rho2 - target[t])
            if first:
                loss[...] += FORCE_WEIGHT * (f0 * f0 + f1 * f1) + pull * (rho2 - target[t])
            saved[slot, 0] = f0
            saved[slot, 1] = f1
            saved[slot, 2] = sy
            saved[slot, 3] = sx
            saved[slot, 10] = pull

    for t in range(steps):
        step_forward(t, t if sz.slots > 1 else 0, True)
    for ref, sem in row_groups + ch_groups:
        sent(but_one(ref), sem.at[0])

    def owner_of(j):
        return wrap(j, sz.rows)

    me = c * sz.rows + r if sz.ways > 1 else r
    chip_slot = (c // 2) * sz.rows + r if sz.ways > 1 else r

    def by_owned(action):
        least, more = sz.early // sz.rows, sz.early % sz.rows
        if more:
            pl.when(r < more)(functools.partial(action, least + 1))
            pl.when(r >= more)(functools.partial(action, least))
        else:
            action(least)

    def for_owned(action):
        for m in range(sz.owned):
            j = r + m * sz.rows
            if (m + 1) * sz.rows <= sz.early:
                action(m, j)
            else:
                pl.when(j < sz.early)(functools.partial(action, m, j))

    def early_start():
        low_half = lane_ids((width, LANES)) < 64
        tiles = [d_mid[kx * width : (kx + 1) * width, 0:LANES] for kx in range(TAPS)]
        rest = [d_mid[kx * width : (kx + 1) * width, LANES:] for kx in range(2)]
        tiles.append(jnp.concatenate(rest, axis=1))
        last = d_mid[2 * width : 3 * width, LANES:]
        for shard in range(sz.ch):
            for h in range(sz.halves):
                at = shard * co + h * 8
                for n, tile in enumerate(tiles):
                    early[shard * sz.early + h * 4 + n, 0:8] = tile[at : at + 8]
            ends = last[shard * co : (shard + 1) * co]
            ends = jnp.concatenate([ends[: co // 2], ends[co // 2 :]], axis=1)
            for j in range(sz.early):
                early[shard * sz.early + j, 8:9] = ends[j : j + 1]
        if sz.ch > 1:
            pl.semaphore_wait(ready, sz.ch - 1)
        for dc in range(sz.ways):
            shard = ch_peer(dc)
            for k in range(sz.early):
                j = wrap(r + k, sz.early)
                slot = j // sz.rows if sz.owned > 1 else 0
                if dc == 0 and k == 0 and sz.early == sz.rows:
                    continue
                copy = remote(
                    early.at[shard * sz.early + j],
                    early_in.at[slot, me],
                    e_send.at[0],
                    e_recv.at[slot],
                    (shard, owner_of(j)),
                )
                if dc or sz.early == sz.rows:
                    copy.start()
                else:
                    pl.when(owner_of(j) != r)(copy.start)

    def early_sum():
        def total(m, j):
            early_in[m, me] = early[c * sz.early + j]
            if sz.sources > 1:
                arrived(but_one(early_in.at[m]), e_recv.at[m])
            acc = early_in[m, 0]
            for k in range(1, sz.sources):
                acc = acc + early_in[m, k]
            early_fin[j] = acc
            line = ssq_early.at[c, j]
            line[...] = jnp.sum(acc * acc, axis=0, keepdims=True)
            for dc in range(1, sz.ch):
                for k in range(sz.rows):
                    remote(line, line, s_send.at[m], s_recv.at[0], (ch_peer(dc), row_peer(k))).start()
            for k in range(1, sz.rows):
                remote(early_fin.at[j], early_fin.at[j], g_send.at[m], g_recv.at[0], (c, row_peer(k))).start()

        for_owned(total)

    def early_left():
        if sz.sources > 1:
            by_owned(lambda n: sent(early.at[pl.ds(0, sz.ways * sz.early - n)], e_send.at[0]))

    def put_line(j, acc):
        ssq_early[c, j] = jnp.sum(acc * acc, axis=0, keepdims=True)

    def early_end():
        if sz.rows > 1:
            by_owned(lambda n: arrived(early_fin.at[pl.ds(0, sz.early - n)], g_recv.at[0]))
        for j in range(sz.early):
            acc = early_fin[j]
            out[j] = acc[0:8]
            out[sz.early + 4, j : j + 1] = acc[8:9]
            if sz.rows > 1:
                pl.when(r != j % sz.rows)(functools.partial(put_line, j, acc))
        if sz.ch > 1:
            arrived(but_one(ssq_early), s_recv.at[0])

    def early_shared():
        def last(m, j):
            if sz.ch > 1:
                sent(but_one(blank), s_send.at[m])
            if sz.rows > 1:
                sent(but_one(early_in.at[m, pl.ds(0, sz.rows)]), g_send.at[m])

        for_owned(last)

    def norm_back(k, slot, sums_d, sums_c):
        gain, mean, inv = gains[k], norm_stats[k, slot], norm_stats[k + 1, slot]
        sums_d = 0.5 * sums_d
        sums_n = inv * (0.5 * sums_c - mean * sums_d)
        scale = 1.0 / float(GSIZE * LANES * grid)
        m1 = spread(group_sum(sums_d * gain) * scale, width)
        m2 = spread(group_sum(sums_n * gain) * scale, width)
        d_norm[k] += sums_n
        d_norm[k + 1] += sums_d
        fc = inv * inv * m2
        back_factors[0] = 0.5 * inv * gain
        back_factors[1] = inv * m1 - fc * mean
        back_factors[2] = fc

    def mid_grad(slot, span):
        def body(it, carry):
            i = it * span
            left = jnp.concatenate([g_taps[i + k + 1] for k in range(span)], axis=1)
            center = slice(width, 2 * width)
            right = [hidden_low[slot, pl.ds(i + k, TAPS), center].reshape(TAPS * width, LANES) for k in range(span)]
            d_mid[...] += dot_nt(left, jnp.concatenate(right, axis=1))
            return carry

        loop(grid // span, 4, body, 0)

    def step_backward(t, slot):
        @block
        def _():
            sy, sx = saved[slot, 2], saved[slot, 3]
            f0, f1 = saved[slot, 0], saved[slot, 1]
            wy, wx = quadratic(sy), quadratic(sx)
            grads = [2.0 * inv_count * saved[slot, 10]]
            if t < steps - 1:
                solid = {d: mask[d + 2] for d in NEAR}
                grads[0] = grads[0] + grad_state[0]
                gu, gv = columns_of(solid[0] * grad_state[1], 1), columns_of(solid[0] * grad_state[2], 2)
                one = {d: 0.125 * solid[d] * (diff_rows(gu[d]) + (gv[d + 1] - gv[d - 1])) for d in NEAR}
                two = 0.25 * solid[0] * (rows_around(one[0]) + one[1] + one[-1])
                two = columns_of(two, 2)
                g_div = {
                    d: one[d] + two[d] + 0.25 * solid[d] * (rows_around(two[d]) + two[d + 1] + two[d - 1]) for d in NEAR
                }
                grads.append(gu[0] + 0.5 * diff_rows(g_div[0]))
                grads.append(gv[0] + 0.5 * (g_div[1] - g_div[-1]))
            spots = []
            g_sy = g_sx = 0.0
            for n, g in enumerate(grads):
                g_sy = g_sy + g * saved[slot, 4 + n]
                g_sx = g_sx + g * saved[slot, 7 + n]
                lines = []
                for b in range(3):
                    gb = wx[b] * g
                    lines.append(from_below(wy[0] * gb) + wy[1] * gb + from_above(wy[2] * gb))
                spots.append(column(lines[0], 1) + lines[1] + column(lines[2], -1))
            ty, tx = sy * (1.0 / COURANT), sx * (1.0 / COURANT)
            g_u1 = g_sy * (COURANT * (1.0 - ty * ty))
            g_v1 = g_sx * (COURANT * (1.0 - tx * tx))
            if t < steps - 1:
                g_u1, g_v1 = spots[1] + g_u1, spots[2] + g_v1
            l0 = (TIME_STEP * g_u1 + 2.0 * FORCE_WEIGHT * inv_count * f0) * (1.0 - f0 * f0)
            l1 = (TIME_STEP * g_v1 + 2.0 * FORCE_WEIGHT * inv_count * f1) * (1.0 - f1 * f1)
            if t > 0:
                grad_state[0] = spots[0]
                grad_state[1] = g_u1
                grad_state[2] = g_v1
            if sz.slots > 1 and t < steps - 1:
                mid_grad(t + 1, 16)
            glog32[pl.ds(0, grid, stride=16), :] = l0
            glog32[pl.ds(1, grid, stride=16), :] = l1

            def pack(it, carry):
                for k in range(4):
                    i = it * 4 + k
                    glog[slot, i] = glog32[pl.ds(pl.multiple_of(i * 16, 16), 16), :].astype(BF16)
                return carry

            loop(grid // 4, 8, pack, 0)

        @block
        def _():
            def back_a(it, carry):
                sums_d, sums_n = carry
                i = it * 2
                gl = jnp.concatenate([glog[slot, i], glog[slot, i + 1]], axis=1)
                p = dot(head_back[...], gl)
                for k in range(2):
                    g = p[:, k * LANES : (k + 1) * LANES]
                    mixed_grad[i + k] = g
                    d = g * slope[slot, 1, i + k]
                    dy[i + k] = d
                    sums_d = sums_d + d
                    sums_n = sums_n + d * conv[slot, 1, i + k]
                return sums_d, sums_n

            zero = jnp.zeros((width, LANES), F32)
            sums = loop(grid // 2, 16, back_a, (zero, zero))
            norm_back(2, slot, *sums)
        @block
        def _():
            fd, f1_, fn = [back_factors[k] for k in range(3)]

            def back_b(it, carry):
                gl = jnp.concatenate([glog[slot, it * 2 + k] for k in range(2)], axis=1)
                ml = jnp.concatenate([mixed_low[slot, it * 2 + k] for k in range(2)], axis=1)
                d_head[...] += dot_nt(gl, ml)
                for k in range(2):
                    i = it * 2 + k
                    g = fd * dy[i] - f1_ - fn * conv[slot, 1, i]
                    low = g.astype(BF16)
                    for kx, tap in enumerate((from_right(low), low, from_left(low))):
                        g_taps[i + 1, kx * width : (kx + 1) * width] = tap
                return carry

            loop(grid // 2, 16, back_b, 0)

        if t == 0:
            mid_grad(slot, 8)
            early_start()
        elif sz.slots == 1:
            mid_grad(slot, 16)

        @block
        def _():
            def back_c(it, carry):
                sums_d, sums_n = carry
                i = it * 4
                rows = rows_of(dot(w_bwd[...], four_rows(g_taps, i)))
                for k in range(4):
                    d = (rows[k] + mixed_grad[i + k]) * slope[slot, 0, i + k]
                    dy[i + k] = d
                    sums_d = sums_d + d
                    sums_n = sums_n + d * conv[slot, 0, i + k]
                return sums_d, sums_n

            zero = jnp.zeros((width, LANES), F32)
            sums = loop(grid // 4, 8, back_c, (zero, zero))
            norm_back(0, slot, *sums)
        @block
        def _():
            fd, f1_, fn = [back_factors[k] for k in range(3)]

            def back_d(it, carry):
                i = it * 2
                lows = []
                for k in range(2):
                    low = (fd * dy[i + k] - f1_ - fn * conv[slot, 0, i + k]).astype(BF16)
                    g_pad[slot, i + k + 1] = low
                    lows.append(low)
                d_in[...] += dot_nt(row_pair(feat.at[slot], i), jnp.concatenate(lows, axis=1))
                return carry

            loop(grid // 2, 16, back_d, 0)
            if t > 0:

                def back_e(it, carry):
                    i = it * 4
                    rows = rows_of(dot(v_bwd[...], four_rows(g_pad.at[slot], i)))
                    for k in range(4):
                        gs_rows[pl.ds(pl.multiple_of((i + k) * 8, 8), 8), :] = combine(rows[k], 8)
                    return carry

                loop(grid // 4, 8, back_e, 0)
                for q in range(3):
                    grad_state[q] += gs_rows[pl.ds(q, grid, stride=8), :]

    for t in reversed(range(steps)):
        if sz.slots == 1:
            step_forward(t, 0, False)
        step_backward(t, t if sz.slots > 1 else 0)

    core = wrap(c, sz.cores)
    mate = (c + 1 - 2 * core, r)
    mine = pl.ds(core * sz.late, sz.late)

    def chip_peer(k):
        if sz.ways == 1:
            return (c, row_peer(k))
        return (wrap(c + 2 * (k // sz.rows), sz.ch), row_peer(k))

    columns = [jnp.sum(d_norm[k], axis=1, keepdims=True) for k in range(4)]
    columns.append(jnp.zeros((width, LANES - 4), F32))
    lines = jnp.transpose(jnp.concatenate(columns, axis=1))
    total = jnp.sum(jnp.sum(loss[...], axis=1, keepdims=True), axis=0, keepdims=True)
    pack = late_pair.at[core] if sz.cores > 1 else late_sum
    inputs = jnp.concatenate([d_in[0:24], d_in[24:48]], axis=1)
    for n in range(3):
        pack[n] = inputs[n * 8 : (n + 1) * 8]
    pack[3] = jnp.zeros((8, LANES), F32)
    pack[3, 0:4, 0:width] = lines[0:4, :]
    pack[3, 4:6, 0:width] = d_head[0:2]
    pack[3, 6:7, 0:width] = jnp.broadcast_to(total, (1, width))
    if sz.cores > 1:
        remote(pack, pack, p_send.at[0], p_recv.at[0], mate).start()
        arrived(pack, p_recv.at[0])
        late_sum[...] = late_pair[0] + late_pair[1]
    for k in range(1, sz.chips):
        remote(late_sum.at[mine], late_in.at[chip_slot], b_send.at[0], b_recv.at[0], chip_peer(k)).start()

    early_sum()

    late_in[chip_slot] = late_sum[mine]
    if sz.chips > 1:
        arrived(but_one(late_in), b_recv.at[0])
    acc = late_in[0]
    for k in range(1, sz.chips):
        acc = acc + late_in[k]
    late_fin[mine] = acc
    if sz.cores > 1:
        remote(late_fin.at[mine], late_fin.at[mine], p_send.at[1], p_recv.at[1], mate).start()
        sent(pack, p_send.at[0])
    early_left()
    if sz.chips > 1:
        sent(but_one(late_in), b_send.at[0])
    if sz.cores > 1:
        arrived(late_fin.at[mine], p_recv.at[1])
    acc = late_fin[...].reshape(32, LANES)
    turned = pltpu.roll(acc, wrap(LANES - c * co, LANES), 1)
    for n in range(4):
        out[sz.early + n] = turned[n * 8 : (n + 1) * 8]
    acc = jnp.where(row_ids(acc.shape) < 30, acc, 0.0)
    late_norm = jnp.sum(acc * acc, axis=0, keepdims=True)

    if sz.early < 8:
        out[sz.early + 4] = jnp.zeros((8, LANES), F32)
    early_end()
    acc = late_norm
    for k in range(sz.ch):
        for j in range(sz.early):
            acc = acc + ssq_early[k, j]
    out_total[...] = jnp.broadcast_to(jnp.sum(acc, axis=1, keepdims=True), (8, LANES))
    early_shared()
    if sz.cores > 1:
        sent(late_fin.at[mine], p_send.at[1])


def adam(weight, grad, moment, square, rate, decay):
    moment = BETA_ONE * moment + (1.0 - BETA_ONE) * grad
    square = BETA_TWO * square + (1.0 - BETA_TWO) * grad * grad
    fix_one = 1.0 - BETA_ONE**STEP_NUM
    fix_two = 1.0 - BETA_TWO**STEP_NUM
    updated = weight - rate * (moment / fix_one / (jnp.sqrt(square / fix_two) + ADAM_EPS) + decay * weight)
    return updated, moment, square


def adam_kernel(sz, grads, total, keyframes, *refs):
    params, firsts, seconds = refs[0:4], refs[4:8], refs[8:12]
    news, moments, squares = refs[12:16], refs[16:20], refs[20:24]
    co, width = sz.co, sz.width
    norm = jnp.sqrt(total[0:1, 0:1])
    factor = CLIP / jnp.maximum(norm, CLIP)

    def put(n, at, grad):
        rate, decay = (RATE, DECAY) if n < 3 else (GAIN_RATE, 0.0)
        new, moment, square = adam(params[n][at], grad, firsts[n][at], seconds[n][at], rate, decay)
        news[n][at] = new
        moments[n][at] = moment
        squares[n][at] = square

    tiles = []
    for n in range(4):
        tiles.append(jnp.concatenate([grads[h * 4 + n] for h in range(sz.halves)], axis=0) * factor)
    last = grads[sz.early + 4, 0 : co // 2] * factor
    last = jnp.concatenate([last[:, :width], last[:, width:]], axis=0)
    thirds = [tiles[3][:, :width], tiles[3][:, width:], last]
    for kx in range(TAPS):
        put(1, (0, kx), tiles[kx][:, :width])
        put(1, (1, kx), tiles[kx][:, width:])
        put(1, (2, kx), thirds[kx])
    tail = jnp.concatenate([grads[sz.early + n] for n in range(3)], axis=0) * factor
    for ky in range(TAPS):
        for kx in range(TAPS):
            at = ky * 16 + kx * 4
            side = width if at >= 24 else 0
            at = at - 24 if at >= 24 else at
            put(0, (ky, kx), tail[at : at + 4, side : side + co])
    tail = grads[sz.early + 3]
    loss = tail[6:7, 0:1]
    tail = tail * factor
    put(2, Ellipsis, tail[4:6, 0:co])
    put(3, Ellipsis, tail[0:4, 0:co])
    marks = keyframes[...].astype(F32)
    valid = jnp.sum(jnp.sum(marks, axis=1, keepdims=True), axis=0, keepdims=True) * float(sz.grid * sz.cols)
    refs[24][...] = norm
    refs[25][...] = loss
    refs[26][...] = valid


def scratch_of(sz):
    grid, width, rows, ch, slots, steps = sz.grid, sz.width, sz.rows, sz.ch, sz.slots, sz.steps
    wide = TAPS * width

    def f32(*shape):
        return pltpu.VMEM(shape, F32)

    def bf16(*shape):
        return pltpu.VMEM(shape, BF16)

    dma = lambda *shape: pltpu.SemaphoreType.DMA(shape)
    return {
        "f_stage": f32(rows, 3, sz.local, LANES),
        "t_stage": f32(rows, steps, sz.local, LANES),
        "m_stage": pltpu.VMEM((rows, sz.local, LANES), jnp.int32),
        "w_in_own": f32(TAPS, TAPS, 4, sz.co),
        "w_mid_own": f32(TAPS, TAPS, sz.co, width),
        "w_head_own": f32(2, sz.co),
        "norms_own": f32(4, sz.co),
        "small": f32(LANES, LANES),
        "ws_all": f32(ch, sz.co, LANES),
        "wm_all": bf16(ch, -(-sz.co // 16) * 16, sz.mid_lanes),
        "w_fwd": bf16(2 * width, 4 * wide),
        "w_bwd": bf16(2 * width, 4 * wide),
        "v_fwd": bf16(width, TAPS * 16),
        "v_bwd": bf16(2 * TAPS * 8, 4 * width),
        "head_back": bf16(width, 16),
        "head": bf16(16, width),
        "gains": f32(4, width, LANES),
        "current": f32(3, 3, grid, LANES),
        "states": f32(1 if slots > 1 else steps, 3, 3, grid, LANES),
        "mask": f32(5, grid, LANES),
        "target": f32(steps, grid, LANES),
        "feat32": f32(grid * 16, LANES),
        "feat": bf16(slots, grid + 2, 16, LANES),
        "conv": f32(slots, 2, grid, width, LANES),
        "slope": f32(slots, 2, grid, width, LANES),
        "norm_stats": f32(4, slots, width, LANES),
        "back_factors": f32(3, width, LANES),
        "hidden": f32(grid, width, LANES),
        "hidden_low": bf16(slots, grid + 2, wide, LANES),
        "mixed_low": bf16(slots, grid, width, LANES),
        "logits": f32(2, grid, LANES),
        "saved": f32(slots, SAVED, grid, LANES),
        "dy": f32(grid, width, LANES),
        "mixed_grad": f32(grid, width, LANES),
        "glog32": f32(grid * 16, LANES),
        "glog": bf16(slots, grid, 16, LANES),
        "g_pad": bf16(slots, grid + 2, width, LANES),
        "g_taps": bf16(grid + 2, wide, LANES),
        "gs_rows": f32(grid * 8, LANES),
        "grad_state": f32(3, grid, LANES),
        "d_mid": f32(wide, wide),
        "d_in": f32(TAPS * 16, width),
        "d_head": f32(16, width),
        "d_norm": f32(4, width, LANES),
        "loss": f32(grid, LANES),
        "early": f32(ch * sz.early, 9, LANES),
        "early_in": f32(sz.owned, sz.sources, 9, LANES),
        "early_fin": f32(sz.early, 9, LANES),
        "blank": f32(ch, rows, 1, LANES),
        "ssq_early": f32(ch, sz.early, 1, LANES),
        "late_pair": f32(2, 4, 8, LANES),
        "late_sum": f32(4, 8, LANES),
        "late_in": f32(sz.chips, sz.late, 8, LANES),
        "late_fin": f32(4, 8, LANES),
        "ready": pltpu.SemaphoreType.REGULAR,
        "local_sem": dma(7),
        "f_sem": dma(2),
        "t_sem": dma(2),
        "m_sem": dma(2),
        "v_sem": dma(2),
        "w_sem": dma(2),
        "e_send": dma(1),
        "e_recv": dma(sz.owned),
        "g_send": dma(sz.owned),
        "g_recv": dma(1),
        "s_send": dma(sz.owned),
        "s_recv": dma(1),
        "b_send": dma(1),
        "b_recv": dma(1),
        "p_send": dma(2),
        "p_recv": dma(2),
    }


def shards(mesh, fields, targets, fluid, keyframes, *rest):
    params, firsts, seconds = rest[0:4], rest[4:8], rest[8:12]

    def native(leaves):
        return (leaves[0], jnp.swapaxes(leaves[1], 2, 3), leaves[2].T, leaves[3])

    params, firsts, seconds = native(params), native(firsts), native(seconds)
    sz = Sizes(mesh, fields.shape, targets.shape, params[0].shape[3])
    marks = keyframes.T
    vmem = pl.BlockSpec(memory_space=pltpu.VMEM)
    hbm = pl.BlockSpec(memory_space=pl.ANY)
    alone = sz.rows == 1 and sz.ch == 1
    grads, total = pl.pallas_call(
        functools.partial(train_kernel, sz),
        out_shape=(
            jax.ShapeDtypeStruct((sz.early + 5, 8, LANES), F32),
            jax.ShapeDtypeStruct((8, LANES), F32),
        ),
        in_specs=[hbm, hbm, hbm, vmem] + [hbm] * 4,
        out_specs=(vmem, vmem),
        scratch_shapes=list(scratch_of(sz).values()),
        compiler_params=pltpu.CompilerParams(
            collective_id=None if alone else 0, has_side_effects=True, vmem_limit_bytes=60 << 20
        ),
        name="train",
    )(fields, targets, fluid, marks, *params)
    shapes = [jax.ShapeDtypeStruct(leaf.shape, F32) for leaf in params] * 3
    shapes += [jax.ShapeDtypeStruct((1, 1), F32)] * 3
    results = pl.pallas_call(
        functools.partial(adam_kernel, sz),
        out_shape=tuple(shapes),
        in_specs=[vmem] * 15,
        out_specs=tuple([vmem] * 15),
        name="adamw",
    )(grads, total, marks, *params, *firsts, *seconds)
    outs = []
    for n in range(3):
        outs.extend(native(results[4 * n : 4 * n + 4]))
    return (*outs, *[leaf.reshape(()) for leaf in results[12:]])


def solution(mesh):
    split = (P(None, None, None, "ch"), P(None, None, None, "ch"), P("ch", None), P(None, "ch"))
    return jax.shard_map(
        functools.partial(shards, mesh),
        mesh=mesh,
        in_specs=(
            P(None, None, "rows", None),
            P(None, None, "rows", None),
            P("rows", None),
            P(),
            *split,
            *split,
            *split,
        ),
        out_specs=(*split, *split, *split, P(), P(), P()),
        check_vma=False,
    )
```

```python
import functools

import jax
import jax.numpy as jnp
from jax import lax
from jax.experimental import pallas as pl
from jax.experimental.pallas import tpu as pltpu
from jax.sharding import PartitionSpec as P

GROUPS = 8
NEAR = (-1, 0, 1)
STEP_NUM = 10
TIME_STEP = 0.5
COURANT = 0.8
FORCE_WEIGHT = 0.5
NORM_EPS = 1e-05
CLIP = 0.0001
BETA_ONE = 0.9
BETA_TWO = 0.999
ADAM_EPS = 1e-10
RATE = 0.1
GAIN_RATE = 0.6
DECAY = 0.01

MESH = pl.DeviceIdType.MESH
F32 = jnp.float32
BF16 = jnp.bfloat16
LANES = 128
GSIZE = 8
TAPS = 3
SAVED = 11
NT = (((1,), (1,)), ((), ()))


def lane_ids(shape):
    return lax.broadcasted_iota(jnp.int32, shape, len(shape) - 1)


def row_ids(shape):
    return lax.broadcasted_iota(jnp.int32, shape, 0)


def from_left(x):
    return jnp.where(lane_ids(x.shape) == 0, jnp.zeros_like(x), pltpu.roll(x, 1, 1))


def from_right(x):
    size = x.shape[1]
    return jnp.where(lane_ids(x.shape) == size - 1, jnp.zeros_like(x), pltpu.roll(x, size - 1, 1))


def from_above(x):
    return jnp.where(row_ids(x.shape) == 0, 0.0, pltpu.roll(x, 1, 0))


def from_below(x):
    size = x.shape[0]
    return jnp.where(row_ids(x.shape) == size - 1, 0.0, pltpu.roll(x, size - 1, 0))


def diff_rows(x):
    return from_below(x) - from_above(x)


def column(x, d):
    if d == 0:
        return x
    size = x.shape[1]
    lane = lane_ids(x.shape)
    inside = lane < size - d if d > 0 else lane >= -d
    return jnp.where(inside, pltpu.roll(x, -d % size, 1), jnp.zeros_like(x))


def columns_of(x, reach):
    return {d: column(x, d) for d in range(-reach, reach + 1)}


def rows_around(x):
    return from_below(x) + from_above(x)


def quadratic(s):
    return (0.5 * s * (s + 1.0), 1.0 - s * s, 0.5 * s * (s - 1.0))


def quadratic_slope(s):
    return (s + 0.5, -2.0 * s, s - 0.5)


def wrap(x, n):
    return x & (n - 1) if n & (n - 1) == 0 else lax.rem(x, n)


def partner(x, k, n):
    return x ^ k if n & (n - 1) == 0 else lax.rem(x + k, n)


def far_first(n):
    return reversed(range(1, n))


def dot(a, b):
    return jnp.dot(a, b, preferred_element_type=F32)


def dot_nt(a, b):
    return lax.dot_general(a, b, NT, preferred_element_type=F32)


def row_pair(ref, i, extra=None):
    depth = ref.shape[1] * TAPS
    sides = []
    for k in range(2):
        side = ref[pl.ds(i + k, TAPS)].reshape(depth, LANES)
        if extra is not None:
            side = jnp.concatenate([side, extra[i + k]], axis=0)
        sides.append(side)
    return jnp.concatenate(sides, axis=1)


def side_by_side(ref, first):
    return jnp.concatenate([ref[i] for i in range(first, ref.shape[0])], axis=1)


def four_rows(ref, i):
    taps = ref.shape[1] // 64
    parts = []
    for n in range(taps):
        sides = [ref[pl.ds(i + 2 * k, 4), n * 64 : (n + 1) * 64].reshape(4 * 64, LANES) for k in range(2)]
        parts.append(jnp.concatenate(sides, axis=1))
    return jnp.concatenate(parts, axis=0) if taps > 1 else parts[0]


def rows_of(p):
    half = p.shape[0] // 2
    return [p[o * half : (o + 1) * half, k * LANES : (k + 1) * LANES] for k in range(2) for o in range(2)]


def two_rows(blocks):
    zero = jnp.zeros_like(blocks[0])
    first = jnp.concatenate(list(blocks) + [zero], axis=1)
    second = jnp.concatenate([zero] + list(blocks), axis=1)
    return jnp.concatenate([first, second], axis=0)


def combine(part, height):
    return (
        part[height : 2 * height] + from_left(part[:height]) + from_right(part[2 * height : 3 * height])
    )


def group_sum(x):
    return jnp.sum(jnp.sum(x.reshape(-1, GSIZE, LANES), axis=1), axis=1, keepdims=True)


def spread(x, width):
    return jnp.broadcast_to(x[:, :, None], (x.shape[0], GSIZE, LANES)).reshape(width, LANES)


def loop(count, per, body, carry):
    per = min(per, count)

    def several(it, carry):
        for k in range(per):
            carry = body(it * per + k, carry)
        return carry

    if count == per:
        return several(0, carry)
    return lax.fori_loop(0, count // per, several, carry)


def in_place(ky, kx):
    at = ky * 16 + kx * 4
    lane = 64 if at >= 24 else 0
    at = at % 24
    return at // 8, at % 8, lane


class Sizes:
    def __init__(self, mesh, fields_shape, targets_shape, co):
        self.ch = mesh.shape["ch"]
        self.rows = mesh.shape["rows"]
        self.batch = fields_shape[0]
        self.local = fields_shape[2]
        self.grid = self.local * self.rows
        self.cols = fields_shape[3]
        self.steps = targets_shape[0]
        self.co = co
        self.width = co * self.ch
        self.per_rows = self.batch // self.rows
        self.ways = self.ch if self.per_rows == self.ch else 1
        assert self.per_rows == self.ways and self.batch % self.rows == 0
        assert self.cols == LANES
        slot = self.grid * self.width * LANES * 20
        self.slots = self.steps if slot * self.steps < (24 << 20) else 1
        self.halves = co // 8
        self.early = 4 * self.halves
        self.owned = -(-self.early // self.rows)
        self.sources = self.ways * self.rows
        self.cores = 2 if self.ways > 1 else 1
        self.chips = self.sources // self.cores
        self.late = 4 // self.cores
        assert self.ways % self.cores == 0
        self.mid_lanes = TAPS * TAPS * self.width
        assert self.width == 64 and co % 8 == 0


IN_AT = 64
HEAD_AT = IN_AT + 36
NORM_AT = HEAD_AT + 2
LOSS_AT = NORM_AT + 4


def train_kernel(
    sz,
    fields,
    targets,
    fluid,
    keyframes,
    w_in,
    w_mid,
    w_head,
    norms,
    first_in,
    first_mid,
    first_head,
    first_norm,
    second_in,
    second_mid,
    second_head,
    second_norm,
    out,
    *scratch,
):
    z = dict(zip(scratch_of(sz), scratch))
    f_stage = z["f_stage"]
    t_stage = z["t_stage"]
    m_stage = z["m_stage"]
    in_own = z["in_own"]
    mid_own = z["mid_own"]
    head_own = z["head_own"]
    norm_own = z["norm_own"]
    marks_own = z["marks_own"]
    held = z["held"]
    total = z["total"]
    small = z["small"]
    ws_all = z["ws_all"]
    wm_all = z["wm_all"]
    w_fwd = z["w_fwd"]
    w_bwd = z["w_bwd"]
    v_fwd = z["v_fwd"]
    v_bwd = z["v_bwd"]
    head_back = z["head_back"]
    head = z["head"]
    gains = z["gains"]
    current = z["current"]
    states = z["states"]
    mask = z["mask"]
    target = z["target"]
    feat32 = z["feat32"]
    feat = z["feat"]
    conv = z["conv"]
    slope = z["slope"]
    norm_stats = z["norm_stats"]
    back_factors = z["back_factors"]
    hidden = z["hidden"]
    hidden_low = z["hidden_low"]
    mixed_low = z["mixed_low"]
    logits = z["logits"]
    saved = z["saved"]
    dy = z["dy"]
    mixed_grad = z["mixed_grad"]
    glog32 = z["glog32"]
    glog = z["glog"]
    g_pad = z["g_pad"]
    g_taps = z["g_taps"]
    gs_rows = z["gs_rows"]
    grad_state = z["grad_state"]
    d_mid = z["d_mid"]
    d_in = z["d_in"]
    d_head = z["d_head"]
    d_norm = z["d_norm"]
    loss = z["loss"]
    early = z["early"]
    early_in = z["early_in"]
    early_fin = z["early_fin"]
    blank = z["blank"]
    ssq_early = z["ssq_early"]
    late_pair = z["late_pair"]
    late_sum = z["late_sum"]
    late_in = z["late_in"]
    late_fin = z["late_fin"]
    ready = z["ready"]
    local_sem = z["local_sem"]
    f_sem = z["f_sem"]
    t_sem = z["t_sem"]
    m_sem = z["m_sem"]
    v_sem = z["v_sem"]
    w_sem = z["w_sem"]
    e_send = z["e_send"]
    e_recv = z["e_recv"]
    g_send = z["g_send"]
    g_recv = z["g_recv"]
    s_send = z["s_send"]
    s_recv = z["s_recv"]
    b_send = z["b_send"]
    b_recv = z["b_recv"]
    p_send = z["p_send"]
    p_recv = z["p_recv"]
    c = lax.axis_index("ch")
    r = lax.axis_index("rows")
    width, grid, steps = sz.width, sz.grid, sz.steps
    co = sz.co

    def row_peer(k):
        return partner(r, k, sz.rows)

    def ch_peer(k):
        return partner(c, k, sz.ch)

    def sample_of(row):
        return row * sz.per_rows + (c if sz.ways > 1 else 0)

    def block(work):
        pl.when(r >= 0)(work)

    peers = sz.rows - 1 + sz.ch - 1
    if peers:
        barrier = pltpu.get_barrier_semaphore()
        for k in far_first(sz.rows):
            pl.semaphore_signal(barrier, inc=1, device_id=(c, row_peer(k)), device_id_type=MESH)
        for k in far_first(sz.ch):
            pl.semaphore_signal(barrier, inc=1, device_id=(ch_peer(k), r), device_id_type=MESH)

    def remote(src, dst, send, recv, where):
        return pltpu.make_async_remote_copy(
            src_ref=src, dst_ref=dst, send_sem=send, recv_sem=recv, device_id=where, device_id_type=MESH
        )

    def arrived(ref, sem):
        remote(ref, ref, sem, sem, (c, r)).wait_recv()

    def sent(ref, sem):
        remote(ref, ref, sem, sem, (c, r)).wait_send()

    def but_one(ref):
        return ref.at[pl.ds(0, ref.shape[0] - 1)]

    own = [
        pltpu.make_async_copy(src, dst, local_sem.at[n])
        for n, (src, dst) in enumerate(
            (
                (w_in, in_own.at[0]),
                (w_head, head_own.at[0]),
                (norms, norm_own.at[0]),
                (w_mid, mid_own.at[0]),
                (fields.at[sample_of(r)], f_stage.at[r]),
                (fluid, m_stage.at[r]),
                (targets.at[:, sample_of(r)], t_stage.at[r]),
                (keyframes, marks_own),
                (first_in, in_own.at[1]),
                (first_mid, mid_own.at[1]),
                (first_head, head_own.at[1]),
                (first_norm, norm_own.at[1]),
                (second_in, in_own.at[2]),
                (second_mid, mid_own.at[2]),
                (second_head, head_own.at[2]),
                (second_norm, norm_own.at[2]),
            )
        )
    ]
    for copy in own:
        copy.start()
    if peers:
        pl.semaphore_wait(barrier, peers)

    for k in far_first(sz.rows):
        src = fields.at[sample_of(row_peer(k))]
        remote(src, f_stage.at[r], f_sem.at[0], f_sem.at[1], (c, row_peer(k))).start()
    for k in far_first(sz.rows):
        remote(fluid, m_stage.at[r], m_sem.at[0], m_sem.at[1], (c, row_peer(k))).start()
    small[...] = jnp.zeros_like(small)
    for n in range(4):
        own[n].wait()
    for ky in range(TAPS):
        for kx in range(TAPS):
            at = IN_AT + (ky * TAPS + kx) * 4
            small[at : at + 4, 0:co] = in_own[0, ky, kx]
    small[HEAD_AT : HEAD_AT + 2, 0:co] = head_own[0]
    small[NORM_AT : NORM_AT + 4, 0:co] = norm_own[0]
    ws_all[c] = jnp.transpose(small[...])[0:co]
    packed = jnp.concatenate([mid_own[0, ky, kx] for kx in range(TAPS) for ky in range(TAPS)], axis=1)
    wm_all[c, 0:co, :] = packed.astype(BF16)
    for k in far_first(sz.ch):
        remote(ws_all.at[c], ws_all.at[c], v_sem.at[0], v_sem.at[1], (ch_peer(k), r)).start()
    for k in far_first(sz.ch):
        remote(wm_all.at[c], wm_all.at[c], w_sem.at[0], w_sem.at[1], (ch_peer(k), r)).start()
    for k in far_first(sz.rows):
        src = targets.at[:, sample_of(row_peer(k))]
        remote(src, t_stage.at[r], t_sem.at[0], t_sem.at[1], (c, row_peer(k))).start()
    row_groups = ((f_stage, f_sem), (m_stage, m_sem), (t_stage, t_sem)) if sz.rows > 1 else ()
    ch_groups = ((ws_all, v_sem), (wm_all, w_sem)) if sz.ch > 1 else ()
    if peers:
        for k in far_first(sz.ch):
            pl.semaphore_signal(ready, inc=1, device_id=(ch_peer(k), r), device_id_type=MESH)

    for n in range(8, 16):
        own[n].wait()
    for n in range(3):
        mid = [[mid_own[n, ky, kx] for kx in range(TAPS)] for ky in range(TAPS)]
        sides = [(mid[0][kx], mid[1][kx]) for kx in range(TAPS)] + [(mid[2][0], mid[2][1])]
        for k, side in enumerate(sides):
            tile = jnp.concatenate(side, axis=1)
            for h in range(sz.halves):
                held[n, h * 4 + k] = tile[h * 8 : (h + 1) * 8]
        for k in range(sz.early, sz.early + 5):
            held[n, k] = jnp.zeros((8, LANES), F32)
        for ky in range(TAPS):
            for kx in range(TAPS):
                tile, row, lane = in_place(ky, kx)
                held[n, sz.early + tile, row : row + 4, lane : lane + co] = in_own[n, ky, kx]
        held[n, sz.early + 3, 0:4, 0:co] = norm_own[n]
        held[n, sz.early + 3, 4:6, 0:co] = head_own[n]
        last = mid[2][2]
        held[n, sz.early + 4, 0 : co // 2] = jnp.concatenate([last[: co // 2], last[co // 2 :]], axis=1)

    for i in (0, grid + 1):
        g_taps[i] = jnp.zeros_like(g_taps[i])
    for ref in (feat, hidden_low, g_pad):
        for slot in range(sz.slots):
            ref[slot, 0] = jnp.zeros_like(ref[slot, 0])
            ref[slot, grid + 1] = jnp.zeros_like(ref[slot, 0])
    feat32[...] = jnp.zeros_like(feat32)
    glog32[...] = jnp.zeros_like(glog32)
    for ref in (d_mid, d_in, d_head, d_norm, loss):
        ref[...] = jnp.zeros_like(ref)

    if ch_groups:
        arrived(but_one(ws_all), v_sem.at[1])
    tail = ws_all[...].reshape(width, LANES)
    tail_t = jnp.transpose(tail)
    parts = []
    for ky in range(TAPS):
        at = IN_AT + ky * 12
        parts.append(jnp.concatenate([tail[:, at : at + 12], jnp.zeros((width, 4), F32)], axis=1))
    v_fwd[...] = jnp.concatenate(parts, axis=1).astype(BF16)
    pieces = []
    for ky in range(TAPS):
        column_taps = []
        for kx in range(TAPS):
            at = IN_AT + ((2 - ky) * TAPS + 2 - kx) * 4
            column_taps += [tail_t[at : at + 4], jnp.zeros((4, width), F32)]
        pieces.append(jnp.concatenate(column_taps, axis=0))
    v_bwd[...] = two_rows(pieces).astype(BF16)
    head_back[...] = jnp.concatenate([tail[:, HEAD_AT : HEAD_AT + 2], jnp.zeros((width, 14), F32)], axis=1).astype(BF16)
    head[...] = jnp.concatenate([tail_t[HEAD_AT : HEAD_AT + 2], jnp.zeros((14, width), F32)], axis=0).astype(BF16)
    for k in range(4):
        gains[k] = jnp.broadcast_to(tail[:, NORM_AT + k : NORM_AT + k + 1], (width, LANES))

    for ref, sem in row_groups[:2]:
        arrived(but_one(ref), sem.at[1])
    own[4].wait()
    own[5].wait()
    for row in range(sz.rows):
        at = pl.ds(row * sz.local, sz.local)
        for q in range(3):
            current[q, 1, at, :] = f_stage[row, q]
        mask[2, at, :] = m_stage[row].astype(F32)
    for q in range(3):
        for d in (-1, 1):
            current[q, d + 1] = column(current[q, 1], d)
    for d in (-2, -1, 1, 2):
        mask[d + 2] = column(mask[2], d)
    for d in NEAR:
        feat32[pl.ds((d + 1) * 4 + 3, grid, stride=16), :] = mask[d + 2]

    def second_layer():
        if ch_groups:
            arrived(but_one(wm_all), w_sem.at[1])
        kind = BF16 if co % 16 == 0 else F32
        mid = jnp.concatenate([wm_all[k, 0:co, :].astype(kind) for k in range(sz.ch)], axis=0)
        for kx in range(TAPS):
            at = [(kx * TAPS + ky) * width for ky in range(TAPS)]
            w_fwd[:, kx * 4 * width : (kx + 1) * 4 * width] = two_rows([mid[:, a : a + width] for a in at]).astype(BF16)

    def second_layer_back():
        for kx in range(TAPS):
            at = kx * 4 * width
            blocks = [w_fwd[0:width, at + ky * width : at + (ky + 1) * width].astype(F32) for ky in range(TAPS)]
            w_bwd[:, at : at + 4 * width] = two_rows([jnp.transpose(b) for b in reversed(blocks)]).astype(BF16)

    def all_targets():
        if row_groups:
            arrived(but_one(t_stage), t_sem.at[1])
        own[6].wait()
        for row in range(sz.rows):
            at = pl.ds(row * sz.local, sz.local)
            for t in range(steps):
                target[t, at, :] = t_stage[row, t]

    second_layer()

    own[7].wait()
    marks = marks_own[...].astype(F32)
    valid = jnp.sum(jnp.sum(marks, axis=1, keepdims=True), axis=0, keepdims=True) * float(grid * sz.cols)
    inv_count = 1.0 / valid
    picked = jnp.where(lane_ids(marks.shape) == sample_of(r), marks, 0.0)
    marked = jnp.sum(picked, axis=1, keepdims=True)

    def key_of(t):
        return jnp.sum(jnp.where(row_ids(marked.shape) == t, marked, 0.0), axis=0, keepdims=True)

    def conv_and_stats(x_ref, w, store, layer, slot):
        zero = jnp.zeros((width, LANES), F32)

        def body(it, carry):
            base, total, squares = carry
            i = it * 4
            if layer:
                rows = rows_of(dot(w[...], four_rows(x_ref, i)))
            else:
                rows = []
                for k in range(2):
                    p = dot(w[...], row_pair(x_ref, i + 2 * k))
                    rows += [p[:, :LANES], p[:, LANES:]]
            base = jnp.where(it == 0, rows[0], base)
            for j in range(4):
                store[i + j] = rows[j]
                d = rows[j] - base
                total = total + d
                squares = squares + d * d
            return base, total, squares

        base, total, squares = loop(grid // 4, 8, body, (zero, zero, zero))
        lane_mean = base + total * (1.0 / grid)
        lane_dev = squares - total * total * (1.0 / grid)
        count = float(GSIZE * LANES)
        middle = spread(group_sum(base) * (1.0 / count), width)
        d = lane_mean - middle
        first = spread(group_sum(d) * (1.0 / count), width)
        second = spread(group_sum(lane_dev + grid * d * d) * (1.0 / (count * grid)), width)
        norm_stats[2 * layer, slot] = middle + first
        norm_stats[2 * layer + 1, slot] = lax.rsqrt(second - first * first + NORM_EPS)

    def silu_parts(half):
        t = jnp.tanh(half)
        a = 1.0 + t
        h = half * a
        return h, a + h * (1.0 - t)

    def half_affine(layer, slot):
        k = 2 * layer
        mean, inv = norm_stats[k, slot], norm_stats[k + 1, slot]
        scale = 0.5 * inv * gains[k]
        return scale, 0.5 * gains[k + 1] - mean * scale

    def step_forward(t, slot, first):
        last = t == steps - 1
        if sz.slots == 1:
            for q in range(3):
                for d in NEAR:
                    if first:
                        states[t, q, d + 1] = current[q, d + 1]
                    else:
                        current[q, d + 1] = states[t, q, d + 1]
        @block
        def _():
            x = [{d: current[q, d + 1] for d in NEAR} for q in range(3)]
            for q in range(3):
                for d in NEAR:
                    feat32[pl.ds((d + 1) * 4 + q, grid, stride=16), :] = x[q][d]

            def pack(it, carry):
                for k in range(4):
                    i = it * 4 + k
                    feat[slot, i + 1] = feat32[pl.ds(pl.multiple_of(i * 16, 16), 16), :].astype(BF16)
                return carry

            loop(grid // 4, 8, pack, 0)

            conv_and_stats(feat.at[slot], v_fwd, conv.at[slot, 0], 0, slot)
        @block
        def _():
            mul, add = half_affine(0, slot)

            def norm_one(it, carry):
                for k in range(2):
                    i = it * 2 + k
                    h, slope[slot, 0, i] = silu_parts(conv[slot, 0, i] * mul + add)
                    hidden[i] = h
                    low = h.astype(BF16)
                    for kx, tap in enumerate((from_left(low), low, from_right(low))):
                        hidden_low[slot, i + 1, kx * width : (kx + 1) * width] = tap
                return carry

            loop(grid // 2, 16, norm_one, 0)

            conv_and_stats(hidden_low.at[slot], w_fwd, conv.at[slot, 1], 1, slot)
        @block
        def _():
            mul, add = half_affine(1, slot)

            def norm_two(it, carry):
                i = it * 2
                lows = []
                for k in range(2):
                    h, slope[slot, 1, i + k] = silu_parts(conv[slot, 1, i + k] * mul + add)
                    low = (hidden[i + k] + h).astype(BF16)
                    mixed_low[slot, i + k] = low
                    lows.append(low)
                p = dot(head[...], jnp.concatenate(lows, axis=1))
                for k in range(2):
                    logits[0, pl.ds(i + k, 1), :] = p[0:1, k * LANES : (k + 1) * LANES]
                    logits[1, pl.ds(i + k, 1), :] = p[1:2, k * LANES : (k + 1) * LANES]
                return carry

            loop(grid // 2, 16, norm_two, 0)

        if first and t == 0:
            all_targets()
            second_layer_back()
        @block
        def _():
            x = [{d: current[q, d + 1] for d in NEAR} for q in range(3)]
            f0, f1 = jnp.tanh(logits[0]), jnp.tanh(logits[1])
            force0, force1 = columns_of(f0, 1), columns_of(f1, 1)
            u1 = {d: x[1][d] + TIME_STEP * force0[d] for d in NEAR}
            v1 = {d: x[2][d] + TIME_STEP * force1[d] for d in NEAR}
            sy = COURANT * jnp.tanh(u1[0])
            sx = COURANT * jnp.tanh(v1[0])
            wy, wx = quadratic(sy), quadratic(sx)
            dwy, dwx = quadratic_slope(sy), quadratic_slope(sx)
            moved = []
            for n, q in enumerate((x[0], u1, v1)):
                lines = [(from_above(q[d]), q[d], from_below(q[d])) for d in NEAR]
                along = [wx[0] * lines[0][a] + wx[1] * lines[1][a] + wx[2] * lines[2][a] for a in range(3)]
                moved.append(wy[0] * along[0] + wy[1] * along[1] + wy[2] * along[2])
                if last and n:
                    continue
                slant = [dwx[0] * lines[0][a] + dwx[1] * lines[1][a] + dwx[2] * lines[2][a] for a in range(3)]
                saved[slot, 4 + n] = dwy[0] * along[0] + dwy[1] * along[1] + dwy[2] * along[2]
                saved[slot, 7 + n] = wy[0] * slant[0] + wy[1] * slant[1] + wy[2] * slant[2]
            rho2 = moved[0]
            if first and not last:
                solid = {d: mask[d + 2] for d in range(-2, 3)}
                rho2s, u2, v2 = columns_of(rho2, 1), columns_of(moved[1], 1), columns_of(moved[2], 2)
                div = {d: 0.5 * (diff_rows(u2[d]) + (v2[d + 1] - v2[d - 1])) for d in NEAR}
                press = {d: -0.25 * solid[d] * div[d] for d in NEAR}
                press = 0.25 * solid[0] * (rows_around(press[0]) + press[1] + press[-1] - div[0])
                press = columns_of(press, 3)
                div[2], div[-2] = column(div[0], 2), column(div[0], -2)
                press = {
                    d: 0.25 * solid[d] * (rows_around(press[d]) + press[d + 1] + press[d - 1] - div[d])
                    for d in range(-2, 3)
                }
                for d in NEAR:
                    current[0, d + 1] = rho2s[d]
                    current[1, d + 1] = solid[d] * (u2[d] - 0.5 * diff_rows(press[d]))
                    current[2, d + 1] = solid[d] * (v2[d] - 0.5 * (press[d + 1] - press[d - 1]))
            pull = key_of(t) * (rho2 - target[t])
            if first:
                loss[...] += FORCE_WEIGHT * (f0 * f0 + f1 * f1) + pull * (rho2 - target[t])
            saved[slot, 0] = f0
            saved[slot, 1] = f1
            saved[slot, 2] = sy
            saved[slot, 3] = sx
            saved[slot, 10] = pull

    for t in range(steps):
        step_forward(t, t if sz.slots > 1 else 0, True)
    for ref, sem in row_groups + ch_groups:
        sent(but_one(ref), sem.at[0])

    def owner_of(j):
        return wrap(j, sz.rows)

    me = c * sz.rows + r if sz.ways > 1 else r
    chip_slot = (c // 2) * sz.rows + r if sz.ways > 1 else r

    def by_owned(action):
        least, more = sz.early // sz.rows, sz.early % sz.rows
        if more:
            pl.when(r < more)(functools.partial(action, least + 1))
            pl.when(r >= more)(functools.partial(action, least))
        else:
            action(least)

    def for_owned(action):
        for m in range(sz.owned):
            j = r + m * sz.rows
            if (m + 1) * sz.rows <= sz.early:
                action(m, j)
            else:
                pl.when(j < sz.early)(functools.partial(action, m, j))

    def early_start():
        low_half = lane_ids((width, LANES)) < 64
        tiles = [d_mid[kx * width : (kx + 1) * width, 0:LANES] for kx in range(TAPS)]
        rest = [d_mid[kx * width : (kx + 1) * width, LANES:] for kx in range(2)]
        tiles.append(jnp.concatenate(rest, axis=1))
        last = d_mid[2 * width : 3 * width, LANES:]
        for shard in range(sz.ch):
            for h in range(sz.halves):
                at = shard * co + h * 8
                for n, tile in enumerate(tiles):
                    early[shard * sz.early + h * 4 + n, 0:8] = tile[at : at + 8]
            ends = last[shard * co : (shard + 1) * co]
            ends = jnp.concatenate([ends[: co // 2], ends[co // 2 :]], axis=1)
            for j in range(sz.early):
                early[shard * sz.early + j, 8:9] = ends[j : j + 1]
        if sz.ch > 1:
            pl.semaphore_wait(ready, sz.ch - 1)
        for dc in reversed(range(sz.ways)):
            shard = ch_peer(dc)
            for k in reversed(range(sz.early)):
                j = partner(r, k, sz.early) if sz.early == sz.rows else wrap(r + k, sz.early)
                slot = j // sz.rows if sz.owned > 1 else 0
                if dc == 0 and k == 0 and sz.early == sz.rows:
                    continue
                copy = remote(
                    early.at[shard * sz.early + j],
                    early_in.at[slot, me],
                    e_send.at[0],
                    e_recv.at[slot],
                    (shard, owner_of(j)),
                )
                if dc or sz.early == sz.rows:
                    copy.start()
                else:
                    pl.when(owner_of(j) != r)(copy.start)

    def early_sum():
        def total(m, j):
            early_in[m, me] = early[c * sz.early + j]
            if sz.sources > 1:
                arrived(but_one(early_in.at[m]), e_recv.at[m])
            acc = early_in[m, 0]
            for k in range(1, sz.sources):
                acc = acc + early_in[m, k]
            early_fin[j] = acc
            line = ssq_early.at[c, j]
            line[...] = jnp.sum(acc * acc, axis=0, keepdims=True)
            for dc in far_first(sz.ch):
                for k in reversed(range(sz.rows)):
                    remote(line, line, s_send.at[m], s_recv.at[0], (ch_peer(dc), row_peer(k))).start()
            for k in far_first(sz.rows):
                remote(early_fin.at[j], early_fin.at[j], g_send.at[m], g_recv.at[0], (c, row_peer(k))).start()

        for_owned(total)

    def early_left():
        if sz.sources > 1:
            by_owned(lambda n: sent(early.at[pl.ds(0, sz.ways * sz.early - n)], e_send.at[0]))

    def put_line(j, acc):
        ssq_early[c, j] = jnp.sum(acc * acc, axis=0, keepdims=True)

    def early_end():
        if sz.rows > 1:
            by_owned(lambda n: arrived(early_fin.at[pl.ds(0, sz.early - n)], g_recv.at[0]))
        for j in range(sz.early):
            acc = early_fin[j]
            total[j] = acc[0:8]
            total[sz.early + 4, j : j + 1] = acc[8:9]
            if sz.rows > 1:
                pl.when(r != j % sz.rows)(functools.partial(put_line, j, acc))
        if sz.ch > 1:
            arrived(but_one(ssq_early), s_recv.at[0])

    def early_shared():
        def last(m, j):
            if sz.ch > 1:
                sent(but_one(blank), s_send.at[m])
            if sz.rows > 1:
                sent(but_one(early_in.at[m, pl.ds(0, sz.rows)]), g_send.at[m])

        for_owned(last)

    def norm_back(k, slot, sums_d, sums_c):
        gain, mean, inv = gains[k], norm_stats[k, slot], norm_stats[k + 1, slot]
        sums_d = 0.5 * sums_d
        sums_n = inv * (0.5 * sums_c - mean * sums_d)
        scale = 1.0 / float(GSIZE * LANES * grid)
        m1 = spread(group_sum(sums_d * gain) * scale, width)
        m2 = spread(group_sum(sums_n * gain) * scale, width)
        d_norm[k] += sums_n
        d_norm[k + 1] += sums_d
        fc = inv * inv * m2
        back_factors[0] = 0.5 * inv * gain
        back_factors[1] = inv * m1 - fc * mean
        back_factors[2] = fc

    def mid_grad(slot, span):
        def body(it, carry):
            i = it * span
            left = jnp.concatenate([g_taps[i + k + 1] for k in range(span)], axis=1)
            center = slice(width, 2 * width)
            right = [hidden_low[slot, pl.ds(i + k, TAPS), center].reshape(TAPS * width, LANES) for k in range(span)]
            d_mid[...] += dot_nt(left, jnp.concatenate(right, axis=1))
            return carry

        loop(grid // span, 4, body, 0)

    def step_backward(t, slot):
        @block
        def _():
            sy, sx = saved[slot, 2], saved[slot, 3]
            f0, f1 = saved[slot, 0], saved[slot, 1]
            wy, wx = quadratic(sy), quadratic(sx)
            grads = [2.0 * inv_count * saved[slot, 10]]
            if t < steps - 1:
                solid = {d: mask[d + 2] for d in NEAR}
                grads[0] = grads[0] + grad_state[0]
                gu, gv = columns_of(solid[0] * grad_state[1], 1), columns_of(solid[0] * grad_state[2], 2)
                one = {d: 0.125 * solid[d] * (diff_rows(gu[d]) + (gv[d + 1] - gv[d - 1])) for d in NEAR}
                two = 0.25 * solid[0] * (rows_around(one[0]) + one[1] + one[-1])
                two = columns_of(two, 2)
                g_div = {
                    d: one[d] + two[d] + 0.25 * solid[d] * (rows_around(two[d]) + two[d + 1] + two[d - 1]) for d in NEAR
                }
                grads.append(gu[0] + 0.5 * diff_rows(g_div[0]))
                grads.append(gv[0] + 0.5 * (g_div[1] - g_div[-1]))
            spots = []
            g_sy = g_sx = 0.0
            for n, g in enumerate(grads):
                g_sy = g_sy + g * saved[slot, 4 + n]
                g_sx = g_sx + g * saved[slot, 7 + n]
                lines = []
                for b in range(3):
                    gb = wx[b] * g
                    lines.append(from_below(wy[0] * gb) + wy[1] * gb + from_above(wy[2] * gb))
                spots.append(column(lines[0], 1) + lines[1] + column(lines[2], -1))
            ty, tx = sy * (1.0 / COURANT), sx * (1.0 / COURANT)
            g_u1 = g_sy * (COURANT * (1.0 - ty * ty))
            g_v1 = g_sx * (COURANT * (1.0 - tx * tx))
            if t < steps - 1:
                g_u1, g_v1 = spots[1] + g_u1, spots[2] + g_v1
            l0 = (TIME_STEP * g_u1 + 2.0 * FORCE_WEIGHT * inv_count * f0) * (1.0 - f0 * f0)
            l1 = (TIME_STEP * g_v1 + 2.0 * FORCE_WEIGHT * inv_count * f1) * (1.0 - f1 * f1)
            if t > 0:
                grad_state[0] = spots[0]
                grad_state[1] = g_u1
                grad_state[2] = g_v1
            if sz.slots > 1 and t < steps - 1:
                mid_grad(t + 1, 16)
            glog32[pl.ds(0, grid, stride=16), :] = l0
            glog32[pl.ds(1, grid, stride=16), :] = l1

            def pack(it, carry):
                for k in range(4):
                    i = it * 4 + k
                    glog[slot, i] = glog32[pl.ds(pl.multiple_of(i * 16, 16), 16), :].astype(BF16)
                return carry

            loop(grid // 4, 8, pack, 0)

        @block
        def _():
            def back_a(it, carry):
                sums_d, sums_n = carry
                i = it * 2
                gl = jnp.concatenate([glog[slot, i], glog[slot, i + 1]], axis=1)
                p = dot(head_back[...], gl)
                for k in range(2):
                    g = p[:, k * LANES : (k + 1) * LANES]
                    mixed_grad[i + k] = g
                    d = g * slope[slot, 1, i + k]
                    dy[i + k] = d
                    sums_d = sums_d + d
                    sums_n = sums_n + d * conv[slot, 1, i + k]
                return sums_d, sums_n

            zero = jnp.zeros((width, LANES), F32)
            sums = loop(grid // 2, 16, back_a, (zero, zero))
            norm_back(2, slot, *sums)
        @block
        def _():
            fd, f1_, fn = [back_factors[k] for k in range(3)]

            def back_b(it, carry):
                gl = jnp.concatenate([glog[slot, it * 2 + k] for k in range(2)], axis=1)
                ml = jnp.concatenate([mixed_low[slot, it * 2 + k] for k in range(2)], axis=1)
                d_head[...] += dot_nt(gl, ml)
                for k in range(2):
                    i = it * 2 + k
                    g = fd * dy[i] - f1_ - fn * conv[slot, 1, i]
                    low = g.astype(BF16)
                    for kx, tap in enumerate((from_right(low), low, from_left(low))):
                        g_taps[i + 1, kx * width : (kx + 1) * width] = tap
                return carry

            loop(grid // 2, 16, back_b, 0)

        if t == 0:
            mid_grad(slot, 8)
            early_start()
        elif sz.slots == 1:
            mid_grad(slot, 16)

        @block
        def _():
            def back_c(it, carry):
                sums_d, sums_n = carry
                i = it * 4
                rows = rows_of(dot(w_bwd[...], four_rows(g_taps, i)))
                for k in range(4):
                    d = (rows[k] + mixed_grad[i + k]) * slope[slot, 0, i + k]
                    dy[i + k] = d
                    sums_d = sums_d + d
                    sums_n = sums_n + d * conv[slot, 0, i + k]
                return sums_d, sums_n

            zero = jnp.zeros((width, LANES), F32)
            sums = loop(grid // 4, 8, back_c, (zero, zero))
            norm_back(0, slot, *sums)
        @block
        def _():
            fd, f1_, fn = [back_factors[k] for k in range(3)]

            def back_d(it, carry):
                i = it * 2
                lows = []
                for k in range(2):
                    low = (fd * dy[i + k] - f1_ - fn * conv[slot, 0, i + k]).astype(BF16)
                    g_pad[slot, i + k + 1] = low
                    lows.append(low)
                d_in[...] += dot_nt(row_pair(feat.at[slot], i), jnp.concatenate(lows, axis=1))
                return carry

            loop(grid // 2, 16, back_d, 0)
            if t > 0:

                def back_e(it, carry):
                    i = it * 4
                    rows = rows_of(dot(v_bwd[...], four_rows(g_pad.at[slot], i)))
                    for k in range(4):
                        gs_rows[pl.ds(pl.multiple_of((i + k) * 8, 8), 8), :] = combine(rows[k], 8)
                    return carry

                loop(grid // 4, 8, back_e, 0)
                for q in range(3):
                    grad_state[q] += gs_rows[pl.ds(q, grid, stride=8), :]

    for t in reversed(range(steps)):
        if sz.slots == 1:
            step_forward(t, 0, False)
        step_backward(t, t if sz.slots > 1 else 0)

    core = wrap(c, sz.cores)
    mate = (c + 1 - 2 * core, r)
    mine = pl.ds(core * sz.late, sz.late)

    def chip_peer(k):
        if sz.ways == 1:
            return (c, row_peer(k))
        return (partner(c // 2, k // sz.rows, sz.ch // 2) * 2 + core, row_peer(wrap(k, sz.rows)))

    columns = [jnp.sum(d_norm[k], axis=1, keepdims=True) for k in range(4)]
    columns.append(jnp.zeros((width, LANES - 4), F32))
    lines = jnp.transpose(jnp.concatenate(columns, axis=1))
    loss_sum = jnp.sum(jnp.sum(loss[...], axis=1, keepdims=True), axis=0, keepdims=True)
    pack = late_pair.at[core] if sz.cores > 1 else late_sum
    inputs = jnp.concatenate([d_in[0:24], d_in[24:48]], axis=1)
    for n in range(3):
        pack[n] = inputs[n * 8 : (n + 1) * 8]
    pack[3] = jnp.zeros((8, LANES), F32)
    pack[3, 0:4, 0:width] = lines[0:4, :]
    pack[3, 4:6, 0:width] = d_head[0:2]
    pack[3, 6:7, 0:width] = jnp.broadcast_to(loss_sum, (1, width))
    if sz.cores > 1:
        remote(pack, pack, p_send.at[0], p_recv.at[0], mate).start()
        arrived(pack, p_recv.at[0])
        late_sum[...] = late_pair[0] + late_pair[1]
    for k in far_first(sz.chips):
        remote(late_sum.at[mine], late_in.at[chip_slot], b_send.at[0], b_recv.at[0], chip_peer(k)).start()

    early_sum()

    late_in[chip_slot] = late_sum[mine]
    if sz.chips > 1:
        arrived(but_one(late_in), b_recv.at[0])
    acc = late_in[0]
    for k in range(1, sz.chips):
        acc = acc + late_in[k]
    late_fin[mine] = acc
    if sz.cores > 1:
        remote(late_fin.at[mine], late_fin.at[mine], p_send.at[1], p_recv.at[1], mate).start()
        sent(pack, p_send.at[0])
    early_left()
    if sz.chips > 1:
        sent(but_one(late_in), b_send.at[0])
    if sz.cores > 1:
        arrived(late_fin.at[mine], p_recv.at[1])
    acc = late_fin[...].reshape(32, LANES)
    turned = pltpu.roll(acc, wrap(LANES - c * co, LANES), 1)
    for n in range(4):
        total[sz.early + n] = turned[n * 8 : (n + 1) * 8]
    acc = jnp.where(row_ids(acc.shape) < 30, acc, 0.0)
    late_norm = jnp.sum(acc * acc, axis=0, keepdims=True)

    if sz.early < 8:
        total[sz.early + 4] = jnp.zeros((8, LANES), F32)
    early_end()
    acc = late_norm
    for k in range(sz.ch):
        for j in range(sz.early):
            acc = acc + ssq_early[k, j]
    grad_norm = jnp.sqrt(jnp.broadcast_to(jnp.sum(acc, axis=1, keepdims=True), (8, LANES)))
    factor = CLIP / jnp.maximum(grad_norm, CLIP)

    count = sz.early + 5
    gain_row = row_ids((8, LANES)) < 4
    for k in range(count):
        rate, decay = RATE, DECAY
        if k == sz.early + 3:
            rate = jnp.where(gain_row, GAIN_RATE, RATE)
            decay = jnp.where(gain_row, 0.0, DECAY)
        results = adam(held[0, k], total[k] * factor, held[1, k], held[2, k], rate, decay)
        for n in range(3):
            out[n * count + k] = results[n]
    row = row_ids((8, LANES))
    lost = jnp.broadcast_to(total[sz.early + 3, 6:7, 0:1], (8, LANES))
    out[3 * count] = jnp.where(row == 0, grad_norm, jnp.where(row == 1, lost, valid))
    early_shared()
    if sz.cores > 1:
        sent(late_fin.at[mine], p_send.at[1])


def adam(weight, grad, moment, square, rate, decay):
    moment = BETA_ONE * moment + (1.0 - BETA_ONE) * grad
    square = BETA_TWO * square + (1.0 - BETA_TWO) * grad * grad
    fix_one = 1.0 - BETA_ONE**STEP_NUM
    fix_two = 1.0 - BETA_TWO**STEP_NUM
    updated = weight - rate * (moment / fix_one / (jnp.sqrt(square / fix_two) + ADAM_EPS) + decay * weight)
    return updated, moment, square


def unpack_kernel(sz, packed, *refs):
    co, width = sz.co, sz.width
    count = sz.early + 5
    for n in range(3):
        new_in, new_mid, new_head, new_norm = refs[4 * n : 4 * n + 4]
        at = n * count
        for k in range(4):
            tile = jnp.concatenate([packed[at + h * 4 + k] for h in range(sz.halves)], axis=0)
            first, second = ((0, k), (1, k)) if k < 3 else ((2, 0), (2, 1))
            new_mid[first] = tile[:, :width]
            new_mid[second] = tile[:, width:]
        last = packed[at + sz.early + 4, 0 : co // 2]
        new_mid[2, 2, 0 : co // 2] = last[:, :width]
        new_mid[2, 2, co // 2 :] = last[:, width:]
        for ky in range(TAPS):
            for kx in range(TAPS):
                tile, row, lane = in_place(ky, kx)
                new_in[ky, kx] = packed[at + sz.early + tile, row : row + 4, lane : lane + co]
        new_norm[...] = packed[at + sz.early + 3, 0:4, 0:co]
        new_head[...] = packed[at + sz.early + 3, 4:6, 0:co]
    for k in range(3):
        refs[12 + k][...] = packed[3 * count, k : k + 1, 0:1]


def scratch_of(sz):
    grid, width, rows, ch, slots, steps = sz.grid, sz.width, sz.rows, sz.ch, sz.slots, sz.steps
    wide = TAPS * width

    def f32(*shape):
        return pltpu.VMEM(shape, F32)

    def bf16(*shape):
        return pltpu.VMEM(shape, BF16)

    dma = lambda *shape: pltpu.SemaphoreType.DMA(shape)
    return {
        "f_stage": f32(rows, 3, sz.local, LANES),
        "t_stage": f32(rows, steps, sz.local, LANES),
        "m_stage": pltpu.VMEM((rows, sz.local, LANES), jnp.int32),
        "in_own": f32(3, TAPS, TAPS, 4, sz.co),
        "mid_own": f32(3, TAPS, TAPS, sz.co, width),
        "head_own": f32(3, 2, sz.co),
        "norm_own": f32(3, 4, sz.co),
        "marks_own": pltpu.VMEM((steps, sz.batch), jnp.int32),
        "held": f32(3, sz.early + 5, 8, LANES),
        "total": f32(sz.early + 5, 8, LANES),
        "small": f32(LANES, LANES),
        "ws_all": f32(ch, sz.co, LANES),
        "wm_all": bf16(ch, -(-sz.co // 16) * 16, sz.mid_lanes),
        "w_fwd": bf16(2 * width, 4 * wide),
        "w_bwd": bf16(2 * width, 4 * wide),
        "v_fwd": bf16(width, TAPS * 16),
        "v_bwd": bf16(2 * TAPS * 8, 4 * width),
        "head_back": bf16(width, 16),
        "head": bf16(16, width),
        "gains": f32(4, width, LANES),
        "current": f32(3, 3, grid, LANES),
        "states": f32(1 if slots > 1 else steps, 3, 3, grid, LANES),
        "mask": f32(5, grid, LANES),
        "target": f32(steps, grid, LANES),
        "feat32": f32(grid * 16, LANES),
        "feat": bf16(slots, grid + 2, 16, LANES),
        "conv": f32(slots, 2, grid, width, LANES),
        "slope": f32(slots, 2, grid, width, LANES),
        "norm_stats": f32(4, slots, width, LANES),
        "back_factors": f32(3, width, LANES),
        "hidden": f32(grid, width, LANES),
        "hidden_low": bf16(slots, grid + 2, wide, LANES),
        "mixed_low": bf16(slots, grid, width, LANES),
        "logits": f32(2, grid, LANES),
        "saved": f32(slots, SAVED, grid, LANES),
        "dy": f32(grid, width, LANES),
        "mixed_grad": f32(grid, width, LANES),
        "glog32": f32(grid * 16, LANES),
        "glog": bf16(slots, grid, 16, LANES),
        "g_pad": bf16(slots, grid + 2, width, LANES),
        "g_taps": bf16(grid + 2, wide, LANES),
        "gs_rows": f32(grid * 8, LANES),
        "grad_state": f32(3, grid, LANES),
        "d_mid": f32(wide, wide),
        "d_in": f32(TAPS * 16, width),
        "d_head": f32(16, width),
        "d_norm": f32(4, width, LANES),
        "loss": f32(grid, LANES),
        "early": f32(ch * sz.early, 9, LANES),
        "early_in": f32(sz.owned, sz.sources, 9, LANES),
        "early_fin": f32(sz.early, 9, LANES),
        "blank": f32(ch, rows, 1, LANES),
        "ssq_early": f32(ch, sz.early, 1, LANES),
        "late_pair": f32(2, 4, 8, LANES),
        "late_sum": f32(4, 8, LANES),
        "late_in": f32(sz.chips, sz.late, 8, LANES),
        "late_fin": f32(4, 8, LANES),
        "ready": pltpu.SemaphoreType.REGULAR,
        "local_sem": dma(16),
        "f_sem": dma(2),
        "t_sem": dma(2),
        "m_sem": dma(2),
        "v_sem": dma(2),
        "w_sem": dma(2),
        "e_send": dma(1),
        "e_recv": dma(sz.owned),
        "g_send": dma(sz.owned),
        "g_recv": dma(1),
        "s_send": dma(sz.owned),
        "s_recv": dma(1),
        "b_send": dma(1),
        "b_recv": dma(1),
        "p_send": dma(2),
        "p_recv": dma(2),
    }


def shards(mesh, fields, targets, fluid, keyframes, *rest):
    params, firsts, seconds = rest[0:4], rest[4:8], rest[8:12]

    def native(leaves):
        return (leaves[0], jnp.swapaxes(leaves[1], 2, 3), leaves[2].T, leaves[3])

    params, firsts, seconds = native(params), native(firsts), native(seconds)
    sz = Sizes(mesh, fields.shape, targets.shape, params[0].shape[3])
    marks = keyframes.T
    vmem = pl.BlockSpec(memory_space=pltpu.VMEM)
    hbm = pl.BlockSpec(memory_space=pl.ANY)
    alone = sz.rows == 1 and sz.ch == 1
    packed = pl.pallas_call(
        functools.partial(train_kernel, sz),
        out_shape=pltpu.VMEM((3 * (sz.early + 5) + 1, 8, LANES), F32),
        in_specs=[hbm] * 16,
        out_specs=vmem,
        scratch_shapes=list(scratch_of(sz).values()),
        compiler_params=pltpu.CompilerParams(
            collective_id=None if alone else 0, has_side_effects=True, vmem_limit_bytes=60 << 20
        ),
        name="train",
    )(fields, targets, fluid, marks, *params, *firsts, *seconds)
    shapes = [jax.ShapeDtypeStruct(leaf.shape, F32) for leaf in params] * 3
    shapes += [jax.ShapeDtypeStruct((1, 1), F32)] * 3
    results = pl.pallas_call(
        functools.partial(unpack_kernel, sz),
        out_shape=tuple(shapes),
        in_specs=[vmem],
        out_specs=tuple([vmem] * 15),
        name="unpack",
    )(pltpu.with_memory_space_constraint(packed, pltpu.VMEM))
    outs = []
    for n in range(3):
        outs.extend(native(results[4 * n : 4 * n + 4]))
    return (*outs, *[leaf.reshape(()) for leaf in results[12:]])


def solution(mesh):
    split = (P(None, None, None, "ch"), P(None, None, None, "ch"), P("ch", None), P(None, "ch"))
    return jax.shard_map(
        functools.partial(shards, mesh),
        mesh=mesh,
        in_specs=(
            P(None, None, "rows", None),
            P(None, None, "rows", None),
            P("rows", None),
            P(),
            *split,
            *split,
            *split,
        ),
        out_specs=(*split, *split, *split, P(), P(), P()),
        check_vma=False,
    )
```

```python
import functools

import jax
import jax.numpy as jnp
from jax import lax
from jax.experimental import pallas as pl
from jax.experimental.pallas import tpu as pltpu
from jax.sharding import PartitionSpec as P

GROUPS = 8
NEAR = (-1, 0, 1)
STEP_NUM = 10
TIME_STEP = 0.5
COURANT = 0.8
FORCE_WEIGHT = 0.5
NORM_EPS = 1e-05
CLIP = 0.0001
BETA_ONE = 0.9
BETA_TWO = 0.999
ADAM_EPS = 1e-10
RATE = 0.1
GAIN_RATE = 0.6
DECAY = 0.01

MESH = pl.DeviceIdType.MESH
F32 = jnp.float32
BF16 = jnp.bfloat16
LANES = 128
GSIZE = 8
TAPS = 3
PARTS = (2, 2)
SAVED = 11
NT = (((1,), (1,)), ((), ()))


def lane_ids(shape):
    return lax.broadcasted_iota(jnp.int32, shape, len(shape) - 1)


def row_ids(shape):
    return lax.broadcasted_iota(jnp.int32, shape, 0)


def from_left(x):
    return jnp.where(lane_ids(x.shape) == 0, jnp.zeros_like(x), pltpu.roll(x, 1, 1))


def from_right(x):
    size = x.shape[1]
    return jnp.where(lane_ids(x.shape) == size - 1, jnp.zeros_like(x), pltpu.roll(x, size - 1, 1))


def from_above(x):
    return jnp.where(row_ids(x.shape) == 0, 0.0, pltpu.roll(x, 1, 0))


def from_below(x):
    size = x.shape[0]
    return jnp.where(row_ids(x.shape) == size - 1, 0.0, pltpu.roll(x, size - 1, 0))


def diff_rows(x):
    return from_below(x) - from_above(x)


def column(x, d):
    if d == 0:
        return x
    size = x.shape[1]
    lane = lane_ids(x.shape)
    inside = lane < size - d if d > 0 else lane >= -d
    return jnp.where(inside, pltpu.roll(x, -d % size, 1), jnp.zeros_like(x))


def columns_of(x, reach):
    return {d: column(x, d) for d in range(-reach, reach + 1)}


def rows_around(x):
    return from_below(x) + from_above(x)


def quadratic(s):
    return (0.5 * s * (s + 1.0), 1.0 - s * s, 0.5 * s * (s - 1.0))


def quadratic_slope(s):
    return (s + 0.5, -2.0 * s, s - 0.5)


def wrap(x, n):
    return x & (n - 1) if n & (n - 1) == 0 else lax.rem(x, n)


def partner(x, k, n):
    return x ^ k if n & (n - 1) == 0 else lax.rem(x + k, n)


def far_first(n):
    return reversed(range(1, n))


def dot(a, b):
    return jnp.dot(a, b, preferred_element_type=F32)


def dot_nt(a, b):
    return lax.dot_general(a, b, NT, preferred_element_type=F32)


def row_pair(ref, i, extra=None):
    depth = ref.shape[1] * TAPS
    sides = []
    for k in range(2):
        side = ref[pl.ds(i + k, TAPS)].reshape(depth, LANES)
        if extra is not None:
            side = jnp.concatenate([side, extra[i + k]], axis=0)
        sides.append(side)
    return jnp.concatenate(sides, axis=1)


def side_by_side(ref, first):
    return jnp.concatenate([ref[i] for i in range(first, ref.shape[0])], axis=1)


def four_rows(ref, i):
    taps = ref.shape[1] // 64
    parts = []
    for n in range(taps):
        sides = [ref[pl.ds(i + 2 * k, 4), n * 64 : (n + 1) * 64].reshape(4 * 64, LANES) for k in range(2)]
        parts.append(jnp.concatenate(sides, axis=1))
    return jnp.concatenate(parts, axis=0) if taps > 1 else parts[0]


def rows_of(p):
    half = p.shape[0] // 2
    return [p[o * half : (o + 1) * half, k * LANES : (k + 1) * LANES] for k in range(2) for o in range(2)]


def two_rows(blocks):
    zero = jnp.zeros_like(blocks[0])
    first = jnp.concatenate(list(blocks) + [zero], axis=1)
    second = jnp.concatenate([zero] + list(blocks), axis=1)
    return jnp.concatenate([first, second], axis=0)


def combine(part, height):
    return (
        part[height : 2 * height] + from_left(part[:height]) + from_right(part[2 * height : 3 * height])
    )


def group_sum(x):
    return jnp.sum(jnp.sum(x.reshape(-1, GSIZE, LANES), axis=1), axis=1, keepdims=True)


def spread(x):
    return jnp.broadcast_to(x[:, :, None], (x.shape[0], GSIZE, LANES)).reshape(-1, LANES)


def loop(count, per, body, carry):
    per = min(per, count)

    def several(it, carry):
        for k in range(per):
            carry = body(it * per + k, carry)
        return carry

    if count == per:
        return several(0, carry)
    return lax.fori_loop(0, count // per, several, carry)


def in_place(ky, kx):
    at = ky * 16 + kx * 4
    lane = 64 if at >= 24 else 0
    at = at % 24
    return at // 8, at % 8, lane


class Sizes:
    def __init__(self, mesh, fields_shape, targets_shape, co):
        self.ch = mesh.shape["ch"]
        self.rows = mesh.shape["rows"]
        self.batch = fields_shape[0]
        self.local = fields_shape[2]
        self.grid = self.local * self.rows
        self.cols = fields_shape[3]
        self.steps = targets_shape[0]
        self.co = co
        self.width = co * self.ch
        self.per_rows = self.batch // self.rows
        self.ways = self.ch if self.per_rows == self.ch else 1
        assert self.per_rows == self.ways and self.batch % self.rows == 0
        assert self.cols == LANES
        slot = self.grid * self.width * LANES * 20
        self.slots = self.steps if slot * self.steps < (24 << 20) else 1
        self.halves = co // 8
        self.early = 4 * self.halves
        self.owned = -(-self.early // self.rows)
        self.sources = self.ways * self.rows
        self.cores = 2 if self.ways > 1 else 1
        self.chips = self.sources // self.cores
        self.late = 4 // self.cores
        assert self.ways % self.cores == 0
        self.mid_lanes = TAPS * TAPS * self.width
        assert self.width == 64 and co % 8 == 0


IN_AT = 64
HEAD_AT = IN_AT + 36
NORM_AT = HEAD_AT + 2
LOSS_AT = NORM_AT + 4


def train_kernel(
    sz,
    fields,
    targets,
    fluid,
    keyframes,
    w_in,
    w_mid,
    w_head,
    norms,
    first_in,
    first_mid,
    first_head,
    first_norm,
    second_in,
    second_mid,
    second_head,
    second_norm,
    out,
    *scratch,
):
    z = dict(zip(scratch_of(sz), scratch))
    f_stage = z["f_stage"]
    f_out = z["f_out"]
    m_own = z["m_own"]
    t_stage = z["t_stage"]
    in_own = z["in_own"]
    mid_own = z["mid_own"]
    head_own = z["head_own"]
    norm_own = z["norm_own"]
    marks_own = z["marks_own"]
    held = z["held"]
    total = z["total"]
    small = z["small"]
    ws_all = z["ws_all"]
    wm_all = z["wm_all"]
    w_fwd = z["w_fwd"]
    w_bwd = z["w_bwd"]
    v_fwd = z["v_fwd"]
    v_bwd = z["v_bwd"]
    head_back = z["head_back"]
    head = z["head"]
    gains = z["gains"]
    current = z["current"]
    states = z["states"]
    mask = z["mask"]
    feat32 = z["feat32"]
    feat = z["feat"]
    conv = z["conv"]
    slope = z["slope"]
    norm_stats = z["norm_stats"]
    back_factors = z["back_factors"]
    hidden = z["hidden"]
    hidden_low = z["hidden_low"]
    mixed_low = z["mixed_low"]
    logits = z["logits"]
    saved = z["saved"]
    dy = z["dy"]
    mixed_grad = z["mixed_grad"]
    glog32 = z["glog32"]
    glog = z["glog"]
    g_pad = z["g_pad"]
    g_taps = z["g_taps"]
    gs_rows = z["gs_rows"]
    grad_state = z["grad_state"]
    d_mid = z["d_mid"]
    d_in = z["d_in"]
    d_head = z["d_head"]
    d_norm = z["d_norm"]
    loss = z["loss"]
    early = z["early"]
    early_in = z["early_in"]
    early_fin = z["early_fin"]
    blank = z["blank"]
    ssq_early = z["ssq_early"]
    late_pair = z["late_pair"]
    late_sum = z["late_sum"]
    late_in = z["late_in"]
    late_fin = z["late_fin"]
    ready = z["ready"]
    local_sem = z["local_sem"]
    f_sem = z["f_sem"]
    t_sem = z["t_sem"]
    v_sem = z["v_sem"]
    w_sem = z["w_sem"]
    e_send = z["e_send"]
    e_recv = z["e_recv"]
    g_send = z["g_send"]
    g_recv = z["g_recv"]
    s_send = z["s_send"]
    s_recv = z["s_recv"]
    b_send = z["b_send"]
    b_recv = z["b_recv"]
    p_send = z["p_send"]
    p_recv = z["p_recv"]
    c = lax.axis_index("ch")
    r = lax.axis_index("rows")
    width, grid, steps = sz.width, sz.grid, sz.steps
    co = sz.co

    def row_peer(k):
        return partner(r, k, sz.rows)

    def ch_peer(k):
        return partner(c, k, sz.ch)

    def sample_of(row):
        return row * sz.per_rows + (c if sz.ways > 1 else 0)

    def block(work):
        pl.when(r >= 0)(work)

    peers = sz.rows - 1 + sz.ch - 1
    if peers:
        barrier = pltpu.get_barrier_semaphore()
        for k in far_first(sz.rows):
            pl.semaphore_signal(barrier, inc=1, device_id=(c, row_peer(k)), device_id_type=MESH)
        for k in far_first(sz.ch):
            pl.semaphore_signal(barrier, inc=1, device_id=(ch_peer(k), r), device_id_type=MESH)

    def remote(src, dst, send, recv, where):
        return pltpu.make_async_remote_copy(
            src_ref=src, dst_ref=dst, send_sem=send, recv_sem=recv, device_id=where, device_id_type=MESH
        )

    def arrived(ref, sem):
        remote(ref, ref, sem, sem, (c, r)).wait_recv()

    def sent(ref, sem):
        remote(ref, ref, sem, sem, (c, r)).wait_send()

    def but_one(ref):
        return ref.at[pl.ds(0, ref.shape[0] - 1)]

    own = [
        pltpu.make_async_copy(src, dst, local_sem.at[n])
        for n, (src, dst) in enumerate(
            (
                (w_in, in_own.at[0]),
                (w_head, head_own.at[0]),
                (norms, norm_own.at[0]),
                (w_mid, mid_own.at[0]),
                (fields.at[:, c if sz.ways > 1 else 0], f_out.at[:, pl.ds(0, 3)]),
                (fluid, m_own),
                (targets.at[:, sample_of(r)], t_stage.at[r]),
                (keyframes, marks_own),
                (first_in, in_own.at[1]),
                (first_mid, mid_own.at[1]),
                (first_head, head_own.at[1]),
                (first_norm, norm_own.at[1]),
                (second_in, in_own.at[2]),
                (second_mid, mid_own.at[2]),
                (second_head, head_own.at[2]),
                (second_norm, norm_own.at[2]),
            )
        )
    ]
    for copy in own:
        copy.start()
    own[4].wait()
    own[5].wait()
    for row in range(sz.rows):
        f_out[row, 3] = m_own[...].astype(F32)
    f_stage[r] = f_out[r]
    if peers:
        pl.semaphore_wait(barrier, peers)

    for k in far_first(sz.rows):
        row = row_peer(k)
        remote(f_out.at[row], f_stage.at[r], f_sem.at[0], f_sem.at[1], (c, row)).start()
    small[...] = jnp.zeros_like(small)
    for n in range(4):
        own[n].wait()
    for ky in range(TAPS):
        for kx in range(TAPS):
            at = IN_AT + (ky * TAPS + kx) * 4
            small[at : at + 4, 0:co] = in_own[0, ky, kx]
    small[HEAD_AT : HEAD_AT + 2, 0:co] = head_own[0]
    small[NORM_AT : NORM_AT + 4, 0:co] = norm_own[0]
    ws_all[c] = jnp.transpose(small[...])[0:co]
    packed = jnp.concatenate([mid_own[0, ky, kx] for kx in range(TAPS) for ky in range(TAPS)], axis=1)
    wm_all[c, 0:co, :] = packed.astype(BF16)
    for k in far_first(sz.ch):
        remote(ws_all.at[c], ws_all.at[c], v_sem.at[0], v_sem.at[1], (ch_peer(k), r)).start()
    for k in far_first(sz.ch):
        remote(wm_all.at[c], wm_all.at[c], w_sem.at[0], w_sem.at[1], (ch_peer(k), r)).start()
    for k in far_first(sz.rows):
        src = targets.at[:, sample_of(row_peer(k))]
        remote(src, t_stage.at[r], t_sem.at[0], t_sem.at[1], (c, row_peer(k))).start()
    row_groups = ((f_stage, f_sem), (t_stage, t_sem)) if sz.rows > 1 else ()
    ch_groups = ((ws_all, v_sem), (wm_all, w_sem)) if sz.ch > 1 else ()
    if peers:
        for k in far_first(sz.ch):
            pl.semaphore_signal(ready, inc=1, device_id=(ch_peer(k), r), device_id_type=MESH)

    for n in range(8, 16):
        own[n].wait()
    for n in range(3):
        mid = [[mid_own[n, ky, kx] for kx in range(TAPS)] for ky in range(TAPS)]
        sides = [(mid[0][kx], mid[1][kx]) for kx in range(TAPS)] + [(mid[2][0], mid[2][1])]
        for k, side in enumerate(sides):
            tile = jnp.concatenate(side, axis=1)
            for h in range(sz.halves):
                held[n, h * 4 + k] = tile[h * 8 : (h + 1) * 8]
        for k in range(sz.early, sz.early + 5):
            held[n, k] = jnp.zeros((8, LANES), F32)
        for ky in range(TAPS):
            for kx in range(TAPS):
                tile, row, lane = in_place(ky, kx)
                held[n, sz.early + tile, row : row + 4, lane : lane + co] = in_own[n, ky, kx]
        held[n, sz.early + 3, 0:4, 0:co] = norm_own[n]
        held[n, sz.early + 3, 4:6, 0:co] = head_own[n]
        last = mid[2][2]
        held[n, sz.early + 4, 0 : co // 2] = jnp.concatenate([last[: co // 2], last[co // 2 :]], axis=1)

    for i in (0, grid + 1):
        g_taps[i] = jnp.zeros_like(g_taps[i])
    for ref in (feat, hidden_low, g_pad):
        for slot in range(sz.slots):
            ref[slot, 0] = jnp.zeros_like(ref[slot, 0])
            ref[slot, grid + 1] = jnp.zeros_like(ref[slot, 0])
    feat32[...] = jnp.zeros_like(feat32)
    glog32[...] = jnp.zeros_like(glog32)
    for ref in (d_mid, d_in, d_head, d_norm, loss):
        ref[...] = jnp.zeros_like(ref)

    if ch_groups:
        arrived(but_one(ws_all), v_sem.at[1])
    tail = ws_all[...].reshape(width, LANES)
    tail_t = jnp.transpose(tail)
    parts = []
    for ky in range(TAPS):
        at = IN_AT + ky * 12
        parts.append(jnp.concatenate([tail[:, at : at + 12], jnp.zeros((width, 4), F32)], axis=1))
    v_fwd[...] = jnp.concatenate(parts, axis=1).astype(BF16)
    pieces = []
    for ky in range(TAPS):
        column_taps = []
        for kx in range(TAPS):
            at = IN_AT + ((2 - ky) * TAPS + 2 - kx) * 4
            column_taps += [tail_t[at : at + 4], jnp.zeros((4, width), F32)]
        pieces.append(jnp.concatenate(column_taps, axis=0))
    v_bwd[...] = two_rows(pieces).astype(BF16)
    head_back[...] = jnp.concatenate([tail[:, HEAD_AT : HEAD_AT + 2], jnp.zeros((width, 14), F32)], axis=1).astype(BF16)
    head[...] = jnp.concatenate([tail_t[HEAD_AT : HEAD_AT + 2], jnp.zeros((14, width), F32)], axis=0).astype(BF16)
    for k in range(4):
        gains[k] = jnp.broadcast_to(tail[:, NORM_AT + k : NORM_AT + k + 1], (width, LANES))

    for ref, sem in row_groups[:1]:
        arrived(but_one(ref), sem.at[1])
    for q in range(3):
        current[q, 1] = jnp.concatenate([f_stage[row, q] for row in range(sz.rows)], axis=0)
    mask[2] = jnp.concatenate([f_stage[row, 3] for row in range(sz.rows)], axis=0)
    for q in range(3):
        for d in (-1, 1):
            current[q, d + 1] = column(current[q, 1], d)
    for d in (-2, -1, 1, 2):
        mask[d + 2] = column(mask[2], d)
    for d in NEAR:
        feat32[pl.ds((d + 1) * 4 + 3, grid, stride=16), :] = mask[d + 2]

    def second_layer():
        if ch_groups:
            arrived(but_one(wm_all), w_sem.at[1])
        kind = BF16 if co % 16 == 0 else F32
        mid = jnp.concatenate([wm_all[k, 0:co, :].astype(kind) for k in range(sz.ch)], axis=0)
        for kx in range(TAPS):
            at = [(kx * TAPS + ky) * width for ky in range(TAPS)]
            w_fwd[:, kx * 4 * width : (kx + 1) * 4 * width] = two_rows([mid[:, a : a + width] for a in at]).astype(BF16)

    def second_layer_back():
        for kx in range(TAPS):
            at = kx * 4 * width
            blocks = [w_fwd[0:width, at + ky * width : at + (ky + 1) * width].astype(F32) for ky in range(TAPS)]
            w_bwd[:, at : at + 4 * width] = two_rows([jnp.transpose(b) for b in reversed(blocks)]).astype(BF16)

    def all_targets():
        if row_groups:
            arrived(but_one(t_stage), t_sem.at[1])
        own[6].wait()
    own[7].wait()
    marks = marks_own[...].astype(F32)
    valid = jnp.sum(jnp.sum(marks, axis=1, keepdims=True), axis=0, keepdims=True) * float(grid * sz.cols)
    inv_count = 1.0 / valid
    picked = jnp.where(lane_ids(marks.shape) == sample_of(r), marks, 0.0)
    marked = jnp.sum(picked, axis=1, keepdims=True)

    def key_of(t):
        return jnp.sum(jnp.where(row_ids(marked.shape) == t, marked, 0.0), axis=0, keepdims=True)

    def parts_of(count):
        size = width // count
        return [slice(n * size, (n + 1) * size) for n in range(count)]

    def conv_and_stats(x_ref, w, layer, slot, span=slice(0, 64)):
        zero = jnp.zeros((span.stop - span.start, LANES), F32)

        def body(it, carry):
            base, total, squares = carry
            i = it * 4
            if layer:
                rows = rows_of(dot(w[...], four_rows(x_ref, i)))
            else:
                rows = []
                for k in range(2):
                    p = dot(w[span], row_pair(x_ref, i + 2 * k))
                    rows += [p[:, :LANES], p[:, LANES:]]
            base = jnp.where(it == 0, rows[0], base)
            for j in range(4):
                conv[slot, layer, i + j, span] = rows[j]
                d = rows[j] - base
                total = total + d
                squares = squares + d * d
            return base, total, squares

        base, total, squares = loop(grid // 4, 8, body, (zero, zero, zero))
        lane_mean = base + total * (1.0 / grid)
        lane_dev = squares - total * total * (1.0 / grid)
        count = float(GSIZE * LANES)
        middle = spread(group_sum(base) * (1.0 / count))
        d = lane_mean - middle
        first = spread(group_sum(d) * (1.0 / count))
        second = spread(group_sum(lane_dev + grid * d * d) * (1.0 / (count * grid)))
        norm_stats[2 * layer, slot, span] = middle + first
        norm_stats[2 * layer + 1, slot, span] = lax.rsqrt(second - first * first + NORM_EPS)

    def silu_parts(half):
        t = jnp.tanh(half)
        a = 1.0 + t
        h = half * a
        return h, a + h * (1.0 - t)

    def half_affine(layer, slot, span=slice(0, 64)):
        k = 2 * layer
        mean, inv = norm_stats[k, slot, span], norm_stats[k + 1, slot, span]
        scale = 0.5 * inv * gains[k, span]
        return scale, 0.5 * gains[k + 1, span] - mean * scale

    def step_forward(t, slot, first):
        last = t == steps - 1
        if sz.slots == 1:
            for q in range(3):
                for d in NEAR:
                    if first:
                        states[t, q, d + 1] = current[q, d + 1]
                    else:
                        current[q, d + 1] = states[t, q, d + 1]
        @block
        def _():
            x = [{d: current[q, d + 1] for d in NEAR} for q in range(3)]
            for q in range(3):
                for d in NEAR:
                    feat32[pl.ds((d + 1) * 4 + q, grid, stride=16), :] = x[q][d]

            def pack(it, carry):
                for k in range(4):
                    i = it * 4 + k
                    feat[slot, i + 1] = feat32[pl.ds(pl.multiple_of(i * 16, 16), 16), :].astype(BF16)
                return carry

            loop(grid // 4, 8, pack, 0)

            for span in parts_of(PARTS[0]):
                conv_and_stats(feat.at[slot], v_fwd, 0, slot, span)
        if first and t == 0:
            second_layer()

        @block
        def _():
            def norm_one(span, it, carry):
                for k in range(2):
                    i = it * 2 + k
                    h, slope[slot, 0, i, span] = silu_parts(conv[slot, 0, i, span] * mul + add)
                    hidden[i, span] = h
                    low = h.astype(BF16)
                    for kx, tap in enumerate((from_left(low), low, from_right(low))):
                        hidden_low[slot, i + 1, kx * width + span.start : kx * width + span.stop] = tap
                return carry

            for span in parts_of(PARTS[0]):
                mul, add = half_affine(0, slot, span)
                loop(grid // 2, 16, functools.partial(norm_one, span), 0)

            conv_and_stats(hidden_low.at[slot], w_fwd, 1, slot)
        @block
        def _():
            if first and t == min(1, steps - 1):
                second_layer_back()
            mul, add = half_affine(1, slot)

            def norm_two(it, carry):
                i = it * 2
                lows = []
                for k in range(2):
                    h, slope[slot, 1, i + k] = silu_parts(conv[slot, 1, i + k] * mul + add)
                    low = (hidden[i + k] + h).astype(BF16)
                    mixed_low[slot, i + k] = low
                    lows.append(low)
                p = dot(head[...], jnp.concatenate(lows, axis=1))
                for k in range(2):
                    logits[0, pl.ds(i + k, 1), :] = p[0:1, k * LANES : (k + 1) * LANES]
                    logits[1, pl.ds(i + k, 1), :] = p[1:2, k * LANES : (k + 1) * LANES]
                return carry

            loop(grid // 2, 16, norm_two, 0)

        if first and t == 0:
            all_targets()
        @block
        def _():
            x = [{d: current[q, d + 1] for d in NEAR} for q in range(3)]
            f0, f1 = jnp.tanh(logits[0]), jnp.tanh(logits[1])
            force0, force1 = columns_of(f0, 1), columns_of(f1, 1)
            u1 = {d: x[1][d] + TIME_STEP * force0[d] for d in NEAR}
            v1 = {d: x[2][d] + TIME_STEP * force1[d] for d in NEAR}
            sy = COURANT * jnp.tanh(u1[0])
            sx = COURANT * jnp.tanh(v1[0])
            wy, wx = quadratic(sy), quadratic(sx)
            dwy, dwx = quadratic_slope(sy), quadratic_slope(sx)
            moved = []
            for n, q in enumerate((x[0], u1, v1)):
                lines = [(from_above(q[d]), q[d], from_below(q[d])) for d in NEAR]
                along = [wx[0] * lines[0][a] + wx[1] * lines[1][a] + wx[2] * lines[2][a] for a in range(3)]
                moved.append(wy[0] * along[0] + wy[1] * along[1] + wy[2] * along[2])
                if last and n:
                    continue
                slant = [dwx[0] * lines[0][a] + dwx[1] * lines[1][a] + dwx[2] * lines[2][a] for a in range(3)]
                saved[slot, 4 + n] = dwy[0] * along[0] + dwy[1] * along[1] + dwy[2] * along[2]
                saved[slot, 7 + n] = wy[0] * slant[0] + wy[1] * slant[1] + wy[2] * slant[2]
            rho2 = moved[0]
            if first and not last:
                solid = {d: mask[d + 2] for d in range(-2, 3)}
                rho2s, u2, v2 = columns_of(rho2, 1), columns_of(moved[1], 1), columns_of(moved[2], 2)
                div = {d: 0.5 * (diff_rows(u2[d]) + (v2[d + 1] - v2[d - 1])) for d in NEAR}
                press = {d: -0.25 * solid[d] * div[d] for d in NEAR}
                press = 0.25 * solid[0] * (rows_around(press[0]) + press[1] + press[-1] - div[0])
                press = columns_of(press, 3)
                div[2], div[-2] = column(div[0], 2), column(div[0], -2)
                press = {
                    d: 0.25 * solid[d] * (rows_around(press[d]) + press[d + 1] + press[d - 1] - div[d])
                    for d in range(-2, 3)
                }
                for d in NEAR:
                    current[0, d + 1] = rho2s[d]
                    current[1, d + 1] = solid[d] * (u2[d] - 0.5 * diff_rows(press[d]))
                    current[2, d + 1] = solid[d] * (v2[d] - 0.5 * (press[d + 1] - press[d - 1]))
            miss = rho2 - jnp.concatenate([t_stage[row, t] for row in range(sz.rows)], axis=0)
            pull = key_of(t) * miss
            if first:
                loss[...] += FORCE_WEIGHT * (f0 * f0 + f1 * f1) + pull * miss
            saved[slot, 0] = f0
            saved[slot, 1] = f1
            saved[slot, 2] = sy
            saved[slot, 3] = sx
            saved[slot, 10] = pull

    for t in range(steps):
        step_forward(t, t if sz.slots > 1 else 0, True)
    for ref, sem in row_groups + ch_groups:
        sent(but_one(ref), sem.at[0])

    def owner_of(j):
        return wrap(j, sz.rows)

    me = c * sz.rows + r if sz.ways > 1 else r
    chip_slot = (c // 2) * sz.rows + r if sz.ways > 1 else r

    def by_owned(action):
        least, more = sz.early // sz.rows, sz.early % sz.rows
        if more:
            pl.when(r < more)(functools.partial(action, least + 1))
            pl.when(r >= more)(functools.partial(action, least))
        else:
            action(least)

    def for_owned(action):
        for m in range(sz.owned):
            j = r + m * sz.rows
            if (m + 1) * sz.rows <= sz.early:
                action(m, j)
            else:
                pl.when(j < sz.early)(functools.partial(action, m, j))

    def early_start():
        low_half = lane_ids((width, LANES)) < 64
        tiles = [d_mid[kx * width : (kx + 1) * width, 0:LANES] for kx in range(TAPS)]
        rest = [d_mid[kx * width : (kx + 1) * width, LANES:] for kx in range(2)]
        tiles.append(jnp.concatenate(rest, axis=1))
        last = d_mid[2 * width : 3 * width, LANES:]
        for shard in range(sz.ch):
            for h in range(sz.halves):
                at = shard * co + h * 8
                for n, tile in enumerate(tiles):
                    early[shard * sz.early + h * 4 + n, 0:8] = tile[at : at + 8]
            ends = last[shard * co : (shard + 1) * co]
            ends = jnp.concatenate([ends[: co // 2], ends[co // 2 :]], axis=1)
            for j in range(sz.early):
                early[shard * sz.early + j, 8:9] = ends[j : j + 1]
        if sz.ch > 1:
            pl.semaphore_wait(ready, sz.ch - 1)
        for dc in reversed(range(sz.ways)):
            shard = ch_peer(dc)
            for k in reversed(range(sz.early)):
                j = partner(r, k, sz.early) if sz.early == sz.rows else wrap(r + k, sz.early)
                slot = j // sz.rows if sz.owned > 1 else 0
                if dc == 0 and k == 0 and sz.early == sz.rows:
                    continue
                copy = remote(
                    early.at[shard * sz.early + j],
                    early_in.at[slot, me],
                    e_send.at[0],
                    e_recv.at[slot],
                    (shard, owner_of(j)),
                )
                if dc or sz.early == sz.rows:
                    copy.start()
                else:
                    pl.when(owner_of(j) != r)(copy.start)

    def early_sum():
        def total(m, j):
            early_in[m, me] = early[c * sz.early + j]
            if sz.sources > 1:
                arrived(but_one(early_in.at[m]), e_recv.at[m])
            acc = early_in[m, 0]
            for k in range(1, sz.sources):
                acc = acc + early_in[m, k]
            early_fin[j] = acc
            line = ssq_early.at[c, j]
            line[...] = jnp.sum(acc * acc, axis=0, keepdims=True)
            for dc in far_first(sz.ch):
                for k in reversed(range(sz.rows)):
                    remote(line, line, s_send.at[m], s_recv.at[0], (ch_peer(dc), row_peer(k))).start()
            for k in far_first(sz.rows):
                remote(early_fin.at[j], early_fin.at[j], g_send.at[m], g_recv.at[0], (c, row_peer(k))).start()

        for_owned(total)

    def early_left():
        if sz.sources > 1:
            by_owned(lambda n: sent(early.at[pl.ds(0, sz.ways * sz.early - n)], e_send.at[0]))

    def put_line(j, acc):
        ssq_early[c, j] = jnp.sum(acc * acc, axis=0, keepdims=True)

    def early_end():
        if sz.rows > 1:
            by_owned(lambda n: arrived(early_fin.at[pl.ds(0, sz.early - n)], g_recv.at[0]))
        for j in range(sz.early):
            acc = early_fin[j]
            total[j] = acc[0:8]
            total[sz.early + 4, j : j + 1] = acc[8:9]
            if sz.rows > 1:
                pl.when(r != j % sz.rows)(functools.partial(put_line, j, acc))
        if sz.ch > 1:
            arrived(but_one(ssq_early), s_recv.at[0])

    def early_shared():
        def last(m, j):
            if sz.ch > 1:
                sent(but_one(blank), s_send.at[m])
            if sz.rows > 1:
                sent(but_one(early_in.at[m, pl.ds(0, sz.rows)]), g_send.at[m])

        for_owned(last)

    def norm_back(k, slot, sums_d, sums_c, span=slice(0, 64)):
        gain, mean, inv = gains[k, span], norm_stats[k, slot, span], norm_stats[k + 1, slot, span]
        sums_d = 0.5 * sums_d
        sums_n = inv * (0.5 * sums_c - mean * sums_d)
        scale = 1.0 / float(GSIZE * LANES * grid)
        m1 = spread(group_sum(sums_d * gain) * scale)
        m2 = spread(group_sum(sums_n * gain) * scale)
        d_norm[k, span] += sums_n
        d_norm[k + 1, span] += sums_d
        fc = inv * inv * m2
        back_factors[0, span] = 0.5 * inv * gain
        back_factors[1, span] = inv * m1 - fc * mean
        back_factors[2, span] = fc

    def mid_grad(slot, part, parts):
        span = grid // parts
        rows = range(part * span, (part + 1) * span)
        center = slice(width, 2 * width)
        left = [g_taps[i + 1] for i in rows]
        right = [hidden_low[slot, i : i + TAPS, center].reshape(TAPS * width, LANES) for i in rows]
        d_mid[...] += dot_nt(jnp.concatenate(left, axis=1), jnp.concatenate(right, axis=1))

    core = wrap(c, sz.cores)
    pack = late_pair.at[core] if sz.cores > 1 else late_sum

    def late_misc():
        columns = [jnp.sum(d_norm[k], axis=1, keepdims=True) for k in range(4)]
        columns.append(jnp.zeros((width, LANES - 4), F32))
        lines = jnp.transpose(jnp.concatenate(columns, axis=1))
        loss_sum = jnp.sum(jnp.sum(loss[...], axis=1, keepdims=True), axis=0, keepdims=True)
        pack[3] = jnp.zeros((8, LANES), F32)
        pack[3, 0:4, 0:width] = lines[0:4, :]
        pack[3, 4:6, 0:width] = d_head[0:2]
        pack[3, 6:7, 0:width] = jnp.broadcast_to(loss_sum, (1, width))

    def step_backward(t, slot):
        @block
        def _():
            sy, sx = saved[slot, 2], saved[slot, 3]
            f0, f1 = saved[slot, 0], saved[slot, 1]
            wy, wx = quadratic(sy), quadratic(sx)
            grads = [2.0 * inv_count * saved[slot, 10]]
            if t < steps - 1:
                solid = {d: mask[d + 2] for d in NEAR}
                grads[0] = grads[0] + grad_state[0]
                gu, gv = columns_of(solid[0] * grad_state[1], 1), columns_of(solid[0] * grad_state[2], 2)
                one = {d: 0.125 * solid[d] * (diff_rows(gu[d]) + (gv[d + 1] - gv[d - 1])) for d in NEAR}
                two = 0.25 * solid[0] * (rows_around(one[0]) + one[1] + one[-1])
                two = columns_of(two, 2)
                g_div = {
                    d: one[d] + two[d] + 0.25 * solid[d] * (rows_around(two[d]) + two[d + 1] + two[d - 1]) for d in NEAR
                }
                grads.append(gu[0] + 0.5 * diff_rows(g_div[0]))
                grads.append(gv[0] + 0.5 * (g_div[1] - g_div[-1]))
            spots = []
            g_sy = g_sx = 0.0
            for n, g in enumerate(grads):
                g_sy = g_sy + g * saved[slot, 4 + n]
                g_sx = g_sx + g * saved[slot, 7 + n]
                lines = []
                for b in range(3):
                    gb = wx[b] * g
                    lines.append(from_below(wy[0] * gb) + wy[1] * gb + from_above(wy[2] * gb))
                spots.append(column(lines[0], 1) + lines[1] + column(lines[2], -1))
            ty, tx = sy * (1.0 / COURANT), sx * (1.0 / COURANT)
            g_u1 = g_sy * (COURANT * (1.0 - ty * ty))
            g_v1 = g_sx * (COURANT * (1.0 - tx * tx))
            if t < steps - 1:
                g_u1, g_v1 = spots[1] + g_u1, spots[2] + g_v1
            l0 = (TIME_STEP * g_u1 + 2.0 * FORCE_WEIGHT * inv_count * f0) * (1.0 - f0 * f0)
            l1 = (TIME_STEP * g_v1 + 2.0 * FORCE_WEIGHT * inv_count * f1) * (1.0 - f1 * f1)
            if t > 0:
                grad_state[0] = spots[0]
                grad_state[1] = g_u1
                grad_state[2] = g_v1
            if sz.slots > 1 and t < steps - 1:
                for part in range(2):
                    mid_grad(t + 1, part, 2)
            glog32[pl.ds(0, grid, stride=16), :] = l0
            glog32[pl.ds(1, grid, stride=16), :] = l1

            def pack(it, carry):
                for k in range(4):
                    i = it * 4 + k
                    glog[slot, i] = glog32[pl.ds(pl.multiple_of(i * 16, 16), 16), :].astype(BF16)
                return carry

            loop(grid // 4, 8, pack, 0)

        @block
        def _():
            def back_a(span, it, carry):
                sums_d, sums_n = carry
                i = it * 2
                gl = jnp.concatenate([glog[slot, i], glog[slot, i + 1]], axis=1)
                p = dot(head_back[span], gl)
                for k in range(2):
                    g = p[:, k * LANES : (k + 1) * LANES]
                    mixed_grad[i + k, span] = g
                    d = g * slope[slot, 1, i + k, span]
                    dy[i + k, span] = d
                    sums_d = sums_d + d
                    sums_n = sums_n + d * conv[slot, 1, i + k, span]
                return sums_d, sums_n

            for span in parts_of(PARTS[1]):
                zero = jnp.zeros((span.stop - span.start, LANES), F32)
                sums = loop(grid // 2, 16, functools.partial(back_a, span), (zero, zero))
                norm_back(2, slot, *sums, span)

        @block
        def _():
            def back_b(span, it, carry):
                if span.start == 0:
                    gl = jnp.concatenate([glog[slot, it * 2 + k] for k in range(2)], axis=1)
                    ml = jnp.concatenate([mixed_low[slot, it * 2 + k] for k in range(2)], axis=1)
                    d_head[...] += dot_nt(gl, ml)
                for k in range(2):
                    i = it * 2 + k
                    g = fd * dy[i, span] - f1_ - fn * conv[slot, 1, i, span]
                    low = g.astype(BF16)
                    for kx, tap in enumerate((from_right(low), low, from_left(low))):
                        g_taps[i + 1, kx * width + span.start : kx * width + span.stop] = tap
                return carry

            spans = parts_of(PARTS[1])
            for span in spans:
                fd, f1_, fn = [back_factors[k, span] for k in range(3)]
                if t > 0 or span is not spans[-1]:
                    loop(grid // 2, 16, functools.partial(back_b, span), 0)
                    continue
                parts = 4
                for k in range(grid // 2):
                    back_b(span, k, 0)
                    if (k + 1) % (grid // 2 // parts) == 0:
                        mid_grad(slot, k // (grid // 2 // parts), parts)

        if t == 0:
            early_start()
        elif sz.slots == 1:
            for part in range(8):
                mid_grad(slot, part, 8)

        @block
        def _():
            def back_c(it, carry):
                sums_d, sums_n = carry
                i = it * 4
                rows = rows_of(dot(w_bwd[...], four_rows(g_taps, i)))
                for k in range(4):
                    d = (rows[k] + mixed_grad[i + k]) * slope[slot, 0, i + k]
                    dy[i + k] = d
                    sums_d = sums_d + d
                    sums_n = sums_n + d * conv[slot, 0, i + k]
                return sums_d, sums_n

            zero = jnp.zeros((width, LANES), F32)
            sums = loop(grid // 4, 8, back_c, (zero, zero))
            norm_back(0, slot, *sums)
        @block
        def _():
            fd, f1_, fn = [back_factors[k] for k in range(3)]

            if t == 0:
                late_misc()

            def back_d(it, carry):
                i = it * 2
                lows = []
                for k in range(2):
                    low = (fd * dy[i + k] - f1_ - fn * conv[slot, 0, i + k]).astype(BF16)
                    g_pad[slot, i + k + 1] = low
                    lows.append(low)
                d_in[...] += dot_nt(row_pair(feat.at[slot], i), jnp.concatenate(lows, axis=1))
                return carry

            loop(grid // 2, 16, back_d, 0)
            if t > 0:

                def back_e(it, carry):
                    i = it * 4
                    rows = rows_of(dot(v_bwd[...], four_rows(g_pad.at[slot], i)))
                    for k in range(4):
                        gs_rows[pl.ds(pl.multiple_of((i + k) * 8, 8), 8), :] = combine(rows[k], 8)
                    return carry

                loop(grid // 4, 8, back_e, 0)
                for q in range(3):
                    grad_state[q] += gs_rows[pl.ds(q, grid, stride=8), :]

    for t in reversed(range(steps)):
        if sz.slots == 1:
            step_forward(t, 0, False)
        step_backward(t, t if sz.slots > 1 else 0)

    mate = (c + 1 - 2 * core, r)
    mine = pl.ds(core * sz.late, sz.late)

    def chip_peer(k):
        if sz.ways == 1:
            return (c, row_peer(k))
        return (partner(c // 2, k // sz.rows, sz.ch // 2) * 2 + core, row_peer(wrap(k, sz.rows)))

    inputs = jnp.concatenate([d_in[0:24], d_in[24:48]], axis=1)
    for n in range(3):
        pack[n] = inputs[n * 8 : (n + 1) * 8]
    if sz.cores > 1:
        remote(pack, pack, p_send.at[0], p_recv.at[0], mate).start()
        arrived(pack, p_recv.at[0])
        late_sum[...] = late_pair[0] + late_pair[1]
    for k in far_first(sz.chips):
        remote(late_sum.at[mine], late_in.at[chip_slot], b_send.at[0], b_recv.at[0], chip_peer(k)).start()

    early_sum()

    late_in[chip_slot] = late_sum[mine]
    if sz.chips > 1:
        arrived(but_one(late_in), b_recv.at[0])
    acc = late_in[0]
    for k in range(1, sz.chips):
        acc = acc + late_in[k]
    late_fin[mine] = acc
    if sz.cores > 1:
        remote(late_fin.at[mine], late_fin.at[mine], p_send.at[1], p_recv.at[1], mate).start()
        sent(pack, p_send.at[0])
    early_left()
    if sz.chips > 1:
        sent(but_one(late_in), b_send.at[0])
    if sz.cores > 1:
        arrived(late_fin.at[mine], p_recv.at[1])
    acc = late_fin[...].reshape(32, LANES)
    turned = pltpu.roll(acc, wrap(LANES - c * co, LANES), 1)
    for n in range(4):
        total[sz.early + n] = turned[n * 8 : (n + 1) * 8]
    acc = jnp.where(row_ids(acc.shape) < 30, acc, 0.0)
    late_norm = jnp.sum(acc * acc, axis=0, keepdims=True)

    if sz.early < 8:
        total[sz.early + 4] = jnp.zeros((8, LANES), F32)
    early_end()
    acc = late_norm
    for k in range(sz.ch):
        for j in range(sz.early):
            acc = acc + ssq_early[k, j]
    grad_norm = jnp.sqrt(jnp.broadcast_to(jnp.sum(acc, axis=1, keepdims=True), (8, LANES)))
    factor = CLIP / jnp.maximum(grad_norm, CLIP)

    count = sz.early + 5
    gain_row = row_ids((8, LANES)) < 4
    for k in range(count):
        rate, decay = RATE, DECAY
        if k == sz.early + 3:
            rate = jnp.where(gain_row, GAIN_RATE, RATE)
            decay = jnp.where(gain_row, 0.0, DECAY)
        results = adam(held[0, k], total[k] * factor, held[1, k], held[2, k], rate, decay)
        for n in range(3):
            out[n * count + k] = results[n]
    row = row_ids((8, LANES))
    lost = jnp.broadcast_to(total[sz.early + 3, 6:7, 0:1], (8, LANES))
    out[3 * count] = jnp.where(row == 0, grad_norm, jnp.where(row == 1, lost, valid))
    early_shared()
    if sz.cores > 1:
        sent(late_fin.at[mine], p_send.at[1])


def adam(weight, grad, moment, square, rate, decay):
    moment = BETA_ONE * moment + (1.0 - BETA_ONE) * grad
    square = BETA_TWO * square + (1.0 - BETA_TWO) * grad * grad
    fix_one = 1.0 - BETA_ONE**STEP_NUM
    fix_two = 1.0 - BETA_TWO**STEP_NUM
    updated = weight - rate * (moment / fix_one / (jnp.sqrt(square / fix_two) + ADAM_EPS) + decay * weight)
    return updated, moment, square


def unpack_kernel(sz, packed, *refs):
    co, width = sz.co, sz.width
    count = sz.early + 5
    for n in range(3):
        new_in, new_mid, new_head, new_norm = refs[4 * n : 4 * n + 4]
        at = n * count
        for k in range(4):
            tile = jnp.concatenate([packed[at + h * 4 + k] for h in range(sz.halves)], axis=0)
            first, second = ((0, k), (1, k)) if k < 3 else ((2, 0), (2, 1))
            new_mid[first] = tile[:, :width]
            new_mid[second] = tile[:, width:]
        last = packed[at + sz.early + 4, 0 : co // 2]
        new_mid[2, 2, 0 : co // 2] = last[:, :width]
        new_mid[2, 2, co // 2 :] = last[:, width:]
        for ky in range(TAPS):
            for kx in range(TAPS):
                tile, row, lane = in_place(ky, kx)
                new_in[ky, kx] = packed[at + sz.early + tile, row : row + 4, lane : lane + co]
        new_norm[...] = packed[at + sz.early + 3, 0:4, 0:co]
        new_head[...] = packed[at + sz.early + 3, 4:6, 0:co]
    for k in range(3):
        refs[12 + k][...] = packed[3 * count, k : k + 1, 0:1]


def scratch_of(sz):
    grid, width, rows, ch, slots, steps = sz.grid, sz.width, sz.rows, sz.ch, sz.slots, sz.steps
    wide = TAPS * width

    def f32(*shape):
        return pltpu.VMEM(shape, F32)

    def bf16(*shape):
        return pltpu.VMEM(shape, BF16)

    dma = lambda *shape: pltpu.SemaphoreType.DMA(shape)
    return {
        "f_stage": f32(rows, 4, sz.local, LANES),
        "f_out": f32(rows, 4, sz.local, LANES),
        "m_own": pltpu.VMEM((sz.local, LANES), jnp.int32),
        "t_stage": f32(rows, steps, sz.local, LANES),
        "in_own": f32(3, TAPS, TAPS, 4, sz.co),
        "mid_own": f32(3, TAPS, TAPS, sz.co, width),
        "head_own": f32(3, 2, sz.co),
        "norm_own": f32(3, 4, sz.co),
        "marks_own": pltpu.VMEM((steps, sz.batch), jnp.int32),
        "held": f32(3, sz.early + 5, 8, LANES),
        "total": f32(sz.early + 5, 8, LANES),
        "small": f32(LANES, LANES),
        "ws_all": f32(ch, sz.co, LANES),
        "wm_all": bf16(ch, -(-sz.co // 16) * 16, sz.mid_lanes),
        "w_fwd": bf16(2 * width, 4 * wide),
        "w_bwd": bf16(2 * width, 4 * wide),
        "v_fwd": bf16(width, TAPS * 16),
        "v_bwd": bf16(2 * TAPS * 8, 4 * width),
        "head_back": bf16(width, 16),
        "head": bf16(16, width),
        "gains": f32(4, width, LANES),
        "current": f32(3, 3, grid, LANES),
        "states": f32(1 if slots > 1 else steps, 3, 3, grid, LANES),
        "mask": f32(5, grid, LANES),
        "feat32": f32(grid * 16, LANES),
        "feat": bf16(slots, grid + 2, 16, LANES),
        "conv": f32(slots, 2, grid, width, LANES),
        "slope": f32(slots, 2, grid, width, LANES),
        "norm_stats": f32(4, slots, width, LANES),
        "back_factors": f32(3, width, LANES),
        "hidden": f32(grid, width, LANES),
        "hidden_low": bf16(slots, grid + 2, wide, LANES),
        "mixed_low": bf16(slots, grid, width, LANES),
        "logits": f32(2, grid, LANES),
        "saved": f32(slots, SAVED, grid, LANES),
        "dy": f32(grid, width, LANES),
        "mixed_grad": f32(grid, width, LANES),
        "glog32": f32(grid * 16, LANES),
        "glog": bf16(slots, grid, 16, LANES),
        "g_pad": bf16(slots, grid + 2, width, LANES),
        "g_taps": bf16(grid + 2, wide, LANES),
        "gs_rows": f32(grid * 8, LANES),
        "grad_state": f32(3, grid, LANES),
        "d_mid": f32(wide, wide),
        "d_in": f32(TAPS * 16, width),
        "d_head": f32(16, width),
        "d_norm": f32(4, width, LANES),
        "loss": f32(grid, LANES),
        "early": f32(ch * sz.early, 9, LANES),
        "early_in": f32(sz.owned, sz.sources, 9, LANES),
        "early_fin": f32(sz.early, 9, LANES),
        "blank": f32(ch, rows, 1, LANES),
        "ssq_early": f32(ch, sz.early, 1, LANES),
        "late_pair": f32(2, 4, 8, LANES),
        "late_sum": f32(4, 8, LANES),
        "late_in": f32(sz.chips, sz.late, 8, LANES),
        "late_fin": f32(4, 8, LANES),
        "ready": pltpu.SemaphoreType.REGULAR,
        "local_sem": dma(16),
        "f_sem": dma(2),
        "t_sem": dma(2),
        "v_sem": dma(2),
        "w_sem": dma(2),
        "e_send": dma(1),
        "e_recv": dma(sz.owned),
        "g_send": dma(sz.owned),
        "g_recv": dma(1),
        "s_send": dma(sz.owned),
        "s_recv": dma(1),
        "b_send": dma(1),
        "b_recv": dma(1),
        "p_send": dma(2),
        "p_recv": dma(2),
    }


def shards(mesh, fields, targets, fluid, keyframes, *rest):
    params, firsts, seconds = rest[0:4], rest[4:8], rest[8:12]

    def native(leaves):
        return (leaves[0], jnp.swapaxes(leaves[1], 2, 3), leaves[2].T, leaves[3])

    params, firsts, seconds = native(params), native(firsts), native(seconds)
    sz = Sizes(mesh, fields.shape, targets.shape, params[0].shape[3])
    marks = keyframes.T
    vmem = pl.BlockSpec(memory_space=pltpu.VMEM)
    hbm = pl.BlockSpec(memory_space=pl.ANY)
    alone = sz.rows == 1 and sz.ch == 1
    packed = pl.pallas_call(
        functools.partial(train_kernel, sz),
        out_shape=pltpu.VMEM((3 * (sz.early + 5) + 1, 8, LANES), F32),
        in_specs=[hbm] * 16,
        out_specs=vmem,
        scratch_shapes=list(scratch_of(sz).values()),
        compiler_params=pltpu.CompilerParams(
            collective_id=None if alone else 0, has_side_effects=True, vmem_limit_bytes=60 << 20
        ),
        name="train",
    )(fields.reshape(sz.rows, sz.per_rows, *fields.shape[1:]), targets, fluid, marks, *params, *firsts, *seconds)
    shapes = [jax.ShapeDtypeStruct(leaf.shape, F32) for leaf in params] * 3
    shapes += [jax.ShapeDtypeStruct((1, 1), F32)] * 3
    results = pl.pallas_call(
        functools.partial(unpack_kernel, sz),
        out_shape=tuple(shapes),
        in_specs=[vmem],
        out_specs=tuple([vmem] * 15),
        name="unpack",
    )(pltpu.with_memory_space_constraint(packed, pltpu.VMEM))
    outs = []
    for n in range(3):
        outs.extend(native(results[4 * n : 4 * n + 4]))
    return (*outs, *[leaf.reshape(()) for leaf in results[12:]])


def solution(mesh):
    split = (P(None, None, None, "ch"), P(None, None, None, "ch"), P("ch", None), P(None, "ch"))
    return jax.shard_map(
        functools.partial(shards, mesh),
        mesh=mesh,
        in_specs=(
            P(None, None, "rows", None),
            P(None, None, "rows", None),
            P("rows", None),
            P(),
            *split,
            *split,
            *split,
        ),
        out_specs=(*split, *split, *split, P(), P(), P()),
        check_vma=False,
    )
```

```python
import functools

import jax
import jax.numpy as jnp
from jax import lax
from jax.experimental import pallas as pl
from jax.experimental.pallas import tpu as pltpu
from jax.sharding import PartitionSpec as P

GROUPS = 8
NEAR = (-1, 0, 1)
STEP_NUM = 10
TIME_STEP = 0.5
COURANT = 0.8
FORCE_WEIGHT = 0.5
NORM_EPS = 1e-05
CLIP = 0.0001
BETA_ONE = 0.9
BETA_TWO = 0.999
ADAM_EPS = 1e-10
RATE = 0.1
GAIN_RATE = 0.6
DECAY = 0.01

MESH = pl.DeviceIdType.MESH
F32 = jnp.float32
BF16 = jnp.bfloat16
LANES = 128
GSIZE = 8
TAPS = 3
PARTS = (2, 2)
SAVED = 11
NT = (((1,), (1,)), ((), ()))


def lane_ids(shape):
    return lax.broadcasted_iota(jnp.int32, shape, len(shape) - 1)


def row_ids(shape):
    return lax.broadcasted_iota(jnp.int32, shape, 0)


def from_left(x):
    return jnp.where(lane_ids(x.shape) == 0, jnp.zeros_like(x), pltpu.roll(x, 1, 1))


def from_right(x):
    size = x.shape[1]
    return jnp.where(lane_ids(x.shape) == size - 1, jnp.zeros_like(x), pltpu.roll(x, size - 1, 1))


def from_above(x):
    return jnp.where(row_ids(x.shape) == 0, 0.0, pltpu.roll(x, 1, 0))


def from_below(x):
    size = x.shape[0]
    return jnp.where(row_ids(x.shape) == size - 1, 0.0, pltpu.roll(x, size - 1, 0))


def diff_rows(x):
    return from_below(x) - from_above(x)


def column(x, d):
    if d == 0:
        return x
    size = x.shape[1]
    lane = lane_ids(x.shape)
    inside = lane < size - d if d > 0 else lane >= -d
    return jnp.where(inside, pltpu.roll(x, -d % size, 1), jnp.zeros_like(x))


def columns_of(x, reach):
    return {d: column(x, d) for d in range(-reach, reach + 1)}


def rows_around(x):
    return from_below(x) + from_above(x)


def quadratic(s):
    return (0.5 * s * (s + 1.0), 1.0 - s * s, 0.5 * s * (s - 1.0))


def quadratic_slope(s):
    return (s + 0.5, -2.0 * s, s - 0.5)


def wrap(x, n):
    return x & (n - 1) if n & (n - 1) == 0 else lax.rem(x, n)


def partner(x, k, n):
    return x ^ k if n & (n - 1) == 0 else lax.rem(x + k, n)


def far_first(n):
    return reversed(range(1, n))


def dot(a, b):
    return jnp.dot(a, b, preferred_element_type=F32)


def dot_nt(a, b):
    return lax.dot_general(a, b, NT, preferred_element_type=F32)


def row_pair(ref, i, extra=None):
    depth = ref.shape[1] * TAPS
    sides = []
    for k in range(2):
        side = ref[pl.ds(i + k, TAPS)].reshape(depth, LANES)
        if extra is not None:
            side = jnp.concatenate([side, extra[i + k]], axis=0)
        sides.append(side)
    return jnp.concatenate(sides, axis=1)


def side_by_side(ref, first):
    return jnp.concatenate([ref[i] for i in range(first, ref.shape[0])], axis=1)


def four_rows(ref, i):
    taps = ref.shape[1] // 64
    parts = []
    for n in range(taps):
        sides = [ref[pl.ds(i + 2 * k, 4), n * 64 : (n + 1) * 64].reshape(4 * 64, LANES) for k in range(2)]
        parts.append(jnp.concatenate(sides, axis=1))
    return jnp.concatenate(parts, axis=0) if taps > 1 else parts[0]


def rows_of(p):
    half = p.shape[0] // 2
    return [p[o * half : (o + 1) * half, k * LANES : (k + 1) * LANES] for k in range(2) for o in range(2)]


def two_rows(blocks):
    zero = jnp.zeros_like(blocks[0])
    first = jnp.concatenate(list(blocks) + [zero], axis=1)
    second = jnp.concatenate([zero] + list(blocks), axis=1)
    return jnp.concatenate([first, second], axis=0)


def combine(part, height):
    return (
        part[height : 2 * height] + from_left(part[:height]) + from_right(part[2 * height : 3 * height])
    )


def group_sum(x):
    return jnp.sum(jnp.sum(x.reshape(-1, GSIZE, LANES), axis=1), axis=1, keepdims=True)


def spread(x):
    return jnp.broadcast_to(x[:, :, None], (x.shape[0], GSIZE, LANES)).reshape(-1, LANES)


def loop(count, per, body, carry):
    per = min(per, count)

    def several(it, carry):
        for k in range(per):
            carry = body(it * per + k, carry)
        return carry

    if count == per:
        return several(0, carry)
    return lax.fori_loop(0, count // per, several, carry)


def in_place(ky, kx):
    at = ky * 16 + kx * 4
    lane = 64 if at >= 24 else 0
    at = at % 24
    return at // 8, at % 8, lane


class Sizes:
    def __init__(self, mesh, fields_shape, targets_shape, co):
        self.ch = mesh.shape["ch"]
        self.rows = mesh.shape["rows"]
        self.batch = fields_shape[0]
        self.local = fields_shape[2]
        self.grid = self.local * self.rows
        self.cols = fields_shape[3]
        self.steps = targets_shape[0]
        self.co = co
        self.width = co * self.ch
        self.per_rows = self.batch // self.rows
        self.ways = self.ch if self.per_rows == self.ch else 1
        assert self.per_rows == self.ways and self.batch % self.rows == 0
        assert self.cols == LANES
        slot = self.grid * self.width * LANES * 20
        self.slots = self.steps if slot * self.steps < (24 << 20) else 1
        self.halves = co // 8
        self.early = 4 * self.halves
        self.owned = -(-self.early // self.rows)
        self.sources = self.ways * self.rows
        self.cores = 2 if self.ways > 1 else 1
        self.chips = self.sources // self.cores
        self.late = 4 // self.cores
        assert self.ways % self.cores == 0
        self.mid_lanes = TAPS * TAPS * self.width
        assert self.width == 64 and co % 8 == 0


IN_AT = 64
HEAD_AT = IN_AT + 36
NORM_AT = HEAD_AT + 2
LOSS_AT = NORM_AT + 4


def train_kernel(
    sz,
    fields,
    targets,
    fluid,
    keyframes,
    w_in,
    w_mid,
    w_head,
    norms,
    first_in,
    first_mid,
    first_head,
    first_norm,
    second_in,
    second_mid,
    second_head,
    second_norm,
    out,
    *scratch,
):
    z = dict(zip(scratch_of(sz), scratch))
    f_stage = z["f_stage"]
    f_out = z["f_out"]
    m_own = z["m_own"]
    t_stage = z["t_stage"]
    in_own = z["in_own"]
    mid_own = z["mid_own"]
    head_own = z["head_own"]
    norm_own = z["norm_own"]
    marks_own = z["marks_own"]
    held = z["held"]
    total = z["total"]
    small = z["small"]
    ws_all = z["ws_all"]
    wm_all = z["wm_all"]
    w_fwd = z["w_fwd"]
    w_bwd = z["w_bwd"]
    v_fwd = z["v_fwd"]
    v_bwd = z["v_bwd"]
    head_back = z["head_back"]
    head = z["head"]
    gains = z["gains"]
    current = z["current"]
    states = z["states"]
    mask = z["mask"]
    feat32 = z["feat32"]
    feat = z["feat"]
    conv = z["conv"]
    slope = z["slope"]
    norm_stats = z["norm_stats"]
    back_factors = z["back_factors"]
    hidden = z["hidden"]
    hidden_low = z["hidden_low"]
    mixed_low = z["mixed_low"]
    logits = z["logits"]
    saved = z["saved"]
    dy = z["dy"]
    mixed_grad = z["mixed_grad"]
    glog32 = z["glog32"]
    glog = z["glog"]
    g_pad = z["g_pad"]
    g_taps = z["g_taps"]
    gs_rows = z["gs_rows"]
    grad_state = z["grad_state"]
    d_mid = z["d_mid"]
    d_in = z["d_in"]
    d_head = z["d_head"]
    d_norm = z["d_norm"]
    loss = z["loss"]
    early = z["early"]
    early_in = z["early_in"]
    early_fin = z["early_fin"]
    blank = z["blank"]
    ssq_early = z["ssq_early"]
    late_pair = z["late_pair"]
    late_sum = z["late_sum"]
    late_in = z["late_in"]
    late_fin = z["late_fin"]
    ready = z["ready"]
    local_sem = z["local_sem"]
    f_sem = z["f_sem"]
    t_sem = z["t_sem"]
    v_sem = z["v_sem"]
    w_sem = z["w_sem"]
    e_send = z["e_send"]
    e_recv = z["e_recv"]
    g_send = z["g_send"]
    g_recv = z["g_recv"]
    s_send = z["s_send"]
    s_recv = z["s_recv"]
    b_send = z["b_send"]
    b_recv = z["b_recv"]
    p_send = z["p_send"]
    p_recv = z["p_recv"]
    c = lax.axis_index("ch")
    r = lax.axis_index("rows")
    width, grid, steps = sz.width, sz.grid, sz.steps
    co = sz.co

    def row_peer(k):
        return partner(r, k, sz.rows)

    def ch_peer(k):
        return partner(c, k, sz.ch)

    def sample_of(row):
        return row * sz.per_rows + (c if sz.ways > 1 else 0)

    def block(work):
        pl.when(r >= 0)(work)

    peers = sz.rows - 1 + sz.ch - 1
    if peers:
        barrier = pltpu.get_barrier_semaphore()
        for k in far_first(sz.rows):
            pl.semaphore_signal(barrier, inc=1, device_id=(c, row_peer(k)), device_id_type=MESH)
        for k in far_first(sz.ch):
            pl.semaphore_signal(barrier, inc=1, device_id=(ch_peer(k), r), device_id_type=MESH)

    def remote(src, dst, send, recv, where):
        return pltpu.make_async_remote_copy(
            src_ref=src, dst_ref=dst, send_sem=send, recv_sem=recv, device_id=where, device_id_type=MESH
        )

    def arrived(ref, sem):
        remote(ref, ref, sem, sem, (c, r)).wait_recv()

    def sent(ref, sem):
        remote(ref, ref, sem, sem, (c, r)).wait_send()

    def but_one(ref):
        return ref.at[pl.ds(0, ref.shape[0] - 1)]

    own = [
        pltpu.make_async_copy(src, dst, local_sem.at[n])
        for n, (src, dst) in enumerate(
            (
                (w_in, in_own.at[0]),
                (w_head, head_own.at[0]),
                (norms, norm_own.at[0]),
                (w_mid, mid_own.at[0]),
                (fields.at[:, c if sz.ways > 1 else 0], f_out.at[:, pl.ds(0, 3)]),
                (fluid, m_own),
                (targets.at[:, sample_of(r)], t_stage.at[r]),
                (keyframes, marks_own),
                (first_in, in_own.at[1]),
                (first_mid, mid_own.at[1]),
                (first_head, head_own.at[1]),
                (first_norm, norm_own.at[1]),
                (second_in, in_own.at[2]),
                (second_mid, mid_own.at[2]),
                (second_head, head_own.at[2]),
                (second_norm, norm_own.at[2]),
            )
        )
    ]
    for copy in own:
        copy.start()
    small[...] = jnp.zeros_like(small)
    for n in range(4):
        own[n].wait()
    for ky in range(TAPS):
        for kx in range(TAPS):
            at = IN_AT + (ky * TAPS + kx) * 4
            small[at : at + 4, 0:co] = in_own[0, ky, kx]
    small[HEAD_AT : HEAD_AT + 2, 0:co] = head_own[0]
    small[NORM_AT : NORM_AT + 4, 0:co] = norm_own[0]
    ws_all[c] = jnp.transpose(small[...])[0:co]
    packed = jnp.concatenate([mid_own[0, ky, kx] for kx in range(TAPS) for ky in range(TAPS)], axis=1)
    wm_all[c, 0:co, :] = packed.astype(BF16)
    own[4].wait()
    own[5].wait()
    for row in range(sz.rows):
        f_out[row, 3] = m_own[...].astype(F32)
    f_stage[r] = f_out[r]
    if peers:
        pl.semaphore_wait(barrier, peers)

    for k in far_first(sz.rows):
        row = row_peer(k)
        remote(f_out.at[row], f_stage.at[r], f_sem.at[0], f_sem.at[1], (c, row)).start()
    for k in far_first(sz.ch):
        remote(ws_all.at[c], ws_all.at[c], v_sem.at[0], v_sem.at[1], (ch_peer(k), r)).start()
    for k in far_first(sz.ch):
        remote(wm_all.at[c], wm_all.at[c], w_sem.at[0], w_sem.at[1], (ch_peer(k), r)).start()
    for k in far_first(sz.rows):
        src = targets.at[:, sample_of(row_peer(k))]
        remote(src, t_stage.at[r], t_sem.at[0], t_sem.at[1], (c, row_peer(k))).start()
    row_groups = ((f_stage, f_sem), (t_stage, t_sem)) if sz.rows > 1 else ()
    ch_groups = ((ws_all, v_sem), (wm_all, w_sem)) if sz.ch > 1 else ()
    if peers:
        for k in far_first(sz.ch):
            pl.semaphore_signal(ready, inc=1, device_id=(ch_peer(k), r), device_id_type=MESH)

    for n in range(8, 16):
        own[n].wait()
    for n in range(3):
        mid = [[mid_own[n, ky, kx] for kx in range(TAPS)] for ky in range(TAPS)]
        sides = [(mid[0][kx], mid[1][kx]) for kx in range(TAPS)] + [(mid[2][0], mid[2][1])]
        for k, side in enumerate(sides):
            tile = jnp.concatenate(side, axis=1)
            for h in range(sz.halves):
                held[n, h * 4 + k] = tile[h * 8 : (h + 1) * 8]
        for k in range(sz.early, sz.early + 5):
            held[n, k] = jnp.zeros((8, LANES), F32)
        for ky in range(TAPS):
            for kx in range(TAPS):
                tile, row, lane = in_place(ky, kx)
                held[n, sz.early + tile, row : row + 4, lane : lane + co] = in_own[n, ky, kx]
        held[n, sz.early + 3, 0:4, 0:co] = norm_own[n]
        held[n, sz.early + 3, 4:6, 0:co] = head_own[n]
        last = mid[2][2]
        held[n, sz.early + 4, 0 : co // 2] = jnp.concatenate([last[: co // 2], last[co // 2 :]], axis=1)

    for i in (0, grid + 1):
        g_taps[i] = jnp.zeros_like(g_taps[i])
    for ref in (feat, hidden_low, g_pad):
        for slot in range(sz.slots):
            ref[slot, 0] = jnp.zeros_like(ref[slot, 0])
            ref[slot, grid + 1] = jnp.zeros_like(ref[slot, 0])
    feat32[...] = jnp.zeros_like(feat32)
    glog32[...] = jnp.zeros_like(glog32)
    for ref in (d_mid, d_in, d_head, d_norm, loss):
        ref[...] = jnp.zeros_like(ref)

    if ch_groups:
        arrived(but_one(ws_all), v_sem.at[1])
    tail = ws_all[...].reshape(width, LANES)
    tail_t = jnp.transpose(tail)
    parts = []
    for ky in range(TAPS):
        at = IN_AT + ky * 12
        parts.append(jnp.concatenate([tail[:, at : at + 12], jnp.zeros((width, 4), F32)], axis=1))
    v_fwd[...] = jnp.concatenate(parts, axis=1).astype(BF16)
    pieces = []
    for ky in range(TAPS):
        column_taps = []
        for kx in range(TAPS):
            at = IN_AT + ((2 - ky) * TAPS + 2 - kx) * 4
            column_taps += [tail_t[at : at + 4], jnp.zeros((4, width), F32)]
        pieces.append(jnp.concatenate(column_taps, axis=0))
    v_bwd[...] = two_rows(pieces).astype(BF16)
    head_back[...] = jnp.concatenate([tail[:, HEAD_AT : HEAD_AT + 2], jnp.zeros((width, 14), F32)], axis=1).astype(BF16)
    head[...] = jnp.concatenate([tail_t[HEAD_AT : HEAD_AT + 2], jnp.zeros((14, width), F32)], axis=0).astype(BF16)
    for k in range(4):
        gains[k] = jnp.broadcast_to(tail[:, NORM_AT + k : NORM_AT + k + 1], (width, LANES))

    own[7].wait()
    marks = marks_own[...].astype(F32)
    valid = jnp.sum(jnp.sum(marks, axis=1, keepdims=True), axis=0, keepdims=True) * float(grid * sz.cols)
    inv_count = 1.0 / valid
    picked = jnp.where(lane_ids(marks.shape) == sample_of(r), marks, 0.0)
    marked = jnp.sum(picked, axis=1, keepdims=True)

    def key_of(t):
        return jnp.sum(jnp.where(row_ids(marked.shape) == t, marked, 0.0), axis=0, keepdims=True)

    def second_layer():
        if ch_groups:
            arrived(but_one(wm_all), w_sem.at[1])
        kind = BF16 if co % 16 == 0 else F32
        mid = jnp.concatenate([wm_all[k, 0:co, :].astype(kind) for k in range(sz.ch)], axis=0)
        for kx in range(TAPS):
            at = [(kx * TAPS + ky) * width for ky in range(TAPS)]
            w_fwd[:, kx * 4 * width : (kx + 1) * 4 * width] = two_rows([mid[:, a : a + width] for a in at]).astype(BF16)

    def second_layer_back():
        for kx in range(TAPS):
            at = kx * 4 * width
            blocks = [w_fwd[0:width, at + ky * width : at + (ky + 1) * width].astype(F32) for ky in range(TAPS)]
            w_bwd[:, at : at + 4 * width] = two_rows([jnp.transpose(b) for b in reversed(blocks)]).astype(BF16)

    second_layer()

    for ref, sem in row_groups[:1]:
        arrived(but_one(ref), sem.at[1])
    for q in range(3):
        current[q, 1] = jnp.concatenate([f_stage[row, q] for row in range(sz.rows)], axis=0)
    mask[2] = jnp.concatenate([f_stage[row, 3] for row in range(sz.rows)], axis=0)
    for q in range(3):
        for d in (-1, 1):
            current[q, d + 1] = column(current[q, 1], d)
    for d in (-2, -1, 1, 2):
        mask[d + 2] = column(mask[2], d)
    for d in NEAR:
        feat32[pl.ds((d + 1) * 4 + 3, grid, stride=16), :] = mask[d + 2]

    def all_targets():
        if row_groups:
            arrived(but_one(t_stage), t_sem.at[1])
        own[6].wait()
    def parts_of(count):
        size = width // count
        return [slice(n * size, (n + 1) * size) for n in range(count)]

    def conv_and_stats(x_ref, w, layer, slot, span=slice(0, 64)):
        zero = jnp.zeros((span.stop - span.start, LANES), F32)

        def body(it, carry):
            base, total, squares = carry
            i = it * 4
            if layer:
                rows = rows_of(dot(w[...], four_rows(x_ref, i)))
            else:
                rows = []
                for k in range(2):
                    p = dot(w[span], row_pair(x_ref, i + 2 * k))
                    rows += [p[:, :LANES], p[:, LANES:]]
            base = jnp.where(it == 0, rows[0], base)
            for j in range(4):
                conv[slot, layer, i + j, span] = rows[j]
                d = rows[j] - base
                total = total + d
                squares = squares + d * d
            return base, total, squares

        base, total, squares = loop(grid // 4, 8, body, (zero, zero, zero))
        lane_mean = base + total * (1.0 / grid)
        lane_dev = squares - total * total * (1.0 / grid)
        count = float(GSIZE * LANES)
        middle = spread(group_sum(base) * (1.0 / count))
        d = lane_mean - middle
        first = spread(group_sum(d) * (1.0 / count))
        second = spread(group_sum(lane_dev + grid * d * d) * (1.0 / (count * grid)))
        norm_stats[2 * layer, slot, span] = middle + first
        norm_stats[2 * layer + 1, slot, span] = lax.rsqrt(second - first * first + NORM_EPS)

    def silu_parts(half):
        t = jnp.tanh(half)
        a = 1.0 + t
        h = half * a
        return h, a + h * (1.0 - t)

    def half_affine(layer, slot, span=slice(0, 64)):
        k = 2 * layer
        mean, inv = norm_stats[k, slot, span], norm_stats[k + 1, slot, span]
        scale = 0.5 * inv * gains[k, span]
        return scale, 0.5 * gains[k + 1, span] - mean * scale

    def step_forward(t, slot, first):
        last = t == steps - 1
        if sz.slots == 1:
            for q in range(3):
                for d in NEAR:
                    if first:
                        states[t, q, d + 1] = current[q, d + 1]
                    else:
                        current[q, d + 1] = states[t, q, d + 1]
        @block
        def _():
            x = [{d: current[q, d + 1] for d in NEAR} for q in range(3)]
            for q in range(3):
                for d in NEAR:
                    feat32[pl.ds((d + 1) * 4 + q, grid, stride=16), :] = x[q][d]

            def pack(it, carry):
                for k in range(4):
                    i = it * 4 + k
                    feat[slot, i + 1] = feat32[pl.ds(pl.multiple_of(i * 16, 16), 16), :].astype(BF16)
                return carry

            loop(grid // 4, 8, pack, 0)

            for span in parts_of(PARTS[0]):
                conv_and_stats(feat.at[slot], v_fwd, 0, slot, span)
        @block
        def _():
            def norm_one(span, it, carry):
                for k in range(2):
                    i = it * 2 + k
                    h, slope[slot, 0, i, span] = silu_parts(conv[slot, 0, i, span] * mul + add)
                    hidden[i, span] = h
                    low = h.astype(BF16)
                    for kx, tap in enumerate((from_left(low), low, from_right(low))):
                        hidden_low[slot, i + 1, kx * width + span.start : kx * width + span.stop] = tap
                return carry

            for span in parts_of(PARTS[0]):
                mul, add = half_affine(0, slot, span)
                loop(grid // 2, 16, functools.partial(norm_one, span), 0)

            conv_and_stats(hidden_low.at[slot], w_fwd, 1, slot)
        @block
        def _():
            if first and t == min(1, steps - 1):
                second_layer_back()
            mul, add = half_affine(1, slot)

            def norm_two(it, carry):
                i = it * 2
                lows = []
                for k in range(2):
                    h, slope[slot, 1, i + k] = silu_parts(conv[slot, 1, i + k] * mul + add)
                    low = (hidden[i + k] + h).astype(BF16)
                    mixed_low[slot, i + k] = low
                    lows.append(low)
                p = dot(head[...], jnp.concatenate(lows, axis=1))
                for k in range(2):
                    logits[0, pl.ds(i + k, 1), :] = p[0:1, k * LANES : (k + 1) * LANES]
                    logits[1, pl.ds(i + k, 1), :] = p[1:2, k * LANES : (k + 1) * LANES]
                return carry

            loop(grid // 2, 16, norm_two, 0)

        if first and t == 0:
            all_targets()
        @block
        def _():
            x = [{d: current[q, d + 1] for d in NEAR} for q in range(3)]
            f0, f1 = jnp.tanh(logits[0]), jnp.tanh(logits[1])
            force0, force1 = columns_of(f0, 1), columns_of(f1, 1)
            u1 = {d: x[1][d] + TIME_STEP * force0[d] for d in NEAR}
            v1 = {d: x[2][d] + TIME_STEP * force1[d] for d in NEAR}
            sy = COURANT * jnp.tanh(u1[0])
            sx = COURANT * jnp.tanh(v1[0])
            wy, wx = quadratic(sy), quadratic(sx)
            dwy, dwx = quadratic_slope(sy), quadratic_slope(sx)
            moved = []
            for n, q in enumerate((x[0], u1, v1)):
                lines = [(from_above(q[d]), q[d], from_below(q[d])) for d in NEAR]
                along = [wx[0] * lines[0][a] + wx[1] * lines[1][a] + wx[2] * lines[2][a] for a in range(3)]
                moved.append(wy[0] * along[0] + wy[1] * along[1] + wy[2] * along[2])
                if last and n:
                    continue
                slant = [dwx[0] * lines[0][a] + dwx[1] * lines[1][a] + dwx[2] * lines[2][a] for a in range(3)]
                saved[slot, 4 + n] = dwy[0] * along[0] + dwy[1] * along[1] + dwy[2] * along[2]
                saved[slot, 7 + n] = wy[0] * slant[0] + wy[1] * slant[1] + wy[2] * slant[2]
            rho2 = moved[0]
            if first and not last:
                solid = {d: mask[d + 2] for d in range(-2, 3)}
                rho2s, u2, v2 = columns_of(rho2, 1), columns_of(moved[1], 1), columns_of(moved[2], 2)
                div = {d: 0.5 * (diff_rows(u2[d]) + (v2[d + 1] - v2[d - 1])) for d in NEAR}
                press = {d: -0.25 * solid[d] * div[d] for d in NEAR}
                press = 0.25 * solid[0] * (rows_around(press[0]) + press[1] + press[-1] - div[0])
                press = columns_of(press, 3)
                div[2], div[-2] = column(div[0], 2), column(div[0], -2)
                press = {
                    d: 0.25 * solid[d] * (rows_around(press[d]) + press[d + 1] + press[d - 1] - div[d])
                    for d in range(-2, 3)
                }
                for d in NEAR:
                    current[0, d + 1] = rho2s[d]
                    current[1, d + 1] = solid[d] * (u2[d] - 0.5 * diff_rows(press[d]))
                    current[2, d + 1] = solid[d] * (v2[d] - 0.5 * (press[d + 1] - press[d - 1]))
            miss = rho2 - jnp.concatenate([t_stage[row, t] for row in range(sz.rows)], axis=0)
            pull = key_of(t) * miss
            if first:
                loss[...] += FORCE_WEIGHT * (f0 * f0 + f1 * f1) + pull * miss
            saved[slot, 0] = f0
            saved[slot, 1] = f1
            saved[slot, 2] = sy
            saved[slot, 3] = sx
            saved[slot, 10] = pull

    for t in range(steps):
        step_forward(t, t if sz.slots > 1 else 0, True)
    for ref, sem in row_groups + ch_groups:
        sent(but_one(ref), sem.at[0])

    def owner_of(j):
        return wrap(j, sz.rows)

    me = c * sz.rows + r if sz.ways > 1 else r
    chip_slot = (c // 2) * sz.rows + r if sz.ways > 1 else r

    def by_owned(action):
        least, more = sz.early // sz.rows, sz.early % sz.rows
        if more:
            pl.when(r < more)(functools.partial(action, least + 1))
            pl.when(r >= more)(functools.partial(action, least))
        else:
            action(least)

    def for_owned(action):
        for m in range(sz.owned):
            j = r + m * sz.rows
            if (m + 1) * sz.rows <= sz.early:
                action(m, j)
            else:
                pl.when(j < sz.early)(functools.partial(action, m, j))

    def early_start():
        low_half = lane_ids((width, LANES)) < 64
        tiles = [d_mid[kx * width : (kx + 1) * width, 0:LANES] for kx in range(TAPS)]
        rest = [d_mid[kx * width : (kx + 1) * width, LANES:] for kx in range(2)]
        tiles.append(jnp.concatenate(rest, axis=1))
        last = d_mid[2 * width : 3 * width, LANES:]
        for shard in range(sz.ch):
            for h in range(sz.halves):
                at = shard * co + h * 8
                for n, tile in enumerate(tiles):
                    early[shard * sz.early + h * 4 + n, 0:8] = tile[at : at + 8]
            ends = last[shard * co : (shard + 1) * co]
            ends = jnp.concatenate([ends[: co // 2], ends[co // 2 :]], axis=1)
            for j in range(sz.early):
                early[shard * sz.early + j, 8:9] = ends[j : j + 1]
        if sz.ch > 1:
            pl.semaphore_wait(ready, sz.ch - 1)
        for dc in reversed(range(sz.ways)):
            shard = ch_peer(dc)
            for k in reversed(range(sz.early)):
                j = partner(r, k, sz.early) if sz.early == sz.rows else wrap(r + k, sz.early)
                slot = j // sz.rows if sz.owned > 1 else 0
                if dc == 0 and k == 0 and sz.early == sz.rows:
                    continue
                copy = remote(
                    early.at[shard * sz.early + j],
                    early_in.at[slot, me],
                    e_send.at[0],
                    e_recv.at[slot],
                    (shard, owner_of(j)),
                )
                if dc or sz.early == sz.rows:
                    copy.start()
                else:
                    pl.when(owner_of(j) != r)(copy.start)

    def early_sum():
        def total(m, j):
            early_in[m, me] = early[c * sz.early + j]
            if sz.sources > 1:
                arrived(but_one(early_in.at[m]), e_recv.at[m])
            acc = early_in[m, 0]
            for k in range(1, sz.sources):
                acc = acc + early_in[m, k]
            early_fin[j] = acc
            line = ssq_early.at[c, j]
            line[...] = jnp.sum(acc * acc, axis=0, keepdims=True)
            for dc in far_first(sz.ch):
                for k in reversed(range(sz.rows)):
                    remote(line, line, s_send.at[m], s_recv.at[0], (ch_peer(dc), row_peer(k))).start()
            for k in far_first(sz.rows):
                remote(early_fin.at[j], early_fin.at[j], g_send.at[m], g_recv.at[0], (c, row_peer(k))).start()

        for_owned(total)

    def early_left():
        if sz.sources > 1:
            by_owned(lambda n: sent(early.at[pl.ds(0, sz.ways * sz.early - n)], e_send.at[0]))

    def put_line(j, acc):
        ssq_early[c, j] = jnp.sum(acc * acc, axis=0, keepdims=True)

    def early_end():
        if sz.rows > 1:
            by_owned(lambda n: arrived(early_fin.at[pl.ds(0, sz.early - n)], g_recv.at[0]))
        for j in range(sz.early):
            acc = early_fin[j]
            total[j] = acc[0:8]
            total[sz.early + 4, j : j + 1] = acc[8:9]
            if sz.rows > 1:
                pl.when(r != j % sz.rows)(functools.partial(put_line, j, acc))
        if sz.ch > 1:
            arrived(but_one(ssq_early), s_recv.at[0])

    def early_shared():
        def last(m, j):
            if sz.ch > 1:
                sent(but_one(blank), s_send.at[m])
            if sz.rows > 1:
                sent(but_one(early_in.at[m, pl.ds(0, sz.rows)]), g_send.at[m])

        for_owned(last)

    def norm_back(k, slot, sums_d, sums_c, span=slice(0, 64)):
        gain, mean, inv = gains[k, span], norm_stats[k, slot, span], norm_stats[k + 1, slot, span]
        sums_d = 0.5 * sums_d
        sums_n = inv * (0.5 * sums_c - mean * sums_d)
        scale = 1.0 / float(GSIZE * LANES * grid)
        m1 = spread(group_sum(sums_d * gain) * scale)
        m2 = spread(group_sum(sums_n * gain) * scale)
        d_norm[k, span] += sums_n
        d_norm[k + 1, span] += sums_d
        fc = inv * inv * m2
        back_factors[0, span] = 0.5 * inv * gain
        back_factors[1, span] = inv * m1 - fc * mean
        back_factors[2, span] = fc

    def mid_grad(slot, part, parts):
        span = grid // parts
        rows = range(part * span, (part + 1) * span)
        center = slice(width, 2 * width)
        left = [g_taps[i + 1] for i in rows]
        right = [hidden_low[slot, i : i + TAPS, center].reshape(TAPS * width, LANES) for i in rows]
        d_mid[...] += dot_nt(jnp.concatenate(left, axis=1), jnp.concatenate(right, axis=1))

    core = wrap(c, sz.cores)
    pack = late_pair.at[core] if sz.cores > 1 else late_sum

    def late_misc():
        columns = [jnp.sum(d_norm[k], axis=1, keepdims=True) for k in range(4)]
        columns.append(jnp.zeros((width, LANES - 4), F32))
        lines = jnp.transpose(jnp.concatenate(columns, axis=1))
        loss_sum = jnp.sum(jnp.sum(loss[...], axis=1, keepdims=True), axis=0, keepdims=True)
        pack[3] = jnp.zeros((8, LANES), F32)
        pack[3, 0:4, 0:width] = lines[0:4, :]
        pack[3, 4:6, 0:width] = d_head[0:2]
        pack[3, 6:7, 0:width] = jnp.broadcast_to(loss_sum, (1, width))

    def step_backward(t, slot):
        @block
        def _():
            sy, sx = saved[slot, 2], saved[slot, 3]
            f0, f1 = saved[slot, 0], saved[slot, 1]
            wy, wx = quadratic(sy), quadratic(sx)
            grads = [2.0 * inv_count * saved[slot, 10]]
            if t < steps - 1:
                solid = {d: mask[d + 2] for d in NEAR}
                grads[0] = grads[0] + grad_state[0]
                gu, gv = columns_of(solid[0] * grad_state[1], 1), columns_of(solid[0] * grad_state[2], 2)
                one = {d: 0.125 * solid[d] * (diff_rows(gu[d]) + (gv[d + 1] - gv[d - 1])) for d in NEAR}
                two = 0.25 * solid[0] * (rows_around(one[0]) + one[1] + one[-1])
                two = columns_of(two, 2)
                g_div = {
                    d: one[d] + two[d] + 0.25 * solid[d] * (rows_around(two[d]) + two[d + 1] + two[d - 1]) for d in NEAR
                }
                grads.append(gu[0] + 0.5 * diff_rows(g_div[0]))
                grads.append(gv[0] + 0.5 * (g_div[1] - g_div[-1]))
            spots = []
            g_sy = g_sx = 0.0
            for n, g in enumerate(grads):
                g_sy = g_sy + g * saved[slot, 4 + n]
                g_sx = g_sx + g * saved[slot, 7 + n]
                lines = []
                for b in range(3):
                    gb = wx[b] * g
                    lines.append(from_below(wy[0] * gb) + wy[1] * gb + from_above(wy[2] * gb))
                spots.append(column(lines[0], 1) + lines[1] + column(lines[2], -1))
            ty, tx = sy * (1.0 / COURANT), sx * (1.0 / COURANT)
            g_u1 = g_sy * (COURANT * (1.0 - ty * ty))
            g_v1 = g_sx * (COURANT * (1.0 - tx * tx))
            if t < steps - 1:
                g_u1, g_v1 = spots[1] + g_u1, spots[2] + g_v1
            l0 = (TIME_STEP * g_u1 + 2.0 * FORCE_WEIGHT * inv_count * f0) * (1.0 - f0 * f0)
            l1 = (TIME_STEP * g_v1 + 2.0 * FORCE_WEIGHT * inv_count * f1) * (1.0 - f1 * f1)
            if t > 0:
                grad_state[0] = spots[0]
                grad_state[1] = g_u1
                grad_state[2] = g_v1
            if sz.slots > 1 and t < steps - 1:
                for part in range(2):
                    mid_grad(t + 1, part, 2)
            glog32[pl.ds(0, grid, stride=16), :] = l0
            glog32[pl.ds(1, grid, stride=16), :] = l1

            def pack(it, carry):
                for k in range(4):
                    i = it * 4 + k
                    glog[slot, i] = glog32[pl.ds(pl.multiple_of(i * 16, 16), 16), :].astype(BF16)
                return carry

            loop(grid // 4, 8, pack, 0)

        @block
        def _():
            def back_a(span, it, carry):
                sums_d, sums_n = carry
                i = it * 2
                gl = jnp.concatenate([glog[slot, i], glog[slot, i + 1]], axis=1)
                p = dot(head_back[span], gl)
                for k in range(2):
                    g = p[:, k * LANES : (k + 1) * LANES]
                    mixed_grad[i + k, span] = g
                    d = g * slope[slot, 1, i + k, span]
                    dy[i + k, span] = d
                    sums_d = sums_d + d
                    sums_n = sums_n + d * conv[slot, 1, i + k, span]
                return sums_d, sums_n

            for span in parts_of(PARTS[1]):
                zero = jnp.zeros((span.stop - span.start, LANES), F32)
                sums = loop(grid // 2, 16, functools.partial(back_a, span), (zero, zero))
                norm_back(2, slot, *sums, span)

        @block
        def _():
            def back_b(span, it, carry):
                if span.start == 0:
                    gl = jnp.concatenate([glog[slot, it * 2 + k] for k in range(2)], axis=1)
                    ml = jnp.concatenate([mixed_low[slot, it * 2 + k] for k in range(2)], axis=1)
                    d_head[...] += dot_nt(gl, ml)
                for k in range(2):
                    i = it * 2 + k
                    g = fd * dy[i, span] - f1_ - fn * conv[slot, 1, i, span]
                    low = g.astype(BF16)
                    for kx, tap in enumerate((from_right(low), low, from_left(low))):
                        g_taps[i + 1, kx * width + span.start : kx * width + span.stop] = tap
                return carry

            spans = parts_of(PARTS[1])
            for span in spans:
                fd, f1_, fn = [back_factors[k, span] for k in range(3)]
                if t > 0 or span is not spans[-1]:
                    loop(grid // 2, 16, functools.partial(back_b, span), 0)
                    continue
                parts = 4
                for k in range(grid // 2):
                    back_b(span, k, 0)
                    if (k + 1) % (grid // 2 // parts) == 0:
                        mid_grad(slot, k // (grid // 2 // parts), parts)

        if t == 0:
            early_start()
        elif sz.slots == 1:
            for part in range(8):
                mid_grad(slot, part, 8)

        @block
        def _():
            def back_c(it, carry):
                sums_d, sums_n = carry
                i = it * 4
                rows = rows_of(dot(w_bwd[...], four_rows(g_taps, i)))
                for k in range(4):
                    d = (rows[k] + mixed_grad[i + k]) * slope[slot, 0, i + k]
                    dy[i + k] = d
                    sums_d = sums_d + d
                    sums_n = sums_n + d * conv[slot, 0, i + k]
                return sums_d, sums_n

            zero = jnp.zeros((width, LANES), F32)
            sums = loop(grid // 4, 8, back_c, (zero, zero))
            norm_back(0, slot, *sums)
        @block
        def _():
            fd, f1_, fn = [back_factors[k] for k in range(3)]

            if t == 0:
                late_misc()

            def back_d(it, carry):
                i = it * 2
                lows = []
                for k in range(2):
                    low = (fd * dy[i + k] - f1_ - fn * conv[slot, 0, i + k]).astype(BF16)
                    g_pad[slot, i + k + 1] = low
                    lows.append(low)
                d_in[...] += dot_nt(row_pair(feat.at[slot], i), jnp.concatenate(lows, axis=1))
                return carry

            loop(grid // 2, 16, back_d, 0)
            if t > 0:

                def back_e(it, carry):
                    i = it * 4
                    rows = rows_of(dot(v_bwd[...], four_rows(g_pad.at[slot], i)))
                    for k in range(4):
                        gs_rows[pl.ds(pl.multiple_of((i + k) * 8, 8), 8), :] = combine(rows[k], 8)
                    return carry

                loop(grid // 4, 8, back_e, 0)
                for q in range(3):
                    grad_state[q] += gs_rows[pl.ds(q, grid, stride=8), :]

    for t in reversed(range(steps)):
        if sz.slots == 1:
            step_forward(t, 0, False)
        step_backward(t, t if sz.slots > 1 else 0)

    mate = (c + 1 - 2 * core, r)
    mine = pl.ds(core * sz.late, sz.late)

    def chip_peer(k):
        if sz.ways == 1:
            return (c, row_peer(k))
        return (partner(c // 2, k // sz.rows, sz.ch // 2) * 2 + core, row_peer(wrap(k, sz.rows)))

    inputs = jnp.concatenate([d_in[0:24], d_in[24:48]], axis=1)
    for n in range(3):
        pack[n] = inputs[n * 8 : (n + 1) * 8]
    if sz.cores > 1:
        remote(pack, pack, p_send.at[0], p_recv.at[0], mate).start()
        arrived(pack, p_recv.at[0])
        late_sum[...] = late_pair[0] + late_pair[1]
    for k in far_first(sz.chips):
        remote(late_sum.at[mine], late_in.at[chip_slot], b_send.at[0], b_recv.at[0], chip_peer(k)).start()

    early_sum()

    late_in[chip_slot] = late_sum[mine]
    if sz.chips > 1:
        arrived(but_one(late_in), b_recv.at[0])
    acc = late_in[0]
    for k in range(1, sz.chips):
        acc = acc + late_in[k]
    late_fin[mine] = acc
    if sz.cores > 1:
        remote(late_fin.at[mine], late_fin.at[mine], p_send.at[1], p_recv.at[1], mate).start()
        sent(pack, p_send.at[0])
    early_left()
    if sz.chips > 1:
        sent(but_one(late_in), b_send.at[0])
    if sz.cores > 1:
        arrived(late_fin.at[mine], p_recv.at[1])
    acc = late_fin[...].reshape(32, LANES)
    turned = pltpu.roll(acc, wrap(LANES - c * co, LANES), 1)
    for n in range(4):
        total[sz.early + n] = turned[n * 8 : (n + 1) * 8]
    acc = jnp.where(row_ids(acc.shape) < 30, acc, 0.0)
    late_norm = jnp.sum(acc * acc, axis=0, keepdims=True)

    if sz.early < 8:
        total[sz.early + 4] = jnp.zeros((8, LANES), F32)
    early_end()
    acc = late_norm
    for k in range(sz.ch):
        for j in range(sz.early):
            acc = acc + ssq_early[k, j]
    grad_norm = jnp.sqrt(jnp.broadcast_to(jnp.sum(acc, axis=1, keepdims=True), (8, LANES)))
    factor = CLIP / jnp.maximum(grad_norm, CLIP)

    count = sz.early + 5
    gain_row = row_ids((8, LANES)) < 4
    for k in range(count):
        rate, decay = RATE, DECAY
        if k == sz.early + 3:
            rate = jnp.where(gain_row, GAIN_RATE, RATE)
            decay = jnp.where(gain_row, 0.0, DECAY)
        results = adam(held[0, k], total[k] * factor, held[1, k], held[2, k], rate, decay)
        for n in range(3):
            out[n * count + k] = results[n]
    row = row_ids((8, LANES))
    lost = jnp.broadcast_to(total[sz.early + 3, 6:7, 0:1], (8, LANES))
    out[3 * count] = jnp.where(row == 0, grad_norm, jnp.where(row == 1, lost, valid))
    early_shared()
    if sz.cores > 1:
        sent(late_fin.at[mine], p_send.at[1])


def adam(weight, grad, moment, square, rate, decay):
    moment = BETA_ONE * moment + (1.0 - BETA_ONE) * grad
    square = BETA_TWO * square + (1.0 - BETA_TWO) * grad * grad
    fix_one = 1.0 - BETA_ONE**STEP_NUM
    fix_two = 1.0 - BETA_TWO**STEP_NUM
    updated = weight - rate * (moment / fix_one / (jnp.sqrt(square / fix_two) + ADAM_EPS) + decay * weight)
    return updated, moment, square


def unpack_kernel(sz, packed, *refs):
    co, width = sz.co, sz.width
    count = sz.early + 5
    for n in range(3):
        new_in, new_mid, new_head, new_norm = refs[4 * n : 4 * n + 4]
        at = n * count
        for k in range(4):
            tile = jnp.concatenate([packed[at + h * 4 + k] for h in range(sz.halves)], axis=0)
            first, second = ((0, k), (1, k)) if k < 3 else ((2, 0), (2, 1))
            new_mid[first] = tile[:, :width]
            new_mid[second] = tile[:, width:]
        last = packed[at + sz.early + 4, 0 : co // 2]
        new_mid[2, 2, 0 : co // 2] = last[:, :width]
        new_mid[2, 2, co // 2 :] = last[:, width:]
        for ky in range(TAPS):
            for kx in range(TAPS):
                tile, row, lane = in_place(ky, kx)
                new_in[ky, kx] = packed[at + sz.early + tile, row : row + 4, lane : lane + co]
        new_norm[...] = packed[at + sz.early + 3, 0:4, 0:co]
        new_head[...] = packed[at + sz.early + 3, 4:6, 0:co]
    for k in range(3):
        refs[12 + k][...] = packed[3 * count, k : k + 1, 0:1]


def scratch_of(sz):
    grid, width, rows, ch, slots, steps = sz.grid, sz.width, sz.rows, sz.ch, sz.slots, sz.steps
    wide = TAPS * width

    def f32(*shape):
        return pltpu.VMEM(shape, F32)

    def bf16(*shape):
        return pltpu.VMEM(shape, BF16)

    dma = lambda *shape: pltpu.SemaphoreType.DMA(shape)
    return {
        "f_stage": f32(rows, 4, sz.local, LANES),
        "f_out": f32(rows, 4, sz.local, LANES),
        "m_own": pltpu.VMEM((sz.local, LANES), jnp.int32),
        "t_stage": f32(rows, steps, sz.local, LANES),
        "in_own": f32(3, TAPS, TAPS, 4, sz.co),
        "mid_own": f32(3, TAPS, TAPS, sz.co, width),
        "head_own": f32(3, 2, sz.co),
        "norm_own": f32(3, 4, sz.co),
        "marks_own": pltpu.VMEM((steps, sz.batch), jnp.int32),
        "held": f32(3, sz.early + 5, 8, LANES),
        "total": f32(sz.early + 5, 8, LANES),
        "small": f32(LANES, LANES),
        "ws_all": f32(ch, sz.co, LANES),
        "wm_all": bf16(ch, -(-sz.co // 16) * 16, sz.mid_lanes),
        "w_fwd": bf16(2 * width, 4 * wide),
        "w_bwd": bf16(2 * width, 4 * wide),
        "v_fwd": bf16(width, TAPS * 16),
        "v_bwd": bf16(2 * TAPS * 8, 4 * width),
        "head_back": bf16(width, 16),
        "head": bf16(16, width),
        "gains": f32(4, width, LANES),
        "current": f32(3, 3, grid, LANES),
        "states": f32(1 if slots > 1 else steps, 3, 3, grid, LANES),
        "mask": f32(5, grid, LANES),
        "feat32": f32(grid * 16, LANES),
        "feat": bf16(slots, grid + 2, 16, LANES),
        "conv": f32(slots, 2, grid, width, LANES),
        "slope": f32(slots, 2, grid, width, LANES),
        "norm_stats": f32(4, slots, width, LANES),
        "back_factors": f32(3, width, LANES),
        "hidden": f32(grid, width, LANES),
        "hidden_low": bf16(slots, grid + 2, wide, LANES),
        "mixed_low": bf16(slots, grid, width, LANES),
        "logits": f32(2, grid, LANES),
        "saved": f32(slots, SAVED, grid, LANES),
        "dy": f32(grid, width, LANES),
        "mixed_grad": f32(grid, width, LANES),
        "glog32": f32(grid * 16, LANES),
        "glog": bf16(slots, grid, 16, LANES),
        "g_pad": bf16(slots, grid + 2, width, LANES),
        "g_taps": bf16(grid + 2, wide, LANES),
        "gs_rows": f32(grid * 8, LANES),
        "grad_state": f32(3, grid, LANES),
        "d_mid": f32(wide, wide),
        "d_in": f32(TAPS * 16, width),
        "d_head": f32(16, width),
        "d_norm": f32(4, width, LANES),
        "loss": f32(grid, LANES),
        "early": f32(ch * sz.early, 9, LANES),
        "early_in": f32(sz.owned, sz.sources, 9, LANES),
        "early_fin": f32(sz.early, 9, LANES),
        "blank": f32(ch, rows, 1, LANES),
        "ssq_early": f32(ch, sz.early, 1, LANES),
        "late_pair": f32(2, 4, 8, LANES),
        "late_sum": f32(4, 8, LANES),
        "late_in": f32(sz.chips, sz.late, 8, LANES),
        "late_fin": f32(4, 8, LANES),
        "ready": pltpu.SemaphoreType.REGULAR,
        "local_sem": dma(16),
        "f_sem": dma(2),
        "t_sem": dma(2),
        "v_sem": dma(2),
        "w_sem": dma(2),
        "e_send": dma(1),
        "e_recv": dma(sz.owned),
        "g_send": dma(sz.owned),
        "g_recv": dma(1),
        "s_send": dma(sz.owned),
        "s_recv": dma(1),
        "b_send": dma(1),
        "b_recv": dma(1),
        "p_send": dma(2),
        "p_recv": dma(2),
    }


def shards(mesh, fields, targets, fluid, keyframes, *rest):
    params, firsts, seconds = rest[0:4], rest[4:8], rest[8:12]

    def native(leaves):
        return (leaves[0], jnp.swapaxes(leaves[1], 2, 3), leaves[2].T, leaves[3])

    params, firsts, seconds = native(params), native(firsts), native(seconds)
    sz = Sizes(mesh, fields.shape, targets.shape, params[0].shape[3])
    marks = keyframes.T
    vmem = pl.BlockSpec(memory_space=pltpu.VMEM)
    hbm = pl.BlockSpec(memory_space=pl.ANY)
    alone = sz.rows == 1 and sz.ch == 1
    packed = pl.pallas_call(
        functools.partial(train_kernel, sz),
        out_shape=pltpu.VMEM((3 * (sz.early + 5) + 1, 8, LANES), F32),
        in_specs=[hbm] * 16,
        out_specs=vmem,
        scratch_shapes=list(scratch_of(sz).values()),
        compiler_params=pltpu.CompilerParams(
            collective_id=None if alone else 0, has_side_effects=True, vmem_limit_bytes=60 << 20
        ),
        name="train",
    )(fields.reshape(sz.rows, sz.per_rows, *fields.shape[1:]), targets, fluid, marks, *params, *firsts, *seconds)
    shapes = [jax.ShapeDtypeStruct(leaf.shape, F32) for leaf in params] * 3
    shapes += [jax.ShapeDtypeStruct((1, 1), F32)] * 3
    results = pl.pallas_call(
        functools.partial(unpack_kernel, sz),
        out_shape=tuple(shapes),
        in_specs=[vmem],
        out_specs=tuple([vmem] * 15),
        name="unpack",
    )(pltpu.with_memory_space_constraint(packed, pltpu.VMEM))
    outs = []
    for n in range(3):
        outs.extend(native(results[4 * n : 4 * n + 4]))
    return (*outs, *[leaf.reshape(()) for leaf in results[12:]])


def solution(mesh):
    split = (P(None, None, None, "ch"), P(None, None, None, "ch"), P("ch", None), P(None, "ch"))
    return jax.shard_map(
        functools.partial(shards, mesh),
        mesh=mesh,
        in_specs=(
            P(None, None, "rows", None),
            P(None, None, "rows", None),
            P("rows", None),
            P(),
            *split,
            *split,
            *split,
        ),
        out_specs=(*split, *split, *split, P(), P(), P()),
        check_vma=False,
    )
```

```python
import functools

import jax
import jax.numpy as jnp
from jax import lax
from jax.experimental import pallas as pl
from jax.experimental.pallas import tpu as pltpu
from jax.sharding import PartitionSpec as P

GROUPS = 8
NEAR = (-1, 0, 1)
STEP_NUM = 10
TIME_STEP = 0.5
COURANT = 0.8
FORCE_WEIGHT = 0.5
NORM_EPS = 1e-05
CLIP = 0.0001
BETA_ONE = 0.9
BETA_TWO = 0.999
ADAM_EPS = 1e-10
RATE = 0.1
GAIN_RATE = 0.6
DECAY = 0.01

MESH = pl.DeviceIdType.MESH
F32 = jnp.float32
BF16 = jnp.bfloat16
LANES = 128
GSIZE = 8
TAPS = 3
PARTS = (2, 2)
SAVED = 11
NT = (((1,), (1,)), ((), ()))


def lane_ids(shape):
    return lax.broadcasted_iota(jnp.int32, shape, len(shape) - 1)


def row_ids(shape):
    return lax.broadcasted_iota(jnp.int32, shape, 0)


def from_left(x):
    return jnp.where(lane_ids(x.shape) == 0, jnp.zeros_like(x), pltpu.roll(x, 1, 1))


def from_right(x):
    size = x.shape[1]
    return jnp.where(lane_ids(x.shape) == size - 1, jnp.zeros_like(x), pltpu.roll(x, size - 1, 1))


def from_above(x):
    return jnp.where(row_ids(x.shape) == 0, 0.0, pltpu.roll(x, 1, 0))


def from_below(x):
    size = x.shape[0]
    return jnp.where(row_ids(x.shape) == size - 1, 0.0, pltpu.roll(x, size - 1, 0))


def diff_rows(x):
    return from_below(x) - from_above(x)


def column(x, d):
    if d == 0:
        return x
    size = x.shape[1]
    lane = lane_ids(x.shape)
    inside = lane < size - d if d > 0 else lane >= -d
    return jnp.where(inside, pltpu.roll(x, -d % size, 1), jnp.zeros_like(x))


def columns_of(x, reach):
    return {d: column(x, d) for d in range(-reach, reach + 1)}


def rows_around(x):
    return from_below(x) + from_above(x)


def quadratic(s):
    return (0.5 * s * (s + 1.0), 1.0 - s * s, 0.5 * s * (s - 1.0))


def quadratic_slope(s):
    return (s + 0.5, -2.0 * s, s - 0.5)


def wrap(x, n):
    return x & (n - 1) if n & (n - 1) == 0 else lax.rem(x, n)


def partner(x, k, n):
    return x ^ k if n & (n - 1) == 0 else lax.rem(x + k, n)


def far_first(n):
    return reversed(range(1, n))


def far_loop(least, n, send):
    def body(i, carry):
        send(n - 1 - i)
        return carry

    if n > least:
        lax.fori_loop(0, n - least, body, 0)


def dot(a, b):
    return jnp.dot(a, b, preferred_element_type=F32)


def dot_nt(a, b):
    return lax.dot_general(a, b, NT, preferred_element_type=F32)


def row_pair(ref, i, extra=None):
    depth = ref.shape[1] * TAPS
    sides = []
    for k in range(2):
        side = ref[pl.ds(i + k, TAPS)].reshape(depth, LANES)
        if extra is not None:
            side = jnp.concatenate([side, extra[i + k]], axis=0)
        sides.append(side)
    return jnp.concatenate(sides, axis=1)


def side_by_side(ref, first):
    return jnp.concatenate([ref[i] for i in range(first, ref.shape[0])], axis=1)


def four_rows(ref, i):
    taps = ref.shape[1] // 64
    parts = []
    for n in range(taps):
        sides = [ref[pl.ds(i + 2 * k, 4), n * 64 : (n + 1) * 64].reshape(4 * 64, LANES) for k in range(2)]
        parts.append(jnp.concatenate(sides, axis=1))
    return jnp.concatenate(parts, axis=0) if taps > 1 else parts[0]


def rows_of(p):
    half = p.shape[0] // 2
    return [p[o * half : (o + 1) * half, k * LANES : (k + 1) * LANES] for k in range(2) for o in range(2)]


def two_rows(blocks):
    zero = jnp.zeros_like(blocks[0])
    first = jnp.concatenate(list(blocks) + [zero], axis=1)
    second = jnp.concatenate([zero] + list(blocks), axis=1)
    return jnp.concatenate([first, second], axis=0)


def combine(part, height):
    return (
        part[height : 2 * height] + from_left(part[:height]) + from_right(part[2 * height : 3 * height])
    )


def group_sum(x):
    return jnp.sum(jnp.sum(x.reshape(-1, GSIZE, LANES), axis=1), axis=1, keepdims=True)


def spread(x):
    return jnp.broadcast_to(x[:, :, None], (x.shape[0], GSIZE, LANES)).reshape(-1, LANES)


def loop(count, per, body, carry):
    per = min(per, count)

    def several(it, carry):
        for k in range(per):
            carry = body(it * per + k, carry)
        return carry

    if count == per:
        return several(0, carry)
    return lax.fori_loop(0, count // per, several, carry)


def in_place(ky, kx):
    at = ky * 16 + kx * 4
    lane = 64 if at >= 24 else 0
    at = at % 24
    return at // 8, at % 8, lane


class Sizes:
    def __init__(self, mesh, fields_shape, targets_shape, co):
        self.ch = mesh.shape["ch"]
        self.rows = mesh.shape["rows"]
        self.batch = fields_shape[0]
        self.local = fields_shape[2]
        self.grid = self.local * self.rows
        self.cols = fields_shape[3]
        self.steps = targets_shape[0]
        self.co = co
        self.width = co * self.ch
        self.per_rows = self.batch // self.rows
        self.ways = self.ch if self.per_rows == self.ch else 1
        assert self.per_rows == self.ways and self.batch % self.rows == 0
        assert self.cols == LANES
        slot = self.grid * self.width * LANES * 20
        self.slots = self.steps if slot * self.steps < (24 << 20) else 1
        self.halves = co // 8
        self.early = 4 * self.halves
        self.owned = -(-self.early // self.rows)
        self.sources = self.ways * self.rows
        self.cores = 2 if self.ways > 1 else 1
        self.chips = self.sources // self.cores
        self.late = 4 // self.cores
        assert self.ways % self.cores == 0
        self.mid_lanes = TAPS * TAPS * self.width
        assert self.width == 64 and co % 8 == 0


IN_AT = 64
HEAD_AT = IN_AT + 36
NORM_AT = HEAD_AT + 2
LOSS_AT = NORM_AT + 4


def train_kernel(
    sz,
    fields,
    targets,
    fluid,
    keyframes,
    w_in,
    w_mid,
    w_head,
    norms,
    first_in,
    first_mid,
    first_head,
    first_norm,
    second_in,
    second_mid,
    second_head,
    second_norm,
    out,
    *scratch,
):
    z = dict(zip(scratch_of(sz), scratch))
    f_stage = z["f_stage"]
    f_out = z["f_out"]
    m_own = z["m_own"]
    t_stage = z["t_stage"]
    in_own = z["in_own"]
    mid_own = z["mid_own"]
    head_own = z["head_own"]
    norm_own = z["norm_own"]
    marks_own = z["marks_own"]
    held = z["held"]
    total = z["total"]
    small = z["small"]
    ws_all = z["ws_all"]
    wm_all = z["wm_all"]
    w_fwd = z["w_fwd"]
    w_bwd = z["w_bwd"]
    v_fwd = z["v_fwd"]
    v_bwd = z["v_bwd"]
    head_back = z["head_back"]
    head = z["head"]
    gains = z["gains"]
    current = z["current"]
    states = z["states"]
    mask = z["mask"]
    feat32 = z["feat32"]
    feat = z["feat"]
    conv = z["conv"]
    slope = z["slope"]
    norm_stats = z["norm_stats"]
    back_factors = z["back_factors"]
    hidden = z["hidden"]
    hidden_low = z["hidden_low"]
    mixed_low = z["mixed_low"]
    logits = z["logits"]
    saved = z["saved"]
    dy = z["dy"]
    mixed_grad = z["mixed_grad"]
    glog32 = z["glog32"]
    glog = z["glog"]
    g_pad = z["g_pad"]
    g_taps = z["g_taps"]
    gs_rows = z["gs_rows"]
    grad_state = z["grad_state"]
    d_mid = z["d_mid"]
    d_in = z["d_in"]
    d_head = z["d_head"]
    d_norm = z["d_norm"]
    loss = z["loss"]
    early = z["early"]
    early_in = z["early_in"]
    early_fin = z["early_fin"]
    blank = z["blank"]
    ssq_early = z["ssq_early"]
    late_pair = z["late_pair"]
    late_sum = z["late_sum"]
    late_in = z["late_in"]
    late_fin = z["late_fin"]
    ready = z["ready"]
    local_sem = z["local_sem"]
    f_sem = z["f_sem"]
    t_sem = z["t_sem"]
    v_sem = z["v_sem"]
    w_sem = z["w_sem"]
    e_send = z["e_send"]
    e_recv = z["e_recv"]
    g_send = z["g_send"]
    g_recv = z["g_recv"]
    s_send = z["s_send"]
    s_recv = z["s_recv"]
    b_send = z["b_send"]
    b_recv = z["b_recv"]
    p_send = z["p_send"]
    p_recv = z["p_recv"]
    c = lax.axis_index("ch")
    r = lax.axis_index("rows")
    width, grid, steps = sz.width, sz.grid, sz.steps
    co = sz.co

    def row_peer(k):
        return partner(r, k, sz.rows)

    def ch_peer(k):
        return partner(c, k, sz.ch)

    def sample_of(row):
        return row * sz.per_rows + (c if sz.ways > 1 else 0)

    def block(work):
        pl.when(r >= 0)(work)

    peers = sz.rows - 1 + sz.ch - 1
    if peers:
        barrier = pltpu.get_barrier_semaphore()
        for k in far_first(sz.rows):
            pl.semaphore_signal(barrier, inc=1, device_id=(c, row_peer(k)), device_id_type=MESH)
        for k in far_first(sz.ch):
            pl.semaphore_signal(barrier, inc=1, device_id=(ch_peer(k), r), device_id_type=MESH)

    def remote(src, dst, send, recv, where):
        return pltpu.make_async_remote_copy(
            src_ref=src, dst_ref=dst, send_sem=send, recv_sem=recv, device_id=where, device_id_type=MESH
        )

    def arrived(ref, sem):
        remote(ref, ref, sem, sem, (c, r)).wait_recv()

    def sent(ref, sem):
        remote(ref, ref, sem, sem, (c, r)).wait_send()

    def but_one(ref):
        return ref.at[pl.ds(0, ref.shape[0] - 1)]

    own = [
        pltpu.make_async_copy(src, dst, local_sem.at[n])
        for n, (src, dst) in enumerate(
            (
                (w_in, in_own.at[0]),
                (w_head, head_own.at[0]),
                (norms, norm_own.at[0]),
                (w_mid, mid_own.at[0]),
                (fields.at[:, c if sz.ways > 1 else 0], f_out.at[:, pl.ds(0, 3)]),
                (fluid, m_own),
                (targets.at[:, sample_of(r)], t_stage.at[r]),
                (keyframes, marks_own),
                (first_in, in_own.at[1]),
                (first_mid, mid_own.at[1]),
                (first_head, head_own.at[1]),
                (first_norm, norm_own.at[1]),
                (second_in, in_own.at[2]),
                (second_mid, mid_own.at[2]),
                (second_head, head_own.at[2]),
                (second_norm, norm_own.at[2]),
            )
        )
    ]
    for copy in own:
        copy.start()
    small[...] = jnp.zeros_like(small)
    for n in range(4):
        own[n].wait()
    for ky in range(TAPS):
        for kx in range(TAPS):
            at = IN_AT + (ky * TAPS + kx) * 4
            small[at : at + 4, 0:co] = in_own[0, ky, kx]
    small[HEAD_AT : HEAD_AT + 2, 0:co] = head_own[0]
    small[NORM_AT : NORM_AT + 4, 0:co] = norm_own[0]
    ws_all[c] = jnp.transpose(small[...])[0:co]
    packed = jnp.concatenate([mid_own[0, ky, kx] for kx in range(TAPS) for ky in range(TAPS)], axis=1)
    wm_all[c, 0:co, :] = packed.astype(BF16)
    own[4].wait()
    own[5].wait()
    for row in range(sz.rows):
        f_out[row, 3] = m_own[...].astype(F32)
    f_stage[r] = f_out[r]
    if peers:
        pl.semaphore_wait(barrier, peers)

    for k in far_first(sz.rows):
        row = row_peer(k)
        remote(f_out.at[row], f_stage.at[r], f_sem.at[0], f_sem.at[1], (c, row)).start()
    for k in far_first(sz.ch):
        remote(ws_all.at[c], ws_all.at[c], v_sem.at[0], v_sem.at[1], (ch_peer(k), r)).start()
    for k in far_first(sz.ch):
        remote(wm_all.at[c], wm_all.at[c], w_sem.at[0], w_sem.at[1], (ch_peer(k), r)).start()
    for k in far_first(sz.rows):
        src = targets.at[:, sample_of(row_peer(k))]
        remote(src, t_stage.at[r], t_sem.at[0], t_sem.at[1], (c, row_peer(k))).start()
    row_groups = ((f_stage, f_sem), (t_stage, t_sem)) if sz.rows > 1 else ()
    ch_groups = ((ws_all, v_sem), (wm_all, w_sem)) if sz.ch > 1 else ()
    if peers:
        for k in far_first(sz.ch):
            pl.semaphore_signal(ready, inc=1, device_id=(ch_peer(k), r), device_id_type=MESH)

    for n in range(8, 16):
        own[n].wait()
    for n in range(3):
        mid = [[mid_own[n, ky, kx] for kx in range(TAPS)] for ky in range(TAPS)]
        sides = [(mid[0][kx], mid[1][kx]) for kx in range(TAPS)] + [(mid[2][0], mid[2][1])]
        for k, side in enumerate(sides):
            tile = jnp.concatenate(side, axis=1)
            for h in range(sz.halves):
                held[n, h * 4 + k] = tile[h * 8 : (h + 1) * 8]
        for k in range(sz.early, sz.early + 5):
            held[n, k] = jnp.zeros((8, LANES), F32)
        for ky in range(TAPS):
            for kx in range(TAPS):
                tile, row, lane = in_place(ky, kx)
                held[n, sz.early + tile, row : row + 4, lane : lane + co] = in_own[n, ky, kx]
        held[n, sz.early + 3, 0:4, 0:co] = norm_own[n]
        held[n, sz.early + 3, 4:6, 0:co] = head_own[n]
        last = mid[2][2]
        held[n, sz.early + 4, 0 : co // 2] = jnp.concatenate([last[: co // 2], last[co // 2 :]], axis=1)

    for i in (0, grid + 1):
        g_taps[i] = jnp.zeros_like(g_taps[i])
    for ref in (feat, hidden_low, g_pad):
        for slot in range(sz.slots):
            ref[slot, 0] = jnp.zeros_like(ref[slot, 0])
            ref[slot, grid + 1] = jnp.zeros_like(ref[slot, 0])
    feat32[...] = jnp.zeros_like(feat32)
    glog32[...] = jnp.zeros_like(glog32)
    for ref in (d_mid, d_in, d_head, d_norm, loss):
        ref[...] = jnp.zeros_like(ref)

    if ch_groups:
        arrived(but_one(ws_all), v_sem.at[1])
    tail = ws_all[...].reshape(width, LANES)
    tail_t = jnp.transpose(tail)
    parts = []
    for ky in range(TAPS):
        at = IN_AT + ky * 12
        parts.append(jnp.concatenate([tail[:, at : at + 12], jnp.zeros((width, 4), F32)], axis=1))
    v_fwd[...] = jnp.concatenate(parts, axis=1).astype(BF16)
    pieces = []
    for ky in range(TAPS):
        column_taps = []
        for kx in range(TAPS):
            at = IN_AT + ((2 - ky) * TAPS + 2 - kx) * 4
            column_taps += [tail_t[at : at + 4], jnp.zeros((4, width), F32)]
        pieces.append(jnp.concatenate(column_taps, axis=0))
    v_bwd[...] = two_rows(pieces).astype(BF16)
    head_back[...] = jnp.concatenate([tail[:, HEAD_AT : HEAD_AT + 2], jnp.zeros((width, 14), F32)], axis=1).astype(BF16)
    head[...] = jnp.concatenate([tail_t[HEAD_AT : HEAD_AT + 2], jnp.zeros((14, width), F32)], axis=0).astype(BF16)
    for k in range(4):
        gains[k] = jnp.broadcast_to(tail[:, NORM_AT + k : NORM_AT + k + 1], (width, LANES))

    own[7].wait()
    marks = marks_own[...].astype(F32)
    valid = jnp.sum(jnp.sum(marks, axis=1, keepdims=True), axis=0, keepdims=True) * float(grid * sz.cols)
    inv_count = 1.0 / valid
    picked = jnp.where(lane_ids(marks.shape) == sample_of(r), marks, 0.0)
    marked = jnp.sum(picked, axis=1, keepdims=True)

    def key_of(t):
        return jnp.sum(jnp.where(row_ids(marked.shape) == t, marked, 0.0), axis=0, keepdims=True)

    def second_layer():
        if ch_groups:
            arrived(but_one(wm_all), w_sem.at[1])
        kind = BF16 if co % 16 == 0 else F32
        mid = jnp.concatenate([wm_all[k, 0:co, :].astype(kind) for k in range(sz.ch)], axis=0)
        for n, kx in enumerate((1, 0, 2)):
            at = [(kx * TAPS + ky) * width for ky in range(TAPS)]
            w_fwd[:, n * 4 * width : (n + 1) * 4 * width] = two_rows([mid[:, a : a + width] for a in at]).astype(BF16)

    def second_layer_back():
        for n, kx in enumerate((1, 0, 2)):
            at = n * 4 * width
            blocks = [w_fwd[0:width, at + ky * width : at + (ky + 1) * width].astype(F32) for ky in range(TAPS)]
            at = kx * 4 * width
            w_bwd[:, at : at + 4 * width] = two_rows([jnp.transpose(b) for b in reversed(blocks)]).astype(BF16)

    second_layer()

    for ref, sem in row_groups[:1]:
        arrived(but_one(ref), sem.at[1])
    for q in range(3):
        current[q, 1] = jnp.concatenate([f_stage[row, q] for row in range(sz.rows)], axis=0)
    mask[2] = jnp.concatenate([f_stage[row, 3] for row in range(sz.rows)], axis=0)
    for q in range(3):
        for d in (-1, 1):
            current[q, d + 1] = column(current[q, 1], d)
    for d in (-2, -1, 1, 2):
        mask[d + 2] = column(mask[2], d)
    for d in NEAR:
        feat32[pl.ds((d + 1) * 4 + 3, grid, stride=16), :] = mask[d + 2]

    def all_targets():
        if row_groups:
            arrived(but_one(t_stage), t_sem.at[1])
        own[6].wait()
    def parts_of(count):
        size = width // count
        return [slice(n * size, (n + 1) * size) for n in range(count)]

    def conv_and_stats(x_ref, w, layer, slot, span=slice(0, 64)):
        zero = jnp.zeros((span.stop - span.start, LANES), F32)

        def body(it, carry):
            base, total, squares = carry
            i = it * 4
            if layer:
                rows = rows_of(dot(w[...], four_rows(x_ref, i)))
            else:
                rows = []
                for k in range(2):
                    p = dot(w[span], row_pair(x_ref, i + 2 * k))
                    rows += [p[:, :LANES], p[:, LANES:]]
            base = jnp.where(it == 0, rows[0], base)
            for j in range(4):
                conv[slot, layer, i + j, span] = rows[j]
                d = rows[j] - base
                total = total + d
                squares = squares + d * d
            return base, total, squares

        base, total, squares = loop(grid // 4, 8, body, (zero, zero, zero))
        lane_mean = base + total * (1.0 / grid)
        lane_dev = squares - total * total * (1.0 / grid)
        count = float(GSIZE * LANES)
        middle = spread(group_sum(base) * (1.0 / count))
        d = lane_mean - middle
        first = spread(group_sum(d) * (1.0 / count))
        second = spread(group_sum(lane_dev + grid * d * d) * (1.0 / (count * grid)))
        norm_stats[2 * layer, slot, span] = middle + first
        norm_stats[2 * layer + 1, slot, span] = lax.rsqrt(second - first * first + NORM_EPS)

    def silu_parts(half):
        t = jnp.tanh(half)
        a = 1.0 + t
        h = half * a
        return h, a + h * (1.0 - t)

    def half_affine(layer, slot, span=slice(0, 64)):
        k = 2 * layer
        mean, inv = norm_stats[k, slot, span], norm_stats[k + 1, slot, span]
        scale = 0.5 * inv * gains[k, span]
        return scale, 0.5 * gains[k + 1, span] - mean * scale

    def step_forward(t, slot, first):
        last = t == steps - 1
        if sz.slots == 1:
            for q in range(3):
                for d in NEAR:
                    if first:
                        states[t, q, d + 1] = current[q, d + 1]
                    else:
                        current[q, d + 1] = states[t, q, d + 1]
        @block
        def _():
            x = [{d: current[q, d + 1] for d in NEAR} for q in range(3)]
            for q in range(3):
                for d in NEAR:
                    feat32[pl.ds((d + 1) * 4 + q, grid, stride=16), :] = x[q][d]

            def pack(it, carry):
                for k in range(4):
                    i = it * 4 + k
                    feat[slot, i + 1] = feat32[pl.ds(pl.multiple_of(i * 16, 16), 16), :].astype(BF16)
                return carry

            loop(grid // 4, 8, pack, 0)

            for span in parts_of(PARTS[0]):
                conv_and_stats(feat.at[slot], v_fwd, 0, slot, span)
        @block
        def _():
            def norm_one(span, it, carry):
                for k in range(2):
                    i = it * 2 + k
                    h, slope[slot, 0, i, span] = silu_parts(conv[slot, 0, i, span] * mul + add)
                    hidden[i, span] = h
                    low = h.astype(BF16)
                    for kx, tap in enumerate((low, from_left(low), from_right(low))):
                        hidden_low[slot, i + 1, kx * width + span.start : kx * width + span.stop] = tap
                return carry

            for span in parts_of(PARTS[0]):
                mul, add = half_affine(0, slot, span)
                loop(grid // 2, 16, functools.partial(norm_one, span), 0)

            conv_and_stats(hidden_low.at[slot], w_fwd, 1, slot)
        @block
        def _():
            if first and t == min(1, steps - 1):
                second_layer_back()
            mul, add = half_affine(1, slot)

            def norm_two(it, carry):
                i = it * 2
                lows = []
                for k in range(2):
                    h, slope[slot, 1, i + k] = silu_parts(conv[slot, 1, i + k] * mul + add)
                    low = (hidden[i + k] + h).astype(BF16)
                    mixed_low[slot, i + k] = low
                    lows.append(low)
                p = dot(head[...], jnp.concatenate(lows, axis=1))
                for k in range(2):
                    logits[0, pl.ds(i + k, 1), :] = p[0:1, k * LANES : (k + 1) * LANES]
                    logits[1, pl.ds(i + k, 1), :] = p[1:2, k * LANES : (k + 1) * LANES]
                return carry

            loop(grid // 2, 16, norm_two, 0)

        if first and t == 0:
            all_targets()
        @block
        def _():
            x = [{d: current[q, d + 1] for d in NEAR} for q in range(3)]
            f0, f1 = jnp.tanh(logits[0]), jnp.tanh(logits[1])
            force0, force1 = columns_of(f0, 1), columns_of(f1, 1)
            u1 = {d: x[1][d] + TIME_STEP * force0[d] for d in NEAR}
            v1 = {d: x[2][d] + TIME_STEP * force1[d] for d in NEAR}
            sy = COURANT * jnp.tanh(u1[0])
            sx = COURANT * jnp.tanh(v1[0])
            wy, wx = quadratic(sy), quadratic(sx)
            dwy, dwx = quadratic_slope(sy), quadratic_slope(sx)
            moved = []
            for n, q in enumerate((x[0], u1, v1)):
                lines = [(from_above(q[d]), q[d], from_below(q[d])) for d in NEAR]
                along = [wx[0] * lines[0][a] + wx[1] * lines[1][a] + wx[2] * lines[2][a] for a in range(3)]
                moved.append(wy[0] * along[0] + wy[1] * along[1] + wy[2] * along[2])
                if last and n:
                    continue
                slant = [dwx[0] * lines[0][a] + dwx[1] * lines[1][a] + dwx[2] * lines[2][a] for a in range(3)]
                saved[slot, 4 + n] = dwy[0] * along[0] + dwy[1] * along[1] + dwy[2] * along[2]
                saved[slot, 7 + n] = wy[0] * slant[0] + wy[1] * slant[1] + wy[2] * slant[2]
            rho2 = moved[0]
            if first and not last:
                solid = {d: mask[d + 2] for d in range(-2, 3)}
                rho2s, u2, v2 = columns_of(rho2, 1), columns_of(moved[1], 1), columns_of(moved[2], 2)
                div = {d: 0.5 * (diff_rows(u2[d]) + (v2[d + 1] - v2[d - 1])) for d in NEAR}
                press = {d: -0.25 * solid[d] * div[d] for d in NEAR}
                press = 0.25 * solid[0] * (rows_around(press[0]) + press[1] + press[-1] - div[0])
                press = columns_of(press, 3)
                div[2], div[-2] = column(div[0], 2), column(div[0], -2)
                press = {
                    d: 0.25 * solid[d] * (rows_around(press[d]) + press[d + 1] + press[d - 1] - div[d])
                    for d in range(-2, 3)
                }
                for d in NEAR:
                    current[0, d + 1] = rho2s[d]
                    current[1, d + 1] = solid[d] * (u2[d] - 0.5 * diff_rows(press[d]))
                    current[2, d + 1] = solid[d] * (v2[d] - 0.5 * (press[d + 1] - press[d - 1]))
            miss = rho2 - jnp.concatenate([t_stage[row, t] for row in range(sz.rows)], axis=0)
            pull = key_of(t) * miss
            if first:
                loss[...] += FORCE_WEIGHT * (f0 * f0 + f1 * f1) + pull * miss
            saved[slot, 0] = f0
            saved[slot, 1] = f1
            saved[slot, 2] = sy
            saved[slot, 3] = sx
            saved[slot, 10] = pull

    for t in range(steps):
        step_forward(t, t if sz.slots > 1 else 0, True)
    for ref, sem in row_groups + ch_groups:
        sent(but_one(ref), sem.at[0])

    def owner_of(j):
        return wrap(j, sz.rows)

    me = c * sz.rows + r if sz.ways > 1 else r
    chip_slot = (c // 2) * sz.rows + r if sz.ways > 1 else r

    def by_owned(action):
        least, more = sz.early // sz.rows, sz.early % sz.rows
        if more:
            pl.when(r < more)(functools.partial(action, least + 1))
            pl.when(r >= more)(functools.partial(action, least))
        else:
            action(least)

    def for_owned(action):
        for m in range(sz.owned):
            j = r + m * sz.rows
            if (m + 1) * sz.rows <= sz.early:
                action(m, j)
            else:
                pl.when(j < sz.early)(functools.partial(action, m, j))

    def early_start():
        low_half = lane_ids((width, LANES)) < 64
        tiles = [d_mid[kx * width : (kx + 1) * width, 0:LANES] for kx in range(TAPS)]
        rest = [d_mid[kx * width : (kx + 1) * width, LANES:] for kx in range(2)]
        tiles.append(jnp.concatenate(rest, axis=1))
        last = d_mid[2 * width : 3 * width, LANES:]
        for shard in range(sz.ch):
            for h in range(sz.halves):
                at = shard * co + h * 8
                for n, tile in enumerate(tiles):
                    early[shard * sz.early + h * 4 + n, 0:8] = tile[at : at + 8]
            ends = last[shard * co : (shard + 1) * co]
            ends = jnp.concatenate([ends[: co // 2], ends[co // 2 :]], axis=1)
            for j in range(sz.early):
                early[shard * sz.early + j, 8:9] = ends[j : j + 1]
        if sz.ch > 1:
            pl.semaphore_wait(ready, sz.ch - 1)
        def send(k):
            dc, k = k // sz.early, wrap(k, sz.early)
            shard = ch_peer(dc)
            j = partner(r, k, sz.early) if sz.early == sz.rows else wrap(r + k, sz.early)
            slot = j // sz.rows if sz.owned > 1 else 0
            copy = remote(
                early.at[shard * sz.early + j], early_in.at[slot, me], e_send.at[0], e_recv.at[slot], (shard, owner_of(j))
            )
            if sz.early == sz.rows:
                copy.start()
            else:
                pl.when(jnp.logical_or(dc > 0, owner_of(j) != r))(copy.start)

        far_loop(1 if sz.early == sz.rows else 0, sz.ways * sz.early, send)

    def early_sum():
        def total(m, j):
            early_in[m, me] = early[c * sz.early + j]
            if sz.sources > 1:
                arrived(but_one(early_in.at[m]), e_recv.at[m])
            acc = early_in[m, 0]
            for k in range(1, sz.sources):
                acc = acc + early_in[m, k]
            early_fin[j] = acc
            line = ssq_early.at[c, j]
            line[...] = jnp.sum(acc * acc, axis=0, keepdims=True)
            for dc in far_first(sz.ch):
                for k in reversed(range(sz.rows)):
                    remote(line, line, s_send.at[m], s_recv.at[0], (ch_peer(dc), row_peer(k))).start()
            for k in far_first(sz.rows):
                remote(early_fin.at[j], early_fin.at[j], g_send.at[m], g_recv.at[0], (c, row_peer(k))).start()

        for_owned(total)

    def early_left():
        if sz.sources > 1:
            by_owned(lambda n: sent(early.at[pl.ds(0, sz.ways * sz.early - n)], e_send.at[0]))

    def put_line(j, acc):
        ssq_early[c, j] = jnp.sum(acc * acc, axis=0, keepdims=True)

    def early_end():
        if sz.rows > 1:
            by_owned(lambda n: arrived(early_fin.at[pl.ds(0, sz.early - n)], g_recv.at[0]))
        for j in range(sz.early):
            acc = early_fin[j]
            total[j] = acc[0:8]
            total[sz.early + 4, j : j + 1] = acc[8:9]
            if sz.rows > 1:
                pl.when(r != j % sz.rows)(functools.partial(put_line, j, acc))
        if sz.ch > 1:
            arrived(but_one(ssq_early), s_recv.at[0])

    def early_shared():
        def last(m, j):
            if sz.ch > 1:
                sent(but_one(blank), s_send.at[m])
            if sz.rows > 1:
                sent(but_one(early_in.at[m, pl.ds(0, sz.rows)]), g_send.at[m])

        for_owned(last)

    def norm_back(k, slot, sums_d, sums_c, span=slice(0, 64)):
        gain, mean, inv = gains[k, span], norm_stats[k, slot, span], norm_stats[k + 1, slot, span]
        sums_d = 0.5 * sums_d
        sums_n = inv * (0.5 * sums_c - mean * sums_d)
        scale = 1.0 / float(GSIZE * LANES * grid)
        m1 = spread(group_sum(sums_d * gain) * scale)
        m2 = spread(group_sum(sums_n * gain) * scale)
        d_norm[k, span] += sums_n
        d_norm[k + 1, span] += sums_d
        fc = inv * inv * m2
        back_factors[0, span] = 0.5 * inv * gain
        back_factors[1, span] = inv * m1 - fc * mean
        back_factors[2, span] = fc

    def mid_grad(slot, part, parts):
        span = grid // parts
        rows = range(part * span, (part + 1) * span)
        center = slice(0, width)
        left = [g_taps[i + 1] for i in rows]
        right = [hidden_low[slot, i : i + TAPS, center].reshape(TAPS * width, LANES) for i in rows]
        d_mid[...] += dot_nt(jnp.concatenate(left, axis=1), jnp.concatenate(right, axis=1))

    core = wrap(c, sz.cores)
    pack = late_pair.at[core] if sz.cores > 1 else late_sum

    def late_misc():
        columns = [jnp.sum(d_norm[k], axis=1, keepdims=True) for k in range(4)]
        columns.append(jnp.zeros((width, LANES - 4), F32))
        lines = jnp.transpose(jnp.concatenate(columns, axis=1))
        loss_sum = jnp.sum(jnp.sum(loss[...], axis=1, keepdims=True), axis=0, keepdims=True)
        pack[3] = jnp.zeros((8, LANES), F32)
        pack[3, 0:4, 0:width] = lines[0:4, :]
        pack[3, 4:6, 0:width] = d_head[0:2]
        pack[3, 6:7, 0:width] = jnp.broadcast_to(loss_sum, (1, width))

    def step_backward(t, slot):
        @block
        def _():
            sy, sx = saved[slot, 2], saved[slot, 3]
            f0, f1 = saved[slot, 0], saved[slot, 1]
            wy, wx = quadratic(sy), quadratic(sx)
            grads = [2.0 * inv_count * saved[slot, 10]]
            if t < steps - 1:
                solid = {d: mask[d + 2] for d in NEAR}
                grads[0] = grads[0] + grad_state[0]
                gu, gv = columns_of(solid[0] * grad_state[1], 1), columns_of(solid[0] * grad_state[2], 2)
                one = {d: 0.125 * solid[d] * (diff_rows(gu[d]) + (gv[d + 1] - gv[d - 1])) for d in NEAR}
                two = 0.25 * solid[0] * (rows_around(one[0]) + one[1] + one[-1])
                two = columns_of(two, 2)
                g_div = {
                    d: one[d] + two[d] + 0.25 * solid[d] * (rows_around(two[d]) + two[d + 1] + two[d - 1]) for d in NEAR
                }
                grads.append(gu[0] + 0.5 * diff_rows(g_div[0]))
                grads.append(gv[0] + 0.5 * (g_div[1] - g_div[-1]))
            spots = []
            g_sy = g_sx = 0.0
            for n, g in enumerate(grads):
                g_sy = g_sy + g * saved[slot, 4 + n]
                g_sx = g_sx + g * saved[slot, 7 + n]
                lines = []
                for b in range(3):
                    gb = wx[b] * g
                    lines.append(from_below(wy[0] * gb) + wy[1] * gb + from_above(wy[2] * gb))
                spots.append(column(lines[0], 1) + lines[1] + column(lines[2], -1))
            ty, tx = sy * (1.0 / COURANT), sx * (1.0 / COURANT)
            g_u1 = g_sy * (COURANT * (1.0 - ty * ty))
            g_v1 = g_sx * (COURANT * (1.0 - tx * tx))
            if t < steps - 1:
                g_u1, g_v1 = spots[1] + g_u1, spots[2] + g_v1
            l0 = (TIME_STEP * g_u1 + 2.0 * FORCE_WEIGHT * inv_count * f0) * (1.0 - f0 * f0)
            l1 = (TIME_STEP * g_v1 + 2.0 * FORCE_WEIGHT * inv_count * f1) * (1.0 - f1 * f1)
            if t > 0:
                grad_state[0] = spots[0]
                grad_state[1] = g_u1
                grad_state[2] = g_v1
            if sz.slots > 1 and t < steps - 1:
                for part in range(2):
                    mid_grad(t + 1, part, 2)
            glog32[pl.ds(0, grid, stride=16), :] = l0
            glog32[pl.ds(1, grid, stride=16), :] = l1

            def pack(it, carry):
                for k in range(4):
                    i = it * 4 + k
                    glog[slot, i] = glog32[pl.ds(pl.multiple_of(i * 16, 16), 16), :].astype(BF16)
                return carry

            loop(grid // 4, 8, pack, 0)

        @block
        def _():
            def back_a(span, it, carry):
                sums_d, sums_n = carry
                i = it * 2
                gl = jnp.concatenate([glog[slot, i], glog[slot, i + 1]], axis=1)
                p = dot(head_back[span], gl)
                for k in range(2):
                    g = p[:, k * LANES : (k + 1) * LANES]
                    mixed_grad[i + k, span] = g
                    d = g * slope[slot, 1, i + k, span]
                    dy[i + k, span] = d
                    sums_d = sums_d + d
                    sums_n = sums_n + d * conv[slot, 1, i + k, span]
                return sums_d, sums_n

            for span in parts_of(PARTS[1]):
                zero = jnp.zeros((span.stop - span.start, LANES), F32)
                sums = loop(grid // 2, 16, functools.partial(back_a, span), (zero, zero))
                norm_back(2, slot, *sums, span)

        @block
        def _():
            def back_b(span, it, carry):
                if span.start == 0:
                    gl = jnp.concatenate([glog[slot, it * 2 + k] for k in range(2)], axis=1)
                    ml = jnp.concatenate([mixed_low[slot, it * 2 + k] for k in range(2)], axis=1)
                    d_head[...] += dot_nt(gl, ml)
                for k in range(2):
                    i = it * 2 + k
                    g = fd * dy[i, span] - f1_ - fn * conv[slot, 1, i, span]
                    low = g.astype(BF16)
                    for kx, tap in enumerate((from_right(low), low, from_left(low))):
                        g_taps[i + 1, kx * width + span.start : kx * width + span.stop] = tap
                return carry

            spans = parts_of(PARTS[1])
            for span in spans:
                fd, f1_, fn = [back_factors[k, span] for k in range(3)]
                if t > 0 or span is not spans[-1]:
                    loop(grid // 2, 16, functools.partial(back_b, span), 0)
                    continue
                parts = 4
                for k in range(grid // 2):
                    back_b(span, k, 0)
                    if (k + 1) % (grid // 2 // parts) == 0:
                        mid_grad(slot, k // (grid // 2 // parts), parts)

        if t == 0:
            early_start()
        elif sz.slots == 1:
            for part in range(8):
                mid_grad(slot, part, 8)

        @block
        def _():
            def back_c(it, carry):
                sums_d, sums_n = carry
                i = it * 4
                rows = rows_of(dot(w_bwd[...], four_rows(g_taps, i)))
                for k in range(4):
                    d = (rows[k] + mixed_grad[i + k]) * slope[slot, 0, i + k]
                    dy[i + k] = d
                    sums_d = sums_d + d
                    sums_n = sums_n + d * conv[slot, 0, i + k]
                return sums_d, sums_n

            zero = jnp.zeros((width, LANES), F32)
            sums = loop(grid // 4, 8, back_c, (zero, zero))
            norm_back(0, slot, *sums)
        @block
        def _():
            fd, f1_, fn = [back_factors[k] for k in range(3)]

            if t == 0:
                late_misc()

            def back_d(it, carry):
                i = it * 2
                lows = []
                for k in range(2):
                    low = (fd * dy[i + k] - f1_ - fn * conv[slot, 0, i + k]).astype(BF16)
                    g_pad[slot, i + k + 1] = low
                    lows.append(low)
                d_in[...] += dot_nt(row_pair(feat.at[slot], i), jnp.concatenate(lows, axis=1))
                return carry

            loop(grid // 2, 16, back_d, 0)
            if t > 0:

                def back_e(it, carry):
                    i = it * 4
                    rows = rows_of(dot(v_bwd[...], four_rows(g_pad.at[slot], i)))
                    for k in range(4):
                        gs_rows[pl.ds(pl.multiple_of((i + k) * 8, 8), 8), :] = combine(rows[k], 8)
                    return carry

                loop(grid // 4, 8, back_e, 0)
                for q in range(3):
                    grad_state[q] += gs_rows[pl.ds(q, grid, stride=8), :]

    for t in reversed(range(steps)):
        if sz.slots == 1:
            step_forward(t, 0, False)
        step_backward(t, t if sz.slots > 1 else 0)

    mate = (c + 1 - 2 * core, r)
    mine = pl.ds(core * sz.late, sz.late)

    def chip_peer(k):
        if sz.ways == 1:
            return (c, row_peer(k))
        return (partner(c // 2, k // sz.rows, sz.ch // 2) * 2 + core, row_peer(wrap(k, sz.rows)))

    inputs = jnp.concatenate([d_in[0:24], d_in[24:48]], axis=1)
    for n in range(3):
        pack[n] = inputs[n * 8 : (n + 1) * 8]
    if sz.cores > 1:
        remote(pack, pack, p_send.at[0], p_recv.at[0], mate).start()
        arrived(pack, p_recv.at[0])
        late_sum[...] = late_pair[0] + late_pair[1]
    for k in far_first(sz.chips):
        remote(late_sum.at[mine], late_in.at[chip_slot], b_send.at[0], b_recv.at[0], chip_peer(k)).start()

    early_sum()

    late_in[chip_slot] = late_sum[mine]
    if sz.chips > 1:
        arrived(but_one(late_in), b_recv.at[0])
    acc = late_in[0]
    for k in range(1, sz.chips):
        acc = acc + late_in[k]
    late_fin[mine] = acc
    if sz.cores > 1:
        remote(late_fin.at[mine], late_fin.at[mine], p_send.at[1], p_recv.at[1], mate).start()
        sent(pack, p_send.at[0])
    early_left()
    if sz.chips > 1:
        sent(but_one(late_in), b_send.at[0])
    if sz.cores > 1:
        arrived(late_fin.at[mine], p_recv.at[1])
    acc = late_fin[...].reshape(32, LANES)
    turned = pltpu.roll(acc, wrap(LANES - c * co, LANES), 1)
    for n in range(4):
        total[sz.early + n] = turned[n * 8 : (n + 1) * 8]
    acc = jnp.where(row_ids(acc.shape) < 30, acc, 0.0)
    late_norm = jnp.sum(acc * acc, axis=0, keepdims=True)

    if sz.early < 8:
        total[sz.early + 4] = jnp.zeros((8, LANES), F32)
    early_end()
    acc = late_norm
    for k in range(sz.ch):
        for j in range(sz.early):
            acc = acc + ssq_early[k, j]
    grad_norm = jnp.sqrt(jnp.broadcast_to(jnp.sum(acc, axis=1, keepdims=True), (8, LANES)))
    factor = CLIP / jnp.maximum(grad_norm, CLIP)

    count = sz.early + 5
    gain_row = row_ids((8, LANES)) < 4
    for k in range(count):
        rate, decay = RATE, DECAY
        if k == sz.early + 3:
            rate = jnp.where(gain_row, GAIN_RATE, RATE)
            decay = jnp.where(gain_row, 0.0, DECAY)
        results = adam(held[0, k], total[k] * factor, held[1, k], held[2, k], rate, decay)
        for n in range(3):
            out[n * count + k] = results[n]
    row = row_ids((8, LANES))
    lost = jnp.broadcast_to(total[sz.early + 3, 6:7, 0:1], (8, LANES))
    out[3 * count] = jnp.where(row == 0, grad_norm, jnp.where(row == 1, lost, valid))
    early_shared()
    if sz.cores > 1:
        sent(late_fin.at[mine], p_send.at[1])


def adam(weight, grad, moment, square, rate, decay):
    moment = BETA_ONE * moment + (1.0 - BETA_ONE) * grad
    square = BETA_TWO * square + (1.0 - BETA_TWO) * grad * grad
    fix_one = 1.0 - BETA_ONE**STEP_NUM
    fix_two = 1.0 - BETA_TWO**STEP_NUM
    updated = weight - rate * (moment / fix_one / (jnp.sqrt(square / fix_two) + ADAM_EPS) + decay * weight)
    return updated, moment, square


def unpack_kernel(sz, packed, *refs):
    co, width = sz.co, sz.width
    count = sz.early + 5
    for n in range(3):
        new_in, new_mid, new_head, new_norm = refs[4 * n : 4 * n + 4]
        at = n * count
        for k in range(4):
            tile = jnp.concatenate([packed[at + h * 4 + k] for h in range(sz.halves)], axis=0)
            first, second = ((0, k), (1, k)) if k < 3 else ((2, 0), (2, 1))
            new_mid[first] = tile[:, :width]
            new_mid[second] = tile[:, width:]
        last = packed[at + sz.early + 4, 0 : co // 2]
        new_mid[2, 2, 0 : co // 2] = last[:, :width]
        new_mid[2, 2, co // 2 :] = last[:, width:]
        for ky in range(TAPS):
            for kx in range(TAPS):
                tile, row, lane = in_place(ky, kx)
                new_in[ky, kx] = packed[at + sz.early + tile, row : row + 4, lane : lane + co]
        new_norm[...] = packed[at + sz.early + 3, 0:4, 0:co]
        new_head[...] = packed[at + sz.early + 3, 4:6, 0:co]
    for k in range(3):
        refs[12 + k][...] = packed[3 * count, k : k + 1, 0:1]


def scratch_of(sz):
    grid, width, rows, ch, slots, steps = sz.grid, sz.width, sz.rows, sz.ch, sz.slots, sz.steps
    wide = TAPS * width

    def f32(*shape):
        return pltpu.VMEM(shape, F32)

    def bf16(*shape):
        return pltpu.VMEM(shape, BF16)

    dma = lambda *shape: pltpu.SemaphoreType.DMA(shape)
    return {
        "f_stage": f32(rows, 4, sz.local, LANES),
        "f_out": f32(rows, 4, sz.local, LANES),
        "m_own": pltpu.VMEM((sz.local, LANES), jnp.int32),
        "t_stage": f32(rows, steps, sz.local, LANES),
        "in_own": f32(3, TAPS, TAPS, 4, sz.co),
        "mid_own": f32(3, TAPS, TAPS, sz.co, width),
        "head_own": f32(3, 2, sz.co),
        "norm_own": f32(3, 4, sz.co),
        "marks_own": pltpu.VMEM((steps, sz.batch), jnp.int32),
        "held": f32(3, sz.early + 5, 8, LANES),
        "total": f32(sz.early + 5, 8, LANES),
        "small": f32(LANES, LANES),
        "ws_all": f32(ch, sz.co, LANES),
        "wm_all": bf16(ch, -(-sz.co // 16) * 16, sz.mid_lanes),
        "w_fwd": bf16(2 * width, 4 * wide),
        "w_bwd": bf16(2 * width, 4 * wide),
        "v_fwd": bf16(width, TAPS * 16),
        "v_bwd": bf16(2 * TAPS * 8, 4 * width),
        "head_back": bf16(width, 16),
        "head": bf16(16, width),
        "gains": f32(4, width, LANES),
        "current": f32(3, 3, grid, LANES),
        "states": f32(1 if slots > 1 else steps, 3, 3, grid, LANES),
        "mask": f32(5, grid, LANES),
        "feat32": f32(grid * 16, LANES),
        "feat": bf16(slots, grid + 2, 16, LANES),
        "conv": f32(slots, 2, grid, width, LANES),
        "slope": f32(slots, 2, grid, width, LANES),
        "norm_stats": f32(4, slots, width, LANES),
        "back_factors": f32(3, width, LANES),
        "hidden": f32(grid, width, LANES),
        "hidden_low": bf16(slots, grid + 2, wide, LANES),
        "mixed_low": bf16(slots, grid, width, LANES),
        "logits": f32(2, grid, LANES),
        "saved": f32(slots, SAVED, grid, LANES),
        "dy": f32(grid, width, LANES),
        "mixed_grad": f32(grid, width, LANES),
        "glog32": f32(grid * 16, LANES),
        "glog": bf16(slots, grid, 16, LANES),
        "g_pad": bf16(slots, grid + 2, width, LANES),
        "g_taps": bf16(grid + 2, wide, LANES),
        "gs_rows": f32(grid * 8, LANES),
        "grad_state": f32(3, grid, LANES),
        "d_mid": f32(wide, wide),
        "d_in": f32(TAPS * 16, width),
        "d_head": f32(16, width),
        "d_norm": f32(4, width, LANES),
        "loss": f32(grid, LANES),
        "early": f32(ch * sz.early, 9, LANES),
        "early_in": f32(sz.owned, sz.sources, 9, LANES),
        "early_fin": f32(sz.early, 9, LANES),
        "blank": f32(ch, rows, 1, LANES),
        "ssq_early": f32(ch, sz.early, 1, LANES),
        "late_pair": f32(2, 4, 8, LANES),
        "late_sum": f32(4, 8, LANES),
        "late_in": f32(sz.chips, sz.late, 8, LANES),
        "late_fin": f32(4, 8, LANES),
        "ready": pltpu.SemaphoreType.REGULAR,
        "local_sem": dma(16),
        "f_sem": dma(2),
        "t_sem": dma(2),
        "v_sem": dma(2),
        "w_sem": dma(2),
        "e_send": dma(1),
        "e_recv": dma(sz.owned),
        "g_send": dma(sz.owned),
        "g_recv": dma(1),
        "s_send": dma(sz.owned),
        "s_recv": dma(1),
        "b_send": dma(1),
        "b_recv": dma(1),
        "p_send": dma(2),
        "p_recv": dma(2),
    }


def shards(mesh, fields, targets, fluid, keyframes, *rest):
    params, firsts, seconds = rest[0:4], rest[4:8], rest[8:12]

    def native(leaves):
        return (leaves[0], jnp.swapaxes(leaves[1], 2, 3), leaves[2].T, leaves[3])

    params, firsts, seconds = native(params), native(firsts), native(seconds)
    sz = Sizes(mesh, fields.shape, targets.shape, params[0].shape[3])
    marks = keyframes.T
    vmem = pl.BlockSpec(memory_space=pltpu.VMEM)
    hbm = pl.BlockSpec(memory_space=pl.ANY)
    alone = sz.rows == 1 and sz.ch == 1
    packed = pl.pallas_call(
        functools.partial(train_kernel, sz),
        out_shape=pltpu.VMEM((3 * (sz.early + 5) + 1, 8, LANES), F32),
        in_specs=[hbm] * 16,
        out_specs=vmem,
        scratch_shapes=list(scratch_of(sz).values()),
        compiler_params=pltpu.CompilerParams(
            collective_id=None if alone else 0, has_side_effects=True, vmem_limit_bytes=60 << 20
        ),
        name="train",
    )(fields.reshape(sz.rows, sz.per_rows, *fields.shape[1:]), targets, fluid, marks, *params, *firsts, *seconds)
    shapes = [jax.ShapeDtypeStruct(leaf.shape, F32) for leaf in params] * 3
    shapes += [jax.ShapeDtypeStruct((1, 1), F32)] * 3
    results = pl.pallas_call(
        functools.partial(unpack_kernel, sz),
        out_shape=tuple(shapes),
        in_specs=[vmem],
        out_specs=tuple([vmem] * 15),
        name="unpack",
    )(pltpu.with_memory_space_constraint(packed, pltpu.VMEM))
    outs = []
    for n in range(3):
        outs.extend(native(results[4 * n : 4 * n + 4]))
    return (*outs, *[leaf.reshape(()) for leaf in results[12:]])


def solution(mesh):
    split = (P(None, None, None, "ch"), P(None, None, None, "ch"), P("ch", None), P(None, "ch"))
    return jax.shard_map(
        functools.partial(shards, mesh),
        mesh=mesh,
        in_specs=(
            P(None, None, "rows", None),
            P(None, None, "rows", None),
            P("rows", None),
            P(),
            *split,
            *split,
            *split,
        ),
        out_specs=(*split, *split, *split, P(), P(), P()),
        check_vma=False,
    )
```
